32 devices in a mesh: seq: 16 (over z, y, core), tp: 2 (over x).
Axes of the slice: x: 2, y: 2, z: 4, core: 2. Of those that a mesh axis runs over, the one named last changes fastest.
Arguments:
- inputs: bfloat16 [2, 2048, 2048], P(None, 'seq', 'tp'), may hold values from -6 to 6
- segments: int32 [2, 2048], P(None, 'seq'), may hold values from 0 to 12, as said below
- keys: bfloat16 [2, 2048, 2048], P(None, 'seq', 'tp'), may hold values from -9 to 9
- values: bfloat16 [2, 2048, 2048], P(None, 'seq', 'tp'), may hold values from -6 to 6
- attn_gain: float32 [2048], replicated, may hold values from 0.5 to 1.5
- query_weight: bfloat16 [2048, 2048], P(None, 'tp'), may hold values from -0.125 to 0.125
- out_weight: bfloat16 [2048, 2048], P(None, 'tp'), may hold values from -0.75 to 0.75
- ffn_gain: float32 [2048], replicated, may hold values from 0.5 to 1.5
- gate_weight: bfloat16 [2048, 5504], P(None, 'tp'), may hold values from -0.125 to 0.125
- up_weight: bfloat16 [2048, 5504], P(None, 'tp'), may hold values from -0.125 to 0.125
- down_weight: bfloat16 [2048, 5504], P(None, 'tp'), may hold values from -0.078125 to 0.078125
- cotangent: bfloat16 [2, 2048, 2048], P(None, 'seq', 'tp'), may hold values from -6 to 6
Outputs:
- mixed: bfloat16 [2, 2048, 2048], P(None, 'seq', 'tp')
- input_grad: float32 [2, 2048, 2048], P(None, 'seq', 'tp')
- key_grad: float32 [2, 2048, 2048], P(None, 'seq', 'tp')
- value_grad: float32 [2, 2048, 2048], P(None, 'seq', 'tp')
- attn_gain_grad: float32 [2048], P('seq')
- query_grad: float32 [2048, 2048], P('seq', 'tp')
- out_grad: float32 [2048, 2048], P('seq', 'tp')
- ffn_gain_grad: float32 [2048], P('seq')
- gate_grad: float32 [2048, 5504], P('seq', 'tp')
- up_grad: float32 [2048, 5504], P('seq', 'tp')
- down_grad: float32 [2048, 5504], P('seq', 'tp')
The draws below stay inside these ranges and needn't reach their ends.
Inputs may be any that keep to these rules, and one draw needn't show every extreme that they name: `segments`: document numbers never fall along a row.
All inputs are finite; a program needn't handle non-finite values.
Results may differ from the reference program's by a relative error of at most 0.02.
Values may be sent and summed in bfloat16 or wider, within the bound.
A program may use at most 448 MiB of HBM per device.

```python
import math
import jax
import jax.numpy as jnp
from jax import lax

D = 2048
HEADS = 16
HEAD_DIM = 128
FF = 5504
TOK_ROW = 128
ROWS = 2
CUTS = 12
LEN = 2048


def draw_segments(key, part):
    key = jax.random.fold_in(key, 7)
    pick_key, side_key, offset_key, top_key, heavy_key = jax.random.split(key, 5)
    long_row = jax.random.randint(pick_key, (), 0, ROWS)
    sides = jax.random.randint(side_key, (ROWS, CUTS), 0, 2)
    offsets = jax.random.randint(offset_key, (ROWS, CUTS), 1, TOK_ROW)
    edge_cuts = jnp.where(sides == 0, offsets, LEN - offsets)
    tops = jax.random.randint(top_key, (ROWS, CUTS), 2, LEN + 1)
    heavy_cuts = jax.random.randint(heavy_key, (ROWS, CUTS), 1, tops)
    row_ids = jnp.arange(ROWS, dtype=jnp.int32)[:, None]
    cuts = jnp.where(row_ids == long_row, edge_cuts, heavy_cuts)
    positions = jnp.arange(LEN, dtype=jnp.int32)
    return jnp.sum((positions[None, :, None] >= cuts[:, None, :]).astype(jnp.int32), axis=-1).astype(jnp.int32)


def levels(stream_key, shape, pieces, least, top_value):
    loudness, own = 1.0, jax.random.fold_in(stream_key, 6)
    for axis_at, parts in pieces:
        heights = jnp.exp(jax.random.uniform(jax.random.fold_in(own, axis_at), (parts,), jnp.float32, least / len(pieces), top_value / len(pieces)))
        loudness = loudness * jnp.repeat(heights, shape[axis_at] // parts).reshape([-1 if axis == axis_at else 1 for axis in range(len(shape))])
    return loudness


def centred(rng, extent, deviation, most, pieces=(), kind=jnp.bfloat16):
    drawn = jax.random.normal(rng, extent, jnp.float32) * deviation
    if len(pieces) > 0:
        drawn = levels(rng, extent, pieces, -0.22, 0.18) * drawn
    return jnp.clip(drawn, min=-most, max=most).astype(kind)


def setup_inputs(seed: int = 0) -> dict:
    key_of = jax.random.split(jax.random.key(seed), 13)
    inputs = centred(key_of[0], (ROWS, LEN, D), 1.0, 6.0, ((1, 16), (2, 2)))
    segments = draw_segments(jax.random.fold_in(key_of[12], 71), 0)
    keys = centred(key_of[2], (ROWS, LEN, D), 1.5, 9.0, ((1, 16), (2, 2)))
    values = centred(key_of[3], (ROWS, LEN, D), 1.0, 6.0, ((1, 16), (2, 2)))
    attn_gain = jnp.clip(1.0 + 0.1 * jax.random.normal(key_of[4], (D,), jnp.float32), 0.5, 1.5)
    query_weight = centred(key_of[5], (D, D), D ** -0.5, 0.125, ((1, 2),))
    out_weight = centred(key_of[6], (D, D), (D // 32) ** -0.5, 0.75, ((1, 2),))
    ffn_gain = jnp.clip(1.0 + 0.1 * jax.random.normal(key_of[7], (D,), jnp.float32), 0.5, 1.5)
    gate_weight = centred(key_of[8], (D, FF), D ** -0.5, 0.125, ((1, 2),))
    up_weight = centred(key_of[9], (D, FF), D ** -0.5, 0.125, ((1, 2),))
    down_weight = centred(key_of[10], (D, FF), FF ** -0.5, 0.078125, ((1, 2),))
    cotangent = centred(key_of[11], (ROWS, LEN, D), 1.0, 6.0, ((1, 16), (2, 2)))
    return dict(inputs=inputs, segments=segments, keys=keys, values=values, attn_gain=attn_gain, query_weight=query_weight, out_weight=out_weight, ffn_gain=ffn_gain, gate_weight=gate_weight, up_weight=up_weight, down_weight=down_weight, cotangent=cotangent)


EPSILON = 1e-06
NEGATIVE_FILL = -1e+30
HIGHEST = lax.Precision.HIGHEST

@jax.custom_vjp
def low(v):
    return lax.optimization_barrier(v.astype(jnp.bfloat16)).astype(jnp.float32)

@jax.custom_vjp
def low_back(v):
    return v

def low_keep(v):
    return (low(v), None)

def low_pass(kept, grad):
    return (grad,)

def back_keep(v):
    return (v, None)

def back_low(kept, grad):
    return (low(grad),)
low.defvjp(low_keep, low_pass)
low_back.defvjp(back_keep, back_low)

def normalize(values_in, gain_in):
    return values_in * lax.rsqrt(lax.optimization_barrier(jnp.mean(values_in * values_in, axis=-1, keepdims=True)) + EPSILON) * gain_in

def attend(packed):
    query_row, key_row, value_row, segment_row = packed
    length = query_row.shape[0]
    key_block = math.gcd(length, 512)
    key_heads = key_row.reshape(length, HEADS, HEAD_DIM)
    value_heads = value_row.reshape(length, HEADS, HEAD_DIM)
    positions = jnp.arange(length, dtype=jnp.int32)
    query_blocks = query_row.reshape(length // key_block, key_block, HEADS, HEAD_DIM)
    segment_blocks = segment_row.reshape(length // key_block, key_block)
    position_blocks = positions.reshape(length // key_block, key_block)

    def one_block(block_args):
        query_block, query_segment, query_position = block_args
        scores = low_back(jnp.einsum('qhe,khe->hqk', query_block, key_heads, precision=HIGHEST))
        allowed = (positions[None, :] <= query_position[:, None]) & (segment_row[None, :] == query_segment[:, None])
        scores = jnp.where(allowed[None], scores, NEGATIVE_FILL)
        largest = lax.optimization_barrier(jnp.max(scores, axis=-1, keepdims=True))
        weights = jnp.where(allowed[None], jnp.exp(scores - largest), 0.0)
        probs = weights / lax.optimization_barrier(jnp.sum(weights, axis=-1, keepdims=True))
        return jnp.einsum('hqk,khe->qhe', low(probs), value_heads, precision=HIGHEST)
    result = lax.map(jax.checkpoint(one_block), (query_blocks, segment_blocks, position_blocks))
    return result.reshape(length, HEADS * HEAD_DIM)

def reference(inputs, segments, keys, values, attn_gain, query_weight, out_weight, ffn_gain, gate_weight, up_weight, down_weight, cotangent):

    def forward(stream, key_all, value_all, gain_one, w_query, w_out, gain_two, w_gate, w_up, w_down):
        normed_one = low(normalize(stream, gain_one))
        query = low_back(low(jnp.einsum('rld,de->rle', normed_one, w_query, precision=HIGHEST) * HEAD_DIM ** (-0.5)))
        attended = lax.map(attend, (query, key_all, value_all, segments))
        attended = low_back(low(attended))
        branch = low_back(jnp.einsum('rlh,dh->rld', attended, w_out, precision=HIGHEST))
        middle = stream + branch
        normed_two = low(normalize(middle, gain_two))
        gate = low_back(jnp.einsum('rld,df->rlf', normed_two, w_gate, precision=HIGHEST))
        up_proj = low_back(jnp.einsum('rld,df->rlf', normed_two, w_up, precision=HIGHEST))
        hidden = low(gate * jax.nn.sigmoid(gate) * up_proj)
        return middle + jnp.einsum('rlf,df->rld', hidden, w_down, precision=HIGHEST)
    primals = (inputs.astype(jnp.float32), keys.astype(jnp.float32), values.astype(jnp.float32), attn_gain.astype(jnp.float32), query_weight.astype(jnp.float32), out_weight.astype(jnp.float32), ffn_gain.astype(jnp.float32), gate_weight.astype(jnp.float32), up_weight.astype(jnp.float32), down_weight.astype(jnp.float32))
    output, pullback = jax.vjp(forward, *primals)
    grads = pullback(cotangent.astype(jnp.float32))
    return (output.astype(jnp.bfloat16), grads[0], grads[1], grads[2], grads[3], grads[4], grads[5], grads[6], grads[7], grads[8], grads[9])
```

```python
import functools
import math

import jax
import jax.numpy as jnp
from jax import lax
from jax.experimental import pallas as pl
from jax.experimental.pallas import tpu as pltpu
from jax.sharding import PartitionSpec as P

HEAD_DIM = 128
CUTS = 12


EPSILON = 1e-06
NEGATIVE_FILL = -1e30

MESH = pl.DeviceIdType.MESH
BF = jnp.bfloat16
F32 = jnp.float32
MIB = 1 << 20
PLANE = 4
LANE = 128


def dot_nn(a, b):
    return lax.dot_general(a, b, (((1,), (0,)), ((), ())), preferred_element_type=F32)


def dot_nt(a, b):
    return lax.dot_general(a, b, (((1,), (1,)), ((), ())), preferred_element_type=F32)


def dot_tn(a, b):
    return lax.dot_general(a, b, (((0,), (0,)), ((), ())), preferred_element_type=F32)


def aligned(index, size):
    return pl.ds(pl.multiple_of(index * size, size), size)


class Place:
    def __init__(self, n):
        self.n = n
        self.s = lax.axis_index("seq")
        self.t = lax.axis_index("tp")
        self.z = self.s // PLANE
        self.p = lax.rem(self.s, PLANE)
        self.y = self.p // 2
        self.c = lax.rem(self.p, 2)
        base = self.z * PLANE
        self.core_p = self.y * 2 + 1 - self.c
        self.side_p = (1 - self.y) * 2 + self.c
        self.cross_p = (1 - self.y) * 2 + 1 - self.c
        self.core = (base + self.core_p, self.t)
        self.side = (base + self.side_p, self.t)
        self.cross = (base + self.cross_p, self.t)
        self.twin = (self.s, 1 - self.t)

    def other(self, k):
        return lax.rem(self.s + k, self.n)

    def enter(self):
        barrier = pltpu.get_barrier_semaphore()

        def greet(k, unused):
            pl.semaphore_signal(barrier, inc=1, device_id=(self.other(k), self.t), device_id_type=MESH)
            return unused

        lax.fori_loop(1, self.n, greet, 0)
        pl.semaphore_signal(barrier, inc=1, device_id=self.twin, device_id_type=MESH)
        pl.semaphore_wait(barrier, self.n)


def remote(src, dst, send, recv, device):
    return pltpu.make_async_remote_copy(
        src_ref=src, dst_ref=dst, send_sem=send, recv_sem=recv, device_id=device, device_id_type=MESH
    )


class Spread:
    def __init__(self, place, src, dst, send, recv, local):
        self.place, self.src, self.dst, self.send, self.recv, self.local = place, src, dst, send, recv, local

    def copy(self, k):
        place = self.place
        d = place.other(k)
        return remote(self.src(d), self.dst(), self.send.at[k], self.recv.at[k], (d, place.t))

    def own(self):
        return pltpu.make_async_copy(self.src(self.place.s), self.dst(), self.local)

    def start(self):
        self.own().start()

        def one(k, unused):
            self.copy(k).start()
            return unused

        lax.fori_loop(1, self.place.n, one, 0)

    def start_to(self, d, unused):
        k = lax.rem(d - self.place.s + self.place.n, self.place.n)

        @pl.when(k == 0)
        def _():
            self.own().start()

        @pl.when(k != 0)
        def _():
            self.copy(k).start()

        return unused

    def wait(self):
        self.own().wait()

        def one(k, unused):
            self.copy(k).wait()
            return unused

        lax.fori_loop(1, self.place.n, one, 0)


def attention_masks(seg_all, seg_row, seg_col, n, tok):
    def one(i, unused):
        piece = seg_all[i]
        seg_row[:, aligned(i, tok)] = piece
        seg_col[aligned(i, tok), :] = jnp.transpose(jnp.broadcast_to(piece, (tok, tok)))
        return unused

    lax.fori_loop(0, n, one, 0)


def readable(seg_col, seg_row, key_block, query_block, block):
    key_seg = seg_col[aligned(key_block, block), :]
    key_seg = jnp.concatenate([key_seg] * (block // LANE), axis=1)
    query_seg = seg_row[:, aligned(query_block, block)]
    key_pos = key_block * block + lax.broadcasted_iota(jnp.int32, (block, block), 0)
    query_pos = query_block * block + lax.broadcasted_iota(jnp.int32, (block, block), 1)
    return (key_seg == query_seg) & (key_pos <= query_pos)


def forward_kernel(
    geo,
    x_in, cot_in, key_in, value_in, seg_in, gain_one, gain_two, wq_in, wo_in,
    x_all, cot_all, left_cot, middle, normed_two, left_two, attended, unit_q, unit_k, unit_v, unit_o, lse, seg_all,
    wq, wo, normed_one, query, value_t, seg_row, seg_col, part, part_in, cot_split,
    tp_s, tp_r, a_s, a_r, br_s, br_r, l_s, l_r, loc,
):
    n, rows, tok, width, half, heads, length = geo
    place = Place(n)
    s, t = place.s, place.t
    place.enter()
    row_s, head_s = s // heads, lax.rem(s, heads)
    half_at = aligned(t, half)

    to_x = remote(x_in, x_all.at[:, half_at], tp_s.at[0], tp_r.at[0], place.twin)
    to_x.start()
    own_x = pltpu.make_async_copy(x_in, x_all.at[:, half_at], loc.at[0])
    own_x.start()
    load_q = pltpu.make_async_copy(wq_in, wq, loc.at[1])
    load_q.start()

    def piece(ref):
        return lambda d: ref.at[aligned(d // heads, tok), aligned(lax.rem(d, heads), HEAD_DIM)]

    keys = Spread(place, piece(key_in), lambda: unit_k.at[aligned(s, tok), :], a_s.at[0], a_r.at[0], loc.at[2])
    vals = Spread(place, piece(value_in), lambda: unit_v.at[aligned(s, tok), :], a_s.at[1], a_r.at[1], loc.at[3])
    segs = Spread(place, lambda d: seg_in.at[d // heads], lambda: seg_all.at[s], a_s.at[2], a_r.at[2], loc.at[4])
    qrys = Spread(place, piece(query), lambda: unit_q.at[aligned(s, tok), :], a_s.at[3], a_r.at[3], loc.at[5])
    segs.start()
    keys.start()
    vals.start()
    to_cot = remote(cot_in, cot_all.at[:, half_at], tp_s.at[1], tp_r.at[1], place.twin)
    to_cot.start()
    own_cot = pltpu.make_async_copy(cot_in, cot_all.at[:, half_at], loc.at[6])
    own_cot.start()
    load_o = pltpu.make_async_copy(wo_in, wo, loc.at[7])
    load_o.start()

    own_x.wait()
    to_x.wait()
    step = 64

    def norm_one(i, unused):
        at = aligned(i, step)
        x = x_all[at, :].astype(F32)
        root = lax.rsqrt(jnp.mean(x * x, axis=-1, keepdims=True) + EPSILON)
        normed_one[at, :] = (x * root * gain_one[...]).astype(BF)
        return unused

    lax.fori_loop(0, rows * tok // step, norm_one, 0)
    load_q.wait()
    query[...] = (dot_nn(normed_one[...], wq[...]) * HEAD_DIM ** (-0.5)).astype(BF)
    qrys.start()

    segs.wait()
    attention_masks(seg_all, seg_row, seg_col, n, tok)
    keys.wait()
    vals.wait()

    def turn(i, unused):
        at = aligned(i, tok)
        value_t[:, at] = jnp.transpose(unit_v[at, :].astype(F32)).astype(BF)
        return unused

    lax.fori_loop(0, n, turn, 0)
    qrys.wait()

    back = Spread(
        place,
        lambda d: unit_o.at[aligned(d, tok), :],
        lambda: attended.at[aligned(row_s, tok), aligned(head_s, HEAD_DIM)],
        a_s.at[4], a_r.at[4], loc.at[8],
    )
    block = 512
    owners = block // tok

    def query_step(qi, unused):
        query_block = unit_q[aligned(qi, block), :]

        def key_step(j, carry):
            top, total, acc = carry
            kj = qi - j
            scores = dot_nt(unit_k[aligned(kj, block), :], query_block)
            scores = jnp.where(readable(seg_col, seg_row, kj, qi, block), scores, NEGATIVE_FILL)
            new_top = jnp.maximum(top, jnp.max(scores, axis=0, keepdims=True))
            weights = jnp.exp(scores - new_top)
            decay = jnp.exp(top - new_top)
            total = total * decay + jnp.sum(weights, axis=0, keepdims=True)
            acc = acc * decay + dot_nn(value_t[:, aligned(kj, block)], weights.astype(BF))
            return new_top, total, acc

        start = (
            jnp.full((1, block), NEGATIVE_FILL, F32),
            jnp.zeros((1, block), F32),
            jnp.zeros((HEAD_DIM, block), F32),
        )
        top, total, acc = lax.fori_loop(0, qi + 1, key_step, start)
        lse[:, aligned(qi, block)] = top + jnp.log(total)
        unit_o[aligned(qi, block), :] = jnp.transpose(acc / total).astype(BF)

        return lax.fori_loop(qi * owners, (qi + 1) * owners, back.start_to, unused)

    lax.fori_loop(0, length // block, query_step, 0)

    own_cot.wait()
    to_cot.wait()
    split_rows(cot_all, cot_split, n)
    plane_cot = Plane(place, cot_split, left_cot, l_s, l_r, loc.at[9], rows * tok)
    plane_cot.start()
    load_o.wait()
    back.wait()

    chunks = part.shape[0]
    wide = width // chunks

    def to_twin(i):
        return remote(part.at[i], part_in.at[i], br_s.at[i], br_r.at[i], place.twin)

    def project(i, unused):
        part[i] = dot_nt(attended[...], wo[aligned(i, wide), :]).astype(BF)
        to_twin(i).start()
        return unused

    lax.fori_loop(0, chunks, project, 0)
    plane_cot.forward()

    def add(i, square):
        to_twin(i).wait()
        at = aligned(i, wide)
        both = part[i].astype(F32) + part_in[i].astype(F32)
        mid = x_all[:, at].astype(F32) + both
        middle[:, at] = mid
        return square + jnp.sum(mid * mid, axis=-1, keepdims=True)

    square = lax.fori_loop(0, chunks, add, jnp.zeros((rows * tok, 1), F32))
    root_two = lax.rsqrt(square * (1.0 / width) + EPSILON)

    def norm_two(i, unused):
        at = aligned(i, wide)
        normed_two[:, at] = (middle[:, at] * root_two * gain_two[:, at]).astype(BF)
        return unused

    lax.fori_loop(0, chunks, norm_two, 0)
    split_rows(normed_two, left_two, n)
    plane_cot.finish()


def split_rows(whole, split, n):
    blk = whole.shape[1] * 2 // n
    for zy in range(n // 2):
        z, y = divmod(zy, 2)
        split[y, :, z * blk : (z + 1) * blk] = whole[:, zy * blk : (zy + 1) * blk]


class Plane:
    def __init__(self, place, split, left, send, recv, local, tokens):
        self.place, self.tokens, self.left = place, tokens, left
        to = left.at[aligned(place.p, tokens), :]
        self.own = pltpu.make_async_copy(split.at[place.y], to, local)
        self.to_core = remote(split.at[place.y], to, send.at[0], recv.at[0], place.core)
        self.to_side = remote(split.at[1 - place.y], to, send.at[1], recv.at[1], place.side)
        passed = left.at[aligned(place.side_p, tokens), :]
        self.on = remote(passed, passed, send.at[2], recv.at[2], place.core)

    def start(self):
        self.to_side.start()
        self.own.start()
        self.to_core.start()

    def forward(self):
        self.to_side.wait()
        self.on.start()

    def finish(self):
        self.own.wait()
        self.to_core.wait()
        self.on.wait()


def vm(shape, dtype):
    return jax.ShapeDtypeStruct(shape, dtype)


def forward_part(geo, x, cot, keys, values, segf, gain_one, gain_two, wq, wo):
    n, rows, tok, width, half, heads, length = geo
    tokens = rows * tok
    dma = pltpu.SemaphoreType.DMA
    anywhere, here = pl.BlockSpec(memory_space=pl.ANY), pl.BlockSpec(memory_space=pltpu.VMEM)
    outs = [
        vm((tokens, width), BF),
        vm((tokens, width), BF),
        vm((PLANE * tokens, width // 2), BF),
        vm((tokens, width), F32),
        vm((tokens, width), BF),
        vm((2, tokens, width // 2), BF),
        vm((tokens, half), BF),
        vm((length, HEAD_DIM), BF),
        vm((length, HEAD_DIM), BF),
        vm((length, HEAD_DIM), BF),
        vm((length, HEAD_DIM), BF),
        vm((1, length), F32),
        vm((n, 1, tok), F32),
    ]
    chunks = 4
    return pl.pallas_call(
        functools.partial(forward_kernel, geo),
        out_shape=outs,
        in_specs=[anywhere] * 5 + [here] * 2 + [anywhere] * 2,
        out_specs=[here] * len(outs),
        scratch_shapes=[
            pltpu.VMEM(wq.shape, BF),
            pltpu.VMEM(wo.shape, BF),
            pltpu.VMEM((tokens, width), BF),
            pltpu.VMEM((tokens, half), BF),
            pltpu.VMEM((HEAD_DIM, length), BF),
            pltpu.VMEM((1, length), F32),
            pltpu.VMEM((length, LANE), F32),
            pltpu.VMEM((chunks, tokens, width // chunks), BF),
            pltpu.VMEM((chunks, tokens, width // chunks), BF),
            pltpu.VMEM((2, tokens, width // 2), BF),
            dma((2,)), dma((2,)), dma((5, n)), dma((5, n)), dma((chunks,)), dma((chunks,)), dma((3,)), dma((3,)), dma((10,)),
        ],
        compiler_params=pltpu.CompilerParams(
            collective_id=0, has_side_effects=True, vmem_limit_bytes=48 * MIB
        ),
        name="attention_forward",
    )(x, cot, keys, values, segf, gain_one, gain_two, wq, wo)


def ffn_kernel(
    blk, ff, x_ref, g_ref, wg_ref, wu_ref, wd_ref, hidden, d_gate, d_up, d_two, mixed, acc_two, acc_mixed
):
    i = pl.program_id(0)

    @pl.when(i == 0)
    def _():
        acc_two[...] = jnp.zeros_like(acc_two)
        acc_mixed[...] = jnp.zeros_like(acc_mixed)

    inside = lax.broadcasted_iota(jnp.int32, wg_ref.shape, 1) < ff - i * blk
    wg, wu, wd = (jnp.where(inside, w[...], jnp.zeros((), BF)) for w in (wg_ref, wu_ref, wd_ref))
    x, g = x_ref[...], g_ref[...]
    gate, up = dot_nn(x, wg), dot_nn(x, wu)
    d_hid = dot_nn(g, wd)
    sigma = jax.nn.sigmoid(gate)
    act = gate * sigma
    hid = (act * up).astype(BF)
    dg = (d_hid * up * sigma * (1.0 + gate * (1.0 - sigma))).astype(BF)
    du = (d_hid * act).astype(BF)
    hidden[...], d_gate[...], d_up[...] = hid, dg, du
    acc_two[...] += dot_nt(dg, wg) + dot_nt(du, wu)
    acc_mixed[...] += dot_nt(hid, wd)

    @pl.when(i == pl.num_programs(0) - 1)
    def _():
        d_two[...] = acc_two[...].astype(BF)
        mixed[...] = acc_mixed[...].astype(BF)


def ffn_part(padded, normed_two, cot_all, wg, wu, wd):
    tokens, width = normed_two.shape
    ff = wg.shape[1]
    blk = 256
    whole = pl.BlockSpec((tokens, width), lambda i: (0, 0))
    weight = pl.BlockSpec((width, blk), lambda i: (0, i))
    out = pl.BlockSpec((tokens, blk), lambda i: (0, i))
    return pl.pallas_call(
        functools.partial(ffn_kernel, blk, ff),
        grid=(padded // blk,),
        out_shape=[vm((tokens, padded), BF)] * 3 + [vm((tokens, width), BF)] * 2,
        in_specs=[whole, whole, weight, weight, weight],
        out_specs=[out, out, out, whole, whole],
        scratch_shapes=[pltpu.VMEM((tokens, width), F32)] * 2,
        compiler_params=pltpu.CompilerParams(
            dimension_semantics=("arbitrary",), vmem_limit_bytes=48 * MIB
        ),
        name="feed_forward",
    )(normed_two, cot_all, wg, wu, wd)


class Gather:
    def __init__(self, place, whole, land, send, recv, local, tokens):
        cols = land.shape[1]
        to = land.at[aligned(place.p, tokens), :]

        def half(c):
            return whole.at[:, aligned(c, cols)]

        c = place.c
        self.own = pltpu.make_async_copy(half(c), to, local)
        self.away = [
            remote(half(c), to, send.at[0], recv.at[0], place.side),
            remote(half(1 - c), to, send.at[1], recv.at[1], place.cross),
            remote(half(1 - c), to, send.at[2], recv.at[2], place.core),
        ]

    def start(self):
        self.own.start()
        for copy in self.away:
            copy.start()

    def wait(self):
        self.own.wait()
        for copy in self.away:
            copy.wait()


class Line:
    def __init__(self, place, nz, blk, land, left, move, got, total, out, sems, work):
        self.place, self.nz, self.blk = place, nz, blk
        self.land, self.left, self.move, self.got, self.total, self.out = land, left, move, got, total, out
        self.cols = land.shape[1]
        self.mv, self.lv, self.acc, self.stage, self.load_sem = work
        self.send, self.recv, self.end_s, self.end_r, self.end_l = sems

    def load(self, left_too):
        a = pltpu.make_async_copy(self.land, self.mv.at[:, : self.cols], self.load_sem.at[0])
        a.start()
        if left_too:
            b = pltpu.make_async_copy(self.left, self.lv, self.load_sem.at[1])
            b.start()
            b.wait()
        a.wait()

    def product(self, b):
        return dot_tn(self.lv[:, aligned(b, self.blk)], self.mv[:, : self.cols])

    def take(self, slot):
        self.arrival(slot).wait_recv()
        copy = pltpu.make_async_copy(self.got.at[slot], self.stage.at[:, : self.cols], self.load_sem.at[2])
        copy.start()
        copy.wait()
        return self.stage[:, : self.cols].astype(F32)

    def arrival(self, slot):
        return remote(self.move.at[0], self.got.at[slot], self.send.at[0], self.recv.at[slot], self.place.core)

    def route(self, j):
        z, nz = self.place.z, self.nz
        b = jnp.where(z < nz // 2, nz - 1 - j, j)
        b = jnp.where((j == nz - 2) & (z == 1), 0, b)
        b = jnp.where((j == nz - 2) & (z == nz - 2), nz - 1, b)
        up = b > z
        to = jnp.where(up, z + 1, z - 1)
        slot_in = jnp.where(up, b - z, nz - z + b)
        slot_out = jnp.where(up, b - to, nz - to + b)
        keep = jnp.where(up, b - 1, b)
        last = jnp.where(up, z == 0, z == nz - 1)
        device = (to * PLANE + self.place.p, self.place.t)
        out = remote(self.move.at[keep], self.got.at[slot_out], self.send.at[keep], self.recv.at[slot_out], device)
        return b, slot_in, keep, last, out

    def step(self, j):
        b, slot_in, keep, last, out = self.route(j)
        self.acc[:, : self.cols] = self.product(b)

        @pl.when(last)
        def _():
            self.move[keep] = self.acc[:, : self.cols].astype(BF)

        @pl.when(jnp.logical_not(last))
        def _():
            self.move[keep] = (self.acc[:, : self.cols] + self.take(slot_in)).astype(BF)

        out.start()

    def steps(self):
        def one(j, unused):
            self.step(j)
            return unused

        lax.fori_loop(0, self.nz - 1, one, 0)

    def own_block(self):
        self.total[...] = self.product(self.place.z)

    def ends(self):
        half = self.blk // 2
        c, core = self.place.c, self.place.core
        columns = self.out.at[:, aligned(c, self.cols)]
        away = remote(self.total.at[aligned(1 - c, half), :], columns, self.end_s, self.end_r, core)
        here = pltpu.make_async_copy(self.total.at[aligned(c, half), :], columns, self.end_l)
        return away, here

    def finish(self):
        z, nz = self.place.z, self.nz

        @pl.when(z > 0)
        def _():
            self.total[...] += self.take(0)

        @pl.when(z < nz - 1)
        def _():
            self.total[...] += self.take(nz)

        for copy in self.ends():
            copy.start()

    def drain(self):
        def one(j, unused):
            self.route(j)[4].wait_send()
            return unused

        lax.fori_loop(0, self.nz - 1, one, 0)
        for copy in self.ends():
            copy.wait()


def backward_kernel(
    geo,
    hidden, d_gate, d_up, d_two, mixed, left_cot, left_two, middle_in, x_in, cot_in, att_in,
    q_in, k_in, v_in, o_in, lse_in, seg_in, wo_in, wq_in, gain_one, gain_two,
    ffn_in, input_grad, d_keys, d_values, gains,
    out_down, out_gate, out_up, out_out, out_query,
    m_down, m_gate, m_up, m_out, m_query, l_two, l_err, l_one,
    g_down, g_gate, g_up, g_out, g_query,
    mid, x_all, cot_all, two_own, two_in, one_part, one_in, err, one, weight, d_att,
    uq, uk, uv, uo, udo, lse, seg_all, seg_row, seg_col, k_t, delta, dk_acc, dv_acc, udq, udk, udv, dq,
    gain_part, gain_in,
    s_down, s_gate, s_up, s_out, s_query, t_down, t_gate, t_up, t_out, t_query,
    mv, lv, acc, stage,
    tp_s, tp_r, a_s, a_r, me_s, me_r, le_s, le_r, c_s, c_r, e_s, e_r, e_l, loc, work_sem,
):
    n, rows, tok, width, half, heads, length = geo
    tokens = rows * tok
    blk = 2 * width // n
    nz = n // PLANE
    place = Place(n)
    s, t, z = place.s, place.t, place.z
    row_s, head_s = s // heads, lax.rem(s, heads)
    place.enter()
    mine = aligned(t, half)
    chunk = tokens // 4

    def two_copy(i):
        at = aligned(i, chunk)
        return remote(d_two.at[at, :], two_in.at[at, :], tp_s.at[i], tp_r.at[i], place.twin)

    for i in range(4):
        two_copy(i).start()
    ffn_copy = remote(mixed.at[:, aligned(1 - t, half)], ffn_in, tp_s.at[4], tp_r.at[4], place.twin)
    ffn_copy.start()

    gathers = [
        Gather(place, whole, land, me_s.at[i], me_r.at[i], loc.at[i], tokens)
        for i, (whole, land) in enumerate(
            ((hidden, m_down), (d_gate, m_gate), (d_up, m_up), (att_in, m_out), (dq, m_query))
        )
    ]
    lefts = [
        Plane(place, split, land, le_s.at[i], le_r.at[i], loc.at[5 + i], tokens)
        for i, (split, land) in enumerate(((left_two, l_two), (err, l_err), (one, l_one)))
    ]
    work = (mv, lv, acc, stage, work_sem)
    lines = [
        Line(place, nz, blk, *refs, (c_s.at[i], c_r.at[i], e_s.at[i], e_r.at[i], e_l.at[i]), work)
        for i, refs in enumerate((
            (m_down, left_cot, s_down, g_down, t_down, out_down),
            (m_gate, l_two, s_gate, g_gate, t_gate, out_gate),
            (m_up, l_two, s_up, g_up, t_up, out_up),
            (m_out, l_err, s_out, g_out, t_out, out_out),
            (m_query, l_one, s_query, g_query, t_query, out_query),
        ))
    ]
    down, gate, up, out, query = lines
    gathers[0].start()

    loads = [
        pltpu.make_async_copy(a, b, loc.at[8 + i])
        for i, (a, b) in enumerate((
            (middle_in, mid), (d_two, two_own), (cot_in, cot_all), (wo_in, weight), (x_in, x_all),
            (q_in, uq), (k_in, uk), (v_in, uv), (o_in, uo), (lse_in, lse), (seg_in, seg_all),
        ))
    ]
    for copy in loads:
        copy.start()
    for copy in loads[:4]:
        copy.wait()

    spread_att = Spread(
        place,
        lambda d: d_att.at[aligned(d // heads, tok), aligned(lax.rem(d, heads), HEAD_DIM)],
        lambda: udo.at[aligned(s, tok), :],
        a_s.at[0], a_r.at[0], loc.at[19],
    )
    fine = 32

    def second_norm(i, gain_sum):
        two_copy(i).wait()

        def some(j, gain_sum):
            at = aligned(i * (chunk // fine) + j, fine)
            m = mid[at, :]
            d2 = two_own[at, :].astype(F32) + two_in[at, :].astype(F32)
            root = lax.rsqrt(jnp.mean(m * m, axis=-1, keepdims=True) + EPSILON)
            gained = d2 * gain_two[...]
            scaled = m * root
            gain_sum = gain_sum + jnp.sum(d2 * scaled, axis=0, keepdims=True)
            slope = jnp.mean(gained * scaled, axis=-1, keepdims=True)
            dm = cot_all[at, :].astype(F32) + root * (gained - scaled * slope)
            mid[at, :] = dm
            low = dm.astype(BF)
            for zy in range(n // 2):
                zz, yy = divmod(zy, 2)
                err[yy, at, zz * blk : (zz + 1) * blk] = low[:, zy * blk : (zy + 1) * blk]
            return gain_sum

        gain_sum = lax.fori_loop(0, chunk // fine, some, gain_sum)
        at = aligned(i, chunk)
        total = jnp.zeros((chunk, half), F32)
        for zy in range(n // 2):
            zz, yy = divmod(zy, 2)
            total += dot_nn(err[yy, at, zz * blk : (zz + 1) * blk], weight[zy * blk : (zy + 1) * blk, :])
        d_att[at, :] = total.astype(BF)
        return gain_sum

    gain_sum = jnp.zeros((1, width), F32)
    per_row = tok // chunk
    for r in range(rows):
        gain_sum = lax.fori_loop(r * per_row, (r + 1) * per_row, second_norm, gain_sum)
        lax.fori_loop(r * heads, (r + 1) * heads, spread_att.start_to, 0)
    for i in range(n):
        gain_part[0, i] = gain_sum[:, i * (width // n) : (i + 1) * (width // n)]
    spread_gain = [
        Spread(place, lambda d, g=g: gain_part.at[g, d], lambda g=g: gain_in.at[g, s], a_s.at[4 + g], a_r.at[4 + g], loc.at[23 + g])
        for g in range(2)
    ]
    spread_gain[0].start()
    load_q = pltpu.make_async_copy(wq_in, weight, loc.at[25])
    load_q.start()

    lefts[0].start()
    gathers[1].start()
    gathers[2].start()
    lefts[1].start()
    gathers[3].start()

    loads[4].wait()

    def first_norm(j, unused):
        at = aligned(j, fine)
        x = x_all[at, :].astype(F32)
        root = lax.rsqrt(jnp.mean(x * x, axis=-1, keepdims=True) + EPSILON)
        low = (x * root * gain_one[...]).astype(BF)
        for zy in range(n // 2):
            zz, yy = divmod(zy, 2)
            one[yy, at, zz * blk : (zz + 1) * blk] = low[:, zy * blk : (zy + 1) * blk]
        return unused

    lax.fori_loop(0, tokens // fine, first_norm, 0)

    for copy in loads[5:]:
        copy.wait()
    attention_masks(seg_all, seg_row, seg_col, n, tok)

    def turn(i, unused):
        at = aligned(i, tok)
        k_t[:, at] = jnp.transpose(uk[at, :].astype(F32)).astype(BF)
        return unused

    lax.fori_loop(0, n, turn, 0)
    dk_acc[...] = jnp.zeros_like(dk_acc)
    dv_acc[...] = jnp.zeros_like(dv_acc)

    gathers[0].wait()
    down.load(True)
    at_end = (z == 0) | (z == nz - 1)

    @pl.when(at_end)
    def _():
        down.steps()

    spread_att.wait()

    def turn_delta(i, unused):
        at = aligned(i, tok)
        both = udo[at, :].astype(F32) * uo[at, :].astype(F32)
        delta[:, at] = jnp.sum(jnp.transpose(both), axis=0, keepdims=True)
        return unused

    lax.fori_loop(0, n, turn_delta, 0)

    block = 512
    owners = block // tok

    def home(ref):
        return lambda: ref.at[aligned(row_s, tok), aligned(head_s, HEAD_DIM)]

    spread_dq, spread_dk, spread_dv = (
        Spread(place, lambda d, unit=unit: unit.at[aligned(d, tok), :], home(whole), a_s.at[i], a_r.at[i], loc.at[19 + i])
        for i, unit, whole in ((1, udq, dq), (2, udk, d_keys), (3, udv, d_values))
    )

    def query_step(i, unused):
        qi = length // block - 1 - i
        qat = aligned(qi, block)
        qb, dob = uq[qat, :], udo[qat, :]

        def key_step(kj, dq_t):
            kat = aligned(kj, block)
            scores = dot_nt(uk[kat, :], qb) - lse[:, qat]
            probs = jnp.exp(jnp.where(readable(seg_col, seg_row, kj, qi, block), scores, NEGATIVE_FILL))
            d_probs = dot_nt(uv[kat, :], dob)
            d_scores = (probs * (d_probs - delta[:, qat])).astype(BF)
            dv_acc[kat, :] += dot_nn(probs.astype(BF), dob)
            dk_acc[kat, :] += dot_nn(d_scores, qb)
            return dq_t + dot_nn(k_t[:, kat], d_scores)

        dq_t = lax.fori_loop(0, qi + 1, key_step, jnp.zeros((HEAD_DIM, block), F32))
        udq[qat, :] = jnp.transpose(dq_t).astype(BF)
        lax.fori_loop(qi * owners, (qi + 1) * owners, spread_dq.start_to, 0)
        udk[qat, :] = dk_acc[qat, :].astype(BF)
        udv[qat, :] = dv_acc[qat, :].astype(BF)
        lax.fori_loop(qi * owners, (qi + 1) * owners, spread_dk.start_to, 0)
        lax.fori_loop(qi * owners, (qi + 1) * owners, spread_dv.start_to, 0)
        return unused

    lax.fori_loop(0, length // block, query_step, 0)

    @pl.when(jnp.logical_not(at_end))
    def _():
        down.steps()

    down.own_block()
    lefts[0].forward()
    gathers[1].wait()
    lefts[0].finish()
    gate.load(True)
    gate.steps()
    gate.own_block()

    load_q.wait()
    spread_dq.wait()
    gathers[4].start()
    lefts[2].start()

    def one_copy(i):
        at = aligned(i, chunk)
        return remote(one_part.at[at, :], one_in.at[at, :], tp_s.at[5 + i], tp_r.at[5 + i], place.twin)

    def back_query(i, unused):
        at = aligned(i, chunk)
        one_part[at, :] = (dot_nt(dq[at, :], weight[...]) * HEAD_DIM ** (-0.5)).astype(BF)
        one_copy(i).start()
        return unused

    lax.fori_loop(0, 4, back_query, 0)

    gathers[2].wait()
    up.load(False)
    up.steps()
    up.own_block()
    down.finish()

    lefts[1].forward()

    def last_norm(i, gain_sum):
        one_copy(i).wait()

        def some(j, gain_sum):
            at = aligned(i * (chunk // fine) + j, fine)
            x = x_all[at, :].astype(F32)
            d1 = one_part[at, :].astype(F32) + one_in[at, :].astype(F32)
            root = lax.rsqrt(jnp.mean(x * x, axis=-1, keepdims=True) + EPSILON)
            gained = d1 * gain_one[...]
            scaled = x * root
            gain_sum = gain_sum + jnp.sum(d1 * scaled, axis=0, keepdims=True)
            slope = jnp.mean(gained * scaled, axis=-1, keepdims=True)
            mid[at, :] = mid[at, :] + root * (gained - scaled * slope)
            return gain_sum

        return lax.fori_loop(0, chunk // fine, some, gain_sum)

    gain_sum = lax.fori_loop(0, 4, last_norm, jnp.zeros((1, width), F32))
    for i in range(n):
        gain_part[1, i] = gain_sum[:, i * (width // n) : (i + 1) * (width // n)]
    spread_gain[1].start()
    give = pltpu.make_async_copy(mid.at[:, mine], input_grad, loc.at[26])
    give.start()

    gathers[3].wait()
    lefts[1].finish()
    out.load(True)
    out.steps()
    out.own_block()
    gate.finish()

    lefts[2].forward()
    gathers[4].wait()
    lefts[2].finish()
    query.load(True)
    query.steps()
    query.own_block()
    up.finish()
    out.finish()
    query.finish()

    spread_dk.wait()
    spread_dv.wait()
    for g in range(2):
        spread_gain[g].wait()
        gains[g] = jnp.sum(gain_in[g], axis=0)
    ffn_copy.wait()
    give.wait()
    for line in lines:
        line.drain()


def backward_part(geo, ffn, forward, wo, wq, gain_one, gain_two):
    n, rows, tok, width, half, heads, length = geo
    tokens = rows * tok
    blk = 2 * width // n
    nz = n // PLANE
    hidden, d_gate, d_up, d_two, mixed = ffn
    x_all, cot_all, left_cot, middle, _, left_two, attended, uq, uk, uv, uo, lse, seg_all = forward
    dma = pltpu.SemaphoreType.DMA
    anywhere, here = pl.BlockSpec(memory_space=pl.ANY), pl.BlockSpec(memory_space=pltpu.VMEM)
    wide = (hidden.shape[1] // 2,) * 3 + (half // 2,) * 2
    outs = [
        (vm((tokens, half), BF), anywhere),
        (vm((tokens, half), F32), anywhere),
        (vm((tokens, half), BF), anywhere),
        (vm((tokens, half), BF), anywhere),
        (vm((2, 1, width // n), F32), here),
        *((vm((blk // 2, 2 * cols), F32), anywhere) for cols in wide),
        *((vm((PLANE * tokens, cols), BF), anywhere) for cols in wide),
        *((vm((PLANE * tokens, width // 2), BF), anywhere) for _ in range(3)),
        *((vm((nz + 1, blk, cols), BF), anywhere) for cols in wide),
    ]
    inputs = [
        hidden, d_gate, d_up, d_two, mixed, left_cot, left_two, middle, x_all, cot_all, attended,
        uq, uk, uv, uo, lse, seg_all, wo, wq, gain_one, gain_two,
    ]
    big = max(wide)
    unit = pltpu.VMEM((length, HEAD_DIM), BF)
    unit_sum = pltpu.VMEM((length, HEAD_DIM), F32)
    line = pltpu.VMEM((1, length), F32)
    act = pltpu.VMEM((tokens, width), BF)
    split = pltpu.VMEM((2, tokens, width // 2), BF)
    scratch = [
        pltpu.VMEM((tokens, width), F32), act, act, act, act, act, act, split, split,
        pltpu.VMEM(wo.shape, BF), pltpu.VMEM((tokens, half), BF),
        unit, unit, unit, unit, unit, line, pltpu.VMEM((n, 1, tok), F32), line,
        pltpu.VMEM((length, LANE), F32), pltpu.VMEM((HEAD_DIM, length), BF), line,
        unit_sum, unit_sum, unit, unit, unit, pltpu.VMEM((tokens, half), BF),
        pltpu.VMEM((2, n, 1, width // n), F32), pltpu.VMEM((2, n, 1, width // n), F32),
        *(pltpu.VMEM((nz - 1, blk, cols), BF) for cols in wide),
        *(pltpu.VMEM((blk, cols), F32) for cols in wide),
        pltpu.VMEM((PLANE * tokens, big), BF), pltpu.VMEM((PLANE * tokens, width // 2), BF),
        pltpu.VMEM((blk, big), F32), pltpu.VMEM((blk, big), BF),
        dma((9,)), dma((9,)), dma((6, n)), dma((6, n)), dma((5, 3)), dma((5, 3)), dma((3, 3)), dma((3, 3)),
        dma((5, nz - 1)), dma((5, nz + 1)), dma((5,)), dma((5,)), dma((5,)), dma((27,)), dma((3,)),
    ]
    return pl.pallas_call(
        functools.partial(backward_kernel, geo),
        out_shape=[o for o, _ in outs],
        in_specs=[anywhere] * (len(inputs) - 2) + [here] * 2,
        out_specs=[spec for _, spec in outs],
        scratch_shapes=scratch,
        compiler_params=pltpu.CompilerParams(
            collective_id=1, has_side_effects=True, vmem_limit_bytes=62 * MIB
        ),
        name="backward",
    )(*inputs)


def fast_device(
    n, inputs, segments, keys, values, attn_gain, query_weight, out_weight, ffn_gain, gate_weight, up_weight, down_weight,
    cotangent,
):
    rows, tok, half = inputs.shape
    tokens, width, ff = rows * tok, query_weight.shape[0], gate_weight.shape[1]
    heads = half // HEAD_DIM
    geo = (n, rows, tok, width, half, heads, n * tok)
    padded = -(-ff // (2 * LANE)) * 2 * LANE

    def flat(a):
        return a.reshape(tokens, half)

    segf = segments.astype(F32).reshape(rows, 1, tok)
    gain_one, gain_two = attn_gain.reshape(1, width), ffn_gain.reshape(1, width)
    forward = forward_part(
        geo, flat(inputs), flat(cotangent), flat(keys), flat(values), segf, gain_one, gain_two, query_weight, out_weight
    )
    x_all, cot_all, _, middle, normed_two = forward[:5]
    ffn = ffn_part(padded, normed_two, cot_all, gate_weight, up_weight, down_weight)
    back = backward_part(geo, ffn, forward, out_weight, query_weight, gain_one, gain_two)
    ffn_in, input_grad, d_keys, d_values, gains, g_down, g_gate, g_up, g_out, g_query = back[:10]
    at = lax.axis_index("tp") * half
    mixed = (
        lax.dynamic_slice_in_dim(middle, at, half, 1)
        + lax.dynamic_slice_in_dim(ffn[4], at, half, 1).astype(F32)
        + ffn_in.astype(F32)
    ).astype(BF)

    def shaped(a):
        return a.reshape(rows, tok, half)

    return (
        shaped(mixed),
        shaped(input_grad),
        shaped(d_keys.astype(F32)),
        shaped(d_values.astype(F32)),
        gains[1, 0],
        g_query * HEAD_DIM ** (-0.5),
        g_out,
        gains[0, 0],
        g_gate[:, :ff],
        g_up[:, :ff],
        g_down[:, :ff],
    )


def inverse_root(stream):
    return lax.rsqrt(jnp.mean(stream * stream, axis=-1, keepdims=True) + EPSILON)


def key_mask(doc_start, query_pos, begin, row_count):
    key_pos = begin + jnp.arange(row_count, dtype=jnp.int32)
    earlier = key_pos[None, None, :] <= query_pos[None, :, None]
    same_doc = key_pos[None, None, :] >= doc_start[:, :, None]
    return (earlier & same_doc)[:, None]


def per_device(
    inputs,
    segments,
    keys,
    values,
    attn_gain,
    query_weight,
    out_weight,
    ffn_gain,
    gate_weight,
    up_weight,
    down_weight,
    cotangent,
):
    batch_rows, local_tokens, half_width = inputs.shape
    local_heads = half_width // HEAD_DIM
    seq_devices = lax.axis_size("seq")
    row_length = local_tokens * seq_devices
    seq_index = lax.axis_index("seq")
    tp_index = lax.axis_index("tp")
    query_scale = HEAD_DIM ** (-0.5)
    bfloat = jnp.bfloat16
    single = jnp.float32
    whole = lax.all_gather(inputs, "tp", axis=2, tiled=True).astype(single)
    root_one = inverse_root(whole)
    scaled_one = whole * root_one
    normed_one = (scaled_one * attn_gain).astype(bfloat)
    query = (
        jnp.einsum("rtd,de->rte", normed_one, query_weight, preferred_element_type=single)
        * query_scale
    ).astype(bfloat)
    query_heads = query.reshape(batch_rows, local_tokens, local_heads, HEAD_DIM)
    bins = jnp.arange(CUTS + 1, dtype=jnp.int32)
    onehot = (segments[:, :, None] == bins[None, None, :]).astype(single)
    totals = lax.psum(jnp.sum(onehot, axis=1), "seq")
    ends = jnp.cumsum(totals, axis=-1)
    before = ends - totals
    doc_start = jnp.sum(onehot * before[:, None, :], axis=-1).astype(jnp.int32)
    query_pos = seq_index * local_tokens + jnp.arange(local_tokens, dtype=jnp.int32)
    first_needed = jnp.min(doc_start)
    last_needed = seq_index * local_tokens + local_tokens - 1
    start_state = (
        jnp.full((batch_rows, local_heads, local_tokens), NEGATIVE_FILL, single),
        jnp.zeros((batch_rows, local_heads, local_tokens), single),
        jnp.zeros((batch_rows, local_heads, local_tokens, HEAD_DIM), single),
    )
    key_piece = lax.all_gather(keys, "seq", axis=1, tiled=True)
    value_piece = lax.all_gather(values, "seq", axis=1, tiled=True)
    piece_rows = key_piece.shape[1]
    fold_key_block = math.gcd(piece_rows, 512)

    def fold_step(block_index, state):
        running_max, running_sum, running_out = state
        begin = block_index * fold_key_block

        def fold_work(unused):
            key_heads = lax.dynamic_slice_in_dim(
                key_piece, block_index * fold_key_block, fold_key_block, 1
            ).reshape(batch_rows, fold_key_block, local_heads, HEAD_DIM)
            value_heads = lax.dynamic_slice_in_dim(
                value_piece, block_index * fold_key_block, fold_key_block, 1
            ).reshape(batch_rows, fold_key_block, local_heads, HEAD_DIM)
            scores = jnp.einsum(
                "rqhe,rkhe->rhqk", query_heads, key_heads, preferred_element_type=single
            )
            allowed = key_mask(doc_start, query_pos, begin, fold_key_block)
            scores = jnp.where(allowed, scores, NEGATIVE_FILL)
            new_max = jnp.maximum(running_max, jnp.max(scores, axis=-1))
            weights = jnp.where(allowed, jnp.exp(scores - new_max[..., None]), 0.0)
            decay = jnp.exp(running_max - new_max)
            new_sum = running_sum * decay + jnp.sum(weights, axis=-1)
            new_out = running_out * decay[..., None] + jnp.einsum(
                "rhqk,rkhe->rhqe",
                weights.astype(bfloat),
                value_heads,
                preferred_element_type=single,
            )
            return (new_max, new_sum, new_out)

        def keep_state(unused):
            return (running_max, running_sum, running_out)

        needed = (begin <= last_needed) & (begin + fold_key_block - 1 >= first_needed)
        return lax.cond(needed, fold_work, keep_state, 0)

    running_max, running_sum, running_out = lax.fori_loop(
        0, piece_rows // fold_key_block, fold_step, start_state
    )
    log_total = running_max + jnp.log(running_sum)
    attended = running_out / running_sum[..., None]
    attended_low = (
        attended.transpose(0, 2, 1, 3).reshape(batch_rows, local_tokens, half_width).astype(bfloat)
    )
    branch = jnp.einsum("rth,dh->rtd", attended_low, out_weight, preferred_element_type=single)
    middle = whole + lax.psum(branch.astype(jnp.bfloat16), "tp").astype(jnp.float32)
    middle_share = lax.dynamic_slice_in_dim(middle, tp_index * half_width, half_width, 2)
    root_two = inverse_root(middle)
    scaled_two = middle * root_two
    normed_two = (scaled_two * ffn_gain).astype(bfloat)
    gate = jnp.einsum("rtd,df->rtf", normed_two, gate_weight, preferred_element_type=single)
    up_proj = jnp.einsum("rtd,df->rtf", normed_two, up_weight, preferred_element_type=single)
    sigma = jax.nn.sigmoid(gate)
    activated = gate * sigma
    hidden = (activated * up_proj).astype(bfloat)
    ffn_part = jnp.einsum("rtf,df->rtd", hidden, down_weight, preferred_element_type=single)
    output = (
        middle_share
        + lax.psum_scatter(
            ffn_part.astype(jnp.bfloat16), "tp", scatter_dimension=2, tiled=True
        ).astype(jnp.float32)
    ).astype(bfloat)
    grad_out = lax.all_gather(cotangent, "tp", axis=2, tiled=True)
    d_hidden = jnp.einsum("rtd,df->rtf", grad_out, down_weight, preferred_element_type=single)
    d_gate = (d_hidden * up_proj * sigma * (1.0 + gate * (1.0 - sigma))).astype(bfloat)
    d_up = (d_hidden * activated).astype(bfloat)
    d_two_part = jnp.einsum(
        "rtf,df->rtd", d_gate, gate_weight, preferred_element_type=single
    ) + jnp.einsum("rtf,df->rtd", d_up, up_weight, preferred_element_type=single)
    d_two = lax.psum(d_two_part.astype(jnp.bfloat16), "tp").astype(jnp.float32)
    gained_two = d_two * ffn_gain
    d_middle = (
        grad_out.astype(single)
        + root_two * gained_two
        - middle * root_two**3 * jnp.mean(gained_two * middle, axis=-1, keepdims=True)
    )
    normed_rows = normed_two
    gate_term = jnp.einsum("rtd,rtf->df", normed_rows, d_gate, preferred_element_type=single)
    up_term = jnp.einsum("rtd,rtf->df", normed_rows, d_up, preferred_element_type=single)
    down_term = jnp.einsum("rtd,rtf->df", grad_out, hidden, preferred_element_type=single)
    gain_term = jnp.sum(d_two * scaled_two, axis=(0, 1))
    gate_grad, up_grad, down_grad, ffn_gain_grad = lax.psum_scatter(
        (gate_term, up_term, down_term, gain_term), "seq", scatter_dimension=0, tiled=True
    )
    error = d_middle.astype(bfloat)
    d_attended = jnp.einsum("rtd,dh->rth", error, out_weight, preferred_element_type=single).astype(
        bfloat
    )
    d_heads = d_attended.reshape(batch_rows, local_tokens, local_heads, HEAD_DIM)
    carried = jnp.einsum("rqhe,rhqe->rhq", d_heads.astype(single), attended)
    key_all, value_all = (
        lax.all_gather(keys, "seq", axis=1, tiled=True),
        lax.all_gather(values, "seq", axis=1, tiled=True),
    )
    key_block = math.gcd(row_length, 512)

    def block_terms(begin):
        key_heads = lax.dynamic_slice_in_dim(key_all, begin, key_block, 1).reshape(
            batch_rows, key_block, local_heads, HEAD_DIM
        )
        value_heads = lax.dynamic_slice_in_dim(value_all, begin, key_block, 1).reshape(
            batch_rows, key_block, local_heads, HEAD_DIM
        )
        scores = jnp.einsum(
            "rqhe,rkhe->rhqk", query_heads, key_heads, preferred_element_type=single
        )
        allowed = key_mask(doc_start, query_pos, begin, key_block)
        probs = jnp.where(
            allowed, jnp.exp(jnp.where(allowed, scores, NEGATIVE_FILL) - log_total[..., None]), 0.0
        )
        d_probs = jnp.einsum("rqhe,rkhe->rhqk", d_heads, value_heads, preferred_element_type=single)
        d_scores = (probs * (d_probs - carried[..., None])).astype(bfloat)
        query_part = jnp.einsum(
            "rhqk,rkhe->rhqe", d_scores, key_heads, preferred_element_type=single
        )
        return (probs, d_scores, query_part)

    query_zero = jnp.zeros((batch_rows, local_heads, local_tokens, HEAD_DIM), single)

    def back_step(block_index, state):
        d_query, key_terms, value_terms = state
        begin = block_index * key_block

        def back_work(unused):
            probs, d_scores, query_part = block_terms(begin)
            value_part = jnp.einsum(
                "rhqk,rqhe->rkhe", probs.astype(bfloat), d_heads, preferred_element_type=single
            )
            key_part = jnp.einsum(
                "rhqk,rqhe->rkhe", d_scores, query_heads, preferred_element_type=single
            )
            return (
                query_part,
                key_part.reshape(batch_rows, key_block, half_width),
                value_part.reshape(batch_rows, key_block, half_width),
            )

        def skip_block(unused):
            empty_rows = jnp.zeros((batch_rows, key_block, half_width), single)
            return (jnp.zeros_like(d_query), empty_rows, empty_rows)

        needed = (begin <= last_needed) & (begin + key_block - 1 >= first_needed)
        query_part, key_part, value_part = lax.cond(needed, back_work, skip_block, 0)
        return (
            d_query + query_part,
            lax.dynamic_update_slice_in_dim(key_terms, key_part, begin, 1),
            lax.dynamic_update_slice_in_dim(value_terms, value_part, begin, 1),
        )

    back_start = (
        query_zero,
        jnp.zeros((batch_rows, row_length, half_width), single),
        jnp.zeros((batch_rows, row_length, half_width), single),
    )
    d_query, key_terms, value_terms = lax.fori_loop(
        0, row_length // key_block, back_step, back_start
    )
    key_grad, value_grad = (
        lax.psum_scatter(key_terms, "seq", scatter_dimension=1, tiled=True),
        lax.psum_scatter(value_terms, "seq", scatter_dimension=1, tiled=True),
    )
    d_query_rows = (
        d_query.transpose(0, 2, 1, 3).reshape(batch_rows, local_tokens, half_width).astype(bfloat)
    )
    d_one_part = (
        jnp.einsum("rte,de->rtd", d_query_rows, query_weight, preferred_element_type=single)
        * query_scale
    )
    d_one = lax.psum(d_one_part.astype(jnp.bfloat16), "tp").astype(jnp.float32)
    gained_one = d_one * attn_gain
    d_whole = (
        d_middle
        + root_one * gained_one
        - whole * root_one**3 * jnp.mean(gained_one * whole, axis=-1, keepdims=True)
    )
    input_grad = lax.dynamic_slice_in_dim(d_whole, tp_index * half_width, half_width, 2)
    normed_rows = normed_one
    query_term = (
        jnp.einsum("rtd,rte->de", normed_rows, d_query_rows, preferred_element_type=single)
        * query_scale
    )
    out_term = jnp.einsum("rtd,rth->dh", error, attended_low, preferred_element_type=single)
    gain_term = jnp.sum(d_one * scaled_one, axis=(0, 1))
    query_grad, out_grad, attn_gain_grad = lax.psum_scatter(
        (query_term, out_term, gain_term), "seq", scatter_dimension=0, tiled=True
    )
    return (
        output,
        input_grad,
        key_grad,
        value_grad,
        attn_gain_grad,
        query_grad,
        out_grad,
        ffn_gain_grad,
        gate_grad,
        up_grad,
        down_grad,
    )


def solution(mesh):
    in_specs = (
        P(None, "seq", "tp"),
        P(None, "seq"),
        P(None, "seq", "tp"),
        P(None, "seq", "tp"),
        P(),
        P(None, "tp"),
        P(None, "tp"),
        P(),
        P(None, "tp"),
        P(None, "tp"),
        P(None, "tp"),
        P(None, "seq", "tp"),
    )
    out_specs = (
        P(None, "seq", "tp"),
        P(None, "seq", "tp"),
        P(None, "seq", "tp"),
        P(None, "seq", "tp"),
        P("seq"),
        P("seq", "tp"),
        P("seq", "tp"),
        P("seq"),
        P("seq", "tp"),
        P("seq", "tp"),
        P("seq", "tp"),
    )
    n = mesh.shape["seq"]

    def step(inputs, *others):
        rows, tok, half = inputs.shape
        units = rows * (half // HEAD_DIM)
        if units == n == PLANE * PLANE and 4 * tok == 512 and mesh.shape["tp"] == 2:
            return fast_device(n, inputs, *others)
        return per_device(inputs, *others)

    return jax.shard_map(
        step, mesh=mesh, in_specs=in_specs, out_specs=out_specs, check_vma=False
    )
```

```python
import functools
import math

import jax
import jax.numpy as jnp
from jax import lax
from jax.experimental import pallas as pl
from jax.experimental.pallas import tpu as pltpu
from jax.sharding import PartitionSpec as P

HEAD_DIM = 128
CUTS = 12


EPSILON = 1e-06
NEGATIVE_FILL = -1e30

MESH = pl.DeviceIdType.MESH
BF = jnp.bfloat16
F32 = jnp.float32
VMEM_GRANT = 62 << 20
PLANE = 4
LANE = 128


def dot_nn(a, b):
    return lax.dot_general(a, b, (((1,), (0,)), ((), ())), preferred_element_type=F32)


def dot_nt(a, b):
    return lax.dot_general(a, b, (((1,), (1,)), ((), ())), preferred_element_type=F32)


def dot_tn(a, b):
    return lax.dot_general(a, b, (((0,), (0,)), ((), ())), preferred_element_type=F32)


def aligned(index, size):
    return pl.ds(pl.multiple_of(index * size, size), size)


class Place:
    def __init__(self, n):
        self.n = n
        self.s = lax.axis_index("seq")
        self.t = lax.axis_index("tp")
        self.z = self.s // PLANE
        self.p = lax.rem(self.s, PLANE)
        self.y = self.p // 2
        self.c = lax.rem(self.p, 2)
        base = self.z * PLANE
        self.core_p = self.y * 2 + 1 - self.c
        self.side_p = (1 - self.y) * 2 + self.c
        self.cross_p = (1 - self.y) * 2 + 1 - self.c
        self.core = (base + self.core_p, self.t)
        self.side = (base + self.side_p, self.t)
        self.cross = (base + self.cross_p, self.t)
        self.twin = (self.s, 1 - self.t)

    def other(self, k):
        return lax.rem(self.s + k, self.n)

    def enter(self):
        barrier = pltpu.get_barrier_semaphore()

        def greet(k, unused):
            pl.semaphore_signal(barrier, inc=1, device_id=(self.other(k), self.t), device_id_type=MESH)
            return unused

        lax.fori_loop(1, self.n, greet, 0)
        pl.semaphore_signal(barrier, inc=1, device_id=self.twin, device_id_type=MESH)
        pl.semaphore_wait(barrier, self.n)


def remote(src, dst, send, recv, device):
    return pltpu.make_async_remote_copy(
        src_ref=src, dst_ref=dst, send_sem=send, recv_sem=recv, device_id=device, device_id_type=MESH
    )


class Spread:
    def __init__(self, place, src, dst, send, recv, local):
        self.place, self.src, self.dst, self.send, self.recv, self.local = place, src, dst, send, recv, local

    def copy(self, k):
        place = self.place
        d = place.other(k)
        return remote(self.src(d), self.dst(), self.send.at[k], self.recv.at[k], (d, place.t))

    def own(self):
        return pltpu.make_async_copy(self.src(self.place.s), self.dst(), self.local)

    def start(self):
        self.own().start()

        def one(k, unused):
            self.copy(k).start()
            return unused

        lax.fori_loop(1, self.place.n, one, 0)

    def start_to(self, d, unused):
        k = lax.rem(d - self.place.s + self.place.n, self.place.n)

        @pl.when(k == 0)
        def _():
            self.own().start()

        @pl.when(k != 0)
        def _():
            self.copy(k).start()

        return unused

    def wait(self):
        self.own().wait()

        def one(k, unused):
            self.copy(k).wait()
            return unused

        lax.fori_loop(1, self.place.n, one, 0)


def attention_masks(seg_all, seg_row, seg_col, n, tok):
    def one(i, unused):
        piece = seg_all[i]
        seg_row[:, aligned(i, tok)] = piece
        seg_col[aligned(i, tok), :] = jnp.transpose(jnp.broadcast_to(piece, (tok, tok)))
        return unused

    lax.fori_loop(0, n, one, 0)


def readable(seg_col, seg_row, key_block, query_block, block):
    key_seg = seg_col[aligned(key_block, block), :]
    key_seg = jnp.concatenate([key_seg] * (block // LANE), axis=1)
    query_seg = seg_row[:, aligned(query_block, block)]
    key_pos = key_block * block + lax.broadcasted_iota(jnp.int32, (block, block), 0)
    query_pos = query_block * block + lax.broadcasted_iota(jnp.int32, (block, block), 1)
    return (key_seg == query_seg) & (key_pos <= query_pos)


def forward_kernel(
    geo,
    x_in, cot_in, key_in, value_in, seg_in, gain_one, gain_two, wq_in, wo_in,
    x_out, cot_out, left_out, middle_out, two_out, split_out, att_out, q_out, k_out, v_out, o_out, lse_out, seg_out,
    x_all, cot_all, left_cot, middle, normed_two, left_two, attended, unit_q, unit_k, unit_v, unit_o, lse, seg_all,
    wq, wo, normed_one, query, value_t, seg_row, seg_col, part, part_in, cot_split,
    tp_s, tp_r, a_s, a_r, br_s, br_r, l_s, l_r, loc, away,
):
    n, rows, tok, width, half, heads, length = geo
    place = Place(n)
    s, t = place.s, place.t
    place.enter()
    row_s, head_s = s // heads, lax.rem(s, heads)
    half_at = aligned(t, half)
    leaving = []

    def leave(*pairs):
        for here, there in pairs:
            copy = pltpu.make_async_copy(here, there, away.at[len(leaving)])
            copy.start()
            leaving.append(copy)


    to_x = remote(x_in, x_all.at[:, half_at], tp_s.at[0], tp_r.at[0], place.twin)
    to_x.start()
    own_x = pltpu.make_async_copy(x_in, x_all.at[:, half_at], loc.at[0])
    own_x.start()
    load_q = pltpu.make_async_copy(wq_in, wq, loc.at[1])
    load_q.start()

    def piece(ref):
        return lambda d: ref.at[aligned(d // heads, tok), aligned(lax.rem(d, heads), HEAD_DIM)]

    keys = Spread(place, piece(key_in), lambda: unit_k.at[aligned(s, tok), :], a_s.at[0], a_r.at[0], loc.at[2])
    vals = Spread(place, piece(value_in), lambda: unit_v.at[aligned(s, tok), :], a_s.at[1], a_r.at[1], loc.at[3])
    segs = Spread(place, lambda d: seg_in.at[d // heads], lambda: seg_all.at[s], a_s.at[2], a_r.at[2], loc.at[4])
    qrys = Spread(place, piece(query), lambda: unit_q.at[aligned(s, tok), :], a_s.at[3], a_r.at[3], loc.at[5])
    segs.start()
    keys.start()
    vals.start()
    to_cot = remote(cot_in, cot_all.at[:, half_at], tp_s.at[1], tp_r.at[1], place.twin)
    to_cot.start()
    own_cot = pltpu.make_async_copy(cot_in, cot_all.at[:, half_at], loc.at[6])
    own_cot.start()
    load_o = pltpu.make_async_copy(wo_in, wo, loc.at[7])
    load_o.start()

    own_x.wait()
    to_x.wait()
    step = 64

    def norm_one(i, unused):
        at = aligned(i, step)
        x = x_all[at, :].astype(F32)
        root = lax.rsqrt(jnp.mean(x * x, axis=-1, keepdims=True) + EPSILON)
        normed_one[at, :] = (x * root * gain_one[...]).astype(BF)
        return unused

    lax.fori_loop(0, rows * tok // step, norm_one, 0)
    leave((x_all, x_out))
    load_q.wait()
    query[...] = (dot_nn(normed_one[...], wq[...]) * HEAD_DIM ** (-0.5)).astype(BF)
    qrys.start()

    segs.wait()
    attention_masks(seg_all, seg_row, seg_col, n, tok)
    keys.wait()
    vals.wait()

    def turn(i, unused):
        at = aligned(i, tok)
        value_t[:, at] = jnp.transpose(unit_v[at, :].astype(F32)).astype(BF)
        return unused

    lax.fori_loop(0, n, turn, 0)
    qrys.wait()
    leave((unit_q, q_out), (unit_k, k_out), (unit_v, v_out), (seg_all, seg_out))

    back = Spread(
        place,
        lambda d: unit_o.at[aligned(d, tok), :],
        lambda: attended.at[aligned(row_s, tok), aligned(head_s, HEAD_DIM)],
        a_s.at[4], a_r.at[4], loc.at[8],
    )
    block = 512
    owners = block // tok

    def query_step(qi, unused):
        query_block = unit_q[aligned(qi, block), :]

        def key_step(j, carry):
            top, total, acc = carry
            kj = qi - j
            scores = dot_nt(unit_k[aligned(kj, block), :], query_block)
            scores = jnp.where(readable(seg_col, seg_row, kj, qi, block), scores, NEGATIVE_FILL)
            new_top = jnp.maximum(top, jnp.max(scores, axis=0, keepdims=True))
            weights = jnp.exp(scores - new_top)
            decay = jnp.exp(top - new_top)
            total = total * decay + jnp.sum(weights, axis=0, keepdims=True)
            acc = acc * decay + dot_nn(value_t[:, aligned(kj, block)], weights.astype(BF))
            return new_top, total, acc

        start = (
            jnp.full((1, block), NEGATIVE_FILL, F32),
            jnp.zeros((1, block), F32),
            jnp.zeros((HEAD_DIM, block), F32),
        )
        top, total, acc = lax.fori_loop(0, qi + 1, key_step, start)
        lse[:, aligned(qi, block)] = top + jnp.log(total)
        unit_o[aligned(qi, block), :] = jnp.transpose(acc / total).astype(BF)

        return lax.fori_loop(qi * owners, (qi + 1) * owners, back.start_to, unused)

    lax.fori_loop(0, length // block, query_step, 0)

    leave((unit_o, o_out), (lse, lse_out))
    own_cot.wait()
    to_cot.wait()
    split_rows(cot_all, cot_split, n)
    plane_cot = Plane(place, cot_split, left_cot, l_s, l_r, loc.at[9], rows * tok)
    plane_cot.start()
    load_o.wait()
    back.wait()
    leave((attended, att_out), (cot_all, cot_out))

    chunks = part.shape[0]
    wide = width // chunks

    def to_twin(i):
        return remote(part.at[i], part_in.at[i], br_s.at[i], br_r.at[i], place.twin)

    def project(i, unused):
        part[i] = dot_nt(attended[...], wo[aligned(i, wide), :]).astype(BF)
        to_twin(i).start()
        return unused

    lax.fori_loop(0, chunks, project, 0)
    plane_cot.forward()

    def add(i, square):
        to_twin(i).wait()
        at = aligned(i, wide)
        both = part[i].astype(F32) + part_in[i].astype(F32)
        mid = x_all[:, at].astype(F32) + both
        middle[:, at] = mid
        return square + jnp.sum(mid * mid, axis=-1, keepdims=True)

    square = lax.fori_loop(0, chunks, add, jnp.zeros((rows * tok, 1), F32))
    root_two = lax.rsqrt(square * (1.0 / width) + EPSILON)

    def norm_two(i, unused):
        at = aligned(i, wide)
        normed_two[:, at] = (middle[:, at] * root_two * gain_two[:, at]).astype(BF)
        return unused

    leave((middle, middle_out))
    lax.fori_loop(0, chunks, norm_two, 0)
    leave((normed_two, two_out))
    split_rows(normed_two, left_two, n)
    plane_cot.finish()
    leave((left_two, split_out), (left_cot, left_out))
    for copy in leaving:
        copy.wait()


def split_rows(whole, split, n):
    blk = whole.shape[1] * 2 // n
    for zy in range(n // 2):
        z, y = divmod(zy, 2)
        split[y, :, z * blk : (z + 1) * blk] = whole[:, zy * blk : (zy + 1) * blk]


class Plane:
    def __init__(self, place, split, left, send, recv, local, tokens):
        self.place, self.tokens, self.left = place, tokens, left
        to = left.at[aligned(place.p, tokens), :]
        self.own = pltpu.make_async_copy(split.at[place.y], to, local)
        self.to_core = remote(split.at[place.y], to, send.at[0], recv.at[0], place.core)
        self.to_side = remote(split.at[1 - place.y], to, send.at[1], recv.at[1], place.side)
        passed = left.at[aligned(place.side_p, tokens), :]
        self.on = remote(passed, passed, send.at[2], recv.at[2], place.core)

    def start(self):
        self.to_side.start()
        self.own.start()
        self.to_core.start()

    def forward(self):
        self.to_side.wait()
        self.on.start()

    def finish(self):
        self.own.wait()
        self.to_core.wait()
        self.on.wait()


def vm(shape, dtype):
    return jax.ShapeDtypeStruct(shape, dtype)


def forward_part(geo, x, cot, keys, values, segf, gain_one, gain_two, wq, wo):
    n, rows, tok, width, half, heads, length = geo
    tokens = rows * tok
    dma = pltpu.SemaphoreType.DMA
    anywhere, here = pl.BlockSpec(memory_space=pl.ANY), pl.BlockSpec(memory_space=pltpu.VMEM)
    outs = [
        vm((tokens, width), BF),
        vm((tokens, width), BF),
        vm((PLANE * tokens, width // 2), BF),
        vm((tokens, width), F32),
        vm((tokens, width), BF),
        vm((2, tokens, width // 2), BF),
        vm((tokens, half), BF),
        vm((length, HEAD_DIM), BF),
        vm((length, HEAD_DIM), BF),
        vm((length, HEAD_DIM), BF),
        vm((length, HEAD_DIM), BF),
        vm((1, length), F32),
        vm((n, 1, tok), F32),
    ]
    chunks = 4
    return pl.pallas_call(
        functools.partial(forward_kernel, geo),
        out_shape=outs,
        in_specs=[anywhere] * 5 + [here] * 2 + [anywhere] * 2,
        out_specs=[anywhere] * len(outs),
        scratch_shapes=[
            *(pltpu.VMEM(o.shape, o.dtype) for o in outs),
            pltpu.VMEM(wq.shape, BF),
            pltpu.VMEM(wo.shape, BF),
            pltpu.VMEM((tokens, width), BF),
            pltpu.VMEM((tokens, half), BF),
            pltpu.VMEM((HEAD_DIM, length), BF),
            pltpu.VMEM((1, length), F32),
            pltpu.VMEM((length, LANE), F32),
            pltpu.VMEM((chunks, tokens, width // chunks), BF),
            pltpu.VMEM((chunks, tokens, width // chunks), BF),
            pltpu.VMEM((2, tokens, width // 2), BF),
            dma((2,)), dma((2,)), dma((5, n)), dma((5, n)), dma((chunks,)), dma((chunks,)), dma((3,)), dma((3,)), dma((10,)), dma((len(outs),)),
        ],
        compiler_params=pltpu.CompilerParams(
            collective_id=0, has_side_effects=True, vmem_limit_bytes=VMEM_GRANT
        ),
        name="attention_forward",
    )(x, cot, keys, values, segf, gain_one, gain_two, wq, wo)


class Gather:
    def __init__(self, place, whole, stride, first, land, send, recv, local, tokens):
        cols = land.shape[1]
        to = land.at[aligned(place.p, tokens), :]

        def half(c):
            return whole.at[:, pl.ds(pl.multiple_of(c * stride + first, LANE), cols)]

        c = place.c
        self.own = pltpu.make_async_copy(half(c), to, local)
        self.away = [
            remote(half(c), to, send.at[0], recv.at[0], place.side),
            remote(half(1 - c), to, send.at[1], recv.at[1], place.cross),
            remote(half(1 - c), to, send.at[2], recv.at[2], place.core),
        ]

    def start(self):
        self.own.start()
        for copy in self.away:
            copy.start()

    def wait(self):
        self.own.wait()
        for copy in self.away:
            copy.wait()


class Line:
    def __init__(self, place, nz, blk, land, left, move, got, total, out, turned, sems, work):
        self.place, self.nz, self.blk = place, nz, blk
        self.land, self.left, self.move, self.got, self.total, self.out = land, left, move, got, total, out
        self.turned = turned
        self.cols = land.shape[1]
        self.mv, self.lv, self.acc, self.stage, self.load_sem = work
        self.send, self.recv, self.end_s, self.end_r, self.end_l = sems

    def load(self, left_too):
        a = pltpu.make_async_copy(self.land, self.mv.at[:, : self.cols], self.load_sem.at[0])
        a.start()
        if left_too:
            b = pltpu.make_async_copy(self.left, self.lv, self.load_sem.at[1])
            b.start()
            b.wait()
        a.wait()

    def product(self, b):
        return dot_tn(self.lv[:, aligned(b, self.blk)], self.mv[:, : self.cols])

    def take(self, slot):
        self.arrival(slot).wait_recv()
        copy = pltpu.make_async_copy(self.got.at[slot], self.stage.at[:, : self.cols], self.load_sem.at[2])
        copy.start()
        copy.wait()
        return self.stage[:, : self.cols].astype(F32)

    def arrival(self, slot):
        return remote(self.move.at[0], self.got.at[slot], self.send.at[0], self.recv.at[slot], self.place.core)

    def route(self, j):
        z, nz = self.place.z, self.nz
        b = jnp.where(z < nz // 2, nz - 1 - j, j)
        b = jnp.where((j == nz - 2) & (z == 1), 0, b)
        b = jnp.where((j == nz - 2) & (z == nz - 2), nz - 1, b)
        up = b > z
        to = jnp.where(up, z + 1, z - 1)
        slot_in = jnp.where(up, b - z, nz - z + b)
        slot_out = jnp.where(up, b - to, nz - to + b)
        keep = jnp.where(up, b - 1, b)
        last = jnp.where(up, z == 0, z == nz - 1)
        device = (to * PLANE + self.place.p, self.place.t)
        out = remote(self.move.at[keep], self.got.at[slot_out], self.send.at[keep], self.recv.at[slot_out], device)
        return b, slot_in, keep, last, out

    def step(self, j):
        b, slot_in, keep, last, out = self.route(j)
        self.acc[:, : self.cols] = self.product(b)

        @pl.when(last)
        def _():
            self.move[keep] = self.acc[:, : self.cols].astype(BF)

        @pl.when(jnp.logical_not(last))
        def _():
            self.move[keep] = (self.acc[:, : self.cols] + self.take(slot_in)).astype(BF)

        out.start()

    def steps(self):
        def one(j, unused):
            self.step(j)
            return unused

        lax.fori_loop(0, self.nz - 1, one, 0)

    def sent(self):
        def one(j, unused):
            self.route(j)[4].wait_send()
            return unused

        lax.fori_loop(0, self.nz - 1, one, 0)

    def own_block(self):
        self.total[...] = self.product(self.place.z)

    def ends(self):
        half = self.blk // 2
        c, core = self.place.c, self.place.core
        if self.turned is None:
            to = self.out.at[:, aligned(c, self.cols)]
            mine, theirs = self.total.at[aligned(c, half), :], self.total.at[aligned(1 - c, half), :]
        else:
            turned, stride, first = self.turned
            to = self.out.at[pl.ds(pl.multiple_of(c * stride + first, LANE), self.cols), :]
            mine, theirs = (turned.at[: self.cols, aligned(k, half)] for k in (c, 1 - c))
        away = remote(theirs, to, self.end_s, self.end_r, core)
        here = pltpu.make_async_copy(mine, to, self.end_l)
        return away, here

    def finish(self):
        z, nz = self.place.z, self.nz

        @pl.when(z > 0)
        def _():
            self.total[...] += self.take(0)

        @pl.when(z < nz - 1)
        def _():
            self.total[...] += self.take(nz)

        if self.turned is not None:
            self.turned[0][: self.cols, :] = jnp.transpose(self.total[...])
        for copy in self.ends():
            copy.start()

    def left_here(self):
        away, here = self.ends()
        away.wait_send()
        here.wait()

    def arrived(self):
        self.ends()[0].wait_recv()


class Weights:
    def __init__(self, weights, buffers, sems, tail_sems, phase, cols, ff):
        self.weights, self.buffers, self.sems, self.tail_sems, self.phase = weights, buffers, sems, tail_sems, phase
        self.size = buffers.shape[1]
        self.cols = cols
        self.regular = 2 * (cols // self.size)
        self.rest = cols % self.size
        self.rest_two = ff - cols - cols // self.size * self.size

    def slot(self, i, w):
        return lax.rem(i + self.phase, 2) * 3 + w

    def copies(self, i):
        at = pl.ds(pl.multiple_of(lax.rem(i, 2) * self.cols + i // 2 * self.size, LANE), self.size)
        return [
            pltpu.make_async_copy(ref.at[at, :], self.buffers.at[self.slot(i, w)], self.sems.at[lax.rem(i, 2), w])
            for w, ref in enumerate(self.weights)
        ]

    def tail(self):
        first = self.cols // self.size * self.size
        copies = []
        for w, ref in enumerate(self.weights):
            to = self.buffers.at[self.slot(self.regular, w)]
            copies += [
                pltpu.make_async_copy(ref.at[pl.ds(first, self.rest), :], to.at[pl.ds(0, self.rest), :], self.tail_sems.at[0, w]),
                pltpu.make_async_copy(
                    ref.at[pl.ds(self.cols + first, self.rest_two), :],
                    to.at[pl.ds(self.rest, self.rest_two), :],
                    self.tail_sems.at[1, w],
                ),
            ]
        return copies

    def begin(self):
        for copy in self.copies(0):
            copy.start()

    def run(self, low, high, work):
        def one(i, unused):
            @pl.when(i + 1 < self.regular)
            def _():
                for copy in self.copies(i + 1):
                    copy.start()

            @pl.when(i + 1 == self.regular)
            def _():
                for copy in self.tail():
                    copy.start()

            for copy in self.copies(i):
                copy.wait()
            work([self.slot(i, w) for w in range(len(self.weights))], lax.rem(i, 2) * self.cols + i // 2 * self.size)
            return unused

        lax.fori_loop(low, high, one, 0)

    def end(self, work):
        for copy in self.tail():
            copy.wait()
        slots = [(self.regular + self.phase) % 2 * 3 + w for w in range(len(self.weights))]
        filled = self.rest + self.rest_two
        for slot in slots:
            self.buffers[slot, filled:, :] = jnp.zeros((self.size - filled, self.buffers.shape[2]), BF)
        work(slots, None)


def backward_kernel(
    geo, sizes,
    wg_in, wu_in, wd_in, two_norm_in, left_cot, left_two, middle_in, x_in, cot_in, att_in,
    q_in, k_in, v_in, o_in, lse_in, seg_in, wo_in, wq_in, gain_one, gain_two,
    ffn_own, ffn_in, input_grad, d_keys, d_values, gains,
    out_down, out_gate, out_up, out_out, out_query,
    m_down_a, m_down_b, m_gate, m_up, m_out, m_query, l_two, l_err, l_one,
    g_down_a, g_down_b, g_gate, g_up, g_out, g_query,
    mid, x_all, cot_all, two_norm, two_own, two_in, one_in, mixed, err, one, wbuf, d_att,
    hidden, d_gate, d_up, sums,
    uq, uk, uv, uo, udo, lse, seg_all, seg_row, seg_col, k_t, delta, udq, udk, udv, dq,
    gain_part, gain_in,
    s_first, s_second, s_out, s_query, t_first, t_second, t_out, t_query, turned,
    mv, lv, acc, stage,
    tp_s, tp_r, a_s, a_r, me_s, me_r, le_s, le_r, c_s, c_r, e_s, e_r, e_l, loc, work_sem, w_sem, tail_sem, o_sem,
):
    n, rows, tok, width, half, heads, length = geo
    ff, cols, cols_a = sizes
    tokens = rows * tok
    blk = 2 * width // n
    nz = n // PLANE
    place = Place(n)
    s, t, z = place.s, place.t, place.z
    row_s, head_s = s // heads, lax.rem(s, heads)
    mine = aligned(t, half)
    chunk = tokens // 4
    fine = 32
    size = wbuf.shape[1]

    first_pass = Weights((wg_in, wu_in, wd_in), wbuf, w_sem.at[0], tail_sem.at[0], 0, cols, ff)
    second_pass = Weights((wg_in, wu_in), wbuf, w_sem.at[1], tail_sem.at[1], 1, cols, ff)
    third_pass = Weights((wd_in,), wbuf, w_sem.at[2], tail_sem.at[2], 0, cols, ff)
    first_pass.begin()
    loads = [
        pltpu.make_async_copy(a, b, loc.at[8 + i])
        for i, (a, b) in enumerate((
            (two_norm_in, two_norm), (cot_in, cot_all), (middle_in, mid), (x_in, x_all),
            (q_in, uq), (k_in, uk), (v_in, uv), (o_in, uo), (lse_in, lse), (seg_in, seg_all),
        ))
    ]
    for copy in loads[:2]:
        copy.start()
    place.enter()

    rest_a = cols - cols_a
    gather_of = (
        (hidden, cols, 0, m_down_a), (hidden, cols, cols_a, m_down_b), (d_gate, cols, 0, m_gate), (d_up, cols, 0, m_up),
        (att_in, half // 2, 0, m_out), (dq, half // 2, 0, m_query),
    )
    gathers = [
        Gather(place, *refs, me_s.at[i], me_r.at[i], loc.at[i], tokens) for i, refs in enumerate(gather_of)
    ]
    lefts = [
        Plane(place, split, land, le_s.at[i], le_r.at[i], loc.at[25 + i], tokens)
        for i, (split, land) in enumerate(((left_two, l_two), (err, l_err), (one, l_one)))
    ]
    work = (mv, lv, acc, stage, work_sem)
    first_a, first_b = pl.ds(0, cols_a), pl.ds(cols_a, rest_a)
    lines = [
        Line(place, nz, blk, *refs, (c_s.at[i], c_r.at[i], e_s.at[i], e_r.at[i], e_l.at[i]), work)
        for i, refs in enumerate((
            (m_down_a, left_cot, s_first.at[:, :, first_a], g_down_a, t_first.at[:, first_a], out_down, (turned, cols, 0)),
            (m_down_b, left_cot, s_first.at[:, :, first_b], g_down_b, t_first.at[:, first_b], out_down, (turned, cols, cols_a)),
            (m_gate, l_two, s_second, g_gate, t_second, out_gate, (turned, cols, 0)),
            (m_up, l_two, s_first, g_up, t_first, out_up, (turned, cols, 0)),
            (m_out, l_err, s_out, g_out, t_out, out_out, None),
            (m_query, l_one, s_query, g_query, t_query, out_query, None),
        ))
    ]
    down_a, down_b, gate, up, out, query = lines

    for copy in loads[:2]:
        copy.wait()

    def units(slots, at):
        wg, wu, wd = (wbuf[slot] for slot in slots)
        x, g = two_norm[...], cot_all[...]
        gate_now, up_now = dot_nt(x, wg), dot_nt(x, wu)
        d_hid = dot_nt(g, wd)
        sigma = jax.nn.sigmoid(gate_now)
        act = gate_now * sigma
        for ref, now in (
            (hidden, act * up_now),
            (d_gate, d_hid * up_now * sigma * (1.0 + gate_now * (1.0 - sigma))),
            (d_up, d_hid * act),
        ):
            now = now.astype(BF)
            if at is None:
                last, rest = cols // size * size, cols % size
                ref[:, last:cols] = now[:, :rest]
                ref[:, cols + last :] = now[:, rest : 2 * rest]
            else:
                ref[:, pl.ds(pl.multiple_of(at, LANE), size)] = now

    first_pass.run(0, 2 * (cols_a // size), units)
    gathers[0].start()
    first_pass.run(2 * (cols_a // size), first_pass.regular, units)
    second_pass.begin()
    first_pass.end(units)
    gathers[1].start()
    lefts[0].start()
    for copy in loads[2:]:
        copy.start()

    def block_of(ref, at):
        if at is None:
            last, rest = cols // size * size, cols % size
            return jnp.concatenate([ref[:, last:cols], ref[:, cols + last :]], axis=1)
        return ref[:, pl.ds(pl.multiple_of(at, LANE), size)]

    def add_up(pairs):
        for db in range(width // size):
            at = slice(db * size, (db + 1) * size)
            sums[db * tokens : (db + 1) * tokens, :] += sum(dot_nn(a, wbuf[slot, :, at]) for a, slot in pairs)

    def back_units(slots, at):
        add_up([(block_of(d_gate, at), slots[0]), (block_of(d_up, at), slots[1])])

    sums[...] = jnp.zeros_like(sums)
    second_pass.run(0, second_pass.regular, back_units)
    second_pass.end(back_units)
    for db in range(width // size):
        two_own[:, db * size : (db + 1) * size] = sums[db * tokens : (db + 1) * tokens, :].astype(BF)

    def two_copy(i):
        at = aligned(i, chunk)
        return remote(two_own.at[at, :], two_in.at[at, :], tp_s.at[i], tp_r.at[i], place.twin)

    for i in range(4):
        two_copy(i).start()
    load_square = []
    for k, ref in enumerate((wo_in, wq_in)):
        for zy in range(n // 2):
            to = wbuf.at[4 * k + zy // 2, :, (zy % 2) * half : (zy % 2 + 1) * half]
            load_square.append(pltpu.make_async_copy(ref.at[zy * blk : (zy + 1) * blk, :], to, o_sem.at[k, zy]))
    for copy in load_square:
        copy.start()

    def square_block(k, zy):
        return wbuf[4 * k + zy // 2, :, (zy % 2) * half : (zy % 2 + 1) * half]

    gathers[0].wait()
    down_a.load(True)
    down_a.steps()
    down_a.own_block()

    spread_att = Spread(
        place,
        lambda d: d_att.at[aligned(d // heads, tok), aligned(lax.rem(d, heads), HEAD_DIM)],
        lambda: udo.at[aligned(s, tok), :],
        a_s.at[0], a_r.at[0], loc.at[18],
    )
    loads[2].wait()
    for copy in load_square[: n // 2]:
        copy.wait()

    def second_norm(i, gain_sum):
        two_copy(i).wait()

        def some(j, gain_sum):
            at = aligned(i * (chunk // fine) + j, fine)
            m = mid[at, :]
            d2 = two_own[at, :].astype(F32) + two_in[at, :].astype(F32)
            root = lax.rsqrt(jnp.mean(m * m, axis=-1, keepdims=True) + EPSILON)
            gained = d2 * gain_two[...]
            scaled = m * root
            gain_sum = gain_sum + jnp.sum(d2 * scaled, axis=0, keepdims=True)
            slope = jnp.mean(gained * scaled, axis=-1, keepdims=True)
            dm = cot_all[at, :].astype(F32) + root * (gained - scaled * slope)
            mid[at, :] = dm
            low = dm.astype(BF)
            for zy in range(n // 2):
                zz, yy = divmod(zy, 2)
                err[yy, at, zz * blk : (zz + 1) * blk] = low[:, zy * blk : (zy + 1) * blk]
            return gain_sum

        gain_sum = lax.fori_loop(0, chunk // fine, some, gain_sum)
        at = aligned(i, chunk)
        total = jnp.zeros((chunk, half), F32)
        for zy in range(n // 2):
            zz, yy = divmod(zy, 2)
            total += dot_nn(err[yy, at, zz * blk : (zz + 1) * blk], square_block(0, zy))
        d_att[at, :] = total.astype(BF)
        return gain_sum

    gain_sum = jnp.zeros((1, width), F32)
    per_row = tok // chunk
    for r in range(rows):
        gain_sum = lax.fori_loop(r * per_row, (r + 1) * per_row, second_norm, gain_sum)
        lax.fori_loop(r * heads, (r + 1) * heads, spread_att.start_to, 0)
    for i in range(n):
        gain_part[0, i] = gain_sum[:, i * (width // n) : (i + 1) * (width // n)]
    spread_gain = [
        Spread(place, lambda d, g=g: gain_part.at[g, d], lambda g=g: gain_in.at[g, s], a_s.at[4 + g], a_r.at[4 + g], loc.at[22 + g])
        for g in range(2)
    ]
    spread_gain[0].start()
    lefts[0].forward()
    gathers[2].start()
    gathers[3].start()
    lefts[1].start()
    gathers[4].start()

    gathers[1].wait()
    down_b.load(False)
    at_end = (z == 0) | (z == nz - 1)

    @pl.when(at_end)
    def _():
        down_b.steps()

    down_b.own_block()

    third_pass.begin()
    sums[...] = jnp.zeros_like(sums)

    def out_units(slots, at):
        add_up([(block_of(hidden, at), slots[0])])

    third_pass.run(0, third_pass.regular, out_units)
    third_pass.end(out_units)
    for db in range(width // size):
        mixed[:, db * size : (db + 1) * size] = sums[db * tokens : (db + 1) * tokens, :].astype(BF)
    ffn_copy = remote(mixed.at[:, aligned(1 - t, half)], ffn_in, tp_s.at[4], tp_r.at[4], place.twin)
    ffn_copy.start()
    ffn_keep = pltpu.make_async_copy(mixed.at[:, mine], ffn_own, loc.at[6])
    ffn_keep.start()

    for copy in loads[3:]:
        copy.wait()

    def first_norm(j, unused):
        at = aligned(j, fine)
        x = x_all[at, :].astype(F32)
        root = lax.rsqrt(jnp.mean(x * x, axis=-1, keepdims=True) + EPSILON)
        low = (x * root * gain_one[...]).astype(BF)
        for zy in range(n // 2):
            zz, yy = divmod(zy, 2)
            one[yy, at, zz * blk : (zz + 1) * blk] = low[:, zy * blk : (zy + 1) * blk]
        return unused

    lax.fori_loop(0, tokens // fine, first_norm, 0)
    attention_masks(seg_all, seg_row, seg_col, n, tok)

    def turn(i, unused):
        at = aligned(i, tok)
        k_t[:, at] = jnp.transpose(uk[at, :].astype(F32)).astype(BF)
        return unused

    lax.fori_loop(0, n, turn, 0)
    sums[...] = jnp.zeros_like(sums)

    spread_att.wait()

    def turn_delta(i, unused):
        at = aligned(i, tok)
        both = udo[at, :].astype(F32) * uo[at, :].astype(F32)
        delta[:, at] = jnp.sum(jnp.transpose(both), axis=0, keepdims=True)
        return unused

    lax.fori_loop(0, n, turn_delta, 0)

    block = 512
    owners = block // tok

    def home(ref):
        return lambda: ref.at[aligned(row_s, tok), aligned(head_s, HEAD_DIM)]

    spread_dq, spread_dk, spread_dv = (
        Spread(place, lambda d, unit=unit: unit.at[aligned(d, tok), :], home(whole), a_s.at[i], a_r.at[i], loc.at[18 + i])
        for i, unit, whole in ((1, udq, dq), (2, udk, d_keys), (3, udv, d_values))
    )

    def query_step(i, unused):
        qi = length // block - 1 - i
        qat = aligned(qi, block)
        qb, dob = uq[qat, :], udo[qat, :]

        def key_step(kj, dq_t):
            kat = aligned(kj, block)
            scores = dot_nt(uk[kat, :], qb) - lse[:, qat]
            probs = jnp.exp(jnp.where(readable(seg_col, seg_row, kj, qi, block), scores, NEGATIVE_FILL))
            d_probs = dot_nt(uv[kat, :], dob)
            d_scores = (probs * (d_probs - delta[:, qat])).astype(BF)
            sums[kat, :HEAD_DIM] += dot_nn(d_scores, qb)
            sums[kat, HEAD_DIM:] += dot_nn(probs.astype(BF), dob)
            return dq_t + dot_nn(k_t[:, kat], d_scores)

        dq_t = lax.fori_loop(0, qi + 1, key_step, jnp.zeros((HEAD_DIM, block), F32))
        udq[qat, :] = jnp.transpose(dq_t).astype(BF)
        lax.fori_loop(qi * owners, (qi + 1) * owners, spread_dq.start_to, 0)
        udk[qat, :] = sums[qat, :HEAD_DIM].astype(BF)
        udv[qat, :] = sums[qat, HEAD_DIM:].astype(BF)
        lax.fori_loop(qi * owners, (qi + 1) * owners, spread_dk.start_to, 0)
        lax.fori_loop(qi * owners, (qi + 1) * owners, spread_dv.start_to, 0)
        return unused

    lax.fori_loop(0, length // block, query_step, 0)

    @pl.when(jnp.logical_not(at_end))
    def _():
        down_b.steps()

    down_a.finish()
    gathers[2].wait()
    lefts[0].finish()
    gate.load(True)
    gate.steps()
    gate.own_block()
    down_a.left_here()
    down_b.finish()

    for copy in load_square[n // 2 :]:
        copy.wait()
    spread_dq.wait()
    gathers[5].start()
    lefts[2].start()
    lefts[1].forward()

    def one_copy(i):
        at = aligned(i, chunk)
        return remote(two_own.at[at, :], one_in.at[at, :], tp_s.at[5 + i], tp_r.at[5 + i], place.twin)

    def back_query(i, unused):
        at = aligned(i, chunk)
        for zy in range(n // 2):
            now = dot_nt(dq[at, :], square_block(1, zy)) * HEAD_DIM ** (-0.5)
            two_own[at, zy * blk : (zy + 1) * blk] = now.astype(BF)
        one_copy(i).start()
        return unused

    lax.fori_loop(0, 4, back_query, 0)

    gathers[3].wait()
    down_a.sent()
    down_b.sent()
    up.load(False)
    up.steps()
    up.own_block()

    def last_norm(i, gain_sum):
        one_copy(i).wait()

        def some(j, gain_sum):
            at = aligned(i * (chunk // fine) + j, fine)
            x = x_all[at, :].astype(F32)
            d1 = two_own[at, :].astype(F32) + one_in[at, :].astype(F32)
            root = lax.rsqrt(jnp.mean(x * x, axis=-1, keepdims=True) + EPSILON)
            gained = d1 * gain_one[...]
            scaled = x * root
            gain_sum = gain_sum + jnp.sum(d1 * scaled, axis=0, keepdims=True)
            slope = jnp.mean(gained * scaled, axis=-1, keepdims=True)
            mid[at, :] = mid[at, :] + root * (gained - scaled * slope)
            return gain_sum

        return lax.fori_loop(0, chunk // fine, some, gain_sum)

    gain_sum = lax.fori_loop(0, 4, last_norm, jnp.zeros((1, width), F32))
    for i in range(n):
        gain_part[1, i] = gain_sum[:, i * (width // n) : (i + 1) * (width // n)]
    spread_gain[1].start()
    give = pltpu.make_async_copy(mid.at[:, mine], input_grad, loc.at[24])
    give.start()

    gathers[4].wait()
    lefts[1].finish()
    lefts[2].forward()
    out.load(True)
    out.steps()
    out.own_block()

    gathers[5].wait()
    lefts[2].finish()
    query.load(True)
    query.steps()
    query.own_block()
    down_b.left_here()
    gate.finish()
    gate.left_here()
    up.finish()
    out.finish()
    query.finish()

    spread_dk.wait()
    spread_dv.wait()
    for g in range(2):
        spread_gain[g].wait()
        gains[g] = jnp.sum(gain_in[g], axis=0)
    ffn_copy.wait()
    ffn_keep.wait()
    give.wait()
    for line in lines[2:]:
        line.sent()
    for line in lines[3:]:
        line.left_here()
    for line in lines:
        line.arrived()


def backward_part(geo, forward, wg, wu, wd, wo, wq, gain_one, gain_two):
    n, rows, tok, width, half, heads, length = geo
    tokens = rows * tok
    blk = 2 * width // n
    nz = n // PLANE
    ff = wg.shape[0]
    size = 2 * LANE
    cols = -(-ff // size) * LANE
    cols_a = cols // size * size // 2 // size * size + (size if cols // size % 2 else 0)
    sizes = (ff, cols, cols_a)
    x_all, cot_all, left_cot, middle, normed_two, left_two, attended, uq, uk, uv, uo, lse, seg_all = forward
    dma = pltpu.SemaphoreType.DMA
    anywhere, here = pl.BlockSpec(memory_space=pl.ANY), pl.BlockSpec(memory_space=pltpu.VMEM)
    wide = (cols_a, cols - cols_a, cols, cols, half // 2, half // 2)
    outs = [
        (vm((tokens, half), BF), anywhere),
        (vm((tokens, half), BF), anywhere),
        (vm((tokens, half), F32), anywhere),
        (vm((tokens, half), BF), anywhere),
        (vm((tokens, half), BF), anywhere),
        (vm((2, 1, width // n), F32), here),
        *((vm((2 * cols, blk // 2), F32), anywhere) for _ in range(3)),
        *((vm((blk // 2, half), F32), anywhere) for _ in range(2)),
        *((vm((PLANE * tokens, c), BF), anywhere) for c in wide),
        *((vm((PLANE * tokens, width // 2), BF), anywhere) for _ in range(3)),
        *((vm((nz + 1, blk, c), BF), anywhere) for c in wide),
    ]
    inputs = [
        wg, wu, wd, normed_two, left_cot, left_two, middle, x_all, cot_all, attended,
        uq, uk, uv, uo, lse, seg_all, wo, wq, gain_one, gain_two,
    ]
    unit = pltpu.VMEM((length, HEAD_DIM), BF)
    line = pltpu.VMEM((1, length), F32)
    act = pltpu.VMEM((tokens, width), BF)
    split = pltpu.VMEM((2, tokens, width // 2), BF)
    hid = pltpu.VMEM((tokens, 2 * cols), BF)
    scratch = [
        pltpu.VMEM((tokens, width), F32), act, act, act, act, act, act, act, split, split,
        pltpu.VMEM((8, size, width), BF), pltpu.VMEM((tokens, half), BF),
        hid, hid, hid, pltpu.VMEM((length, size), F32),
        unit, unit, unit, unit, unit, line, pltpu.VMEM((n, 1, tok), F32), line,
        pltpu.VMEM((length, LANE), F32), pltpu.VMEM((HEAD_DIM, length), BF), line,
        unit, unit, unit, pltpu.VMEM((tokens, half), BF),
        pltpu.VMEM((2, n, 1, width // n), F32), pltpu.VMEM((2, n, 1, width // n), F32),
        *(pltpu.VMEM((nz - 1, blk, c), BF) for c in wide[2:]),
        *(pltpu.VMEM((blk, c), F32) for c in wide[2:]),
        pltpu.VMEM((cols, blk), F32),
        pltpu.VMEM((PLANE * tokens, cols), BF), pltpu.VMEM((PLANE * tokens, width // 2), BF),
        pltpu.VMEM((blk, cols), F32), pltpu.VMEM((blk, cols), BF),
        dma((9,)), dma((9,)), dma((6, n)), dma((6, n)), dma((6, 3)), dma((6, 3)), dma((3, 3)), dma((3, 3)),
        dma((6, nz - 1)), dma((6, nz + 1)), dma((6,)), dma((6,)), dma((6,)), dma((28,)), dma((3,)),
        dma((3, 2, 3)), dma((3, 2, 3)), dma((2, n // 2)),
    ]
    return pl.pallas_call(
        functools.partial(backward_kernel, geo, sizes),
        out_shape=[o for o, _ in outs],
        in_specs=[anywhere] * (len(inputs) - 2) + [here] * 2,
        out_specs=[spec for _, spec in outs],
        scratch_shapes=scratch,
        compiler_params=pltpu.CompilerParams(
            collective_id=1, has_side_effects=True, vmem_limit_bytes=VMEM_GRANT
        ),
        name="feed_forward_and_backward",
    )(*inputs)


def fast_device(
    n, inputs, segments, keys, values, attn_gain, query_weight, out_weight, ffn_gain, gate_weight, up_weight, down_weight,
    cotangent,
):
    rows, tok, half = inputs.shape
    tokens, width, ff = rows * tok, query_weight.shape[0], gate_weight.shape[1]
    heads = half // HEAD_DIM
    geo = (n, rows, tok, width, half, heads, n * tok)

    def flat(a):
        return a.reshape(tokens, half)

    segf = segments.astype(F32).reshape(rows, 1, tok)
    gain_one, gain_two = attn_gain.reshape(1, width), ffn_gain.reshape(1, width)
    forward = forward_part(
        geo, flat(inputs), flat(cotangent), flat(keys), flat(values), segf, gain_one, gain_two, query_weight, out_weight
    )
    back = backward_part(
        geo, forward, gate_weight.T, up_weight.T, down_weight.T, out_weight, query_weight, gain_one, gain_two
    )
    ffn_own, ffn_in, input_grad, d_keys, d_values, gains, g_down, g_gate, g_up, g_out, g_query = back[:11]
    middle = lax.dynamic_slice_in_dim(forward[3], lax.axis_index("tp") * half, half, 1)
    mixed = (middle + ffn_own.astype(F32) + ffn_in.astype(F32)).astype(BF)

    def shaped(a):
        return a.reshape(rows, tok, half)

    return (
        shaped(mixed),
        shaped(input_grad),
        shaped(d_keys.astype(F32)),
        shaped(d_values.astype(F32)),
        gains[1, 0],
        g_query * HEAD_DIM ** (-0.5),
        g_out,
        gains[0, 0],
        g_gate[:ff].T,
        g_up[:ff].T,
        g_down[:ff].T,
    )


def inverse_root(stream):
    return lax.rsqrt(jnp.mean(stream * stream, axis=-1, keepdims=True) + EPSILON)


def key_mask(doc_start, query_pos, begin, row_count):
    key_pos = begin + jnp.arange(row_count, dtype=jnp.int32)
    earlier = key_pos[None, None, :] <= query_pos[None, :, None]
    same_doc = key_pos[None, None, :] >= doc_start[:, :, None]
    return (earlier & same_doc)[:, None]


def per_device(
    inputs,
    segments,
    keys,
    values,
    attn_gain,
    query_weight,
    out_weight,
    ffn_gain,
    gate_weight,
    up_weight,
    down_weight,
    cotangent,
):
    batch_rows, local_tokens, half_width = inputs.shape
    local_heads = half_width // HEAD_DIM
    seq_devices = lax.axis_size("seq")
    row_length = local_tokens * seq_devices
    seq_index = lax.axis_index("seq")
    tp_index = lax.axis_index("tp")
    query_scale = HEAD_DIM ** (-0.5)
    bfloat = jnp.bfloat16
    single = jnp.float32
    whole = lax.all_gather(inputs, "tp", axis=2, tiled=True).astype(single)
    root_one = inverse_root(whole)
    scaled_one = whole * root_one
    normed_one = (scaled_one * attn_gain).astype(bfloat)
    query = (
        jnp.einsum("rtd,de->rte", normed_one, query_weight, preferred_element_type=single)
        * query_scale
    ).astype(bfloat)
    query_heads = query.reshape(batch_rows, local_tokens, local_heads, HEAD_DIM)
    bins = jnp.arange(CUTS + 1, dtype=jnp.int32)
    onehot = (segments[:, :, None] == bins[None, None, :]).astype(single)
    totals = lax.psum(jnp.sum(onehot, axis=1), "seq")
    ends = jnp.cumsum(totals, axis=-1)
    before = ends - totals
    doc_start = jnp.sum(onehot * before[:, None, :], axis=-1).astype(jnp.int32)
    query_pos = seq_index * local_tokens + jnp.arange(local_tokens, dtype=jnp.int32)
    first_needed = jnp.min(doc_start)
    last_needed = seq_index * local_tokens + local_tokens - 1
    start_state = (
        jnp.full((batch_rows, local_heads, local_tokens), NEGATIVE_FILL, single),
        jnp.zeros((batch_rows, local_heads, local_tokens), single),
        jnp.zeros((batch_rows, local_heads, local_tokens, HEAD_DIM), single),
    )
    key_piece = lax.all_gather(keys, "seq", axis=1, tiled=True)
    value_piece = lax.all_gather(values, "seq", axis=1, tiled=True)
    piece_rows = key_piece.shape[1]
    fold_key_block = math.gcd(piece_rows, 512)

    def fold_step(block_index, state):
        running_max, running_sum, running_out = state
        begin = block_index * fold_key_block

        def fold_work(unused):
            key_heads = lax.dynamic_slice_in_dim(
                key_piece, block_index * fold_key_block, fold_key_block, 1
            ).reshape(batch_rows, fold_key_block, local_heads, HEAD_DIM)
            value_heads = lax.dynamic_slice_in_dim(
                value_piece, block_index * fold_key_block, fold_key_block, 1
            ).reshape(batch_rows, fold_key_block, local_heads, HEAD_DIM)
            scores = jnp.einsum(
                "rqhe,rkhe->rhqk", query_heads, key_heads, preferred_element_type=single
            )
            allowed = key_mask(doc_start, query_pos, begin, fold_key_block)
            scores = jnp.where(allowed, scores, NEGATIVE_FILL)
            new_max = jnp.maximum(running_max, jnp.max(scores, axis=-1))
            weights = jnp.where(allowed, jnp.exp(scores - new_max[..., None]), 0.0)
            decay = jnp.exp(running_max - new_max)
            new_sum = running_sum * decay + jnp.sum(weights, axis=-1)
            new_out = running_out * decay[..., None] + jnp.einsum(
                "rhqk,rkhe->rhqe",
                weights.astype(bfloat),
                value_heads,
                preferred_element_type=single,
            )
            return (new_max, new_sum, new_out)

        def keep_state(unused):
            return (running_max, running_sum, running_out)

        needed = (begin <= last_needed) & (begin + fold_key_block - 1 >= first_needed)
        return lax.cond(needed, fold_work, keep_state, 0)

    running_max, running_sum, running_out = lax.fori_loop(
        0, piece_rows // fold_key_block, fold_step, start_state
    )
    log_total = running_max + jnp.log(running_sum)
    attended = running_out / running_sum[..., None]
    attended_low = (
        attended.transpose(0, 2, 1, 3).reshape(batch_rows, local_tokens, half_width).astype(bfloat)
    )
    branch = jnp.einsum("rth,dh->rtd", attended_low, out_weight, preferred_element_type=single)
    middle = whole + lax.psum(branch.astype(jnp.bfloat16), "tp").astype(jnp.float32)
    middle_share = lax.dynamic_slice_in_dim(middle, tp_index * half_width, half_width, 2)
    root_two = inverse_root(middle)
    scaled_two = middle * root_two
    normed_two = (scaled_two * ffn_gain).astype(bfloat)
    gate = jnp.einsum("rtd,df->rtf", normed_two, gate_weight, preferred_element_type=single)
    up_proj = jnp.einsum("rtd,df->rtf", normed_two, up_weight, preferred_element_type=single)
    sigma = jax.nn.sigmoid(gate)
    activated = gate * sigma
    hidden = (activated * up_proj).astype(bfloat)
    ffn_part = jnp.einsum("rtf,df->rtd", hidden, down_weight, preferred_element_type=single)
    output = (
        middle_share
        + lax.psum_scatter(
            ffn_part.astype(jnp.bfloat16), "tp", scatter_dimension=2, tiled=True
        ).astype(jnp.float32)
    ).astype(bfloat)
    grad_out = lax.all_gather(cotangent, "tp", axis=2, tiled=True)
    d_hidden = jnp.einsum("rtd,df->rtf", grad_out, down_weight, preferred_element_type=single)
    d_gate = (d_hidden * up_proj * sigma * (1.0 + gate * (1.0 - sigma))).astype(bfloat)
    d_up = (d_hidden * activated).astype(bfloat)
    d_two_part = jnp.einsum(
        "rtf,df->rtd", d_gate, gate_weight, preferred_element_type=single
    ) + jnp.einsum("rtf,df->rtd", d_up, up_weight, preferred_element_type=single)
    d_two = lax.psum(d_two_part.astype(jnp.bfloat16), "tp").astype(jnp.float32)
    gained_two = d_two * ffn_gain
    d_middle = (
        grad_out.astype(single)
        + root_two * gained_two
        - middle * root_two**3 * jnp.mean(gained_two * middle, axis=-1, keepdims=True)
    )
    normed_rows = normed_two
    gate_term = jnp.einsum("rtd,rtf->df", normed_rows, d_gate, preferred_element_type=single)
    up_term = jnp.einsum("rtd,rtf->df", normed_rows, d_up, preferred_element_type=single)
    down_term = jnp.einsum("rtd,rtf->df", grad_out, hidden, preferred_element_type=single)
    gain_term = jnp.sum(d_two * scaled_two, axis=(0, 1))
    gate_grad, up_grad, down_grad, ffn_gain_grad = lax.psum_scatter(
        (gate_term, up_term, down_term, gain_term), "seq", scatter_dimension=0, tiled=True
    )
    error = d_middle.astype(bfloat)
    d_attended = jnp.einsum("rtd,dh->rth", error, out_weight, preferred_element_type=single).astype(
        bfloat
    )
    d_heads = d_attended.reshape(batch_rows, local_tokens, local_heads, HEAD_DIM)
    carried = jnp.einsum("rqhe,rhqe->rhq", d_heads.astype(single), attended)
    key_all, value_all = (
        lax.all_gather(keys, "seq", axis=1, tiled=True),
        lax.all_gather(values, "seq", axis=1, tiled=True),
    )
    key_block = math.gcd(row_length, 512)

    def block_terms(begin):
        key_heads = lax.dynamic_slice_in_dim(key_all, begin, key_block, 1).reshape(
            batch_rows, key_block, local_heads, HEAD_DIM
        )
        value_heads = lax.dynamic_slice_in_dim(value_all, begin, key_block, 1).reshape(
            batch_rows, key_block, local_heads, HEAD_DIM
        )
        scores = jnp.einsum(
            "rqhe,rkhe->rhqk", query_heads, key_heads, preferred_element_type=single
        )
        allowed = key_mask(doc_start, query_pos, begin, key_block)
        probs = jnp.where(
            allowed, jnp.exp(jnp.where(allowed, scores, NEGATIVE_FILL) - log_total[..., None]), 0.0
        )
        d_probs = jnp.einsum("rqhe,rkhe->rhqk", d_heads, value_heads, preferred_element_type=single)
        d_scores = (probs * (d_probs - carried[..., None])).astype(bfloat)
        query_part = jnp.einsum(
            "rhqk,rkhe->rhqe", d_scores, key_heads, preferred_element_type=single
        )
        return (probs, d_scores, query_part)

    query_zero = jnp.zeros((batch_rows, local_heads, local_tokens, HEAD_DIM), single)

    def back_step(block_index, state):
        d_query, key_terms, value_terms = state
        begin = block_index * key_block

        def back_work(unused):
            probs, d_scores, query_part = block_terms(begin)
            value_part = jnp.einsum(
                "rhqk,rqhe->rkhe", probs.astype(bfloat), d_heads, preferred_element_type=single
            )
            key_part = jnp.einsum(
                "rhqk,rqhe->rkhe", d_scores, query_heads, preferred_element_type=single
            )
            return (
                query_part,
                key_part.reshape(batch_rows, key_block, half_width),
                value_part.reshape(batch_rows, key_block, half_width),
            )

        def skip_block(unused):
            empty_rows = jnp.zeros((batch_rows, key_block, half_width), single)
            return (jnp.zeros_like(d_query), empty_rows, empty_rows)

        needed = (begin <= last_needed) & (begin + key_block - 1 >= first_needed)
        query_part, key_part, value_part = lax.cond(needed, back_work, skip_block, 0)
        return (
            d_query + query_part,
            lax.dynamic_update_slice_in_dim(key_terms, key_part, begin, 1),
            lax.dynamic_update_slice_in_dim(value_terms, value_part, begin, 1),
        )

    back_start = (
        query_zero,
        jnp.zeros((batch_rows, row_length, half_width), single),
        jnp.zeros((batch_rows, row_length, half_width), single),
    )
    d_query, key_terms, value_terms = lax.fori_loop(
        0, row_length // key_block, back_step, back_start
    )
    key_grad, value_grad = (
        lax.psum_scatter(key_terms, "seq", scatter_dimension=1, tiled=True),
        lax.psum_scatter(value_terms, "seq", scatter_dimension=1, tiled=True),
    )
    d_query_rows = (
        d_query.transpose(0, 2, 1, 3).reshape(batch_rows, local_tokens, half_width).astype(bfloat)
    )
    d_one_part = (
        jnp.einsum("rte,de->rtd", d_query_rows, query_weight, preferred_element_type=single)
        * query_scale
    )
    d_one = lax.psum(d_one_part.astype(jnp.bfloat16), "tp").astype(jnp.float32)
    gained_one = d_one * attn_gain
    d_whole = (
        d_middle
        + root_one * gained_one
        - whole * root_one**3 * jnp.mean(gained_one * whole, axis=-1, keepdims=True)
    )
    input_grad = lax.dynamic_slice_in_dim(d_whole, tp_index * half_width, half_width, 2)
    normed_rows = normed_one
    query_term = (
        jnp.einsum("rtd,rte->de", normed_rows, d_query_rows, preferred_element_type=single)
        * query_scale
    )
    out_term = jnp.einsum("rtd,rth->dh", error, attended_low, preferred_element_type=single)
    gain_term = jnp.sum(d_one * scaled_one, axis=(0, 1))
    query_grad, out_grad, attn_gain_grad = lax.psum_scatter(
        (query_term, out_term, gain_term), "seq", scatter_dimension=0, tiled=True
    )
    return (
        output,
        input_grad,
        key_grad,
        value_grad,
        attn_gain_grad,
        query_grad,
        out_grad,
        ffn_gain_grad,
        gate_grad,
        up_grad,
        down_grad,
    )


def solution(mesh):
    in_specs = (
        P(None, "seq", "tp"),
        P(None, "seq"),
        P(None, "seq", "tp"),
        P(None, "seq", "tp"),
        P(),
        P(None, "tp"),
        P(None, "tp"),
        P(),
        P(None, "tp"),
        P(None, "tp"),
        P(None, "tp"),
        P(None, "seq", "tp"),
    )
    out_specs = (
        P(None, "seq", "tp"),
        P(None, "seq", "tp"),
        P(None, "seq", "tp"),
        P(None, "seq", "tp"),
        P("seq"),
        P("seq", "tp"),
        P("seq", "tp"),
        P("seq"),
        P("seq", "tp"),
        P("seq", "tp"),
        P("seq", "tp"),
    )
    n = mesh.shape["seq"]

    def step(inputs, *others):
        rows, tok, half = inputs.shape
        units = rows * (half // HEAD_DIM)
        if units == n == PLANE * PLANE and 4 * tok == 512 and mesh.shape["tp"] == 2:
            return fast_device(n, inputs, *others)
        return per_device(inputs, *others)

    return jax.shard_map(
        step, mesh=mesh, in_specs=in_specs, out_specs=out_specs, check_vma=False
    )
```

```python
import functools
import math

import jax
import jax.numpy as jnp
from jax import lax
from jax.experimental import pallas as pl
from jax.experimental.pallas import tpu as pltpu
from jax.sharding import PartitionSpec as P

HEAD_DIM = 128
CUTS = 12


EPSILON = 1e-06
NEGATIVE_FILL = -1e30

MESH = pl.DeviceIdType.MESH
BF = jnp.bfloat16
F32 = jnp.float32
VMEM_GRANT = 62 << 20
PLANE = 4
LANE = 128


def dot_nn(a, b):
    return lax.dot_general(a, b, (((1,), (0,)), ((), ())), preferred_element_type=F32)


def dot_nt(a, b):
    return lax.dot_general(a, b, (((1,), (1,)), ((), ())), preferred_element_type=F32)


def dot_tn(a, b):
    return lax.dot_general(a, b, (((0,), (0,)), ((), ())), preferred_element_type=F32)


def aligned(index, size):
    return pl.ds(pl.multiple_of(index * size, size), size)


class Place:
    def __init__(self, n):
        self.n = n
        self.s = lax.axis_index("seq")
        self.t = lax.axis_index("tp")
        self.z = self.s // PLANE
        self.p = lax.rem(self.s, PLANE)
        self.y = self.p // 2
        self.c = lax.rem(self.p, 2)
        base = self.z * PLANE
        self.core_p = self.y * 2 + 1 - self.c
        self.side_p = (1 - self.y) * 2 + self.c
        self.cross_p = (1 - self.y) * 2 + 1 - self.c
        self.core = (base + self.core_p, self.t)
        self.side = (base + self.side_p, self.t)
        self.cross = (base + self.cross_p, self.t)
        self.twin = (self.s, 1 - self.t)

    def other(self, k):
        return lax.rem(self.s + k, self.n)

    def enter(self):
        barrier = pltpu.get_barrier_semaphore()

        def greet(k, unused):
            pl.semaphore_signal(barrier, inc=1, device_id=(self.other(k), self.t), device_id_type=MESH)
            return unused

        lax.fori_loop(1, self.n, greet, 0)
        pl.semaphore_signal(barrier, inc=1, device_id=self.twin, device_id_type=MESH)
        pl.semaphore_wait(barrier, self.n)


def remote(src, dst, send, recv, device):
    return pltpu.make_async_remote_copy(
        src_ref=src, dst_ref=dst, send_sem=send, recv_sem=recv, device_id=device, device_id_type=MESH
    )


class Spread:
    def __init__(self, place, src, dst, send, recv, local):
        self.place, self.src, self.dst, self.send, self.recv, self.local = place, src, dst, send, recv, local

    def copy(self, k):
        place = self.place
        d = place.other(k)
        return remote(self.src(d), self.dst(), self.send.at[k], self.recv.at[k], (d, place.t))

    def own(self):
        return pltpu.make_async_copy(self.src(self.place.s), self.dst(), self.local)

    def start(self):
        self.own().start()

        def one(k, unused):
            self.copy(k).start()
            return unused

        lax.fori_loop(1, self.place.n, one, 0)

    def start_to(self, d, unused):
        k = lax.rem(d - self.place.s + self.place.n, self.place.n)

        @pl.when(k == 0)
        def _():
            self.own().start()

        @pl.when(k != 0)
        def _():
            self.copy(k).start()

        return unused

    def wait(self):
        self.own().wait()

        def one(k, unused):
            self.copy(k).wait()
            return unused

        lax.fori_loop(1, self.place.n, one, 0)


def attention_masks(seg_all, seg_row, seg_col, n, tok):
    def one(i, unused):
        piece = seg_all[i]
        seg_row[:, aligned(i, tok)] = piece
        seg_col[aligned(i, tok), :] = jnp.transpose(jnp.broadcast_to(piece, (tok, tok)))
        return unused

    lax.fori_loop(0, n, one, 0)


def readable(seg_col, seg_row, key_block, query_block, block):
    key_seg = seg_col[aligned(key_block, block), :]
    key_seg = jnp.concatenate([key_seg] * (block // LANE), axis=1)
    query_seg = seg_row[:, aligned(query_block, block)]
    key_pos = key_block * block + lax.broadcasted_iota(jnp.int32, (block, block), 0)
    query_pos = query_block * block + lax.broadcasted_iota(jnp.int32, (block, block), 1)
    return (key_seg == query_seg) & (key_pos <= query_pos)


def forward_kernel(
    geo,
    x_in, cot_in, key_in, value_in, seg_in, gain_one, gain_two, wq_in, wo_in,
    x_out, cot_out, left_out, middle_out, two_out, split_out, att_out, q_out, k_out, v_out, o_out, lse_out, seg_out,
    x_all, cot_all, left_cot, middle, normed_two, left_two, attended, unit_q, unit_k, unit_v, unit_o, lse, seg_all,
    wq, wo, normed_one, query, value_t, seg_row, seg_col, part, part_in, cot_split,
    tp_s, tp_r, a_s, a_r, br_s, br_r, l_s, l_r, loc, away,
):
    n, rows, tok, width, half, heads, length = geo
    place = Place(n)
    s, t = place.s, place.t
    place.enter()
    row_s, head_s = s // heads, lax.rem(s, heads)
    half_at = aligned(t, half)
    leaving = []

    def leave(*pairs):
        for here, there in pairs:
            copy = pltpu.make_async_copy(here, there, away.at[len(leaving)])
            copy.start()
            leaving.append(copy)


    to_x = remote(x_in, x_all.at[:, half_at], tp_s.at[0], tp_r.at[0], place.twin)
    to_x.start()
    own_x = pltpu.make_async_copy(x_in, x_all.at[:, half_at], loc.at[0])
    own_x.start()
    load_q = pltpu.make_async_copy(wq_in, wq, loc.at[1])
    load_q.start()

    def piece(ref):
        return lambda d: ref.at[aligned(d // heads, tok), aligned(lax.rem(d, heads), HEAD_DIM)]

    keys = Spread(place, piece(key_in), lambda: unit_k.at[aligned(s, tok), :], a_s.at[0], a_r.at[0], loc.at[2])
    vals = Spread(place, piece(value_in), lambda: unit_v.at[aligned(s, tok), :], a_s.at[1], a_r.at[1], loc.at[3])
    segs = Spread(place, lambda d: seg_in.at[d // heads], lambda: seg_all.at[s], a_s.at[2], a_r.at[2], loc.at[4])
    qrys = Spread(place, piece(query), lambda: unit_q.at[aligned(s, tok), :], a_s.at[3], a_r.at[3], loc.at[5])
    segs.start()
    keys.start()
    vals.start()
    to_cot = remote(cot_in, cot_all.at[:, half_at], tp_s.at[1], tp_r.at[1], place.twin)
    to_cot.start()
    own_cot = pltpu.make_async_copy(cot_in, cot_all.at[:, half_at], loc.at[6])
    own_cot.start()
    load_o = pltpu.make_async_copy(wo_in, wo, loc.at[7])
    load_o.start()

    own_x.wait()
    to_x.wait()
    step = 64

    def norm_one(i, unused):
        at = aligned(i, step)
        x = x_all[at, :].astype(F32)
        root = lax.rsqrt(jnp.mean(x * x, axis=-1, keepdims=True) + EPSILON)
        normed_one[at, :] = (x * root * gain_one[...]).astype(BF)
        return unused

    lax.fori_loop(0, rows * tok // step, norm_one, 0)
    leave((x_all, x_out))
    load_q.wait()
    query[...] = (dot_nn(normed_one[...], wq[...]) * HEAD_DIM ** (-0.5)).astype(BF)
    qrys.start()

    segs.wait()
    attention_masks(seg_all, seg_row, seg_col, n, tok)
    keys.wait()
    vals.wait()

    def turn(i, unused):
        at = aligned(i, tok)
        value_t[:, at] = jnp.transpose(unit_v[at, :].astype(F32)).astype(BF)
        return unused

    lax.fori_loop(0, n, turn, 0)
    qrys.wait()
    leave((unit_q, q_out), (unit_k, k_out), (unit_v, v_out), (seg_all, seg_out))

    back = Spread(
        place,
        lambda d: unit_o.at[aligned(d, tok), :],
        lambda: attended.at[aligned(row_s, tok), aligned(head_s, HEAD_DIM)],
        a_s.at[4], a_r.at[4], loc.at[8],
    )
    block = 512
    owners = block // tok

    def query_step(qi, unused):
        query_block = unit_q[aligned(qi, block), :]

        def key_step(j, carry):
            top, total, acc = carry
            kj = qi - j
            scores = dot_nt(unit_k[aligned(kj, block), :], query_block)
            scores = jnp.where(readable(seg_col, seg_row, kj, qi, block), scores, NEGATIVE_FILL)
            new_top = jnp.maximum(top, jnp.max(scores, axis=0, keepdims=True))
            weights = jnp.exp(scores - new_top)
            decay = jnp.exp(top - new_top)
            total = total * decay + jnp.sum(weights, axis=0, keepdims=True)
            acc = acc * decay + dot_nn(value_t[:, aligned(kj, block)], weights.astype(BF))
            return new_top, total, acc

        start = (
            jnp.full((1, block), NEGATIVE_FILL, F32),
            jnp.zeros((1, block), F32),
            jnp.zeros((HEAD_DIM, block), F32),
        )
        top, total, acc = lax.fori_loop(0, qi + 1, key_step, start)
        lse[:, aligned(qi, block)] = top + jnp.log(total)
        unit_o[aligned(qi, block), :] = jnp.transpose(acc / total).astype(BF)

        return lax.fori_loop(qi * owners, (qi + 1) * owners, back.start_to, unused)

    lax.fori_loop(0, length // block, query_step, 0)

    leave((unit_o, o_out), (lse, lse_out))
    own_cot.wait()
    to_cot.wait()
    split_rows(cot_all, cot_split, n)
    plane_cot = Plane(place, cot_split, left_cot, l_s, l_r, loc.at[9], rows * tok)
    plane_cot.start()
    load_o.wait()
    back.wait()
    leave((attended, att_out), (cot_all, cot_out))

    chunks = part.shape[0]
    wide = width // chunks

    def to_twin(i):
        return remote(part.at[i], part_in.at[i], br_s.at[i], br_r.at[i], place.twin)

    def project(i, unused):
        part[i] = dot_nt(attended[...], wo[aligned(i, wide), :]).astype(BF)
        to_twin(i).start()
        return unused

    lax.fori_loop(0, chunks, project, 0)
    plane_cot.forward()

    def add(i, square):
        to_twin(i).wait()
        at = aligned(i, wide)
        both = part[i].astype(F32) + part_in[i].astype(F32)
        mid = x_all[:, at].astype(F32) + both
        middle[:, at] = mid
        return square + jnp.sum(mid * mid, axis=-1, keepdims=True)

    square = lax.fori_loop(0, chunks, add, jnp.zeros((rows * tok, 1), F32))
    root_two = lax.rsqrt(square * (1.0 / width) + EPSILON)

    def norm_two(i, unused):
        at = aligned(i, wide)
        normed_two[:, at] = (middle[:, at] * root_two * gain_two[:, at]).astype(BF)
        return unused

    leave((middle, middle_out))
    lax.fori_loop(0, chunks, norm_two, 0)
    leave((normed_two, two_out))
    split_rows(normed_two, left_two, n)
    plane_cot.finish()
    leave((left_two, split_out), (left_cot, left_out))
    for copy in leaving:
        copy.wait()


def split_rows(whole, split, n):
    blk = whole.shape[1] * 2 // n
    for zy in range(n // 2):
        z, y = divmod(zy, 2)
        split[y, :, z * blk : (z + 1) * blk] = whole[:, zy * blk : (zy + 1) * blk]


class Plane:
    def __init__(self, place, split, left, send, recv, local, tokens):
        self.place, self.tokens, self.left = place, tokens, left
        to = left.at[aligned(place.p, tokens), :]
        self.own = pltpu.make_async_copy(split.at[place.y], to, local)
        self.to_core = remote(split.at[place.y], to, send.at[0], recv.at[0], place.core)
        self.to_side = remote(split.at[1 - place.y], to, send.at[1], recv.at[1], place.side)
        passed = left.at[aligned(place.side_p, tokens), :]
        self.on = remote(passed, passed, send.at[2], recv.at[2], place.core)

    def start(self):
        self.to_side.start()
        self.own.start()
        self.to_core.start()

    def forward(self):
        self.to_side.wait()
        self.on.start()

    def finish(self):
        self.own.wait()
        self.to_core.wait()
        self.on.wait()


def vm(shape, dtype):
    return jax.ShapeDtypeStruct(shape, dtype)


def forward_part(geo, x, cot, keys, values, segf, gain_one, gain_two, wq, wo):
    n, rows, tok, width, half, heads, length = geo
    tokens = rows * tok
    dma = pltpu.SemaphoreType.DMA
    anywhere, here = pl.BlockSpec(memory_space=pl.ANY), pl.BlockSpec(memory_space=pltpu.VMEM)
    outs = [
        vm((tokens, width), BF),
        vm((tokens, width), BF),
        vm((PLANE * tokens, width // 2), BF),
        vm((tokens, width), F32),
        vm((tokens, width), BF),
        vm((2, tokens, width // 2), BF),
        vm((tokens, half), BF),
        vm((length, HEAD_DIM), BF),
        vm((length, HEAD_DIM), BF),
        vm((length, HEAD_DIM), BF),
        vm((length, HEAD_DIM), BF),
        vm((1, length), F32),
        vm((n, 1, tok), F32),
    ]
    chunks = 4
    return pl.pallas_call(
        functools.partial(forward_kernel, geo),
        out_shape=outs,
        in_specs=[anywhere] * 5 + [here] * 2 + [anywhere] * 2,
        out_specs=[anywhere] * len(outs),
        scratch_shapes=[
            *(pltpu.VMEM(o.shape, o.dtype) for o in outs),
            pltpu.VMEM(wq.shape, BF),
            pltpu.VMEM(wo.shape, BF),
            pltpu.VMEM((tokens, width), BF),
            pltpu.VMEM((tokens, half), BF),
            pltpu.VMEM((HEAD_DIM, length), BF),
            pltpu.VMEM((1, length), F32),
            pltpu.VMEM((length, LANE), F32),
            pltpu.VMEM((chunks, tokens, width // chunks), BF),
            pltpu.VMEM((chunks, tokens, width // chunks), BF),
            pltpu.VMEM((2, tokens, width // 2), BF),
            dma((2,)), dma((2,)), dma((5, n)), dma((5, n)), dma((chunks,)), dma((chunks,)), dma((3,)), dma((3,)), dma((10,)), dma((len(outs),)),
        ],
        compiler_params=pltpu.CompilerParams(
            collective_id=0, has_side_effects=True, vmem_limit_bytes=VMEM_GRANT
        ),
        name="attention_forward",
    )(x, cot, keys, values, segf, gain_one, gain_two, wq, wo)


class Gather:
    def __init__(self, place, whole, stride, first, land, send, recv, local, tokens):
        cols = land.shape[1]
        to = land.at[aligned(place.p, tokens), :]

        def half(c):
            return whole.at[:, pl.ds(pl.multiple_of(c * stride + first, LANE), cols)]

        c = place.c
        self.own = pltpu.make_async_copy(half(c), to, local)
        self.away = [
            remote(half(c), to, send.at[0], recv.at[0], place.side),
            remote(half(1 - c), to, send.at[1], recv.at[1], place.cross),
            remote(half(1 - c), to, send.at[2], recv.at[2], place.core),
        ]

    def start(self):
        self.own.start()
        for copy in self.away:
            copy.start()

    def wait(self):
        self.own.wait()
        for copy in self.away:
            copy.wait()


class Line:
    def __init__(self, place, nz, blk, gather, land, left, lv, mv, move, got, total, out, turned, sems, work):
        self.place, self.nz, self.blk, self.gather = place, nz, blk, gather
        self.land, self.left, self.move, self.got, self.total, self.out = land, left, move, got, total, out
        self.turned = turned
        self.cols = land.shape[1]
        self.lv, self.mv = lv, mv
        self.acc, self.stage, self.load_sem = work
        self.send, self.recv, self.end_s, self.end_r, self.end_l = sems
        self.at_end = (place.z == 0) | (place.z == nz - 1)

    def load(self, left_too=False):
        self.gather.wait()
        a = pltpu.make_async_copy(self.land, self.mv, self.load_sem.at[0])
        a.start()
        if left_too:
            b = pltpu.make_async_copy(self.left, self.lv, self.load_sem.at[1])
            b.start()
            b.wait()
        a.wait()

    def product(self, b):
        return dot_tn(self.lv[:, aligned(b, self.blk)], self.mv[...])

    def take(self, slot):
        self.arrival(slot).wait_recv()
        copy = pltpu.make_async_copy(self.got.at[slot], self.stage.at[:, : self.cols], self.load_sem.at[2])
        copy.start()
        copy.wait()
        return self.stage[:, : self.cols].astype(F32)

    def arrival(self, slot):
        return remote(self.move.at[0], self.got.at[slot], self.send.at[0], self.recv.at[slot], self.place.core)

    def route(self, j):
        z, nz = self.place.z, self.nz
        b = jnp.where(z < nz // 2, nz - 1 - j, j)
        b = jnp.where((j == nz - 2) & (z == 1), 0, b)
        b = jnp.where((j == nz - 2) & (z == nz - 2), nz - 1, b)
        up = b > z
        to = jnp.where(up, z + 1, z - 1)
        slot_in = jnp.where(up, b - z, nz - z + b)
        slot_out = jnp.where(up, b - to, nz - to + b)
        keep = jnp.where(up, b - 1, b)
        last = jnp.where(up, z == 0, z == nz - 1)
        device = (to * PLANE + self.place.p, self.place.t)

        def out():
            return remote(self.move.at[keep], self.got.at[slot_out], self.send.at[keep], self.recv.at[slot_out], device)

        return b, slot_in, keep, last, out

    def step(self, j):
        b, slot_in, keep, last, out = self.route(j)
        self.acc[:, : self.cols] = self.product(b)

        @pl.when(last)
        def _():
            self.move[keep] = self.acc[:, : self.cols].astype(BF)

        @pl.when(jnp.logical_not(last))
        def _():
            self.move[keep] = (self.acc[:, : self.cols] + self.take(slot_in)).astype(BF)

        out().start()

    def steps(self, low, high):
        def one(j, unused):
            self.step(j)
            return unused

        lax.fori_loop(low, high, one, 0)

    def from_end(self):
        pl.when(self.at_end)(lambda: self.steps(0, self.nz - 1))
        self.total[...] = self.product(self.place.z)

    def between(self, low, high):
        pl.when(jnp.logical_not(self.at_end))(lambda: self.steps(low, high))

    def sent(self):
        def one(j, unused):
            self.route(j)[4]().wait_send()
            return unused

        lax.fori_loop(0, self.nz - 1, one, 0)

    def end(self, c):
        half = self.blk // 2
        mine = self.place.c
        if self.turned is None:
            return self.out.at[:, aligned(mine, self.cols)], self.total.at[aligned(c, half), :]
        turned, stride, first = self.turned
        to = self.out.at[pl.ds(pl.multiple_of(mine * stride + first, LANE), self.cols), :]
        return to, turned.at[first : first + self.cols, aligned(c, half)]

    def away(self):
        to, theirs = self.end(1 - self.place.c)
        return remote(theirs, to, self.end_s, self.end_r, self.place.core)

    def here(self):
        to, mine = self.end(self.place.c)
        return pltpu.make_async_copy(mine, to, self.end_l)

    def finish(self):
        z, nz = self.place.z, self.nz

        @pl.when(z > 0)
        def _():
            self.total[...] += self.take(0)

        @pl.when(z < nz - 1)
        def _():
            self.total[...] += self.take(nz)

        if self.turned is not None:
            turned, _, first = self.turned
            turned[first : first + self.cols, :] = jnp.transpose(self.total[...])
        self.away().start()
        self.here().start()

    def left_here(self):
        self.away().wait_send()
        self.here().wait()

    def arrived(self):
        self.away().wait_recv()


class Weights:
    def __init__(self, weights, buffers, sems, tail_sems, phase, first, cols, ff):
        self.weights, self.buffers, self.sems, self.tail_sems, self.phase = weights, buffers, sems, tail_sems, phase
        self.first, self.each = first, len(weights)
        self.size = buffers.shape[1]
        self.cols = cols
        self.regular = 2 * (cols // self.size)
        self.rest = cols % self.size
        self.rest_two = ff - cols - cols // self.size * self.size

    def slot(self, i, w):
        return self.first + lax.rem(i + self.phase, 2) * self.each + w

    def copies(self, i):
        at = pl.ds(pl.multiple_of(lax.rem(i, 2) * self.cols + i // 2 * self.size, LANE), self.size)
        return [
            pltpu.make_async_copy(ref.at[at, :], self.buffers.at[self.slot(i, w)], self.sems.at[lax.rem(i, 2), w])
            for w, ref in enumerate(self.weights)
        ]

    def tail(self):
        first = self.cols // self.size * self.size
        copies = []
        for w, ref in enumerate(self.weights):
            to = self.buffers.at[self.slot(self.regular, w)]
            copies += [
                pltpu.make_async_copy(ref.at[pl.ds(first, self.rest), :], to.at[pl.ds(0, self.rest), :], self.tail_sems.at[0, w]),
                pltpu.make_async_copy(
                    ref.at[pl.ds(self.cols + first, self.rest_two), :],
                    to.at[pl.ds(self.rest, self.rest_two), :],
                    self.tail_sems.at[1, w],
                ),
            ]
        return copies

    def begin(self):
        for copy in self.copies(0):
            copy.start()

    def run(self, low, high, work):
        def one(i, unused):
            @pl.when(i + 1 < self.regular)
            def _():
                for copy in self.copies(i + 1):
                    copy.start()

            @pl.when(i + 1 == self.regular)
            def _():
                for copy in self.tail():
                    copy.start()

            for copy in self.copies(i):
                copy.wait()
            work([self.slot(i, w) for w in range(len(self.weights))], lax.rem(i, 2) * self.cols + i // 2 * self.size)
            return unused

        lax.fori_loop(low, high, one, 0)

    def end(self, work):
        for copy in self.tail():
            copy.wait()
        slots = [self.first + (self.regular + self.phase) % 2 * self.each + w for w in range(self.each)]
        filled = self.rest + self.rest_two
        for slot in slots:
            self.buffers[slot, filled:, :] = jnp.zeros((self.size - filled, self.buffers.shape[2]), BF)
        work(slots, None)


def backward_kernel(
    geo, sizes,
    wg_in, wu_in, wd_in, two_norm_in, left_cot, left_two, middle_in, x_in, cot_in, att_in,
    q_in, k_in, v_in, o_in, lse_in, seg_in, wo_in, wq_in, gain_one, gain_two,
    ffn_own, ffn_in, input_grad, d_keys, d_values, gains,
    out_down, out_gate, out_up, out_out, out_query,
    *rest,
):
    n, rows, tok, width, half, heads, length = geo
    ff, cols, cuts = sizes
    n_lines = len(cuts) + 2
    lands, (l_two, l_err, l_one), gots = rest[:n_lines], rest[n_lines : n_lines + 3], rest[n_lines + 3 : 2 * n_lines + 3]
    (
        mid, x_all, cot_all, two_norm, two_own, two_in, one_in, mixed, err, one, wbuf, d_att,
        hidden, d_gate, d_up, sums,
        uq, uk, uv, uo, udo, lse, seg_all, seg_row, seg_col, k_t, delta, udq, udk, udv, dq,
        gain_part, gain_in,
        s_first, s_second, s_out, s_query, t_first, t_second, t_out, t_query, turned,
        mv, mv_out, mv_query, lv_one, lv_two, acc, stage,
        tp_s, tp_r, a_s, a_r, me_s, me_r, le_s, le_r, c_s, c_r, e_s, e_r, e_l, loc, g_loc, work_sem, w_sem, tail_sem, o_sem,
    ) = rest[2 * n_lines + 3 :]
    tokens = rows * tok
    blk = 2 * width // n
    nz = n // PLANE
    place = Place(n)
    s, t, z = place.s, place.t, place.z
    row_s, head_s = s // heads, lax.rem(s, heads)
    mine = aligned(t, half)
    chunk = tokens // 4
    fine = 32
    size = wbuf.shape[1]

    first_pass = Weights((wg_in, wu_in, wd_in), wbuf, w_sem.at[0], tail_sem.at[0], 0, 0, cols, ff)
    second_pass = Weights((wg_in, wu_in), wbuf, w_sem.at[1], tail_sem.at[1], 0, 3, cols, ff)
    third_pass = Weights((wd_in,), wbuf, w_sem.at[2], tail_sem.at[2], 0, 4, cols, ff)
    first_pass.begin()
    loads = [
        pltpu.make_async_copy(a, b, loc.at[8 + i])
        for i, (a, b) in enumerate((
            (two_norm_in, two_norm), (cot_in, cot_all), (middle_in, mid), (x_in, x_all),
            (q_in, uq), (k_in, uk), (v_in, uv), (o_in, uo), (lse_in, lse), (seg_in, seg_all),
        ))
    ]
    for copy in loads[:2]:
        copy.start()
    place.enter()

    work = (acc, stage, work_sem)
    sources = {"down": hidden, "gate": d_gate, "up": d_up}
    lefts_of = {"down": (left_cot, lv_one), "gate": (l_two, lv_two), "up": (l_two, lv_two)}
    kept = {"down": (s_first, t_first, out_down), "gate": (s_second, t_second, out_gate), "up": (s_first, t_first, out_up)}
    plans = []
    for kind, first, wide in cuts:
        at = pl.ds(first, wide)
        left, lv = lefts_of[kind]
        move, total, out_ref = kept[kind]
        plans.append((
            (sources[kind], cols, first), left, lv, mv.at[:, at], move.at[:, :, at], total.at[:, at], out_ref,
            (turned, cols, first),
        ))
    plans.append(((att_in, half // 2, 0), l_err, lv_one, mv_out, s_out, t_out, out_out, None))
    plans.append(((dq, half // 2, 0), l_one, lv_two, mv_query, s_query, t_query, out_query, None))
    lines = []
    for i, (source, left, lv, m_here, move, total, out_ref, turn_at) in enumerate(plans):
        gather = Gather(place, *source, lands[i], me_s.at[i], me_r.at[i], g_loc.at[i], tokens)
        sems = (c_s.at[i], c_r.at[i], e_s.at[i], e_r.at[i], e_l.at[i])
        lines.append(
            Line(place, nz, blk, gather, lands[i], left, lv, m_here, move, gots[i], total, out_ref, turn_at, sems, work)
        )
    down_a, down_b, down_c, gate_a, gate_b, up_a, up_b, out, query = lines
    lefts = [
        Plane(place, split, land, le_s.at[i], le_r.at[i], loc.at[i], tokens)
        for i, (split, land) in enumerate(((left_two, l_two), (err, l_err), (one, l_one)))
    ]

    for copy in loads[:2]:
        copy.wait()

    def units(slots, at):
        wg, wu, wd = (wbuf[slot] for slot in slots)
        x, g = two_norm[...], cot_all[...]
        gate_now, up_now = dot_nt(x, wg), dot_nt(x, wu)
        d_hid = dot_nt(g, wd)
        sigma = jax.nn.sigmoid(gate_now)
        act = gate_now * sigma
        for ref, now in (
            (hidden, act * up_now),
            (d_gate, d_hid * up_now * sigma * (1.0 + gate_now * (1.0 - sigma))),
            (d_up, d_hid * act),
        ):
            now = now.astype(BF)
            if at is None:
                last, rest = cols // size * size, cols % size
                ref[:, last:cols] = now[:, :rest]
                ref[:, cols + last :] = now[:, rest : 2 * rest]
            else:
                ref[:, pl.ds(pl.multiple_of(at, LANE), size)] = now

    done_a, done_b = (2 * ((first + wide) // size) for _, first, wide in cuts[:2])
    first_pass.run(0, done_a, units)
    down_a.gather.start()
    first_pass.run(done_a, done_b, units)
    down_b.gather.start()
    down_a.load(True)
    down_a.from_end()
    first_pass.run(done_b, first_pass.regular, units)
    second_pass.begin()
    first_pass.end(units)
    down_c.gather.start()
    lefts[0].start()
    for copy in loads[2:]:
        copy.start()
    down_b.load()
    down_b.from_end()
    down_a.between(0, 2)

    def block_of(ref, at):
        if at is None:
            last, rest = cols // size * size, cols % size
            return jnp.concatenate([ref[:, last:cols], ref[:, cols + last :]], axis=1)
        return ref[:, pl.ds(pl.multiple_of(at, LANE), size)]

    def add_up(pairs):
        for db in range(width // size):
            at = slice(db * size, (db + 1) * size)
            sums[db * tokens : (db + 1) * tokens, :] += sum(dot_nn(a, wbuf[slot, :, at]) for a, slot in pairs)

    def back_units(slots, at):
        add_up([(block_of(d_gate, at), slots[0]), (block_of(d_up, at), slots[1])])

    sums[...] = jnp.zeros_like(sums)
    second_pass.run(0, second_pass.regular, back_units)
    second_pass.end(back_units)
    for db in range(width // size):
        two_own[:, db * size : (db + 1) * size] = sums[db * tokens : (db + 1) * tokens, :].astype(BF)

    def two_copy(i):
        at = aligned(i, chunk)
        return remote(two_own.at[at, :], two_in.at[at, :], tp_s.at[i], tp_r.at[i], place.twin)

    for i in range(4):
        two_copy(i).start()
    load_square = []
    for k, ref in enumerate((wo_in, wq_in)):
        for zy in range(n // 2):
            to = wbuf.at[4 * k + zy // 2, :, (zy % 2) * half : (zy % 2 + 1) * half]
            load_square.append(pltpu.make_async_copy(ref.at[zy * blk : (zy + 1) * blk, :], to, o_sem.at[k, zy]))
    for copy in load_square[: n // 2]:
        copy.start()

    def square_block(k, zy):
        return wbuf[4 * k + zy // 2, :, (zy % 2) * half : (zy % 2 + 1) * half]

    gate_a.gather.start()
    down_a.between(2, 3)
    down_b.between(0, 2)
    down_c.load()
    down_c.from_end()

    third_pass.begin()
    sums[...] = jnp.zeros_like(sums)

    def out_units(slots, at):
        add_up([(block_of(hidden, at), slots[0])])

    third_pass.run(0, third_pass.regular, out_units)
    third_pass.end(out_units)
    for db in range(width // size):
        mixed[:, db * size : (db + 1) * size] = sums[db * tokens : (db + 1) * tokens, :].astype(BF)
    ffn_copy = remote(mixed.at[:, aligned(1 - t, half)], ffn_in, tp_s.at[4], tp_r.at[4], place.twin)
    ffn_copy.start()
    ffn_keep = pltpu.make_async_copy(mixed.at[:, mine], ffn_own, loc.at[6])
    ffn_keep.start()
    for copy in load_square[n // 2 :]:
        copy.start()
    down_b.between(2, 3)

    for copy in loads[3:]:
        copy.wait()

    def first_norm(j, unused):
        at = aligned(j, fine)
        x = x_all[at, :].astype(F32)
        root = lax.rsqrt(jnp.mean(x * x, axis=-1, keepdims=True) + EPSILON)
        low = (x * root * gain_one[...]).astype(BF)
        for zy in range(n // 2):
            zz, yy = divmod(zy, 2)
            one[yy, at, zz * blk : (zz + 1) * blk] = low[:, zy * blk : (zy + 1) * blk]
        return unused

    lax.fori_loop(0, tokens // fine, first_norm, 0)
    attention_masks(seg_all, seg_row, seg_col, n, tok)

    def turn(i, unused):
        at = aligned(i, tok)
        k_t[:, at] = jnp.transpose(uk[at, :].astype(F32)).astype(BF)
        return unused

    lax.fori_loop(0, n, turn, 0)
    sums[...] = jnp.zeros_like(sums)
    down_c.between(0, 2)

    spread_att = Spread(
        place,
        lambda d: d_att.at[aligned(d // heads, tok), aligned(lax.rem(d, heads), HEAD_DIM)],
        lambda: udo.at[aligned(s, tok), :],
        a_s.at[0], a_r.at[0], loc.at[18],
    )
    loads[2].wait()
    for copy in load_square[: n // 2]:
        copy.wait()

    def second_norm(i, gain_sum):
        two_copy(i).wait()

        def some(j, gain_sum):
            at = aligned(i * (chunk // fine) + j, fine)
            m = mid[at, :]
            d2 = two_own[at, :].astype(F32) + two_in[at, :].astype(F32)
            root = lax.rsqrt(jnp.mean(m * m, axis=-1, keepdims=True) + EPSILON)
            gained = d2 * gain_two[...]
            scaled = m * root
            gain_sum = gain_sum + jnp.sum(d2 * scaled, axis=0, keepdims=True)
            slope = jnp.mean(gained * scaled, axis=-1, keepdims=True)
            dm = cot_all[at, :].astype(F32) + root * (gained - scaled * slope)
            mid[at, :] = dm
            low = dm.astype(BF)
            for zy in range(n // 2):
                zz, yy = divmod(zy, 2)
                err[yy, at, zz * blk : (zz + 1) * blk] = low[:, zy * blk : (zy + 1) * blk]
            return gain_sum

        gain_sum = lax.fori_loop(0, chunk // fine, some, gain_sum)
        at = aligned(i, chunk)
        total = jnp.zeros((chunk, half), F32)
        for zy in range(n // 2):
            zz, yy = divmod(zy, 2)
            total += dot_nn(err[yy, at, zz * blk : (zz + 1) * blk], square_block(0, zy))
        d_att[at, :] = total.astype(BF)
        return gain_sum

    gain_sum = jnp.zeros((1, width), F32)
    per_row = tok // chunk
    for r in range(rows):
        gain_sum = lax.fori_loop(r * per_row, (r + 1) * per_row, second_norm, gain_sum)
        lax.fori_loop(r * heads, (r + 1) * heads, spread_att.start_to, 0)
    for i in range(n):
        gain_part[0, i] = gain_sum[:, i * (width // n) : (i + 1) * (width // n)]
    spread_gain = [
        Spread(place, lambda d, g=g: gain_part.at[g, d], lambda g=g: gain_in.at[g, s], a_s.at[4 + g], a_r.at[4 + g], loc.at[22 + g])
        for g in range(2)
    ]
    spread_gain[0].start()
    gate_b.gather.start()
    lefts[0].forward()

    down_c.between(2, 3)
    lefts[0].finish()
    gate_a.load(True)
    gate_a.from_end()

    spread_att.wait()

    def turn_delta(i, unused):
        at = aligned(i, tok)
        both = udo[at, :].astype(F32) * uo[at, :].astype(F32)
        delta[:, at] = jnp.sum(jnp.transpose(both), axis=0, keepdims=True)
        return unused

    lax.fori_loop(0, n, turn_delta, 0)

    block = 512
    owners = block // tok

    def home(ref):
        return lambda: ref.at[aligned(row_s, tok), aligned(head_s, HEAD_DIM)]

    spread_dq, spread_dk, spread_dv = (
        Spread(place, lambda d, unit=unit: unit.at[aligned(d, tok), :], home(whole), a_s.at[i], a_r.at[i], loc.at[18 + i])
        for i, unit, whole in ((1, udq, dq), (2, udk, d_keys), (3, udv, d_values))
    )

    def query_step(i, unused):
        qi = length // block - 1 - i
        qat = aligned(qi, block)
        qb, dob = uq[qat, :], udo[qat, :]

        def key_step(kj, dq_t):
            kat = aligned(kj, block)
            scores = dot_nt(uk[kat, :], qb) - lse[:, qat]
            probs = jnp.exp(jnp.where(readable(seg_col, seg_row, kj, qi, block), scores, NEGATIVE_FILL))
            d_probs = dot_nt(uv[kat, :], dob)
            d_scores = (probs * (d_probs - delta[:, qat])).astype(BF)
            sums[kat, :HEAD_DIM] += dot_nn(d_scores, qb)
            sums[kat, HEAD_DIM:] += dot_nn(probs.astype(BF), dob)
            return dq_t + dot_nn(k_t[:, kat], d_scores)

        dq_t = lax.fori_loop(0, qi + 1, key_step, jnp.zeros((HEAD_DIM, block), F32))
        udq[qat, :] = jnp.transpose(dq_t).astype(BF)
        lax.fori_loop(qi * owners, (qi + 1) * owners, spread_dq.start_to, 0)
        udk[qat, :] = sums[qat, :HEAD_DIM].astype(BF)
        udv[qat, :] = sums[qat, HEAD_DIM:].astype(BF)
        return unused

    lax.fori_loop(0, length // block, query_step, 0)

    up_a.gather.start()
    up_b.gather.start()
    gate_a.between(0, 2)
    gate_b.load()
    gate_b.from_end()
    gate_a.between(2, 3)
    gate_b.between(0, 2)
    down_a.finish()
    down_b.finish()
    down_c.finish()

    for copy in load_square[n // 2 :]:
        copy.wait()
    spread_dq.wait()

    def one_copy(i):
        at = aligned(i, chunk)
        return remote(two_own.at[at, :], one_in.at[at, :], tp_s.at[5 + i], tp_r.at[5 + i], place.twin)

    def back_query(i, unused):
        at = aligned(i, chunk)
        for zy in range(n // 2):
            now = dot_nt(dq[at, :], square_block(1, zy)) * HEAD_DIM ** (-0.5)
            two_own[at, zy * blk : (zy + 1) * blk] = now.astype(BF)
        one_copy(i).start()
        return unused

    lax.fori_loop(0, 4, back_query, 0)

    gate_b.between(2, 3)
    for line in (down_a, down_b, down_c):
        line.sent()
    up_a.load()
    up_a.from_end()
    up_a.between(0, 2)
    lefts[1].start()
    out.gather.start()
    lefts[2].start()
    query.gather.start()

    def last_norm(i, gain_sum):
        one_copy(i).wait()

        def some(j, gain_sum):
            at = aligned(i * (chunk // fine) + j, fine)
            x = x_all[at, :].astype(F32)
            d1 = two_own[at, :].astype(F32) + one_in[at, :].astype(F32)
            root = lax.rsqrt(jnp.mean(x * x, axis=-1, keepdims=True) + EPSILON)
            gained = d1 * gain_one[...]
            scaled = x * root
            gain_sum = gain_sum + jnp.sum(d1 * scaled, axis=0, keepdims=True)
            slope = jnp.mean(gained * scaled, axis=-1, keepdims=True)
            mid[at, :] = mid[at, :] + root * (gained - scaled * slope)
            return gain_sum

        return lax.fori_loop(0, chunk // fine, some, gain_sum)

    gain_sum = lax.fori_loop(0, 4, last_norm, jnp.zeros((1, width), F32))
    for i in range(n):
        gain_part[1, i] = gain_sum[:, i * (width // n) : (i + 1) * (width // n)]
    spread_gain[1].start()
    give = pltpu.make_async_copy(mid.at[:, mine], input_grad, loc.at[24])
    give.start()

    up_b.load()
    up_b.from_end()
    spread_dk.start()
    spread_dv.start()
    up_a.between(2, 3)
    up_b.between(0, 2)
    for line in (down_a, down_b, down_c):
        line.left_here()
    gate_a.finish()
    gate_b.finish()
    lefts[1].forward()
    lefts[1].finish()
    out.load(True)
    out.from_end()
    up_b.between(2, 3)
    out.between(0, 2)
    lefts[2].forward()
    lefts[2].finish()
    query.load(True)
    query.from_end()
    out.between(2, 3)
    query.between(0, 3)
    for line in (gate_a, gate_b):
        line.left_here()
    up_a.finish()
    up_b.finish()
    out.finish()
    query.finish()

    spread_dk.wait()
    spread_dv.wait()
    for g in range(2):
        spread_gain[g].wait()
        gains[g] = jnp.sum(gain_in[g], axis=0)
    ffn_copy.wait()
    ffn_keep.wait()
    give.wait()
    for line in lines[3:]:
        line.sent()
    for line in lines[5:]:
        line.left_here()
    for line in lines:
        line.arrived()


def backward_part(geo, forward, wg, wu, wd, wo, wq, gain_one, gain_two):
    n, rows, tok, width, half, heads, length = geo
    tokens = rows * tok
    blk = 2 * width // n
    nz = n // PLANE
    ff = wg.shape[0]
    size = 2 * LANE
    cols = -(-ff // size) * LANE
    firsts = (0, size, 3 * size, cols)
    thirds = [(firsts[i], firsts[i + 1] - firsts[i]) for i in range(3)]
    halves = [(0, firsts[2]), (firsts[2], cols - firsts[2])]
    cuts = tuple((kind, *cut) for kind, parts in (("down", thirds), ("gate", halves), ("up", halves)) for cut in parts)
    sizes = (ff, cols, cuts)
    x_all, cot_all, left_cot, middle, normed_two, left_two, attended, uq, uk, uv, uo, lse, seg_all = forward
    dma = pltpu.SemaphoreType.DMA
    anywhere, here = pl.BlockSpec(memory_space=pl.ANY), pl.BlockSpec(memory_space=pltpu.VMEM)
    wide = (*(w for _, _, w in cuts), half // 2, half // 2)
    kept = (cols, cols, half // 2, half // 2)
    outs = [
        (vm((tokens, half), BF), anywhere),
        (vm((tokens, half), BF), anywhere),
        (vm((tokens, half), F32), anywhere),
        (vm((tokens, half), BF), anywhere),
        (vm((tokens, half), BF), anywhere),
        (vm((2, 1, width // n), F32), here),
        *((vm((2 * cols, blk // 2), F32), anywhere) for _ in range(3)),
        *((vm((blk // 2, half), F32), anywhere) for _ in range(2)),
        *((vm((PLANE * tokens, c), BF), anywhere) for c in wide),
        *((vm((PLANE * tokens, width // 2), BF), anywhere) for _ in range(3)),
        *((vm((nz + 1, blk, c), BF), anywhere) for c in wide),
    ]
    inputs = [
        wg, wu, wd, normed_two, left_cot, left_two, middle, x_all, cot_all, attended,
        uq, uk, uv, uo, lse, seg_all, wo, wq, gain_one, gain_two,
    ]
    unit = pltpu.VMEM((length, HEAD_DIM), BF)
    line = pltpu.VMEM((1, length), F32)
    act = pltpu.VMEM((tokens, width), BF)
    split = pltpu.VMEM((2, tokens, width // 2), BF)
    hid = pltpu.VMEM((tokens, 2 * cols), BF)
    scratch = [
        pltpu.VMEM((tokens, width), F32), act, act, act, act, act, act, act, split, split,
        pltpu.VMEM((8, size, width), BF), pltpu.VMEM((tokens, half), BF),
        hid, hid, hid, pltpu.VMEM((length, size), F32),
        unit, unit, unit, unit, unit, line, pltpu.VMEM((n, 1, tok), F32), line,
        pltpu.VMEM((length, LANE), F32), pltpu.VMEM((HEAD_DIM, length), BF), line,
        unit, unit, unit, pltpu.VMEM((tokens, half), BF),
        pltpu.VMEM((2, n, 1, width // n), F32), pltpu.VMEM((2, n, 1, width // n), F32),
        *(pltpu.VMEM((nz - 1, blk, c), BF) for c in kept),
        *(pltpu.VMEM((blk, c), F32) for c in kept),
        pltpu.VMEM((cols, blk), F32),
        pltpu.VMEM((PLANE * tokens, cols), BF), *(pltpu.VMEM((PLANE * tokens, half // 2), BF) for _ in range(2)),
        *(pltpu.VMEM((PLANE * tokens, width // 2), BF) for _ in range(2)),
        pltpu.VMEM((blk, cols), F32), pltpu.VMEM((blk, cols), BF),
        dma((9,)), dma((9,)), dma((6, n)), dma((6, n)), dma((len(wide), 3)), dma((len(wide), 3)), dma((3, 3)), dma((3, 3)),
        dma((len(wide), nz - 1)), dma((len(wide), nz + 1)), *(dma((len(wide),)) for _ in range(3)), dma((28,)),
        dma((len(wide),)), dma((3,)),
        dma((3, 2, 3)), dma((3, 2, 3)), dma((2, n // 2)),
    ]
    return pl.pallas_call(
        functools.partial(backward_kernel, geo, sizes),
        out_shape=[o for o, _ in outs],
        in_specs=[anywhere] * (len(inputs) - 2) + [here] * 2,
        out_specs=[spec for _, spec in outs],
        scratch_shapes=scratch,
        compiler_params=pltpu.CompilerParams(
            collective_id=1, has_side_effects=True, vmem_limit_bytes=VMEM_GRANT
        ),
        name="feed_forward_and_backward",
    )(*inputs)


def fast_device(
    n, inputs, segments, keys, values, attn_gain, query_weight, out_weight, ffn_gain, gate_weight, up_weight, down_weight,
    cotangent,
):
    rows, tok, half = inputs.shape
    tokens, width, ff = rows * tok, query_weight.shape[0], gate_weight.shape[1]
    heads = half // HEAD_DIM
    geo = (n, rows, tok, width, half, heads, n * tok)

    def flat(a):
        return a.reshape(tokens, half)

    segf = segments.astype(F32).reshape(rows, 1, tok)
    gain_one, gain_two = attn_gain.reshape(1, width), ffn_gain.reshape(1, width)
    forward = forward_part(
        geo, flat(inputs), flat(cotangent), flat(keys), flat(values), segf, gain_one, gain_two, query_weight, out_weight
    )
    back = backward_part(
        geo, forward, gate_weight.T, up_weight.T, down_weight.T, out_weight, query_weight, gain_one, gain_two
    )
    ffn_own, ffn_in, input_grad, d_keys, d_values, gains, g_down, g_gate, g_up, g_out, g_query = back[:11]
    middle = lax.dynamic_slice_in_dim(forward[3], lax.axis_index("tp") * half, half, 1)
    mixed = (middle + ffn_own.astype(F32) + ffn_in.astype(F32)).astype(BF)

    def shaped(a):
        return a.reshape(rows, tok, half)

    return (
        shaped(mixed),
        shaped(input_grad),
        shaped(d_keys.astype(F32)),
        shaped(d_values.astype(F32)),
        gains[1, 0],
        g_query * HEAD_DIM ** (-0.5),
        g_out,
        gains[0, 0],
        g_gate[:ff].T,
        g_up[:ff].T,
        g_down[:ff].T,
    )


def inverse_root(stream):
    return lax.rsqrt(jnp.mean(stream * stream, axis=-1, keepdims=True) + EPSILON)


def key_mask(doc_start, query_pos, begin, row_count):
    key_pos = begin + jnp.arange(row_count, dtype=jnp.int32)
    earlier = key_pos[None, None, :] <= query_pos[None, :, None]
    same_doc = key_pos[None, None, :] >= doc_start[:, :, None]
    return (earlier & same_doc)[:, None]


def per_device(
    inputs,
    segments,
    keys,
    values,
    attn_gain,
    query_weight,
    out_weight,
    ffn_gain,
    gate_weight,
    up_weight,
    down_weight,
    cotangent,
):
    batch_rows, local_tokens, half_width = inputs.shape
    local_heads = half_width // HEAD_DIM
    seq_devices = lax.axis_size("seq")
    row_length = local_tokens * seq_devices
    seq_index = lax.axis_index("seq")
    tp_index = lax.axis_index("tp")
    query_scale = HEAD_DIM ** (-0.5)
    bfloat = jnp.bfloat16
    single = jnp.float32
    whole = lax.all_gather(inputs, "tp", axis=2, tiled=True).astype(single)
    root_one = inverse_root(whole)
    scaled_one = whole * root_one
    normed_one = (scaled_one * attn_gain).astype(bfloat)
    query = (
        jnp.einsum("rtd,de->rte", normed_one, query_weight, preferred_element_type=single)
        * query_scale
    ).astype(bfloat)
    query_heads = query.reshape(batch_rows, local_tokens, local_heads, HEAD_DIM)
    bins = jnp.arange(CUTS + 1, dtype=jnp.int32)
    onehot = (segments[:, :, None] == bins[None, None, :]).astype(single)
    totals = lax.psum(jnp.sum(onehot, axis=1), "seq")
    ends = jnp.cumsum(totals, axis=-1)
    before = ends - totals
    doc_start = jnp.sum(onehot * before[:, None, :], axis=-1).astype(jnp.int32)
    query_pos = seq_index * local_tokens + jnp.arange(local_tokens, dtype=jnp.int32)
    first_needed = jnp.min(doc_start)
    last_needed = seq_index * local_tokens + local_tokens - 1
    start_state = (
        jnp.full((batch_rows, local_heads, local_tokens), NEGATIVE_FILL, single),
        jnp.zeros((batch_rows, local_heads, local_tokens), single),
        jnp.zeros((batch_rows, local_heads, local_tokens, HEAD_DIM), single),
    )
    key_piece = lax.all_gather(keys, "seq", axis=1, tiled=True)
    value_piece = lax.all_gather(values, "seq", axis=1, tiled=True)
    piece_rows = key_piece.shape[1]
    fold_key_block = math.gcd(piece_rows, 512)

    def fold_step(block_index, state):
        running_max, running_sum, running_out = state
        begin = block_index * fold_key_block

        def fold_work(unused):
            key_heads = lax.dynamic_slice_in_dim(
                key_piece, block_index * fold_key_block, fold_key_block, 1
            ).reshape(batch_rows, fold_key_block, local_heads, HEAD_DIM)
            value_heads = lax.dynamic_slice_in_dim(
                value_piece, block_index * fold_key_block, fold_key_block, 1
            ).reshape(batch_rows, fold_key_block, local_heads, HEAD_DIM)
            scores = jnp.einsum(
                "rqhe,rkhe->rhqk", query_heads, key_heads, preferred_element_type=single
            )
            allowed = key_mask(doc_start, query_pos, begin, fold_key_block)
            scores = jnp.where(allowed, scores, NEGATIVE_FILL)
            new_max = jnp.maximum(running_max, jnp.max(scores, axis=-1))
            weights = jnp.where(allowed, jnp.exp(scores - new_max[..., None]), 0.0)
            decay = jnp.exp(running_max - new_max)
            new_sum = running_sum * decay + jnp.sum(weights, axis=-1)
            new_out = running_out * decay[..., None] + jnp.einsum(
                "rhqk,rkhe->rhqe",
                weights.astype(bfloat),
                value_heads,
                preferred_element_type=single,
            )
            return (new_max, new_sum, new_out)

        def keep_state(unused):
            return (running_max, running_sum, running_out)

        needed = (begin <= last_needed) & (begin + fold_key_block - 1 >= first_needed)
        return lax.cond(needed, fold_work, keep_state, 0)

    running_max, running_sum, running_out = lax.fori_loop(
        0, piece_rows // fold_key_block, fold_step, start_state
    )
    log_total = running_max + jnp.log(running_sum)
    attended = running_out / running_sum[..., None]
    attended_low = (
        attended.transpose(0, 2, 1, 3).reshape(batch_rows, local_tokens, half_width).astype(bfloat)
    )
    branch = jnp.einsum("rth,dh->rtd", attended_low, out_weight, preferred_element_type=single)
    middle = whole + lax.psum(branch.astype(jnp.bfloat16), "tp").astype(jnp.float32)
    middle_share = lax.dynamic_slice_in_dim(middle, tp_index * half_width, half_width, 2)
    root_two = inverse_root(middle)
    scaled_two = middle * root_two
    normed_two = (scaled_two * ffn_gain).astype(bfloat)
    gate = jnp.einsum("rtd,df->rtf", normed_two, gate_weight, preferred_element_type=single)
    up_proj = jnp.einsum("rtd,df->rtf", normed_two, up_weight, preferred_element_type=single)
    sigma = jax.nn.sigmoid(gate)
    activated = gate * sigma
    hidden = (activated * up_proj).astype(bfloat)
    ffn_part = jnp.einsum("rtf,df->rtd", hidden, down_weight, preferred_element_type=single)
    output = (
        middle_share
        + lax.psum_scatter(
            ffn_part.astype(jnp.bfloat16), "tp", scatter_dimension=2, tiled=True
        ).astype(jnp.float32)
    ).astype(bfloat)
    grad_out = lax.all_gather(cotangent, "tp", axis=2, tiled=True)
    d_hidden = jnp.einsum("rtd,df->rtf", grad_out, down_weight, preferred_element_type=single)
    d_gate = (d_hidden * up_proj * sigma * (1.0 + gate * (1.0 - sigma))).astype(bfloat)
    d_up = (d_hidden * activated).astype(bfloat)
    d_two_part = jnp.einsum(
        "rtf,df->rtd", d_gate, gate_weight, preferred_element_type=single
    ) + jnp.einsum("rtf,df->rtd", d_up, up_weight, preferred_element_type=single)
    d_two = lax.psum(d_two_part.astype(jnp.bfloat16), "tp").astype(jnp.float32)
    gained_two = d_two * ffn_gain
    d_middle = (
        grad_out.astype(single)
        + root_two * gained_two
        - middle * root_two**3 * jnp.mean(gained_two * middle, axis=-1, keepdims=True)
    )
    normed_rows = normed_two
    gate_term = jnp.einsum("rtd,rtf->df", normed_rows, d_gate, preferred_element_type=single)
    up_term = jnp.einsum("rtd,rtf->df", normed_rows, d_up, preferred_element_type=single)
    down_term = jnp.einsum("rtd,rtf->df", grad_out, hidden, preferred_element_type=single)
    gain_term = jnp.sum(d_two * scaled_two, axis=(0, 1))
    gate_grad, up_grad, down_grad, ffn_gain_grad = lax.psum_scatter(
        (gate_term, up_term, down_term, gain_term), "seq", scatter_dimension=0, tiled=True
    )
    error = d_middle.astype(bfloat)
    d_attended = jnp.einsum("rtd,dh->rth", error, out_weight, preferred_element_type=single).astype(
        bfloat
    )
    d_heads = d_attended.reshape(batch_rows, local_tokens, local_heads, HEAD_DIM)
    carried = jnp.einsum("rqhe,rhqe->rhq", d_heads.astype(single), attended)
    key_all, value_all = (
        lax.all_gather(keys, "seq", axis=1, tiled=True),
        lax.all_gather(values, "seq", axis=1, tiled=True),
    )
    key_block = math.gcd(row_length, 512)

    def block_terms(begin):
        key_heads = lax.dynamic_slice_in_dim(key_all, begin, key_block, 1).reshape(
            batch_rows, key_block, local_heads, HEAD_DIM
        )
        value_heads = lax.dynamic_slice_in_dim(value_all, begin, key_block, 1).reshape(
            batch_rows, key_block, local_heads, HEAD_DIM
        )
        scores = jnp.einsum(
            "rqhe,rkhe->rhqk", query_heads, key_heads, preferred_element_type=single
        )
        allowed = key_mask(doc_start, query_pos, begin, key_block)
        probs = jnp.where(
            allowed, jnp.exp(jnp.where(allowed, scores, NEGATIVE_FILL) - log_total[..., None]), 0.0
        )
        d_probs = jnp.einsum("rqhe,rkhe->rhqk", d_heads, value_heads, preferred_element_type=single)
        d_scores = (probs * (d_probs - carried[..., None])).astype(bfloat)
        query_part = jnp.einsum(
            "rhqk,rkhe->rhqe", d_scores, key_heads, preferred_element_type=single
        )
        return (probs, d_scores, query_part)

    query_zero = jnp.zeros((batch_rows, local_heads, local_tokens, HEAD_DIM), single)

    def back_step(block_index, state):
        d_query, key_terms, value_terms = state
        begin = block_index * key_block

        def back_work(unused):
            probs, d_scores, query_part = block_terms(begin)
            value_part = jnp.einsum(
                "rhqk,rqhe->rkhe", probs.astype(bfloat), d_heads, preferred_element_type=single
            )
            key_part = jnp.einsum(
                "rhqk,rqhe->rkhe", d_scores, query_heads, preferred_element_type=single
            )
            return (
                query_part,
                key_part.reshape(batch_rows, key_block, half_width),
                value_part.reshape(batch_rows, key_block, half_width),
            )

        def skip_block(unused):
            empty_rows = jnp.zeros((batch_rows, key_block, half_width), single)
            return (jnp.zeros_like(d_query), empty_rows, empty_rows)

        needed = (begin <= last_needed) & (begin + key_block - 1 >= first_needed)
        query_part, key_part, value_part = lax.cond(needed, back_work, skip_block, 0)
        return (
            d_query + query_part,
            lax.dynamic_update_slice_in_dim(key_terms, key_part, begin, 1),
            lax.dynamic_update_slice_in_dim(value_terms, value_part, begin, 1),
        )

    back_start = (
        query_zero,
        jnp.zeros((batch_rows, row_length, half_width), single),
        jnp.zeros((batch_rows, row_length, half_width), single),
    )
    d_query, key_terms, value_terms = lax.fori_loop(
        0, row_length // key_block, back_step, back_start
    )
    key_grad, value_grad = (
        lax.psum_scatter(key_terms, "seq", scatter_dimension=1, tiled=True),
        lax.psum_scatter(value_terms, "seq", scatter_dimension=1, tiled=True),
    )
    d_query_rows = (
        d_query.transpose(0, 2, 1, 3).reshape(batch_rows, local_tokens, half_width).astype(bfloat)
    )
    d_one_part = (
        jnp.einsum("rte,de->rtd", d_query_rows, query_weight, preferred_element_type=single)
        * query_scale
    )
    d_one = lax.psum(d_one_part.astype(jnp.bfloat16), "tp").astype(jnp.float32)
    gained_one = d_one * attn_gain
    d_whole = (
        d_middle
        + root_one * gained_one
        - whole * root_one**3 * jnp.mean(gained_one * whole, axis=-1, keepdims=True)
    )
    input_grad = lax.dynamic_slice_in_dim(d_whole, tp_index * half_width, half_width, 2)
    normed_rows = normed_one
    query_term = (
        jnp.einsum("rtd,rte->de", normed_rows, d_query_rows, preferred_element_type=single)
        * query_scale
    )
    out_term = jnp.einsum("rtd,rth->dh", error, attended_low, preferred_element_type=single)
    gain_term = jnp.sum(d_one * scaled_one, axis=(0, 1))
    query_grad, out_grad, attn_gain_grad = lax.psum_scatter(
        (query_term, out_term, gain_term), "seq", scatter_dimension=0, tiled=True
    )
    return (
        output,
        input_grad,
        key_grad,
        value_grad,
        attn_gain_grad,
        query_grad,
        out_grad,
        ffn_gain_grad,
        gate_grad,
        up_grad,
        down_grad,
    )


def solution(mesh):
    in_specs = (
        P(None, "seq", "tp"),
        P(None, "seq"),
        P(None, "seq", "tp"),
        P(None, "seq", "tp"),
        P(),
        P(None, "tp"),
        P(None, "tp"),
        P(),
        P(None, "tp"),
        P(None, "tp"),
        P(None, "tp"),
        P(None, "seq", "tp"),
    )
    out_specs = (
        P(None, "seq", "tp"),
        P(None, "seq", "tp"),
        P(None, "seq", "tp"),
        P(None, "seq", "tp"),
        P("seq"),
        P("seq", "tp"),
        P("seq", "tp"),
        P("seq"),
        P("seq", "tp"),
        P("seq", "tp"),
        P("seq", "tp"),
    )
    n = mesh.shape["seq"]

    def step(inputs, *others):
        rows, tok, half = inputs.shape
        units = rows * (half // HEAD_DIM)
        if units == n == PLANE * PLANE and 4 * tok == 512 and mesh.shape["tp"] == 2:
            return fast_device(n, inputs, *others)
        return per_device(inputs, *others)

    return jax.shard_map(
        step, mesh=mesh, in_specs=in_specs, out_specs=out_specs, check_vma=False
    )
```

```python
import functools
import math
import types

import jax
import jax.numpy as jnp
from jax import lax
from jax.experimental import pallas as pl
from jax.experimental.pallas import tpu as pltpu
from jax.sharding import PartitionSpec as P

HEAD_DIM = 128
CUTS = 12


EPSILON = 1e-06
NEGATIVE_FILL = -1e30

MESH = pl.DeviceIdType.MESH
BF = jnp.bfloat16
F32 = jnp.float32
VMEM_GRANT = 63 << 20
PLANE = 4
LANE = 128


def dot_nn(a, b):
    return lax.dot_general(a, b, (((1,), (0,)), ((), ())), preferred_element_type=F32)


def dot_nt(a, b):
    return lax.dot_general(a, b, (((1,), (1,)), ((), ())), preferred_element_type=F32)


def dot_tn(a, b):
    return lax.dot_general(a, b, (((0,), (0,)), ((), ())), preferred_element_type=F32)


def aligned(index, size):
    return pl.ds(pl.multiple_of(index * size, size), size)


class Place:
    def __init__(self, n):
        self.n = n
        self.s = lax.axis_index("seq")
        self.t = lax.axis_index("tp")
        self.z = self.s // PLANE
        self.p = lax.rem(self.s, PLANE)
        self.y = self.p // 2
        self.c = lax.rem(self.p, 2)
        base = self.z * PLANE
        self.core_p = self.y * 2 + 1 - self.c
        self.side_p = (1 - self.y) * 2 + self.c
        self.cross_p = (1 - self.y) * 2 + 1 - self.c
        self.core = (base + self.core_p, self.t)
        self.side = (base + self.side_p, self.t)
        self.cross = (base + self.cross_p, self.t)
        self.twin = (self.s, 1 - self.t)

    def other(self, k):
        return lax.rem(self.s + k, self.n)

    def enter(self):
        barrier = pltpu.get_barrier_semaphore()

        def greet(k, unused):
            pl.semaphore_signal(barrier, inc=1, device_id=(self.other(k), self.t), device_id_type=MESH)
            return unused

        lax.fori_loop(1, self.n, greet, 0)
        pl.semaphore_signal(barrier, inc=1, device_id=self.twin, device_id_type=MESH)
        pl.semaphore_wait(barrier, self.n)


def remote(src, dst, send, recv, device):
    return pltpu.make_async_remote_copy(
        src_ref=src, dst_ref=dst, send_sem=send, recv_sem=recv, device_id=device, device_id_type=MESH
    )


class Spread:
    def __init__(self, place, src, dst, send, recv, local, bulk):
        self.place, self.src, self.dst, self.send, self.recv, self.local = place, src, dst, send, recv, local
        self.bulk = bulk

    def copy(self, k):
        place = self.place
        d = place.other(k)
        return remote(self.src(d), self.dst(), self.send, self.recv, (d, place.t))

    def own(self):
        return pltpu.make_async_copy(self.src(self.place.s), self.dst(), self.local)

    def start(self):
        self.own().start()

        def one(k, unused):
            self.copy(k).start()
            return unused

        lax.fori_loop(1, self.place.n, one, 0)

    def start_to(self, d, unused):
        k = lax.rem(d - self.place.s + self.place.n, self.place.n)

        @pl.when(k == 0)
        def _():
            self.own().start()

        @pl.when(k != 0)
        def _():
            self.copy(k).start()

        return unused

    def wait(self):
        self.own().wait()
        remote(self.bulk, self.bulk, self.send, self.recv, self.place.core).wait()


def attention_masks(seg_all, seg_row, seg_col, n, tok):
    def one(i, unused):
        piece = seg_all[i]
        seg_row[:, aligned(i, tok)] = piece
        seg_col[aligned(i, tok), :] = jnp.transpose(jnp.broadcast_to(piece, (tok, tok)))
        return unused

    lax.fori_loop(0, n, one, 0)


def readable(seg_col, seg_row, key_block, query_block, block):
    key_seg = seg_col[aligned(key_block, block), :]
    key_seg = jnp.concatenate([key_seg] * (block // LANE), axis=1)
    query_seg = seg_row[:, aligned(query_block, block)]
    key_pos = key_block * block + lax.broadcasted_iota(jnp.int32, (block, block), 0)
    query_pos = query_block * block + lax.broadcasted_iota(jnp.int32, (block, block), 1)
    return (key_seg == query_seg) & (key_pos <= query_pos)


def split_rows(whole, split, n):
    blk = whole.shape[1] * 2 // n
    for zy in range(n // 2):
        z, y = divmod(zy, 2)
        split[y, :, z * blk : (z + 1) * blk] = whole[:, zy * blk : (zy + 1) * blk]


class Plane:
    def __init__(self, place, split, left, send, recv, local, tokens):
        self.place, self.tokens, self.left = place, tokens, left
        to = left.at[aligned(place.p, tokens), :]
        self.own = pltpu.make_async_copy(split.at[place.y], to, local)
        self.to_core = remote(split.at[place.y], to, send.at[0], recv.at[0], place.core)
        self.to_side = remote(split.at[1 - place.y], to, send.at[1], recv.at[1], place.side)
        passed = left.at[aligned(place.side_p, tokens), :]
        self.on = remote(passed, passed, send.at[2], recv.at[2], place.core)

    def start(self):
        self.to_side.start()
        self.own.start()
        self.to_core.start()

    def forward(self):
        self.to_side.wait()
        self.on.start()

    def gone(self):
        self.own.wait()
        self.to_core.wait_send()

    def finish(self):
        self.to_core.wait_recv()
        self.on.wait()


def vm(shape, dtype):
    return jax.ShapeDtypeStruct(shape, dtype)


class Gather:
    def __init__(self, place, whole, stride, first, land, send, recv, local, tokens):
        cols = land.shape[1]
        to = land.at[aligned(place.p, tokens), :]

        def half(c):
            return whole.at[:, pl.ds(pl.multiple_of(c * stride + first, LANE), cols)]

        c = place.c
        self.own = pltpu.make_async_copy(half(c), to, local)
        self.away = [
            remote(half(c), to, send.at[0], recv.at[0], place.side),
            remote(half(1 - c), to, send.at[1], recv.at[1], place.cross),
            remote(half(1 - c), to, send.at[2], recv.at[2], place.core),
        ]

    def start(self):
        self.own.start()
        for copy in self.away:
            copy.start()

    def wait(self):
        self.own.wait()
        for copy in self.away:
            copy.wait()


class Line:
    def __init__(self, place, nz, blk, gather, land, left, lv, mv, move, got, total, out, turned, sems, work):
        self.place, self.nz, self.blk, self.gather = place, nz, blk, gather
        self.land, self.left, self.move, self.got, self.total, self.out = land, left, move, got, total, out
        self.turned = turned
        self.cols = land.shape[1]
        self.lv, self.mv = lv, mv
        self.acc, self.stage, self.load_sem = work
        self.send, self.recv, self.end_s, self.end_r, self.end_l = sems
        self.at_end = (place.z == 0) | (place.z == nz - 1)

    def load(self, left_too=False, gathered=False):
        if not gathered:
            self.gather.wait()
        copies = []
        if self.land is not self.mv:
            copies.append(pltpu.make_async_copy(self.land, self.mv, self.load_sem.at[0]))
        if left_too and self.left is not self.lv:
            copies.append(pltpu.make_async_copy(self.left, self.lv, self.load_sem.at[1]))
        for copy in copies:
            copy.start()
        for copy in copies:
            copy.wait()

    def product(self, b):
        return dot_tn(self.lv[:, aligned(b, self.blk)], self.mv[...])

    def take(self, slot):
        self.arrival(slot).wait_recv()
        copy = pltpu.make_async_copy(self.got.at[slot], self.stage.at[:, : self.cols], self.load_sem.at[2])
        copy.start()
        copy.wait()
        return self.stage[:, : self.cols].astype(F32)

    def arrival(self, slot):
        return remote(self.move.at[0], self.got.at[slot], self.send.at[0], self.recv.at[slot], self.place.core)

    def route(self, j):
        z, nz = self.place.z, self.nz
        b = jnp.where(z < nz // 2, nz - 1 - j, j)
        b = jnp.where((j == nz - 2) & (z == 1), 0, b)
        b = jnp.where((j == nz - 2) & (z == nz - 2), nz - 1, b)
        up = b > z
        to = jnp.where(up, z + 1, z - 1)
        slot_in = jnp.where(up, b - z, nz - z + b)
        slot_out = jnp.where(up, b - to, nz - to + b)
        keep = jnp.where(up, b - 1, b)
        last = jnp.where(up, z == 0, z == nz - 1)
        device = (to * PLANE + self.place.p, self.place.t)

        def out():
            return remote(self.move.at[keep], self.got.at[slot_out], self.send.at[keep], self.recv.at[slot_out], device)

        return b, slot_in, keep, last, out

    def step(self, j):
        b, slot_in, keep, last, out = self.route(j)
        self.acc[:, : self.cols] = self.product(b)

        @pl.when(last)
        def _():
            self.move[keep] = self.acc[:, : self.cols].astype(BF)

        @pl.when(jnp.logical_not(last))
        def _():
            self.move[keep] = (self.acc[:, : self.cols] + self.take(slot_in)).astype(BF)

        out().start()

    def steps(self, low, high):
        def one(j, unused):
            self.step(j)
            return unused

        lax.fori_loop(low, high, one, 0)

    def own(self):
        self.total[...] = self.product(self.place.z)

    def begin(self):
        self.steps(0, self.nz - 1)
        self.own()

    def from_end(self):
        pl.when(self.at_end)(lambda: self.steps(0, self.nz - 1))
        self.own()

    def between(self, low, high):
        pl.when(jnp.logical_not(self.at_end))(lambda: self.steps(low, high))

    def sent(self):
        def one(j, unused):
            self.route(j)[4]().wait_send()
            return unused

        lax.fori_loop(0, self.nz - 1, one, 0)

    def end(self, c):
        half = self.blk // 2
        mine = self.place.c
        if self.turned is None:
            return self.out.at[:, aligned(mine, self.cols)], self.total.at[aligned(c, half), :]
        turned, stride, first = self.turned
        to = self.out.at[pl.ds(pl.multiple_of(mine * stride + first, LANE), self.cols), :]
        return to, turned.at[first : first + self.cols, aligned(c, half)]

    def away(self):
        to, theirs = self.end(1 - self.place.c)
        return remote(theirs, to, self.end_s, self.end_r, self.place.core)

    def here(self):
        to, mine = self.end(self.place.c)
        return pltpu.make_async_copy(mine, to, self.end_l)

    def finish(self):
        z, nz = self.place.z, self.nz

        @pl.when(z > 0)
        def _():
            self.total[...] += self.take(0)

        @pl.when(z < nz - 1)
        def _():
            self.total[...] += self.take(nz)

        if self.turned is not None:
            turned, _, first = self.turned
            turned[first : first + self.cols, :] = jnp.transpose(self.total[...])
        self.away().start()
        self.here().start()

    def left_here(self):
        self.away().wait_send()
        self.here().wait()

    def arrived(self):
        self.away().wait_recv()


class Weights:
    def __init__(self, weights, buffers, sems, tail_sems, phase, first, cols, ff):
        self.weights, self.buffers, self.sems, self.tail_sems, self.phase = weights, buffers, sems, tail_sems, phase
        self.first, self.each = first, len(weights)
        self.size = buffers.shape[1]
        self.cols = cols
        self.regular = 2 * (cols // self.size)
        self.rest = cols % self.size
        self.rest_two = ff - cols - cols // self.size * self.size

    def slot(self, i, w):
        return self.first + lax.rem(i + self.phase, 2) * self.each + w

    def copies(self, i):
        at = pl.ds(pl.multiple_of(lax.rem(i, 2) * self.cols + i // 2 * self.size, LANE), self.size)
        return [
            pltpu.make_async_copy(ref.at[at, :], self.buffers.at[self.slot(i, w)], self.sems.at[lax.rem(i, 2), w])
            for w, ref in enumerate(self.weights)
        ]

    def tail(self):
        first = self.cols // self.size * self.size
        copies = []
        for w, ref in enumerate(self.weights):
            to = self.buffers.at[self.slot(self.regular, w)]
            copies += [
                pltpu.make_async_copy(ref.at[pl.ds(first, self.rest), :], to.at[pl.ds(0, self.rest), :], self.tail_sems.at[0, w]),
                pltpu.make_async_copy(
                    ref.at[pl.ds(self.cols + first, self.rest_two), :],
                    to.at[pl.ds(self.rest, self.rest_two), :],
                    self.tail_sems.at[1, w],
                ),
            ]
        return copies

    def begin(self, blocks=1):
        self.begun = blocks
        for i in range(blocks):
            for copy in self.copies(i):
                copy.start()

    def run(self, low, high, work):
        def one(i, unused):
            @pl.when((i + 1 < self.regular) & (i + 1 >= self.begun))
            def _():
                for copy in self.copies(i + 1):
                    copy.start()

            @pl.when(i + 1 == self.regular)
            def _():
                for copy in self.tail():
                    copy.start()

            for copy in self.copies(i):
                copy.wait()
            work([self.slot(i, w) for w in range(len(self.weights))], lax.rem(i, 2) * self.cols + i // 2 * self.size)
            return unused

        lax.fori_loop(low, high, one, 0)

    def end(self, work):
        for copy in self.tail():
            copy.wait()
        slots = [self.first + (self.regular + self.phase) % 2 * self.each + w for w in range(self.each)]
        filled = self.rest + self.rest_two
        for slot in slots:
            self.buffers[slot, filled:, :] = jnp.zeros((self.size - filled, self.buffers.shape[2]), BF)
        work(slots, None)


class Units:
    def __init__(self, place, nz, heads, tok):
        self.place, self.nz, self.heads, self.tok = place, nz, heads, tok
        z, s = place.z, place.s
        self.at_end = (z == 0) | (z == nz - 1)
        self.second = jnp.where(z < nz // 2, s - PLANE, s + PLANE)
        self.near = (jnp.where(z == 0, s + PLANE, s - PLANE), place.t)

    def host(self, u):
        z = u // PLANE
        inner = jnp.clip(z, 1, self.nz - 2)
        return inner * PLANE + lax.rem(u, PLANE), jnp.where(inner == z, 0, 1)

    def unit(self, slot):
        return jnp.where(slot == 0, self.place.s, self.second)

    def home(self, ref, u):
        return ref.at[aligned(u // self.heads, self.tok), aligned(lax.rem(u, self.heads), HEAD_DIM)]


class ToUnits:
    def __init__(self, units, src, land, send, recv, local):
        self.units, self.src, self.land, self.send, self.recv, self.local = units, src, land, send, recv, local
        self.n, self.s, self.t, self.tok = units.place.n, units.place.s, units.place.t, units.tok

    def away(self, u):
        host, slot = self.units.host(u)
        to = self.land.at[slot, aligned(self.s, self.tok), :]
        return remote(self.units.home(self.src, u), to, self.send, self.recv.at[slot], (host, self.t))

    def here(self, u):
        slot = self.units.host(u)[1]
        to = self.land.at[slot, aligned(self.s, self.tok), :]
        return pltpu.make_async_copy(self.units.home(self.src, u), to, self.local.at[slot])

    def start(self, u, unused):
        host = self.units.host(u)[0]
        pl.when(host == self.s)(lambda: self.here(u).start())
        pl.when(host != self.s)(lambda: self.away(u).start())
        return unused

    def bulk(self, copies, recv):
        some = self.land.at[0, pl.ds(0, copies * self.tok), :]
        return remote(some, some, self.send, recv, self.units.place.core)

    def wait(self, slot):
        self.here(self.units.unit(slot)).wait()
        self.bulk(self.n - 1, self.recv.at[slot]).wait_recv()

    def sent(self):
        pl.when(self.units.at_end)(lambda: self.bulk(self.n, self.recv.at[0]).wait_send())
        pl.when(jnp.logical_not(self.units.at_end))(lambda: self.bulk(self.n - 2, self.recv.at[0]).wait_send())


class FromUnits:
    def __init__(self, units, src, whole, send, recv, local):
        self.units, self.src, self.whole, self.send, self.recv, self.local = units, src, whole, send, recv, local
        self.n, self.s, self.t, self.tok = units.place.n, units.place.s, units.place.t, units.tok

    def away(self, slot, d):
        u = self.units.unit(slot)
        src = self.src.at[slot, aligned(d, self.tok), :]
        return remote(src, self.units.home(self.whole, u), self.send.at[slot], self.recv, (d, self.t))

    def here(self, slot):
        src = self.src.at[slot, aligned(self.s, self.tok), :]
        return pltpu.make_async_copy(src, self.units.home(self.whole, self.units.unit(slot)), self.local.at[slot])

    def start(self, slot, low, high):
        def one(d, unused):
            pl.when(d == self.s)(lambda: self.here(slot).start())
            pl.when(d != self.s)(lambda: self.away(slot, d).start())
            return unused

        lax.fori_loop(low, high, one, 0)

    def bulk(self, copies, slot):
        some = self.src.at[0, pl.ds(0, copies * self.tok), :]
        return remote(some, some, self.send.at[slot], self.recv, self.units.place.core)

    def wait(self):
        pl.when(self.units.at_end)(lambda: self.bulk(self.n, 0).wait_recv())

        @pl.when(jnp.logical_not(self.units.at_end))
        def _():
            for slot in range(2):
                self.here(slot).wait()
            self.bulk(self.n - 2, 0).wait_recv()

    def sent(self, slot):
        self.bulk(self.n - 1, slot).wait_send()


def layer_kernel(
    geo, sizes, names,
    x_in, cot_in, key_in, value_in, seg_in, wg_in, wu_in, wd_in, wo_in, wq_in, gain_one, gain_two, *refs,
):
    n, rows, tok, width, half, heads, length = geo
    ff, cols, cuts = sizes
    r = types.SimpleNamespace(**dict(zip(names, refs, strict=True)))
    tokens = rows * tok
    blk = 2 * width // n
    nz = n // PLANE
    place = Place(n)
    s, t, z = place.s, place.t, place.z
    row_s, head_s = s // heads, lax.rem(s, heads)
    mine = aligned(t, half)
    chunk = tokens // 4
    fine = 32
    wbuf = r.wbuf
    size = wbuf.shape[1]
    mid, x_all, cot_all, two_norm, two_own, two_in, one_in = (
        r.mid, r.x_all, r.cot_all, r.two_norm, r.two_own, r.two_in, r.one_in
    )
    mixed, err, one, attended, dq = r.mixed, r.err, r.one, r.attended, r.dq
    d_att = attended
    hidden, d_gate, d_up, sums = r.hidden, r.d_gate, r.d_up, r.sums
    uq, uk, uv, uo, lse, k_t = (ref.at[0] for ref in (r.uqs, r.uks, r.uvs, r.uos, r.lses, r.k_ts))
    delta = r.delta
    seg_all, seg_row, seg_col = r.seg_all, r.seg_row, r.seg_col
    udq, udk, udv = r.udq, r.udk, r.udv
    tp_s, tp_r, a_s, a_r, loc = r.tp_s, r.tp_r, r.a_s, r.a_r, r.loc
    units = Units(place, nz, heads, tok)
    at_end = units.at_end
    place.enter()

    to_x = remote(x_in, x_all.at[:, mine], tp_s.at[0], tp_r.at[0], place.twin)
    to_x.start()
    own_x = pltpu.make_async_copy(x_in, x_all.at[:, mine], loc.at[0])
    own_x.start()

    def piece(ref):
        return lambda d: ref.at[aligned(d // heads, tok), aligned(lax.rem(d, heads), HEAD_DIM)]

    keys = Spread(place, piece(key_in), lambda: uk.at[aligned(s, tok), :], a_s.at[0], a_r.at[0], loc.at[2], uk.at[: length - tok, :])
    vals = Spread(place, piece(value_in), lambda: uv.at[aligned(s, tok), :], a_s.at[1], a_r.at[1], loc.at[3], uv.at[: length - tok, :])
    segs = Spread(place, lambda d: seg_in.at[d // heads], lambda: seg_all.at[s], a_s.at[2], a_r.at[2], loc.at[4], seg_all.at[: n - 1])
    qrys = Spread(place, piece(dq), lambda: uq.at[aligned(s, tok), :], a_s.at[3], a_r.at[3], loc.at[5], uq.at[: length - tok, :])
    segs.start()
    keys.start()
    vals.start()
    to_cot = remote(cot_in, cot_all.at[:, mine], tp_s.at[1], tp_r.at[1], place.twin)
    to_cot.start()
    own_cot = pltpu.make_async_copy(cot_in, cot_all.at[:, mine], loc.at[6])
    own_cot.start()

    def square_copies(k, ref, sems):
        copies = []
        for zy in range(n // 2):
            to = wbuf.at[4 * k + zy // 2, :, (zy % 2) * half : (zy % 2 + 1) * half]
            copies.append(pltpu.make_async_copy(ref.at[zy * blk : (zy + 1) * blk, :], to, sems.at[zy]))
        return copies

    def square_block(k, zy):
        return wbuf[4 * k + zy // 2, :, (zy % 2) * half : (zy % 2 + 1) * half]

    def split_block(ref, at, zy):
        zz, yy = divmod(zy, 2)
        return ref[yy, at, zz * blk : (zz + 1) * blk]

    def store_split(ref, at, now):
        for zy in range(n // 2):
            zz, yy = divmod(zy, 2)
            ref[yy, at, zz * blk : (zz + 1) * blk] = now[:, zy * blk : (zy + 1) * blk]

    load_wq = square_copies(1, wq_in, r.o_sem.at[0])
    load_wo = square_copies(0, wo_in, r.o_sem.at[1])
    for copy in load_wq + load_wo:
        copy.start()
    own_x.wait()
    to_x.wait()

    def first_norm(i, unused):
        at = aligned(i, fine)
        x = x_all[at, :].astype(F32)
        root = lax.rsqrt(jnp.mean(x * x, axis=-1, keepdims=True) + EPSILON)
        store_split(one, at, (x * root * gain_one[...]).astype(BF))
        return unused

    lax.fori_loop(0, tokens // fine, first_norm, 0)
    for copy in load_wq:
        copy.wait()
    every = slice(0, tokens)
    total = jnp.zeros((tokens, half), F32)
    for zy in range(n // 2):
        total += dot_nn(split_block(one, every, zy), square_block(1, zy))
    dq[...] = (total * HEAD_DIM ** (-0.5)).astype(BF)
    qrys.start()
    lv_one, lv_two = r.lv_one, r.lv_two
    left_cot, left_two, left_err, left_one = (
        Plane(place, split, land, r.le_s.at[i], r.le_r.at[i], r.l_loc.at[i], tokens)
        for i, (split, land) in enumerate(((err, lv_one), (mixed, lv_two), (err, r.l_err), (one, r.l_one)))
    )
    left_one.start()

    segs.wait()
    attention_masks(seg_all, seg_row, seg_col, n, tok)
    keys.wait()
    vals.wait()

    def turn_into(ref, to):
        def turn(i, unused):
            at = aligned(i, tok)
            to[:, at] = jnp.transpose(ref[at, :].astype(F32)).astype(BF)
            return unused

        lax.fori_loop(0, n, turn, 0)

    turn_into(uv, k_t)
    qrys.wait()
    block = 512
    owners = block // tok
    back = Spread(
        place,
        lambda d: uo.at[aligned(d, tok), :],
        lambda: attended.at[aligned(row_s, tok), aligned(head_s, HEAD_DIM)],
        a_s.at[4], a_r.at[4], loc.at[8], uo.at[: length - tok, :],
    )

    def query_step(qi, unused):
        query_block = uq[aligned(qi, block), :]

        def key_step(j, carry):
            top, total, acc = carry
            kj = qi - j
            scores = dot_nt(uk[aligned(kj, block), :], query_block)
            scores = jnp.where(readable(seg_col, seg_row, kj, qi, block), scores, NEGATIVE_FILL)
            new_top = jnp.maximum(top, jnp.max(scores, axis=0, keepdims=True))
            weights = jnp.exp(scores - new_top)
            decay = jnp.exp(top - new_top)
            total = total * decay + jnp.sum(weights, axis=0, keepdims=True)
            acc = acc * decay + dot_nn(k_t[:, aligned(kj, block)], weights.astype(BF))
            return new_top, total, acc

        start = (
            jnp.full((1, block), NEGATIVE_FILL, F32),
            jnp.zeros((1, block), F32),
            jnp.zeros((HEAD_DIM, block), F32),
        )
        top, total, acc = lax.fori_loop(0, qi + 1, key_step, start)
        lse[:, aligned(qi, block)] = top + jnp.log(total)
        uo[aligned(qi, block), :] = jnp.transpose(acc / total).astype(BF)
        return lax.fori_loop(qi * owners, (qi + 1) * owners, back.start_to, unused)

    lax.fori_loop(0, length // block, query_step, 0)

    work = (r.acc, r.stage, r.work_sem)
    mv, turned = r.mv, r.turned
    s_first, s_second, t_first, t_second = r.s_first, r.s_second, r.t_first, r.t_second
    sources = (hidden, d_gate, d_up)
    lefts_of = ((lv_one, lv_one), (lv_two, lv_two), (lv_two, lv_two))
    kept = ((s_first, t_first, r.out_down), (s_second, t_second, r.out_gate), (s_first, t_first, r.out_up))
    gots = (r.g0, r.g1, r.g2, r.g3, r.g4, r.g5, r.g6)
    lands = (None, None, None, r.m3, r.m4, r.m5, r.m6)
    plans = []
    for i, (kind, first, wide) in enumerate(cuts):
        at = pl.ds(first, wide)
        left, lv = lefts_of[kind]
        move, total_ref, out_ref = kept[kind]
        here = mv.at[:, at]
        plans.append((
            (sources[kind], cols, first), here if lands[i] is None else lands[i], left, lv, here, move.at[:, :, at], gots[i], total_ref.at[:, at],
            out_ref, (turned, cols, first),
        ))
    for source, left, lv, *rest in (
        (attended, r.l_err, lv_one, r.mv_out, r.s_out, r.g_out, r.t_out, r.out_out),
        (dq, r.l_one, lv_two, r.mv_query, r.s_query, r.g_query, r.t_query, r.out_query),
    ):
        plans.append(((source, half // 2, 0), rest[0], left, lv, *rest, None))
    lines = []
    for i, (source, land, *rest) in enumerate(plans):
        gather = Gather(place, *source, land, r.me_s.at[i], r.me_r.at[i], r.g_loc.at[i], tokens)
        sems = (r.c_s.at[i], r.c_r.at[i], r.e_s.at[i], r.e_r.at[i], r.e_l.at[i])
        lines.append(Line(place, nz, blk, gather, land, *rest, sems, work))
    down_a, down_b, down_c, gate_a, gate_b, up_a, up_b, out, query = lines
    ship = [
        remote(a.at[0], a.at[1], r.sh_s.at[i], r.sh_r.at[i], units.near)
        for i, a in enumerate((r.uqs, r.uks, r.uvs, r.uos, r.lses))
    ]

    @pl.when(at_end)
    def _():
        for copy in ship:
            copy.start()

    own_cot.wait()
    to_cot.wait()

    def split_cot(i, unused):
        at = aligned(i, fine)
        store_split(err, at, cot_all[at, :])
        return unused

    lax.fori_loop(0, tokens // fine, split_cot, 0)
    left_cot.start()
    left_one.forward()
    for copy in load_wo:
        copy.wait()
    back.wait()

    chunks = 4
    wide = width // chunks

    def to_twin(i):
        at = slice(i * wide, (i + 1) * wide)
        return remote(two_own.at[:, at], one_in.at[:, at], tp_s.at[9 + i], tp_r.at[9 + i], place.twin)

    for i in range(chunks):
        for zy in range(2 * i, 2 * i + 2):
            two_own[:, zy * blk : (zy + 1) * blk] = dot_nt(attended[...], square_block(0, zy)).astype(BF)
        to_twin(i).start()
    out.gather.start()
    first_pass = Weights((wg_in, wu_in, wd_in), wbuf, r.w_sem.at[0], r.tail_sem.at[0], 0, 0, cols, ff)
    second_pass = Weights((wg_in, wu_in), wbuf, r.w_sem.at[1], r.tail_sem.at[1], 0, 3, cols, ff)
    third_pass = Weights((wd_in,), wbuf, r.w_sem.at[2], r.tail_sem.at[2], 0, 4, cols, ff)
    first_pass.begin(2)
    left_cot.forward()
    square = jnp.zeros((tokens, 1), F32)
    for i in range(chunks):
        to_twin(i).wait()
        at = slice(i * wide, (i + 1) * wide)
        now = x_all[:, at].astype(F32) + (two_own[:, at].astype(F32) + one_in[:, at].astype(F32))
        mid[:, at] = now
        square += jnp.sum(now * now, axis=-1, keepdims=True)
    root_two = lax.rsqrt(square * (1.0 / width) + EPSILON)
    for i in range(chunks):
        at = slice(i * wide, (i + 1) * wide)
        two_norm[:, at] = (mid[:, at] * root_two * gain_two[:, at]).astype(BF)

    def units_block(slots, at):
        wg, wu, wd = (wbuf[slot] for slot in slots)
        x, g = two_norm[...], cot_all[...]
        gate_now, up_now = dot_nt(x, wg), dot_nt(x, wu)
        d_hid = dot_nt(g, wd)
        sigma = jax.nn.sigmoid(gate_now)
        act = gate_now * sigma
        for ref, now in (
            (hidden, act * up_now),
            (d_gate, d_hid * up_now * sigma * (1.0 + gate_now * (1.0 - sigma))),
            (d_up, d_hid * act),
        ):
            now = now.astype(BF)
            if at is None:
                last, rest = cols // size * size, cols % size
                ref[:, last:cols] = now[:, :rest]
                ref[:, cols + last :] = now[:, rest : 2 * rest]
            else:
                ref[:, pl.ds(pl.multiple_of(at, LANE), size)] = now

    done_a, done_b = (2 * ((first + wide) // size) for _, first, wide in cuts[:2])
    first_pass.run(0, done_a, units_block)
    down_a.gather.start()

    def split_two(i, unused):
        at = aligned(i, fine)
        store_split(mixed, at, two_norm[at, :])
        return unused

    lax.fori_loop(0, tokens // fine, split_two, 0)
    first_pass.run(done_a, done_b, units_block)
    down_b.gather.start()
    left_cot.gone()
    left_cot.finish()
    down_a.load()
    down_a.from_end()
    first_pass.run(done_b, first_pass.regular, units_block)
    second_pass.begin()
    first_pass.end(units_block)
    down_c.gather.start()
    left_two.start()
    down_b.load()
    down_b.from_end()
    down_a.between(0, 2)

    def block_of(ref, at):
        if at is None:
            last, rest = cols // size * size, cols % size
            return jnp.concatenate([ref[:, last:cols], ref[:, cols + last :]], axis=1)
        return ref[:, pl.ds(pl.multiple_of(at, LANE), size)]

    def add_up(pairs):
        for db in range(width // size):
            at = slice(db * size, (db + 1) * size)
            sums[db * tokens : (db + 1) * tokens, :] += sum(dot_nn(a, wbuf[slot, :, at]) for a, slot in pairs)

    def back_units(slots, at):
        add_up([(block_of(d_gate, at), slots[0]), (block_of(d_up, at), slots[1])])

    sums[...] = jnp.zeros_like(sums)
    second_pass.run(0, second_pass.regular, back_units)
    second_pass.end(back_units)
    for db in range(width // size):
        two_own[:, db * size : (db + 1) * size] = sums[db * tokens : (db + 1) * tokens, :].astype(BF)

    def two_copy(i):
        at = aligned(i, chunk)
        return remote(two_own.at[at, :], two_in.at[at, :], tp_s.at[2 + i], tp_r.at[2 + i], place.twin)

    for i in range(4):
        two_copy(i).start()
    load_wo = square_copies(0, wo_in, r.o_sem.at[2])
    for copy in load_wo:
        copy.start()
    gate_a.gather.start()
    down_a.between(2, 3)
    down_b.between(0, 2)
    down_c.load()
    down_c.from_end()

    third_pass.begin()
    sums[...] = jnp.zeros_like(sums)

    def out_units(slots, at):
        add_up([(block_of(hidden, at), slots[0])])

    third_pass.run(0, third_pass.regular, out_units)
    third_pass.end(out_units)
    left_two.forward()
    left_two.gone()
    for db in range(width // size):
        per = half // size
        mixed[db // per, :, (db % per) * size : (db % per + 1) * size] = sums[db * tokens : (db + 1) * tokens, :].astype(BF)
    ffn_copy = remote(mixed.at[1 - t], r.ffn_in, tp_s.at[6], tp_r.at[6], place.twin)
    ffn_copy.start()
    per = half // size
    for i in range(per):
        at = t * per + i
        sums[aligned(at, tokens), :] += mid[:, aligned(at, size)]
    hold = pltpu.make_async_copy(sums.at[aligned(t, per * tokens), :], r.mix, loc.at[11])
    hold.start()
    load_wq = square_copies(1, wq_in, r.o_sem.at[3])
    for copy in load_wq:
        copy.start()
    down_b.between(2, 3)
    down_c.between(0, 2)
    hold.wait()

    to_units = ToUnits(units, d_att, r.udo, r.u_s.at[0], r.u_r, r.u_l)
    out.gather.wait()
    for copy in load_wo:
        copy.wait()

    def second_norm(i, gain_sum):
        two_copy(i).wait()

        def some(j, gain_sum):
            at = aligned(i * (chunk // fine) + j, fine)
            m = mid[at, :]
            d2 = two_own[at, :].astype(F32) + two_in[at, :].astype(F32)
            root = lax.rsqrt(jnp.mean(m * m, axis=-1, keepdims=True) + EPSILON)
            gained = d2 * gain_two[...]
            scaled = m * root
            gain_sum = gain_sum + jnp.sum(d2 * scaled, axis=0, keepdims=True)
            slope = jnp.mean(gained * scaled, axis=-1, keepdims=True)
            dm = cot_all[at, :].astype(F32) + root * (gained - scaled * slope)
            mid[at, :] = dm
            store_split(err, at, dm.astype(BF))
            return gain_sum

        gain_sum = lax.fori_loop(0, chunk // fine, some, gain_sum)
        at = aligned(i, chunk)
        total = jnp.zeros((chunk, half), F32)
        for zy in range(n // 2):
            total += dot_nn(split_block(err, at, zy), square_block(0, zy))
        d_att[at, :] = total.astype(BF)
        return gain_sum

    gain_sum = jnp.zeros((1, width), F32)
    per_row = tok // chunk
    for row in range(rows):
        gain_sum = lax.fori_loop(row * per_row, (row + 1) * per_row, second_norm, gain_sum)
        lax.fori_loop(row * heads, (row + 1) * heads, to_units.start, 0)
    gain_part, gain_in = r.gain_part, r.gain_in
    for i in range(n):
        gain_part[0, i] = gain_sum[:, i * (width // n) : (i + 1) * (width // n)]
    spread_gain = [
        Spread(place, lambda d, g=g: gain_part.at[g, d], lambda g=g: gain_in.at[g, s], a_s.at[5 + g], a_r.at[5 + g], loc.at[9 + g],
               gain_in.at[g, : n - 1])
        for g in range(2)
    ]
    spread_gain[0].start()
    gate_b.gather.start()
    down_c.between(2, 3)
    left_two.finish()
    gate_a.load()
    gate_a.from_end()

    back_dq, back_dk, back_dv = (
        FromUnits(units, src, whole, r.f_s.at[i], r.f_r.at[i], r.f_l.at[i])
        for i, (src, whole) in enumerate(((udq, dq), (udk, r.d_keys), (udv, r.d_values)))
    )

    def one_unit(slot, between):
        unit_q, unit_k, unit_v, unit_o, unit_lse, unit_kt = (
            ref.at[slot] for ref in (r.uqs, r.uks, r.uvs, r.uos, r.lses, r.k_ts)
        )
        unit_do = r.udo.at[slot]
        sums[...] = jnp.zeros_like(sums)
        to_units.wait(slot)

        def turn_delta(i, unused):
            at = aligned(i, tok)
            both = unit_do[at, :].astype(F32) * unit_o[at, :].astype(F32)
            delta[:, at] = jnp.sum(jnp.transpose(both), axis=0, keepdims=True)
            return unused

        lax.fori_loop(0, n, turn_delta, 0)

        def query_step(qi):
            qat = aligned(qi, block)
            qb, dob = unit_q[qat, :], unit_do[qat, :]

            def key_step(kj, dq_t):
                kat = aligned(kj, block)
                scores = dot_nt(unit_k[kat, :], qb) - unit_lse[:, qat]
                probs = jnp.exp(jnp.where(readable(seg_col, seg_row, kj, qi, block), scores, NEGATIVE_FILL))
                d_probs = dot_nt(unit_v[kat, :], dob)
                d_scores = (probs * (d_probs - delta[:, qat])).astype(BF)
                sums[kat, :HEAD_DIM] += dot_nn(d_scores, qb)
                sums[kat, HEAD_DIM:] += dot_nn(probs.astype(BF), dob)
                return dq_t + dot_nn(unit_kt[:, kat], d_scores)

            dq_t = lax.fori_loop(0, qi + 1, key_step, jnp.zeros((HEAD_DIM, block), F32))
            udq[slot, qat, :] = jnp.transpose(dq_t).astype(BF)
            back_dq.start(slot, qi * owners, (qi + 1) * owners)
            udk[slot, qat, :] = sums[qat, :HEAD_DIM].astype(BF)
            udv[slot, qat, :] = sums[qat, HEAD_DIM:].astype(BF)

        for qi in reversed(range(length // block)):
            query_step(qi)
            for step in between.get(qi, ()):
                step()

    def one_copy(i):
        at = aligned(i, chunk)
        return remote(two_own.at[at, :], one_in.at[at, :], tp_s.at[13 + i], tp_r.at[13 + i], place.twin)

    def through_query():
        for copy in load_wq:
            copy.wait()
        back_dq.wait()
        query.gather.start()

        def back_query(i, unused):
            at = aligned(i, chunk)
            for zy in range(n // 2):
                now = dot_nt(dq[at, :], square_block(1, zy)) * HEAD_DIM ** (-0.5)
                two_own[at, zy * blk : (zy + 1) * blk] = now.astype(BF)
            one_copy(i).start()
            return unused

        lax.fori_loop(0, 4, back_query, 0)

    def last_norm(i, gain_sum):
        one_copy(i).wait()

        def some(j, gain_sum):
            at = aligned(i * (chunk // fine) + j, fine)
            x = x_all[at, :].astype(F32)
            d1 = two_own[at, :].astype(F32) + one_in[at, :].astype(F32)
            root = lax.rsqrt(jnp.mean(x * x, axis=-1, keepdims=True) + EPSILON)
            gained = d1 * gain_one[...]
            scaled = x * root
            gain_sum = gain_sum + jnp.sum(d1 * scaled, axis=0, keepdims=True)
            slope = jnp.mean(gained * scaled, axis=-1, keepdims=True)
            mid[at, :] = mid[at, :] + root * (gained - scaled * slope)
            return gain_sum

        return lax.fori_loop(0, chunk // fine, some, gain_sum)

    give = pltpu.make_async_copy(mid.at[:, mine], r.input_grad, loc.at[19])

    def through_first_norm():
        gain_sum = lax.fori_loop(0, 4, last_norm, jnp.zeros((1, width), F32))
        for i in range(n):
            gain_part[1, i] = gain_sum[:, i * (width // n) : (i + 1) * (width // n)]
        spread_gain[1].start()
        give.start()

    def finish_all(*some):
        for line in some:
            line.finish()

    def left_all(*some):
        for line in some:
            line.left_here()

    def sent_all(*some):
        for line in some:
            line.sent()

    def err_here():
        left_err.forward()
        left_err.gone()
        left_err.finish()

    def one_here():
        left_one.gone()
        left_one.finish()

    up_a.gather.start()
    up_b.gather.start()
    left_err.start()

    with jax.named_scope("between"):
        @pl.when(jnp.logical_not(at_end))
        def _():
            turn_into(r.uks.at[0], r.k_ts.at[0])
            for copy in ship:
                copy.wait_recv()
            turn_into(r.uks.at[1], r.k_ts.at[1])
            gate_a.step(0)
            one_unit(0, {3: [lambda: gate_a.step(1)]})
            back_dk.start(0, 0, n)
            back_dv.start(0, 0, n)
            one_unit(1, {3: [lambda: gate_a.step(2), gate_b.load, gate_b.own, lambda: gate_b.step(0)], 2: [lambda: gate_b.step(1)]})
            finish_all(down_a, down_b)
            sent_all(down_a, down_b, down_c)
            up_a.load()
            up_a.own()
            up_a.step(0)
            gate_b.step(2)
            finish_all(down_c)
            back_dk.start(1, 0, n)
            through_query()
            up_a.step(1)
            up_b.load()
            up_b.own()
            back_dv.start(1, 0, n)
            err_here()
            up_a.step(2)
            up_b.step(0)
            left_all(down_a, down_b)
            finish_all(gate_a)
            up_b.step(1)
            left_all(down_c)
            finish_all(gate_b)
            out.load(True, gathered=True)
            out.own()
            up_b.step(2)
            out.step(0)
            one_here()
            through_first_norm()
            out.step(1)
            query.load(True)
            query.own()
            left_all(gate_a)
            finish_all(up_a)
            out.step(2)
            query.step(0)
            query.step(1)
            left_all(gate_b)
            finish_all(up_b)
            query.step(2)
            finish_all(out, query)

    with jax.named_scope("ends"):
        @pl.when(at_end)
        def _():
            gate_b.load()
            gate_b.begin()
            finish_all(down_a, down_b, down_c)
            sent_all(down_a, down_b, down_c)
            up_a.load()
            up_a.begin()
            up_b.load()
            up_b.begin()
            left_all(down_a, down_b, down_c)
            err_here()
            out.load(True, gathered=True)
            out.begin()
            through_query()
            one_here()
            query.load(True)
            query.begin()
            through_first_norm()
            finish_all(gate_a, gate_b)
            left_all(gate_a, gate_b)
            finish_all(up_a, up_b, out, query)

    ffn_copy.wait()
    to_units.sent()
    fetch = pltpu.make_async_copy(r.mix, sums.at[: per * tokens, :], loc.at[11])
    fetch.start()
    fetch.wait()
    for i in range(per):
        at = slice(i * size, (i + 1) * size)
        attended[:, at] = (sums[i * tokens : (i + 1) * tokens, :] + r.ffn_in[:, at].astype(F32)).astype(BF)
    give_mixed = pltpu.make_async_copy(attended, r.out_mixed, loc.at[20])
    give_mixed.start()
    back_dk.wait()
    back_dv.wait()
    for g in range(2):
        spread_gain[g].wait()
        r.gains[g] = jnp.sum(gain_in[g], axis=0)

    @pl.when(at_end)
    def _():
        for copy in ship:
            copy.wait_send()

    @pl.when(jnp.logical_not(at_end))
    def _():
        for slot in range(2):
            for sent in (back_dq, back_dk, back_dv):
                sent.sent(slot)

    give.wait()
    give_mixed.wait()
    for line in lines[3:]:
        line.sent()
    for line in lines[5:]:
        line.left_here()
    for line in lines:
        line.arrived()


def fast_device(
    n, inputs, segments, keys, values, attn_gain, query_weight, out_weight, ffn_gain, gate_weight, up_weight, down_weight,
    cotangent,
):
    rows, tok, half = inputs.shape
    tokens, width, ff = rows * tok, query_weight.shape[0], gate_weight.shape[1]
    heads, length = half // HEAD_DIM, n * tok
    geo = (n, rows, tok, width, half, heads, length)
    blk, nz, size = 2 * width // n, n // PLANE, 2 * LANE
    cols = -(-ff // size) * LANE
    firsts = (0, size, 3 * size, cols)
    thirds = [(firsts[i], firsts[i + 1] - firsts[i]) for i in range(3)]
    halves = [(0, firsts[2]), (firsts[2], cols - firsts[2])]
    cuts = tuple((kind, *cut) for kind, parts in enumerate((thirds, halves, halves)) for cut in parts)
    sizes = (ff, cols, cuts)
    square = half // 2
    n_lines = len(cuts) + 2
    dma = pltpu.SemaphoreType.DMA
    anywhere, here = pl.BlockSpec(memory_space=pl.ANY), pl.BlockSpec(memory_space=pltpu.VMEM)

    def pieces(letter, shapes):
        return {letter + str(i): shape for i, shape in shapes}

    tall, flat_left = vm((2 * cols, blk // 2), F32), vm((PLANE * tokens, width // 2), BF)
    sum_square = vm((nz + 1, blk, square), BF)
    outs = dict(
        out_mixed=vm((tokens, half), BF),
        input_grad=vm((tokens, half), F32),
        d_keys=vm((tokens, half), BF),
        d_values=vm((tokens, half), BF),
        gains=vm((2, 1, width // n), F32),
        out_down=tall,
        out_gate=tall,
        out_up=tall,
        out_out=vm((blk // 2, half), F32),
        out_query=vm((blk // 2, half), F32),
        mix=vm((half // size * tokens, size), F32),
        l_err=flat_left,
        l_one=flat_left,
        g_out=sum_square,
        g_query=sum_square,
        **pieces("m", [(i, vm((PLANE * tokens, w), BF)) for i, (kind, _, w) in enumerate(cuts) if kind > 0]),
        **pieces("g", [(i, vm((nz + 1, blk, w), BF)) for i, (_, _, w) in enumerate(cuts)]),
    )
    row = pltpu.VMEM((1, length), F32)
    act, own = pltpu.VMEM((tokens, width), BF), pltpu.VMEM((tokens, half), BF)
    split = pltpu.VMEM((2, tokens, width // 2), BF)
    hid = pltpu.VMEM((tokens, 2 * cols), BF)
    gain = pltpu.VMEM((2, n, 1, width // n), F32)
    left = pltpu.VMEM((PLANE * tokens, width // 2), BF)
    two = pltpu.VMEM((2, length, HEAD_DIM), BF)
    move, move_square = (pltpu.VMEM((nz - 1, blk, c), BF) for c in (cols, square))
    total, total_square = (pltpu.VMEM((blk, c), F32) for c in (cols, square))
    taken = pltpu.VMEM((PLANE * tokens, square), BF)
    scratch = dict(
        mid=pltpu.VMEM((tokens, width), F32),
        x_all=act, cot_all=act, two_norm=act, two_own=act, two_in=act, one_in=act, mixed=split, err=split, one=split,
        wbuf=pltpu.VMEM((8, size, width), BF),
        attended=own, dq=own, ffn_in=own, hidden=hid, d_gate=hid, d_up=hid,
        sums=pltpu.VMEM((length, size), F32),
        uqs=two, uks=two, uvs=two, uos=two, udo=two, udq=two, udk=two, udv=two,
        delta=row, seg_row=row, lses=pltpu.VMEM((2, 1, length), F32),
        seg_all=pltpu.VMEM((n, 1, tok), F32),
        seg_col=pltpu.VMEM((length, LANE), F32),
        k_ts=pltpu.VMEM((2, HEAD_DIM, length), BF),
        gain_part=gain, gain_in=gain,
        s_first=move, s_second=move, s_out=move_square, s_query=move_square,
        t_first=total, t_second=total, t_out=total_square, t_query=total_square,
        turned=pltpu.VMEM((cols, blk), F32),
        mv=pltpu.VMEM((PLANE * tokens, cols), BF), mv_out=taken, mv_query=taken,
        lv_one=left, lv_two=left,
        acc=total,
        stage=pltpu.VMEM((blk, cols), BF),
        tp_s=dma((17,)), tp_r=dma((17,)), a_s=dma((7,)), a_r=dma((7,)),
        me_s=dma((n_lines, 3)), me_r=dma((n_lines, 3)), le_s=dma((4, 3)), le_r=dma((4, 3)),
        c_s=dma((n_lines, nz - 1)), c_r=dma((n_lines, nz + 1)),
        e_s=dma((n_lines,)), e_r=dma((n_lines,)), e_l=dma((n_lines,)),
        sh_s=dma((5,)), sh_r=dma((5,)), u_s=dma((1,)), u_r=dma((2,)), u_l=dma((2,)),
        f_s=dma((3, 2)), f_r=dma((3,)), f_l=dma((3, 2)),
        loc=dma((21,)), g_loc=dma((n_lines,)), l_loc=dma((4,)), work_sem=dma((3,)),
        w_sem=dma((3, 2, 3)), tail_sem=dma((3, 2, 3)), o_sem=dma((4, n // 2)),
    )
    names = (*outs, *scratch)

    def flat(a):
        return a.reshape(tokens, half)

    segf = segments.astype(F32).reshape(rows, 1, tok)
    got = pl.pallas_call(
        functools.partial(layer_kernel, geo, sizes, names),
        out_shape=list(outs.values()),
        in_specs=[anywhere] * 10 + [here] * 2,
        out_specs=[here if i == 4 else anywhere for i in range(len(outs))],
        scratch_shapes=list(scratch.values()),
        compiler_params=pltpu.CompilerParams(
            collective_id=0, has_side_effects=True, vmem_limit_bytes=VMEM_GRANT
        ),
        name="layer",
    )(
        flat(inputs), flat(cotangent), flat(keys), flat(values), segf, gate_weight.T, up_weight.T, down_weight.T,
        out_weight, query_weight, attn_gain.reshape(1, width), ffn_gain.reshape(1, width),
    )
    got = types.SimpleNamespace(**dict(zip(outs, got)))

    def shaped(a):
        return a.reshape(rows, tok, half)

    return (
        shaped(got.out_mixed),
        shaped(got.input_grad),
        shaped(got.d_keys.astype(F32)),
        shaped(got.d_values.astype(F32)),
        got.gains[1, 0],
        got.out_query * HEAD_DIM ** (-0.5),
        got.out_out,
        got.gains[0, 0],
        got.out_gate[:ff].T,
        got.out_up[:ff].T,
        got.out_down[:ff].T,
    )


def inverse_root(stream):
    return lax.rsqrt(jnp.mean(stream * stream, axis=-1, keepdims=True) + EPSILON)


def key_mask(doc_start, query_pos, begin, row_count):
    key_pos = begin + jnp.arange(row_count, dtype=jnp.int32)
    earlier = key_pos[None, None, :] <= query_pos[None, :, None]
    same_doc = key_pos[None, None, :] >= doc_start[:, :, None]
    return (earlier & same_doc)[:, None]


def per_device(
    inputs,
    segments,
    keys,
    values,
    attn_gain,
    query_weight,
    out_weight,
    ffn_gain,
    gate_weight,
    up_weight,
    down_weight,
    cotangent,
):
    batch_rows, local_tokens, half_width = inputs.shape
    local_heads = half_width // HEAD_DIM
    seq_devices = lax.axis_size("seq")
    row_length = local_tokens * seq_devices
    seq_index = lax.axis_index("seq")
    tp_index = lax.axis_index("tp")
    query_scale = HEAD_DIM ** (-0.5)
    bfloat = jnp.bfloat16
    single = jnp.float32
    whole = lax.all_gather(inputs, "tp", axis=2, tiled=True).astype(single)
    root_one = inverse_root(whole)
    scaled_one = whole * root_one
    normed_one = (scaled_one * attn_gain).astype(bfloat)
    query = (
        jnp.einsum("rtd,de->rte", normed_one, query_weight, preferred_element_type=single)
        * query_scale
    ).astype(bfloat)
    query_heads = query.reshape(batch_rows, local_tokens, local_heads, HEAD_DIM)
    bins = jnp.arange(CUTS + 1, dtype=jnp.int32)
    onehot = (segments[:, :, None] == bins[None, None, :]).astype(single)
    totals = lax.psum(jnp.sum(onehot, axis=1), "seq")
    ends = jnp.cumsum(totals, axis=-1)
    before = ends - totals
    doc_start = jnp.sum(onehot * before[:, None, :], axis=-1).astype(jnp.int32)
    query_pos = seq_index * local_tokens + jnp.arange(local_tokens, dtype=jnp.int32)
    first_needed = jnp.min(doc_start)
    last_needed = seq_index * local_tokens + local_tokens - 1
    start_state = (
        jnp.full((batch_rows, local_heads, local_tokens), NEGATIVE_FILL, single),
        jnp.zeros((batch_rows, local_heads, local_tokens), single),
        jnp.zeros((batch_rows, local_heads, local_tokens, HEAD_DIM), single),
    )
    key_piece = lax.all_gather(keys, "seq", axis=1, tiled=True)
    value_piece = lax.all_gather(values, "seq", axis=1, tiled=True)
    piece_rows = key_piece.shape[1]
    fold_key_block = math.gcd(piece_rows, 512)

    def fold_step(block_index, state):
        running_max, running_sum, running_out = state
        begin = block_index * fold_key_block

        def fold_work(unused):
            key_heads = lax.dynamic_slice_in_dim(
                key_piece, block_index * fold_key_block, fold_key_block, 1
            ).reshape(batch_rows, fold_key_block, local_heads, HEAD_DIM)
            value_heads = lax.dynamic_slice_in_dim(
                value_piece, block_index * fold_key_block, fold_key_block, 1
            ).reshape(batch_rows, fold_key_block, local_heads, HEAD_DIM)
            scores = jnp.einsum(
                "rqhe,rkhe->rhqk", query_heads, key_heads, preferred_element_type=single
            )
            allowed = key_mask(doc_start, query_pos, begin, fold_key_block)
            scores = jnp.where(allowed, scores, NEGATIVE_FILL)
            new_max = jnp.maximum(running_max, jnp.max(scores, axis=-1))
            weights = jnp.where(allowed, jnp.exp(scores - new_max[..., None]), 0.0)
            decay = jnp.exp(running_max - new_max)
            new_sum = running_sum * decay + jnp.sum(weights, axis=-1)
            new_out = running_out * decay[..., None] + jnp.einsum(
                "rhqk,rkhe->rhqe",
                weights.astype(bfloat),
                value_heads,
                preferred_element_type=single,
            )
            return (new_max, new_sum, new_out)

        def keep_state(unused):
            return (running_max, running_sum, running_out)

        needed = (begin <= last_needed) & (begin + fold_key_block - 1 >= first_needed)
        return lax.cond(needed, fold_work, keep_state, 0)

    running_max, running_sum, running_out = lax.fori_loop(
        0, piece_rows // fold_key_block, fold_step, start_state
    )
    log_total = running_max + jnp.log(running_sum)
    attended = running_out / running_sum[..., None]
    attended_low = (
        attended.transpose(0, 2, 1, 3).reshape(batch_rows, local_tokens, half_width).astype(bfloat)
    )
    branch = jnp.einsum("rth,dh->rtd", attended_low, out_weight, preferred_element_type=single)
    middle = whole + lax.psum(branch.astype(jnp.bfloat16), "tp").astype(jnp.float32)
    middle_share = lax.dynamic_slice_in_dim(middle, tp_index * half_width, half_width, 2)
    root_two = inverse_root(middle)
    scaled_two = middle * root_two
    normed_two = (scaled_two * ffn_gain).astype(bfloat)
    gate = jnp.einsum("rtd,df->rtf", normed_two, gate_weight, preferred_element_type=single)
    up_proj = jnp.einsum("rtd,df->rtf", normed_two, up_weight, preferred_element_type=single)
    sigma = jax.nn.sigmoid(gate)
    activated = gate * sigma
    hidden = (activated * up_proj).astype(bfloat)
    ffn_part = jnp.einsum("rtf,df->rtd", hidden, down_weight, preferred_element_type=single)
    output = (
        middle_share
        + lax.psum_scatter(
            ffn_part.astype(jnp.bfloat16), "tp", scatter_dimension=2, tiled=True
        ).astype(jnp.float32)
    ).astype(bfloat)
    grad_out = lax.all_gather(cotangent, "tp", axis=2, tiled=True)
    d_hidden = jnp.einsum("rtd,df->rtf", grad_out, down_weight, preferred_element_type=single)
    d_gate = (d_hidden * up_proj * sigma * (1.0 + gate * (1.0 - sigma))).astype(bfloat)
    d_up = (d_hidden * activated).astype(bfloat)
    d_two_part = jnp.einsum(
        "rtf,df->rtd", d_gate, gate_weight, preferred_element_type=single
    ) + jnp.einsum("rtf,df->rtd", d_up, up_weight, preferred_element_type=single)
    d_two = lax.psum(d_two_part.astype(jnp.bfloat16), "tp").astype(jnp.float32)
    gained_two = d_two * ffn_gain
    d_middle = (
        grad_out.astype(single)
        + root_two * gained_two
        - middle * root_two**3 * jnp.mean(gained_two * middle, axis=-1, keepdims=True)
    )
    normed_rows = normed_two
    gate_term = jnp.einsum("rtd,rtf->df", normed_rows, d_gate, preferred_element_type=single)
    up_term = jnp.einsum("rtd,rtf->df", normed_rows, d_up, preferred_element_type=single)
    down_term = jnp.einsum("rtd,rtf->df", grad_out, hidden, preferred_element_type=single)
    gain_term = jnp.sum(d_two * scaled_two, axis=(0, 1))
    gate_grad, up_grad, down_grad, ffn_gain_grad = lax.psum_scatter(
        (gate_term, up_term, down_term, gain_term), "seq", scatter_dimension=0, tiled=True
    )
    error = d_middle.astype(bfloat)
    d_attended = jnp.einsum("rtd,dh->rth", error, out_weight, preferred_element_type=single).astype(
        bfloat
    )
    d_heads = d_attended.reshape(batch_rows, local_tokens, local_heads, HEAD_DIM)
    carried = jnp.einsum("rqhe,rhqe->rhq", d_heads.astype(single), attended)
    key_all, value_all = (
        lax.all_gather(keys, "seq", axis=1, tiled=True),
        lax.all_gather(values, "seq", axis=1, tiled=True),
    )
    key_block = math.gcd(row_length, 512)

    def block_terms(begin):
        key_heads = lax.dynamic_slice_in_dim(key_all, begin, key_block, 1).reshape(
            batch_rows, key_block, local_heads, HEAD_DIM
        )
        value_heads = lax.dynamic_slice_in_dim(value_all, begin, key_block, 1).reshape(
            batch_rows, key_block, local_heads, HEAD_DIM
        )
        scores = jnp.einsum(
            "rqhe,rkhe->rhqk", query_heads, key_heads, preferred_element_type=single
        )
        allowed = key_mask(doc_start, query_pos, begin, key_block)
        probs = jnp.where(
            allowed, jnp.exp(jnp.where(allowed, scores, NEGATIVE_FILL) - log_total[..., None]), 0.0
        )
        d_probs = jnp.einsum("rqhe,rkhe->rhqk", d_heads, value_heads, preferred_element_type=single)
        d_scores = (probs * (d_probs - carried[..., None])).astype(bfloat)
        query_part = jnp.einsum(
            "rhqk,rkhe->rhqe", d_scores, key_heads, preferred_element_type=single
        )
        return (probs, d_scores, query_part)

    query_zero = jnp.zeros((batch_rows, local_heads, local_tokens, HEAD_DIM), single)

    def back_step(block_index, state):
        d_query, key_terms, value_terms = state
        begin = block_index * key_block

        def back_work(unused):
            probs, d_scores, query_part = block_terms(begin)
            value_part = jnp.einsum(
                "rhqk,rqhe->rkhe", probs.astype(bfloat), d_heads, preferred_element_type=single
            )
            key_part = jnp.einsum(
                "rhqk,rqhe->rkhe", d_scores, query_heads, preferred_element_type=single
            )
            return (
                query_part,
                key_part.reshape(batch_rows, key_block, half_width),
                value_part.reshape(batch_rows, key_block, half_width),
            )

        def skip_block(unused):
            empty_rows = jnp.zeros((batch_rows, key_block, half_width), single)
            return (jnp.zeros_like(d_query), empty_rows, empty_rows)

        needed = (begin <= last_needed) & (begin + key_block - 1 >= first_needed)
        query_part, key_part, value_part = lax.cond(needed, back_work, skip_block, 0)
        return (
            d_query + query_part,
            lax.dynamic_update_slice_in_dim(key_terms, key_part, begin, 1),
            lax.dynamic_update_slice_in_dim(value_terms, value_part, begin, 1),
        )

    back_start = (
        query_zero,
        jnp.zeros((batch_rows, row_length, half_width), single),
        jnp.zeros((batch_rows, row_length, half_width), single),
    )
    d_query, key_terms, value_terms = lax.fori_loop(
        0, row_length // key_block, back_step, back_start
    )
    key_grad, value_grad = (
        lax.psum_scatter(key_terms, "seq", scatter_dimension=1, tiled=True),
        lax.psum_scatter(value_terms, "seq", scatter_dimension=1, tiled=True),
    )
    d_query_rows = (
        d_query.transpose(0, 2, 1, 3).reshape(batch_rows, local_tokens, half_width).astype(bfloat)
    )
    d_one_part = (
        jnp.einsum("rte,de->rtd", d_query_rows, query_weight, preferred_element_type=single)
        * query_scale
    )
    d_one = lax.psum(d_one_part.astype(jnp.bfloat16), "tp").astype(jnp.float32)
    gained_one = d_one * attn_gain
    d_whole = (
        d_middle
        + root_one * gained_one
        - whole * root_one**3 * jnp.mean(gained_one * whole, axis=-1, keepdims=True)
    )
    input_grad = lax.dynamic_slice_in_dim(d_whole, tp_index * half_width, half_width, 2)
    normed_rows = normed_one
    query_term = (
        jnp.einsum("rtd,rte->de", normed_rows, d_query_rows, preferred_element_type=single)
        * query_scale
    )
    out_term = jnp.einsum("rtd,rth->dh", error, attended_low, preferred_element_type=single)
    gain_term = jnp.sum(d_one * scaled_one, axis=(0, 1))
    query_grad, out_grad, attn_gain_grad = lax.psum_scatter(
        (query_term, out_term, gain_term), "seq", scatter_dimension=0, tiled=True
    )
    return (
        output,
        input_grad,
        key_grad,
        value_grad,
        attn_gain_grad,
        query_grad,
        out_grad,
        ffn_gain_grad,
        gate_grad,
        up_grad,
        down_grad,
    )


def solution(mesh):
    in_specs = (
        P(None, "seq", "tp"),
        P(None, "seq"),
        P(None, "seq", "tp"),
        P(None, "seq", "tp"),
        P(),
        P(None, "tp"),
        P(None, "tp"),
        P(),
        P(None, "tp"),
        P(None, "tp"),
        P(None, "tp"),
        P(None, "seq", "tp"),
    )
    out_specs = (
        P(None, "seq", "tp"),
        P(None, "seq", "tp"),
        P(None, "seq", "tp"),
        P(None, "seq", "tp"),
        P("seq"),
        P("seq", "tp"),
        P("seq", "tp"),
        P("seq"),
        P("seq", "tp"),
        P("seq", "tp"),
        P("seq", "tp"),
    )
    n = mesh.shape["seq"]

    def step(inputs, *others):
        rows, tok, half = inputs.shape
        units = rows * (half // HEAD_DIM)
        if units == n == PLANE * PLANE and 4 * tok == 512 and mesh.shape["tp"] == 2:
            return fast_device(n, inputs, *others)
        return per_device(inputs, *others)

    return jax.shard_map(
        step, mesh=mesh, in_specs=in_specs, out_specs=out_specs, check_vma=False
    )
```

```python
import functools
import math
import types

import jax
import jax.numpy as jnp
from jax import lax
from jax.experimental import pallas as pl
from jax.experimental.pallas import tpu as pltpu
from jax.sharding import PartitionSpec as P

HEAD_DIM = 128
CUTS = 12


EPSILON = 1e-06
NEGATIVE_FILL = -1e30

MESH = pl.DeviceIdType.MESH
BF = jnp.bfloat16
F32 = jnp.float32
VMEM_GRANT = 63 << 20
PLANE = 4
LANE = 128


def dot_nn(a, b):
    return lax.dot_general(a, b, (((1,), (0,)), ((), ())), preferred_element_type=F32)


def dot_nt(a, b):
    return lax.dot_general(a, b, (((1,), (1,)), ((), ())), preferred_element_type=F32)


def dot_tn(a, b):
    return lax.dot_general(a, b, (((0,), (0,)), ((), ())), preferred_element_type=F32)


def aligned(index, size):
    return pl.ds(pl.multiple_of(index * size, size), size)


class Place:
    def __init__(self, n):
        self.n = n
        self.s = lax.axis_index("seq")
        self.t = lax.axis_index("tp")
        self.z = self.s // PLANE
        self.p = lax.rem(self.s, PLANE)
        self.y = self.p // 2
        self.c = lax.rem(self.p, 2)
        base = self.z * PLANE
        self.core_p = self.y * 2 + 1 - self.c
        self.side_p = (1 - self.y) * 2 + self.c
        self.cross_p = (1 - self.y) * 2 + 1 - self.c
        self.core = (base + self.core_p, self.t)
        self.side = (base + self.side_p, self.t)
        self.cross = (base + self.cross_p, self.t)
        self.twin = (self.s, 1 - self.t)

    def other(self, k):
        return lax.rem(self.s + k, self.n)

    def enter(self):
        barrier = pltpu.get_barrier_semaphore()

        def greet(k, unused):
            pl.semaphore_signal(barrier, inc=1, device_id=(self.other(k), self.t), device_id_type=MESH)
            return unused

        lax.fori_loop(1, self.n, greet, 0)
        pl.semaphore_signal(barrier, inc=1, device_id=self.twin, device_id_type=MESH)
        pl.semaphore_wait(barrier, self.n)


def remote(src, dst, send, recv, device):
    return pltpu.make_async_remote_copy(
        src_ref=src, dst_ref=dst, send_sem=send, recv_sem=recv, device_id=device, device_id_type=MESH
    )


class Spread:
    def __init__(self, place, src, dst, send, recv, local, bulk):
        self.place, self.src, self.dst, self.send, self.recv, self.local = place, src, dst, send, recv, local
        self.bulk = bulk

    def copy(self, k):
        place = self.place
        d = place.other(k)
        return remote(self.src(d), self.dst(), self.send, self.recv, (d, place.t))

    def own(self):
        return pltpu.make_async_copy(self.src(self.place.s), self.dst(), self.local)

    def start(self):
        self.own().start()

        def one(k, unused):
            self.copy(k).start()
            return unused

        lax.fori_loop(1, self.place.n, one, 0)

    def start_to(self, d, unused):
        k = lax.rem(d - self.place.s + self.place.n, self.place.n)

        @pl.when(k == 0)
        def _():
            self.own().start()

        @pl.when(k != 0)
        def _():
            self.copy(k).start()

        return unused

    def wait(self):
        self.own().wait()
        remote(self.bulk, self.bulk, self.send, self.recv, self.place.core).wait()


def attention_masks(seg_all, seg_row, seg_col, n, tok):
    def one(i, unused):
        piece = seg_all[i]
        seg_row[:, aligned(i, tok)] = piece
        seg_col[aligned(i, tok), :] = jnp.transpose(jnp.broadcast_to(piece, (tok, tok)))
        return unused

    lax.fori_loop(0, n, one, 0)


def readable(seg_col, seg_row, key_block, query_block, block):
    key_seg = seg_col[aligned(key_block, block), :]
    key_seg = jnp.concatenate([key_seg] * (block // LANE), axis=1)
    query_seg = seg_row[:, aligned(query_block, block)]
    key_pos = key_block * block + lax.broadcasted_iota(jnp.int32, (block, block), 0)
    query_pos = query_block * block + lax.broadcasted_iota(jnp.int32, (block, block), 1)
    return (key_seg == query_seg) & (key_pos <= query_pos)


def split_rows(whole, split, n):
    blk = whole.shape[1] * 2 // n
    for zy in range(n // 2):
        z, y = divmod(zy, 2)
        split[y, :, z * blk : (z + 1) * blk] = whole[:, zy * blk : (zy + 1) * blk]


class Plane:
    def __init__(self, place, split, left, send, recv, local, tokens):
        self.place, self.tokens, self.left = place, tokens, left
        to = left.at[aligned(place.p, tokens), :]
        self.own = pltpu.make_async_copy(split.at[place.y], to, local)
        self.to_core = remote(split.at[place.y], to, send.at[0], recv.at[0], place.core)
        self.to_side = remote(split.at[1 - place.y], to, send.at[1], recv.at[1], place.side)
        passed = left.at[aligned(place.side_p, tokens), :]
        self.on = remote(passed, passed, send.at[2], recv.at[2], place.core)

    def start(self):
        self.to_side.start()
        self.own.start()
        self.to_core.start()

    def forward(self):
        self.to_side.wait()
        self.on.start()

    def gone(self):
        self.own.wait()
        self.to_core.wait_send()

    def finish(self):
        self.to_core.wait_recv()
        self.on.wait()


def vm(shape, dtype):
    return jax.ShapeDtypeStruct(shape, dtype)


class Gather:
    def __init__(self, place, whole, stride, first, land, send, recv, local, tokens):
        cols = land.shape[1]
        to = land.at[aligned(place.p, tokens), :]

        def half(c):
            return whole.at[:, pl.ds(pl.multiple_of(c * stride + first, LANE), cols)]

        c = place.c
        self.own = pltpu.make_async_copy(half(c), to, local)
        self.away = [
            remote(half(c), to, send.at[0], recv.at[0], place.side),
            remote(half(1 - c), to, send.at[1], recv.at[1], place.cross),
            remote(half(1 - c), to, send.at[2], recv.at[2], place.core),
        ]

    def start(self):
        self.own.start()
        for copy in self.away:
            copy.start()

    def wait(self):
        self.own.wait()
        for copy in self.away:
            copy.wait()


class Line:
    def __init__(self, place, nz, blk, gather, land, left, lv, mv, move, got, total, out, turned, sems, work):
        self.place, self.nz, self.blk, self.gather = place, nz, blk, gather
        self.land, self.left, self.move, self.got, self.total, self.out = land, left, move, got, total, out
        self.turned = turned
        self.cols = land.shape[1]
        self.lv, self.mv = lv, mv
        self.acc, self.stage, self.load_sem = work
        self.send, self.recv, self.end_s, self.end_r, self.end_l = sems
        self.at_end = (place.z == 0) | (place.z == nz - 1)

    def load(self, left_too=False, gathered=False):
        if not gathered:
            self.gather.wait()
        copies = []
        if self.land is not self.mv:
            copies.append(pltpu.make_async_copy(self.land, self.mv, self.load_sem.at[0]))
        if left_too and self.left is not self.lv:
            copies.append(pltpu.make_async_copy(self.left, self.lv, self.load_sem.at[1]))
        for copy in copies:
            copy.start()
        for copy in copies:
            copy.wait()

    def product(self, b):
        return dot_tn(self.lv[:, aligned(b, self.blk)], self.mv[...])

    def take(self, slot):
        self.arrival(slot).wait_recv()
        copy = pltpu.make_async_copy(self.got.at[slot], self.stage.at[:, : self.cols], self.load_sem.at[2])
        copy.start()
        copy.wait()
        return self.stage[:, : self.cols].astype(F32)

    def arrival(self, slot):
        return remote(self.move.at[0], self.got.at[slot], self.send.at[0], self.recv.at[slot], self.place.core)

    def route(self, j):
        z, nz = self.place.z, self.nz
        b = jnp.where(z < nz // 2, nz - 1 - j, j)
        b = jnp.where((j == nz - 2) & (z == 1), 0, b)
        b = jnp.where((j == nz - 2) & (z == nz - 2), nz - 1, b)
        b = jnp.where(j == nz - 1, z, b)
        up = b > z
        to = jnp.where(up, z + 1, z - 1)
        slot_in = jnp.where(up, b - z, nz - z + b)
        slot_out = jnp.where(up, b - to, nz - to + b)
        keep = jnp.where(up, b - 1, b)
        last = jnp.where(up, z == 0, z == nz - 1)
        device = (to * PLANE + self.place.p, self.place.t)

        def out():
            return remote(self.move.at[keep], self.got.at[slot_out], self.send.at[keep], self.recv.at[slot_out], device)

        return b, slot_in, keep, last, out

    def step(self, j):
        b, slot_in, keep, last, out = self.route(j)
        self.acc[:, : self.cols] = self.product(b)
        sends = j < self.nz - 1

        @pl.when(jnp.logical_not(sends))
        def _():
            self.total[...] = self.acc[:, : self.cols]

        @pl.when(sends & last)
        def _():
            self.move[keep] = self.acc[:, : self.cols].astype(BF)

        @pl.when(sends & jnp.logical_not(last))
        def _():
            self.move[keep] = (self.acc[:, : self.cols] + self.take(slot_in)).astype(BF)

        @pl.when(sends)
        def _():
            out().start()

    def steps(self, low, high):
        def one(j, unused):
            self.step(j)
            return unused

        lax.fori_loop(low, high, one, 0)

    def some(self, *order):
        def one(i, unused):
            j = order[0]
            for k, then in enumerate(order):
                j = jnp.where(i == k, then, j)
            self.step(j)
            return unused

        lax.fori_loop(0, len(order), one, 0)

    def begin(self):
        self.steps(0, self.nz)

    def from_end(self):
        self.steps(jnp.where(self.at_end, 0, self.nz - 1), self.nz)

    def between(self, low, high):
        pl.when(jnp.logical_not(self.at_end))(lambda: self.steps(low, high))

    def sent(self):
        def one(j, unused):
            self.route(j)[4]().wait_send()
            return unused

        lax.fori_loop(0, self.nz - 1, one, 0)

    def end(self, c):
        half = self.blk // 2
        mine = self.place.c
        if self.turned is None:
            return self.out.at[:, aligned(mine, self.cols)], self.total.at[aligned(c, half), :]
        turned, stride, first = self.turned
        to = self.out.at[pl.ds(pl.multiple_of(mine * stride + first, LANE), self.cols), :]
        return to, turned.at[first : first + self.cols, aligned(c, half)]

    def away(self):
        to, theirs = self.end(1 - self.place.c)
        return remote(theirs, to, self.end_s, self.end_r, self.place.core)

    def here(self):
        to, mine = self.end(self.place.c)
        return pltpu.make_async_copy(mine, to, self.end_l)

    def finish(self):
        z, nz = self.place.z, self.nz

        @pl.when(z > 0)
        def _():
            self.total[...] += self.take(0)

        @pl.when(z < nz - 1)
        def _():
            self.total[...] += self.take(nz)

        if self.turned is not None:
            turned, _, first = self.turned
            turned[first : first + self.cols, :] = jnp.transpose(self.total[...])
        self.away().start()
        self.here().start()

    def left_here(self):
        self.away().wait_send()
        self.here().wait()

    def arrived(self):
        self.away().wait_recv()


class Weights:
    def __init__(self, weights, buffers, sems, tail_sems, phase, first, cols, ff):
        self.weights, self.buffers, self.sems, self.tail_sems, self.phase = weights, buffers, sems, tail_sems, phase
        self.first, self.each = first, len(weights)
        self.size = buffers.shape[1]
        self.cols = cols
        self.regular = 2 * (cols // self.size)
        self.rest = cols % self.size
        self.rest_two = ff - cols - cols // self.size * self.size

    def slot(self, i, w):
        return self.first + lax.rem(i + self.phase, 2) * self.each + w

    def copies(self, i):
        at = pl.ds(pl.multiple_of(lax.rem(i, 2) * self.cols + i // 2 * self.size, LANE), self.size)
        return [
            pltpu.make_async_copy(ref.at[at, :], self.buffers.at[self.slot(i, w)], self.sems.at[lax.rem(i, 2), w])
            for w, ref in enumerate(self.weights)
        ]

    def tail(self):
        first = self.cols // self.size * self.size
        copies = []
        for w, ref in enumerate(self.weights):
            to = self.buffers.at[self.slot(self.regular, w)]
            copies += [
                pltpu.make_async_copy(ref.at[pl.ds(first, self.rest), :], to.at[pl.ds(0, self.rest), :], self.tail_sems.at[0, w]),
                pltpu.make_async_copy(
                    ref.at[pl.ds(self.cols + first, self.rest_two), :],
                    to.at[pl.ds(self.rest, self.rest_two), :],
                    self.tail_sems.at[1, w],
                ),
            ]
        return copies

    def begin(self, blocks=1):
        self.begun = blocks
        for i in range(blocks):
            for copy in self.copies(i):
                copy.start()

    def run(self, work, after=()):
        first = self.cols // self.size * self.size
        filled = self.rest + self.rest_two

        def one(i, unused):
            is_tail = i == self.regular

            @pl.when((i + 1 < self.regular) & (i + 1 >= self.begun))
            def _():
                for copy in self.copies(i + 1):
                    copy.start()

            @pl.when(i + 1 == self.regular)
            def _():
                for copy in self.tail():
                    copy.start()

            @pl.when(jnp.logical_not(is_tail))
            def _():
                for copy in self.copies(i):
                    copy.wait()

            @pl.when(is_tail)
            def _():
                for copy in self.tail():
                    copy.wait()
                for w in range(self.each):
                    slot = self.slot(self.regular, w)
                    self.buffers[slot, filled:, :] = jnp.zeros((self.size - filled, self.buffers.shape[2]), BF)

            at = lax.rem(i, 2) * self.cols + i // 2 * self.size
            columns = [
                pl.ds(pl.multiple_of(jnp.where(is_tail, tail_at, at + k * LANE), LANE), LANE)
                for k, tail_at in enumerate((first, self.cols + first))
            ]
            work([self.slot(i, w) for w in range(self.each)], columns)
            for at_block, things in after:
                pl.when(i == at_block)(lambda things=things: [thing() for thing in things] and None)
            return unused

        lax.fori_loop(0, self.regular + 1, one, 0)


class Units:
    def __init__(self, place, nz, heads, tok):
        self.place, self.nz, self.heads, self.tok = place, nz, heads, tok
        z, s = place.z, place.s
        self.at_end = (z == 0) | (z == nz - 1)
        self.second = jnp.where(z < nz // 2, s - PLANE, s + PLANE)
        self.near = (jnp.where(z == 0, s + PLANE, s - PLANE), place.t)

    def host(self, u):
        z = u // PLANE
        inner = jnp.clip(z, 1, self.nz - 2)
        return inner * PLANE + lax.rem(u, PLANE), jnp.where(inner == z, 0, 1)

    def unit(self, slot):
        return jnp.where(slot == 0, self.place.s, self.second)

    def home(self, ref, u):
        return ref.at[aligned(u // self.heads, self.tok), aligned(lax.rem(u, self.heads), HEAD_DIM)]


class ToUnits:
    def __init__(self, units, src, land, send, recv, local):
        self.units, self.src, self.land, self.send, self.recv, self.local = units, src, land, send, recv, local
        self.n, self.s, self.t, self.tok = units.place.n, units.place.s, units.place.t, units.tok

    def away(self, u):
        host, slot = self.units.host(u)
        to = self.land.at[slot, aligned(self.s, self.tok), :]
        return remote(self.units.home(self.src, u), to, self.send, self.recv.at[slot], (host, self.t))

    def here(self, u):
        slot = self.units.host(u)[1]
        to = self.land.at[slot, aligned(self.s, self.tok), :]
        return pltpu.make_async_copy(self.units.home(self.src, u), to, self.local.at[slot])

    def start(self, u, unused):
        host = self.units.host(u)[0]
        pl.when(host == self.s)(lambda: self.here(u).start())
        pl.when(host != self.s)(lambda: self.away(u).start())
        return unused

    def bulk(self, copies, recv):
        some = self.land.at[0, pl.ds(0, copies * self.tok), :]
        return remote(some, some, self.send, recv, self.units.place.core)

    def wait(self, slot):
        self.here(self.units.unit(slot)).wait()
        self.bulk(self.n - 1, self.recv.at[slot]).wait_recv()

    def sent(self):
        pl.when(self.units.at_end)(lambda: self.bulk(self.n, self.recv.at[0]).wait_send())
        pl.when(jnp.logical_not(self.units.at_end))(lambda: self.bulk(self.n - 2, self.recv.at[0]).wait_send())


class FromUnits:
    def __init__(self, units, src, whole, send, recv, local):
        self.units, self.src, self.whole, self.send, self.recv, self.local = units, src, whole, send, recv, local
        self.n, self.s, self.t, self.tok = units.place.n, units.place.s, units.place.t, units.tok

    def away(self, slot, d):
        u = self.units.unit(slot)
        src = self.src.at[slot, aligned(d, self.tok), :]
        return remote(src, self.units.home(self.whole, u), self.send.at[slot], self.recv, (d, self.t))

    def here(self, slot):
        src = self.src.at[slot, aligned(self.s, self.tok), :]
        return pltpu.make_async_copy(src, self.units.home(self.whole, self.units.unit(slot)), self.local.at[slot])

    def start(self, slot, low, high):
        def one(d, unused):
            pl.when(d == self.s)(lambda: self.here(slot).start())
            pl.when(d != self.s)(lambda: self.away(slot, d).start())
            return unused

        lax.fori_loop(low, high, one, 0)

    def bulk(self, copies, slot):
        some = self.src.at[0, pl.ds(0, copies * self.tok), :]
        return remote(some, some, self.send.at[slot], self.recv, self.units.place.core)

    def wait(self):
        pl.when(self.units.at_end)(lambda: self.bulk(self.n, 0).wait_recv())

        @pl.when(jnp.logical_not(self.units.at_end))
        def _():
            for slot in range(2):
                self.here(slot).wait()
            self.bulk(self.n - 2, 0).wait_recv()

    def sent(self, slot):
        self.bulk(self.n - 1, slot).wait_send()


def layer_kernel(
    geo, sizes, names,
    x_in, cot_in, key_in, value_in, seg_in, wg_in, wu_in, wd_in, wo_in, wq_in, gain_one, gain_two, *refs,
):
    n, rows, tok, width, half, heads, length = geo
    ff, cols, cuts = sizes
    r = types.SimpleNamespace(**dict(zip(names, refs, strict=True)))
    tokens = rows * tok
    blk = 2 * width // n
    nz = n // PLANE
    place = Place(n)
    s, t, z = place.s, place.t, place.z
    row_s, head_s = s // heads, lax.rem(s, heads)
    mine = aligned(t, half)
    chunk = tokens // 4
    fine = 32
    wbuf = r.wbuf
    size = wbuf.shape[1]
    mid, x_all, cot_all, two_norm, two_own, two_in, one_in = (
        r.mid, r.x_all, r.cot_all, r.two_norm, r.two_own, r.two_in, r.one_in
    )
    mixed, err, one, attended, dq = r.mixed, r.err, r.one, r.attended, r.dq
    d_att = attended
    hidden, d_gate, d_up, sums = r.hidden, r.d_gate, r.d_up, r.sums
    uq, uk, uv, uo, lse, k_t = (ref.at[0] for ref in (r.uqs, r.uks, r.uvs, r.uos, r.lses, r.k_ts))
    delta = r.delta
    seg_all, seg_row, seg_col = r.seg_all, r.seg_row, r.seg_col
    udq, udk, udv = r.udq, r.udk, r.udv
    tp_s, tp_r, a_s, a_r, loc = r.tp_s, r.tp_r, r.a_s, r.a_r, r.loc
    units = Units(place, nz, heads, tok)
    at_end = units.at_end
    place.enter()

    to_x = remote(x_in, x_all.at[:, mine], tp_s.at[0], tp_r.at[0], place.twin)
    to_x.start()
    own_x = pltpu.make_async_copy(x_in, x_all.at[:, mine], loc.at[0])
    own_x.start()

    def piece(ref):
        return lambda d: ref.at[aligned(d // heads, tok), aligned(lax.rem(d, heads), HEAD_DIM)]

    keys = Spread(place, piece(key_in), lambda: uk.at[aligned(s, tok), :], a_s.at[0], a_r.at[0], loc.at[2], uk.at[: length - tok, :])
    vals = Spread(place, piece(value_in), lambda: uv.at[aligned(s, tok), :], a_s.at[1], a_r.at[1], loc.at[3], uv.at[: length - tok, :])
    segs = Spread(place, lambda d: seg_in.at[d // heads], lambda: seg_all.at[s], a_s.at[2], a_r.at[2], loc.at[4], seg_all.at[: n - 1])
    qrys = Spread(place, piece(dq), lambda: uq.at[aligned(s, tok), :], a_s.at[3], a_r.at[3], loc.at[5], uq.at[: length - tok, :])
    segs.start()
    keys.start()
    vals.start()
    to_cot = remote(cot_in, cot_all.at[:, mine], tp_s.at[1], tp_r.at[1], place.twin)
    to_cot.start()
    own_cot = pltpu.make_async_copy(cot_in, cot_all.at[:, mine], loc.at[6])
    own_cot.start()

    def square_copies(k, ref, sems):
        copies = []
        for zy in range(n // 2):
            to = wbuf.at[4 * k + zy // 2, :, (zy % 2) * half : (zy % 2 + 1) * half]
            copies.append(pltpu.make_async_copy(ref.at[zy * blk : (zy + 1) * blk, :], to, sems.at[zy]))
        return copies

    def square_block(k, zy):
        return wbuf[4 * k + zy // 2, :, (zy % 2) * half : (zy % 2 + 1) * half]

    def split_block(ref, at, zy):
        zz, yy = divmod(zy, 2)
        return ref[yy, at, zz * blk : (zz + 1) * blk]

    def store_split(ref, at, now):
        for zy in range(n // 2):
            zz, yy = divmod(zy, 2)
            ref[yy, at, zz * blk : (zz + 1) * blk] = now[:, zy * blk : (zy + 1) * blk]

    load_wq = square_copies(1, wq_in, r.o_sem.at[0])
    load_wo = square_copies(0, wo_in, r.o_sem.at[1])
    for copy in load_wq + load_wo:
        copy.start()
    own_x.wait()
    to_x.wait()

    def first_norm(i, unused):
        at = aligned(i, fine)
        x = x_all[at, :].astype(F32)
        root = lax.rsqrt(jnp.mean(x * x, axis=-1, keepdims=True) + EPSILON)
        store_split(one, at, (x * root * gain_one[...]).astype(BF))
        return unused

    lax.fori_loop(0, tokens // fine, first_norm, 0)
    for copy in load_wq:
        copy.wait()
    every = slice(0, tokens)
    total = jnp.zeros((tokens, half), F32)
    for zy in range(n // 2):
        total += dot_nn(split_block(one, every, zy), square_block(1, zy))
    dq[...] = (total * HEAD_DIM ** (-0.5)).astype(BF)
    qrys.start()
    lv_one, lv_two = r.lv_one, r.lv_two
    left_cot, left_two, left_err, left_one = (
        Plane(place, split, land, r.le_s.at[i], r.le_r.at[i], r.l_loc.at[i], tokens)
        for i, (split, land) in enumerate(((err, lv_one), (mixed, lv_two), (err, r.l_err), (one, r.l_one)))
    )
    left_one.start()

    segs.wait()
    attention_masks(seg_all, seg_row, seg_col, n, tok)
    keys.wait()
    vals.wait()

    def turn_into(ref, to):
        def turn(i, unused):
            at = aligned(i, tok)
            to[:, at] = jnp.transpose(ref[at, :].astype(F32)).astype(BF)
            return unused

        lax.fori_loop(0, n, turn, 0)

    turn_into(uv, k_t)
    qrys.wait()
    block = 512
    owners = block // tok
    back = Spread(
        place,
        lambda d: uo.at[aligned(d, tok), :],
        lambda: attended.at[aligned(row_s, tok), aligned(head_s, HEAD_DIM)],
        a_s.at[4], a_r.at[4], loc.at[8], uo.at[: length - tok, :],
    )

    def query_step(qi, unused):
        query_block = uq[aligned(qi, block), :]

        def key_step(j, carry):
            top, total, acc = carry
            kj = qi - j
            scores = dot_nt(uk[aligned(kj, block), :], query_block)
            scores = jnp.where(readable(seg_col, seg_row, kj, qi, block), scores, NEGATIVE_FILL)
            new_top = jnp.maximum(top, jnp.max(scores, axis=0, keepdims=True))
            weights = jnp.exp(scores - new_top)
            decay = jnp.exp(top - new_top)
            total = total * decay + jnp.sum(weights, axis=0, keepdims=True)
            acc = acc * decay + dot_nn(k_t[:, aligned(kj, block)], weights.astype(BF))
            return new_top, total, acc

        start = (
            jnp.full((1, block), NEGATIVE_FILL, F32),
            jnp.zeros((1, block), F32),
            jnp.zeros((HEAD_DIM, block), F32),
        )
        top, total, acc = lax.fori_loop(0, qi + 1, key_step, start)
        lse[:, aligned(qi, block)] = top + jnp.log(total)
        uo[aligned(qi, block), :] = jnp.transpose(acc / total).astype(BF)
        return lax.fori_loop(qi * owners, (qi + 1) * owners, back.start_to, unused)

    lax.fori_loop(0, length // block, query_step, 0)

    work = (r.acc, r.stage, r.work_sem)
    mv, turned = r.mv, r.turned
    s_first, s_second, t_first, t_second = r.s_first, r.s_second, r.t_first, r.t_second
    sources = (hidden, d_gate, d_up)
    lefts_of = ((lv_one, lv_one), (lv_two, lv_two), (lv_two, lv_two))
    kept = ((s_first, t_first, r.out_down), (s_second, t_second, r.out_gate), (s_first, t_first, r.out_up))
    gots = (r.g0, r.g1, r.g2, r.g3, r.g4, r.g5, r.g6)
    lands = (None, None, None, r.m3, r.m4, r.m5, r.m6)
    plans = []
    for i, (kind, first, wide) in enumerate(cuts):
        at = pl.ds(first, wide)
        left, lv = lefts_of[kind]
        move, total_ref, out_ref = kept[kind]
        here = mv.at[:, at]
        plans.append((
            (sources[kind], cols, first), here if lands[i] is None else lands[i], left, lv, here, move.at[:, :, at], gots[i], total_ref.at[:, at],
            out_ref, (turned, cols, first),
        ))
    for source, left, lv, *rest in (
        (attended, r.l_err, lv_one, r.mv_out, r.s_out, r.g_out, r.t_out, r.out_out),
        (dq, r.l_one, lv_two, r.mv_query, r.s_query, r.g_query, r.t_query, r.out_query),
    ):
        plans.append(((source, half // 2, 0), rest[0], left, lv, *rest, None))
    lines = []
    for i, (source, land, *rest) in enumerate(plans):
        gather = Gather(place, *source, land, r.me_s.at[i], r.me_r.at[i], r.g_loc.at[i], tokens)
        sems = (r.c_s.at[i], r.c_r.at[i], r.e_s.at[i], r.e_r.at[i], r.e_l.at[i])
        lines.append(Line(place, nz, blk, gather, land, *rest, sems, work))
    down_a, down_b, down_c, gate_a, gate_b, up_a, up_b, out, query = lines
    ship = [
        remote(a.at[0], a.at[1], r.sh_s.at[i], r.sh_r.at[i], units.near)
        for i, a in enumerate((r.uqs, r.uks, r.uvs, r.uos, r.lses))
    ]

    @pl.when(at_end)
    def _():
        for copy in ship:
            copy.start()

    own_cot.wait()
    to_cot.wait()

    def split_cot(i, unused):
        at = aligned(i, fine)
        store_split(err, at, cot_all[at, :])
        return unused

    lax.fori_loop(0, tokens // fine, split_cot, 0)
    left_cot.start()
    left_one.forward()
    for copy in load_wo:
        copy.wait()
    back.wait()

    chunks = 4
    wide = width // chunks

    def to_twin(i):
        at = slice(i * wide, (i + 1) * wide)
        return remote(two_own.at[:, at], one_in.at[:, at], tp_s.at[9 + i], tp_r.at[9 + i], place.twin)

    for i in range(chunks):
        for zy in range(2 * i, 2 * i + 2):
            two_own[:, zy * blk : (zy + 1) * blk] = dot_nt(attended[...], square_block(0, zy)).astype(BF)
        to_twin(i).start()
    out.gather.start()
    zeroth_pass = Weights((wd_in,), wbuf, r.w_sem.at[3], r.tail_sem.at[3], 0, 4, cols, ff)
    first_pass = Weights((wg_in, wu_in), wbuf, r.w_sem.at[0], r.tail_sem.at[0], 0, 0, cols, ff)
    second_pass = Weights((wg_in, wu_in), wbuf, r.w_sem.at[1], r.tail_sem.at[1], 0, 4, cols, ff)
    third_pass = Weights((wd_in,), wbuf, r.w_sem.at[2], r.tail_sem.at[2], 0, 4, cols, ff)
    zeroth_pass.begin(2)
    first_pass.begin(2)

    def to_hidden(slots, at):
        now = dot_nt(cot_all[...], wbuf[slots[0]]).astype(BF)
        for k in range(2):
            d_gate[:, at[k]] = now[:, k * LANE : (k + 1) * LANE]

    zeroth_pass.run(to_hidden)
    left_cot.forward()
    square = jnp.zeros((tokens, 1), F32)
    for i in range(chunks):
        to_twin(i).wait()
        at = slice(i * wide, (i + 1) * wide)
        now = x_all[:, at].astype(F32) + (two_own[:, at].astype(F32) + one_in[:, at].astype(F32))
        mid[:, at] = now
        square += jnp.sum(now * now, axis=-1, keepdims=True)
    root_two = lax.rsqrt(square * (1.0 / width) + EPSILON)
    for i in range(chunks):
        at = slice(i * wide, (i + 1) * wide)
        two_norm[:, at] = (mid[:, at] * root_two * gain_two[:, at]).astype(BF)

    def units_block(slots, at):
        x = two_norm[...]
        gate_now, up_now = (dot_nt(x, wbuf[slot]) for slot in slots)
        d_hid = jnp.concatenate([d_gate[:, at[0]], d_gate[:, at[1]]], axis=1).astype(F32)
        sigma = jax.nn.sigmoid(gate_now)
        act = gate_now * sigma
        for ref, now in (
            (hidden, act * up_now),
            (d_gate, d_hid * up_now * sigma * (1.0 + gate_now * (1.0 - sigma))),
            (d_up, d_hid * act),
        ):
            now = now.astype(BF)
            for k in range(2):
                ref[:, at[k]] = now[:, k * LANE : (k + 1) * LANE]

    done_a, done_b = (2 * ((first + wide) // size) for _, first, wide in cuts[:2])

    def split_two(i, unused):
        at = aligned(i, fine)
        store_split(mixed, at, two_norm[at, :])
        return unused

    def begin_down():
        down_a.gather.start()
        lax.fori_loop(0, tokens // fine, split_two, 0)

    def go_on_down():
        down_b.gather.start()
        left_cot.gone()
        left_cot.finish()
        down_a.load()
        down_a.from_end()

    first_pass.run(
        units_block,
        ((done_a - 1, [begin_down]), (done_b - 1, [go_on_down]), (first_pass.regular - 1, [second_pass.begin])),
    )
    down_c.gather.start()
    left_two.start()
    down_b.load()
    down_b.from_end()
    down_a.between(0, 2)

    def block_of(ref, at):
        return jnp.concatenate([ref[:, at[0]], ref[:, at[1]]], axis=1)

    def add_up(pairs):
        for db in range(width // size):
            at = slice(db * size, (db + 1) * size)
            sums[db * tokens : (db + 1) * tokens, :] += sum(dot_nn(a, wbuf[slot, :, at]) for a, slot in pairs)

    def back_units(slots, at):
        add_up([(block_of(d_gate, at), slots[0]), (block_of(d_up, at), slots[1])])

    sums[...] = jnp.zeros_like(sums)
    second_pass.run(back_units)
    for db in range(width // size):
        two_own[:, db * size : (db + 1) * size] = sums[db * tokens : (db + 1) * tokens, :].astype(BF)

    def two_copy(i):
        at = aligned(i, chunk)
        return remote(two_own.at[at, :], two_in.at[at, :], tp_s.at[2 + i], tp_r.at[2 + i], place.twin)

    for i in range(4):
        two_copy(i).start()
    load_wo = square_copies(0, wo_in, r.o_sem.at[2])
    for copy in load_wo:
        copy.start()
    gate_a.gather.start()
    down_a.between(2, 3)
    down_b.between(0, 2)
    down_c.load()
    down_c.from_end()

    third_pass.begin()
    sums[...] = jnp.zeros_like(sums)

    def out_units(slots, at):
        add_up([(block_of(hidden, at), slots[0])])

    third_pass.run(out_units)
    left_two.forward()
    left_two.gone()
    for db in range(width // size):
        per = half // size
        mixed[db // per, :, (db % per) * size : (db % per + 1) * size] = sums[db * tokens : (db + 1) * tokens, :].astype(BF)
    ffn_copy = remote(mixed.at[1 - t], r.ffn_in, tp_s.at[6], tp_r.at[6], place.twin)
    ffn_copy.start()
    per = half // size
    for i in range(per):
        at = t * per + i
        sums[aligned(at, tokens), :] += mid[:, aligned(at, size)]
    hold = pltpu.make_async_copy(sums.at[aligned(t, per * tokens), :], r.mix, loc.at[11])
    hold.start()
    load_wq = square_copies(1, wq_in, r.o_sem.at[3])
    for copy in load_wq:
        copy.start()
    down_b.between(2, 3)
    down_c.between(0, 2)
    hold.wait()

    to_units = ToUnits(units, d_att, r.udo, r.u_s.at[0], r.u_r, r.u_l)
    out.gather.wait()
    for copy in load_wo:
        copy.wait()

    def second_norm(i, gain_sum):
        two_copy(i).wait()

        def some(j, gain_sum):
            at = aligned(i * (chunk // fine) + j, fine)
            m = mid[at, :]
            d2 = two_own[at, :].astype(F32) + two_in[at, :].astype(F32)
            root = lax.rsqrt(jnp.mean(m * m, axis=-1, keepdims=True) + EPSILON)
            gained = d2 * gain_two[...]
            scaled = m * root
            gain_sum = gain_sum + jnp.sum(d2 * scaled, axis=0, keepdims=True)
            slope = jnp.mean(gained * scaled, axis=-1, keepdims=True)
            dm = cot_all[at, :].astype(F32) + root * (gained - scaled * slope)
            mid[at, :] = dm
            store_split(err, at, dm.astype(BF))
            return gain_sum

        gain_sum = lax.fori_loop(0, chunk // fine, some, gain_sum)
        at = aligned(i, chunk)
        total = jnp.zeros((chunk, half), F32)
        for zy in range(n // 2):
            total += dot_nn(split_block(err, at, zy), square_block(0, zy))
        d_att[at, :] = total.astype(BF)
        return gain_sum

    gain_sum = jnp.zeros((1, width), F32)
    per_row = tok // chunk
    for row in range(rows):
        gain_sum = lax.fori_loop(row * per_row, (row + 1) * per_row, second_norm, gain_sum)
        lax.fori_loop(row * heads, (row + 1) * heads, to_units.start, 0)
    gain_part, gain_in = r.gain_part, r.gain_in
    for i in range(n):
        gain_part[0, i] = gain_sum[:, i * (width // n) : (i + 1) * (width // n)]
    spread_gain = [
        Spread(place, lambda d, g=g: gain_part.at[g, d], lambda g=g: gain_in.at[g, s], a_s.at[5 + g], a_r.at[5 + g], loc.at[9 + g],
               gain_in.at[g, : n - 1])
        for g in range(2)
    ]
    spread_gain[0].start()
    gate_b.gather.start()
    down_c.between(2, 3)
    left_two.finish()
    gate_a.load()
    gate_a.from_end()

    back_dq, back_dk, back_dv = (
        FromUnits(units, src, whole, r.f_s.at[i], r.f_r.at[i], r.f_l.at[i])
        for i, (src, whole) in enumerate(((udq, dq), (udk, r.d_keys), (udv, r.d_values)))
    )

    def one_unit(slot, unused):
        unit_q, unit_k, unit_v, unit_o, unit_lse, unit_kt = (
            ref.at[slot] for ref in (r.uqs, r.uks, r.uvs, r.uos, r.lses, r.k_ts)
        )
        unit_do = r.udo.at[slot]
        sums[...] = jnp.zeros_like(sums)
        to_units.wait(slot)

        def turn_delta(i, unused):
            at = aligned(i, tok)
            both = unit_do[at, :].astype(F32) * unit_o[at, :].astype(F32)
            delta[:, at] = jnp.sum(jnp.transpose(both), axis=0, keepdims=True)
            return unused

        lax.fori_loop(0, n, turn_delta, 0)

        def query_step(i, unused_too):
            qi = length // block - 1 - i
            qat = aligned(qi, block)
            qb, dob = unit_q[qat, :], unit_do[qat, :]

            def key_step(kj, dq_t):
                kat = aligned(kj, block)
                scores = dot_nt(unit_k[kat, :], qb) - unit_lse[:, qat]
                probs = jnp.exp(jnp.where(readable(seg_col, seg_row, kj, qi, block), scores, NEGATIVE_FILL))
                d_probs = dot_nt(unit_v[kat, :], dob)
                d_scores = (probs * (d_probs - delta[:, qat])).astype(BF)
                sums[kat, :HEAD_DIM] += dot_nn(d_scores, qb)
                sums[kat, HEAD_DIM:] += dot_nn(probs.astype(BF), dob)
                return dq_t + dot_nn(unit_kt[:, kat], d_scores)

            dq_t = lax.fori_loop(0, qi + 1, key_step, jnp.zeros((HEAD_DIM, block), F32))
            udq[slot, qat, :] = jnp.transpose(dq_t).astype(BF)
            back_dq.start(slot, qi * owners, (qi + 1) * owners)
            udk[slot, qat, :] = sums[qat, :HEAD_DIM].astype(BF)
            udv[slot, qat, :] = sums[qat, HEAD_DIM:].astype(BF)

            @pl.when((slot == 0) & (i == 0))
            def _():
                gate_a.step(1)

            @pl.when((slot == 1) & (i == 0))
            def _():
                gate_a.step(2)
                gate_b.load()
                gate_b.some(nz - 1, 0)

            @pl.when((slot == 1) & (i == 1))
            def _():
                gate_b.step(1)

            return unused_too

        lax.fori_loop(0, length // block, query_step, 0)

        @pl.when(slot == 0)
        def _():
            back_dk.start(0, 0, n)
            back_dv.start(0, 0, n)

        return unused

    def one_copy(i):
        at = aligned(i, chunk)
        return remote(two_own.at[at, :], one_in.at[at, :], tp_s.at[13 + i], tp_r.at[13 + i], place.twin)

    def through_query():
        for copy in load_wq:
            copy.wait()
        back_dq.wait()
        query.gather.start()

        def back_query(i, unused):
            at = aligned(i, chunk)
            for zy in range(n // 2):
                now = dot_nt(dq[at, :], square_block(1, zy)) * HEAD_DIM ** (-0.5)
                two_own[at, zy * blk : (zy + 1) * blk] = now.astype(BF)
            one_copy(i).start()
            return unused

        lax.fori_loop(0, 4, back_query, 0)

    def last_norm(i, gain_sum):
        one_copy(i).wait()

        def some(j, gain_sum):
            at = aligned(i * (chunk // fine) + j, fine)
            x = x_all[at, :].astype(F32)
            d1 = two_own[at, :].astype(F32) + one_in[at, :].astype(F32)
            root = lax.rsqrt(jnp.mean(x * x, axis=-1, keepdims=True) + EPSILON)
            gained = d1 * gain_one[...]
            scaled = x * root
            gain_sum = gain_sum + jnp.sum(d1 * scaled, axis=0, keepdims=True)
            slope = jnp.mean(gained * scaled, axis=-1, keepdims=True)
            mid[at, :] = mid[at, :] + root * (gained - scaled * slope)
            return gain_sum

        return lax.fori_loop(0, chunk // fine, some, gain_sum)

    give = pltpu.make_async_copy(mid.at[:, mine], r.input_grad, loc.at[19])

    def through_first_norm():
        gain_sum = lax.fori_loop(0, 4, last_norm, jnp.zeros((1, width), F32))
        for i in range(n):
            gain_part[1, i] = gain_sum[:, i * (width // n) : (i + 1) * (width // n)]
        spread_gain[1].start()
        give.start()

    def finish_all(*some):
        for line in some:
            line.finish()

    def left_all(*some):
        for line in some:
            line.left_here()

    def sent_all(*some):
        for line in some:
            line.sent()

    def err_here():
        left_err.forward()
        left_err.gone()
        left_err.finish()

    def one_here():
        left_one.gone()
        left_one.finish()

    up_a.gather.start()
    up_b.gather.start()
    left_err.start()

    with jax.named_scope("between"):
        @pl.when(jnp.logical_not(at_end))
        def _():
            for copy in ship:
                copy.wait_recv()
            for slot in range(2):
                turn_into(r.uks.at[slot], r.k_ts.at[slot])
            gate_a.step(0)
            lax.fori_loop(0, 2, one_unit, 0)
            finish_all(down_a, down_b)
            sent_all(down_a, down_b, down_c)
            up_a.load()
            up_a.some(nz - 1, 0)
            gate_b.step(2)
            finish_all(down_c)
            up_a.step(1)
            up_b.load()
            back_dk.start(1, 0, n)
            up_a.step(2)
            up_b.some(nz - 1, 0)
            back_dv.start(1, 0, n)
            through_query()
            up_b.step(1)
            err_here()
            left_all(down_a, down_b)
            finish_all(gate_a)
            left_all(down_c)
            finish_all(gate_b)
            out.load(True, gathered=True)
            up_b.step(2)
            out.some(nz - 1, 0)
            one_here()
            through_first_norm()
            out.step(1)
            query.load(True)
            left_all(gate_a)
            finish_all(up_a)
            out.step(2)
            query.some(nz - 1, 0, 1)
            left_all(gate_b)
            finish_all(up_b)
            query.step(2)
            finish_all(out, query)

    with jax.named_scope("ends"):
        @pl.when(at_end)
        def _():
            gate_b.load()
            gate_b.begin()
            finish_all(down_a, down_b, down_c)
            sent_all(down_a, down_b, down_c)
            up_a.load()
            up_a.begin()
            up_b.load()
            up_b.begin()
            left_all(down_a, down_b, down_c)
            err_here()
            out.load(True, gathered=True)
            out.begin()
            through_query()
            one_here()
            query.load(True)
            query.begin()
            through_first_norm()
            finish_all(gate_a, gate_b)
            left_all(gate_a, gate_b)
            finish_all(up_a, up_b, out, query)

    ffn_copy.wait()
    to_units.sent()
    fetch = pltpu.make_async_copy(r.mix, sums.at[: per * tokens, :], loc.at[11])
    fetch.start()
    fetch.wait()
    for i in range(per):
        at = slice(i * size, (i + 1) * size)
        attended[:, at] = (sums[i * tokens : (i + 1) * tokens, :] + r.ffn_in[:, at].astype(F32)).astype(BF)
    give_mixed = pltpu.make_async_copy(attended, r.out_mixed, loc.at[20])
    give_mixed.start()
    back_dk.wait()
    back_dv.wait()
    for g in range(2):
        spread_gain[g].wait()
        r.gains[g] = jnp.sum(gain_in[g], axis=0)

    @pl.when(at_end)
    def _():
        for copy in ship:
            copy.wait_send()

    @pl.when(jnp.logical_not(at_end))
    def _():
        for slot in range(2):
            for sent in (back_dq, back_dk, back_dv):
                sent.sent(slot)

    give.wait()
    give_mixed.wait()
    for line in lines[3:]:
        line.sent()
    for line in lines[5:]:
        line.left_here()
    for line in lines:
        line.arrived()


def results_kernel(rows, factors, *refs):
    count = len(rows)
    ins, outs, held, sems = refs[:count], refs[count : 2 * count], refs[2 * count : -1], refs[-1]
    come = [pltpu.make_async_copy(ins[i].at[: rows[i]], held[2 * i], sems.at[0, i]) for i in range(count)]
    go = [pltpu.make_async_copy(held[2 * i + 1], outs[i], sems.at[1, i]) for i in range(count)]
    for copy in come:
        copy.start()
    for i, factor in enumerate(factors):
        come[i].wait()
        if factor is not None:
            held[2 * i + 1][...] = held[2 * i][...].astype(F32) * factor
        go[i].start()
    for copy in go:
        copy.wait()


def results(*some):
    anywhere = pl.BlockSpec(memory_space=pl.ANY)
    arrays, rows, factors = zip(*some)
    shapes = [vm((k, *a.shape[1:]), a.dtype if f is None else F32) for a, k, f in some]
    held = []
    for (a, k, f), shape in zip(some, shapes):
        held += [pltpu.VMEM((k, *a.shape[1:]) if f is not None else (8, LANE), a.dtype), pltpu.VMEM(shape.shape, shape.dtype)]

    def kernel(*refs):
        count = len(rows)
        refs = list(refs)
        for i, factor in enumerate(factors):
            if factor is None:
                refs[2 * count + 2 * i] = refs[2 * count + 2 * i + 1]
        results_kernel(rows, factors, *refs)

    return pl.pallas_call(
        kernel,
        out_shape=shapes,
        in_specs=[anywhere] * len(arrays),
        out_specs=[anywhere] * len(arrays),
        scratch_shapes=[*held, pltpu.SemaphoreType.DMA((2, len(arrays)))],
        compiler_params=pltpu.CompilerParams(vmem_limit_bytes=VMEM_GRANT),
        name="results",
    )(*arrays)


def fast_device(
    n, inputs, segments, keys, values, attn_gain, query_weight, out_weight, ffn_gain, gate_weight, up_weight, down_weight,
    cotangent,
):
    rows, tok, half = inputs.shape
    tokens, width, ff = rows * tok, query_weight.shape[0], gate_weight.shape[1]
    heads, length = half // HEAD_DIM, n * tok
    geo = (n, rows, tok, width, half, heads, length)
    blk, nz, size = 2 * width // n, n // PLANE, 2 * LANE
    cols = -(-ff // size) * LANE
    firsts = (0, size, 3 * size, cols)
    thirds = [(firsts[i], firsts[i + 1] - firsts[i]) for i in range(3)]
    halves = [(0, firsts[2]), (firsts[2], cols - firsts[2])]
    cuts = tuple((kind, *cut) for kind, parts in enumerate((thirds, halves, halves)) for cut in parts)
    sizes = (ff, cols, cuts)
    square = half // 2
    n_lines = len(cuts) + 2
    dma = pltpu.SemaphoreType.DMA
    anywhere, here = pl.BlockSpec(memory_space=pl.ANY), pl.BlockSpec(memory_space=pltpu.VMEM)

    def pieces(letter, shapes):
        return {letter + str(i): shape for i, shape in shapes}

    tall, flat_left = vm((2 * cols, blk // 2), F32), vm((PLANE * tokens, width // 2), BF)
    sum_square = vm((nz + 1, blk, square), BF)
    outs = dict(
        out_mixed=vm((tokens, half), BF),
        input_grad=vm((tokens, half), F32),
        d_keys=vm((tokens, half), BF),
        d_values=vm((tokens, half), BF),
        gains=vm((2, 1, width // n), F32),
        out_down=tall,
        out_gate=tall,
        out_up=tall,
        out_out=vm((blk // 2, half), F32),
        out_query=vm((blk // 2, half), F32),
        mix=vm((half // size * tokens, size), F32),
        l_err=flat_left,
        l_one=flat_left,
        g_out=sum_square,
        g_query=sum_square,
        **pieces("m", [(i, vm((PLANE * tokens, w), BF)) for i, (kind, _, w) in enumerate(cuts) if kind > 0]),
        **pieces("g", [(i, vm((nz + 1, blk, w), BF)) for i, (_, _, w) in enumerate(cuts)]),
    )
    row = pltpu.VMEM((1, length), F32)
    act, own = pltpu.VMEM((tokens, width), BF), pltpu.VMEM((tokens, half), BF)
    split = pltpu.VMEM((2, tokens, width // 2), BF)
    hid = pltpu.VMEM((tokens, 2 * cols), BF)
    gain = pltpu.VMEM((2, n, 1, width // n), F32)
    left = pltpu.VMEM((PLANE * tokens, width // 2), BF)
    two = pltpu.VMEM((2, length, HEAD_DIM), BF)
    move, move_square = (pltpu.VMEM((nz - 1, blk, c), BF) for c in (cols, square))
    total, total_square = (pltpu.VMEM((blk, c), F32) for c in (cols, square))
    taken = pltpu.VMEM((PLANE * tokens, square), BF)
    scratch = dict(
        mid=pltpu.VMEM((tokens, width), F32),
        x_all=act, cot_all=act, two_norm=act, two_own=act, two_in=act, one_in=act, mixed=split, err=split, one=split,
        wbuf=pltpu.VMEM((8, size, width), BF),
        attended=own, dq=own, ffn_in=own, hidden=hid, d_gate=hid, d_up=hid,
        sums=pltpu.VMEM((length, size), F32),
        uqs=two, uks=two, uvs=two, uos=two, udo=two, udq=two, udk=two, udv=two,
        delta=row, seg_row=row, lses=pltpu.VMEM((2, 1, length), F32),
        seg_all=pltpu.VMEM((n, 1, tok), F32),
        seg_col=pltpu.VMEM((length, LANE), F32),
        k_ts=pltpu.VMEM((2, HEAD_DIM, length), BF),
        gain_part=gain, gain_in=gain,
        s_first=move, s_second=move, s_out=move_square, s_query=move_square,
        t_first=total, t_second=total, t_out=total_square, t_query=total_square,
        turned=pltpu.VMEM((cols, blk), F32),
        mv=pltpu.VMEM((PLANE * tokens, cols), BF), mv_out=taken, mv_query=taken,
        lv_one=left, lv_two=left,
        acc=total,
        stage=pltpu.VMEM((blk, cols), BF),
        tp_s=dma((17,)), tp_r=dma((17,)), a_s=dma((7,)), a_r=dma((7,)),
        me_s=dma((n_lines, 3)), me_r=dma((n_lines, 3)), le_s=dma((4, 3)), le_r=dma((4, 3)),
        c_s=dma((n_lines, nz - 1)), c_r=dma((n_lines, nz + 1)),
        e_s=dma((n_lines,)), e_r=dma((n_lines,)), e_l=dma((n_lines,)),
        sh_s=dma((5,)), sh_r=dma((5,)), u_s=dma((1,)), u_r=dma((2,)), u_l=dma((2,)),
        f_s=dma((3, 2)), f_r=dma((3,)), f_l=dma((3, 2)),
        loc=dma((21,)), g_loc=dma((n_lines,)), l_loc=dma((4,)), work_sem=dma((3,)),
        w_sem=dma((4, 2, 2)), tail_sem=dma((4, 2, 2)), o_sem=dma((4, n // 2)),
    )
    names = (*outs, *scratch)

    def flat(a):
        return a.reshape(tokens, half)

    segf = segments.astype(F32).reshape(rows, 1, tok)
    got = pl.pallas_call(
        functools.partial(layer_kernel, geo, sizes, names),
        out_shape=list(outs.values()),
        in_specs=[anywhere] * 10 + [here] * 2,
        out_specs=[here if i == 4 else anywhere for i in range(len(outs))],
        scratch_shapes=list(scratch.values()),
        compiler_params=pltpu.CompilerParams(
            collective_id=0, has_side_effects=True, vmem_limit_bytes=VMEM_GRANT
        ),
        name="layer",
    )(
        flat(inputs), flat(cotangent), flat(keys), flat(values), segf, gate_weight.T, up_weight.T, down_weight.T,
        out_weight, query_weight, attn_gain.reshape(1, width), ffn_gain.reshape(1, width),
    )
    got = types.SimpleNamespace(**dict(zip(outs, got)))

    def shaped(a):
        return a.reshape(rows, tok, half)

    d_keys, d_values, g_query, g_down, g_gate, g_up, input_grad, mixed, g_out = results(
        (got.d_keys, tokens, 1.0),
        (got.d_values, tokens, 1.0),
        (got.out_query, blk // 2, HEAD_DIM ** (-0.5)),
        (got.out_down, ff, None),
        (got.out_gate, ff, None),
        (got.out_up, ff, None),
        (got.input_grad, tokens, None),
        (got.out_mixed, tokens, None),
        (got.out_out, blk // 2, None),
    )
    return (
        shaped(mixed),
        shaped(input_grad),
        shaped(d_keys),
        shaped(d_values),
        got.gains[1, 0],
        g_query,
        g_out,
        got.gains[0, 0],
        g_gate.T,
        g_up.T,
        g_down.T,
    )


def inverse_root(stream):
    return lax.rsqrt(jnp.mean(stream * stream, axis=-1, keepdims=True) + EPSILON)


def key_mask(doc_start, query_pos, begin, row_count):
    key_pos = begin + jnp.arange(row_count, dtype=jnp.int32)
    earlier = key_pos[None, None, :] <= query_pos[None, :, None]
    same_doc = key_pos[None, None, :] >= doc_start[:, :, None]
    return (earlier & same_doc)[:, None]


def per_device(
    inputs,
    segments,
    keys,
    values,
    attn_gain,
    query_weight,
    out_weight,
    ffn_gain,
    gate_weight,
    up_weight,
    down_weight,
    cotangent,
):
    batch_rows, local_tokens, half_width = inputs.shape
    local_heads = half_width // HEAD_DIM
    seq_devices = lax.axis_size("seq")
    row_length = local_tokens * seq_devices
    seq_index = lax.axis_index("seq")
    tp_index = lax.axis_index("tp")
    query_scale = HEAD_DIM ** (-0.5)
    bfloat = jnp.bfloat16
    single = jnp.float32
    whole = lax.all_gather(inputs, "tp", axis=2, tiled=True).astype(single)
    root_one = inverse_root(whole)
    scaled_one = whole * root_one
    normed_one = (scaled_one * attn_gain).astype(bfloat)
    query = (
        jnp.einsum("rtd,de->rte", normed_one, query_weight, preferred_element_type=single)
        * query_scale
    ).astype(bfloat)
    query_heads = query.reshape(batch_rows, local_tokens, local_heads, HEAD_DIM)
    bins = jnp.arange(CUTS + 1, dtype=jnp.int32)
    onehot = (segments[:, :, None] == bins[None, None, :]).astype(single)
    totals = lax.psum(jnp.sum(onehot, axis=1), "seq")
    ends = jnp.cumsum(totals, axis=-1)
    before = ends - totals
    doc_start = jnp.sum(onehot * before[:, None, :], axis=-1).astype(jnp.int32)
    query_pos = seq_index * local_tokens + jnp.arange(local_tokens, dtype=jnp.int32)
    first_needed = jnp.min(doc_start)
    last_needed = seq_index * local_tokens + local_tokens - 1
    start_state = (
        jnp.full((batch_rows, local_heads, local_tokens), NEGATIVE_FILL, single),
        jnp.zeros((batch_rows, local_heads, local_tokens), single),
        jnp.zeros((batch_rows, local_heads, local_tokens, HEAD_DIM), single),
    )
    key_piece = lax.all_gather(keys, "seq", axis=1, tiled=True)
    value_piece = lax.all_gather(values, "seq", axis=1, tiled=True)
    piece_rows = key_piece.shape[1]
    fold_key_block = math.gcd(piece_rows, 512)

    def fold_step(block_index, state):
        running_max, running_sum, running_out = state
        begin = block_index * fold_key_block

        def fold_work(unused):
            key_heads = lax.dynamic_slice_in_dim(
                key_piece, block_index * fold_key_block, fold_key_block, 1
            ).reshape(batch_rows, fold_key_block, local_heads, HEAD_DIM)
            value_heads = lax.dynamic_slice_in_dim(
                value_piece, block_index * fold_key_block, fold_key_block, 1
            ).reshape(batch_rows, fold_key_block, local_heads, HEAD_DIM)
            scores = jnp.einsum(
                "rqhe,rkhe->rhqk", query_heads, key_heads, preferred_element_type=single
            )
            allowed = key_mask(doc_start, query_pos, begin, fold_key_block)
            scores = jnp.where(allowed, scores, NEGATIVE_FILL)
            new_max = jnp.maximum(running_max, jnp.max(scores, axis=-1))
            weights = jnp.where(allowed, jnp.exp(scores - new_max[..., None]), 0.0)
            decay = jnp.exp(running_max - new_max)
            new_sum = running_sum * decay + jnp.sum(weights, axis=-1)
            new_out = running_out * decay[..., None] + jnp.einsum(
                "rhqk,rkhe->rhqe",
                weights.astype(bfloat),
                value_heads,
                preferred_element_type=single,
            )
            return (new_max, new_sum, new_out)

        def keep_state(unused):
            return (running_max, running_sum, running_out)

        needed = (begin <= last_needed) & (begin + fold_key_block - 1 >= first_needed)
        return lax.cond(needed, fold_work, keep_state, 0)

    running_max, running_sum, running_out = lax.fori_loop(
        0, piece_rows // fold_key_block, fold_step, start_state
    )
    log_total = running_max + jnp.log(running_sum)
    attended = running_out / running_sum[..., None]
    attended_low = (
        attended.transpose(0, 2, 1, 3).reshape(batch_rows, local_tokens, half_width).astype(bfloat)
    )
    branch = jnp.einsum("rth,dh->rtd", attended_low, out_weight, preferred_element_type=single)
    middle = whole + lax.psum(branch.astype(jnp.bfloat16), "tp").astype(jnp.float32)
    middle_share = lax.dynamic_slice_in_dim(middle, tp_index * half_width, half_width, 2)
    root_two = inverse_root(middle)
    scaled_two = middle * root_two
    normed_two = (scaled_two * ffn_gain).astype(bfloat)
    gate = jnp.einsum("rtd,df->rtf", normed_two, gate_weight, preferred_element_type=single)
    up_proj = jnp.einsum("rtd,df->rtf", normed_two, up_weight, preferred_element_type=single)
    sigma = jax.nn.sigmoid(gate)
    activated = gate * sigma
    hidden = (activated * up_proj).astype(bfloat)
    ffn_part = jnp.einsum("rtf,df->rtd", hidden, down_weight, preferred_element_type=single)
    output = (
        middle_share
        + lax.psum_scatter(
            ffn_part.astype(jnp.bfloat16), "tp", scatter_dimension=2, tiled=True
        ).astype(jnp.float32)
    ).astype(bfloat)
    grad_out = lax.all_gather(cotangent, "tp", axis=2, tiled=True)
    d_hidden = jnp.einsum("rtd,df->rtf", grad_out, down_weight, preferred_element_type=single)
    d_gate = (d_hidden * up_proj * sigma * (1.0 + gate * (1.0 - sigma))).astype(bfloat)
    d_up = (d_hidden * activated).astype(bfloat)
    d_two_part = jnp.einsum(
        "rtf,df->rtd", d_gate, gate_weight, preferred_element_type=single
    ) + jnp.einsum("rtf,df->rtd", d_up, up_weight, preferred_element_type=single)
    d_two = lax.psum(d_two_part.astype(jnp.bfloat16), "tp").astype(jnp.float32)
    gained_two = d_two * ffn_gain
    d_middle = (
        grad_out.astype(single)
        + root_two * gained_two
        - middle * root_two**3 * jnp.mean(gained_two * middle, axis=-1, keepdims=True)
    )
    normed_rows = normed_two
    gate_term = jnp.einsum("rtd,rtf->df", normed_rows, d_gate, preferred_element_type=single)
    up_term = jnp.einsum("rtd,rtf->df", normed_rows, d_up, preferred_element_type=single)
    down_term = jnp.einsum("rtd,rtf->df", grad_out, hidden, preferred_element_type=single)
    gain_term = jnp.sum(d_two * scaled_two, axis=(0, 1))
    gate_grad, up_grad, down_grad, ffn_gain_grad = lax.psum_scatter(
        (gate_term, up_term, down_term, gain_term), "seq", scatter_dimension=0, tiled=True
    )
    error = d_middle.astype(bfloat)
    d_attended = jnp.einsum("rtd,dh->rth", error, out_weight, preferred_element_type=single).astype(
        bfloat
    )
    d_heads = d_attended.reshape(batch_rows, local_tokens, local_heads, HEAD_DIM)
    carried = jnp.einsum("rqhe,rhqe->rhq", d_heads.astype(single), attended)
    key_all, value_all = (
        lax.all_gather(keys, "seq", axis=1, tiled=True),
        lax.all_gather(values, "seq", axis=1, tiled=True),
    )
    key_block = math.gcd(row_length, 512)

    def block_terms(begin):
        key_heads = lax.dynamic_slice_in_dim(key_all, begin, key_block, 1).reshape(
            batch_rows, key_block, local_heads, HEAD_DIM
        )
        value_heads = lax.dynamic_slice_in_dim(value_all, begin, key_block, 1).reshape(
            batch_rows, key_block, local_heads, HEAD_DIM
        )
        scores = jnp.einsum(
            "rqhe,rkhe->rhqk", query_heads, key_heads, preferred_element_type=single
        )
        allowed = key_mask(doc_start, query_pos, begin, key_block)
        probs = jnp.where(
            allowed, jnp.exp(jnp.where(allowed, scores, NEGATIVE_FILL) - log_total[..., None]), 0.0
        )
        d_probs = jnp.einsum("rqhe,rkhe->rhqk", d_heads, value_heads, preferred_element_type=single)
        d_scores = (probs * (d_probs - carried[..., None])).astype(bfloat)
        query_part = jnp.einsum(
            "rhqk,rkhe->rhqe", d_scores, key_heads, preferred_element_type=single
        )
        return (probs, d_scores, query_part)

    query_zero = jnp.zeros((batch_rows, local_heads, local_tokens, HEAD_DIM), single)

    def back_step(block_index, state):
        d_query, key_terms, value_terms = state
        begin = block_index * key_block

        def back_work(unused):
            probs, d_scores, query_part = block_terms(begin)
            value_part = jnp.einsum(
                "rhqk,rqhe->rkhe", probs.astype(bfloat), d_heads, preferred_element_type=single
            )
            key_part = jnp.einsum(
                "rhqk,rqhe->rkhe", d_scores, query_heads, preferred_element_type=single
            )
            return (
                query_part,
                key_part.reshape(batch_rows, key_block, half_width),
                value_part.reshape(batch_rows, key_block, half_width),
            )

        def skip_block(unused):
            empty_rows = jnp.zeros((batch_rows, key_block, half_width), single)
            return (jnp.zeros_like(d_query), empty_rows, empty_rows)

        needed = (begin <= last_needed) & (begin + key_block - 1 >= first_needed)
        query_part, key_part, value_part = lax.cond(needed, back_work, skip_block, 0)
        return (
            d_query + query_part,
            lax.dynamic_update_slice_in_dim(key_terms, key_part, begin, 1),
            lax.dynamic_update_slice_in_dim(value_terms, value_part, begin, 1),
        )

    back_start = (
        query_zero,
        jnp.zeros((batch_rows, row_length, half_width), single),
        jnp.zeros((batch_rows, row_length, half_width), single),
    )
    d_query, key_terms, value_terms = lax.fori_loop(
        0, row_length // key_block, back_step, back_start
    )
    key_grad, value_grad = (
        lax.psum_scatter(key_terms, "seq", scatter_dimension=1, tiled=True),
        lax.psum_scatter(value_terms, "seq", scatter_dimension=1, tiled=True),
    )
    d_query_rows = (
        d_query.transpose(0, 2, 1, 3).reshape(batch_rows, local_tokens, half_width).astype(bfloat)
    )
    d_one_part = (
        jnp.einsum("rte,de->rtd", d_query_rows, query_weight, preferred_element_type=single)
        * query_scale
    )
    d_one = lax.psum(d_one_part.astype(jnp.bfloat16), "tp").astype(jnp.float32)
    gained_one = d_one * attn_gain
    d_whole = (
        d_middle
        + root_one * gained_one
        - whole * root_one**3 * jnp.mean(gained_one * whole, axis=-1, keepdims=True)
    )
    input_grad = lax.dynamic_slice_in_dim(d_whole, tp_index * half_width, half_width, 2)
    normed_rows = normed_one
    query_term = (
        jnp.einsum("rtd,rte->de", normed_rows, d_query_rows, preferred_element_type=single)
        * query_scale
    )
    out_term = jnp.einsum("rtd,rth->dh", error, attended_low, preferred_element_type=single)
    gain_term = jnp.sum(d_one * scaled_one, axis=(0, 1))
    query_grad, out_grad, attn_gain_grad = lax.psum_scatter(
        (query_term, out_term, gain_term), "seq", scatter_dimension=0, tiled=True
    )
    return (
        output,
        input_grad,
        key_grad,
        value_grad,
        attn_gain_grad,
        query_grad,
        out_grad,
        ffn_gain_grad,
        gate_grad,
        up_grad,
        down_grad,
    )


def solution(mesh):
    in_specs = (
        P(None, "seq", "tp"),
        P(None, "seq"),
        P(None, "seq", "tp"),
        P(None, "seq", "tp"),
        P(),
        P(None, "tp"),
        P(None, "tp"),
        P(),
        P(None, "tp"),
        P(None, "tp"),
        P(None, "tp"),
        P(None, "seq", "tp"),
    )
    out_specs = (
        P(None, "seq", "tp"),
        P(None, "seq", "tp"),
        P(None, "seq", "tp"),
        P(None, "seq", "tp"),
        P("seq"),
        P("seq", "tp"),
        P("seq", "tp"),
        P("seq"),
        P("seq", "tp"),
        P("seq", "tp"),
        P("seq", "tp"),
    )
    n = mesh.shape["seq"]

    def step(inputs, *others):
        rows, tok, half = inputs.shape
        units = rows * (half // HEAD_DIM)
        if units == n == PLANE * PLANE and tok == LANE and mesh.shape["tp"] == 2 and -(-others[7].shape[1] // (2 * LANE)) % 2:
            return fast_device(n, inputs, *others)
        return per_device(inputs, *others)

    return jax.shard_map(
        step, mesh=mesh, in_specs=in_specs, out_specs=out_specs, check_vma=False
    )
```

```python
import functools
import math
import types

import jax
import jax.numpy as jnp
from jax import lax
from jax.experimental import pallas as pl
from jax.experimental.pallas import tpu as pltpu
from jax.sharding import PartitionSpec as P

HEAD_DIM = 128
CUTS = 12


EPSILON = 1e-06
NEGATIVE_FILL = -1e30

MESH = pl.DeviceIdType.MESH
BF = jnp.bfloat16
F32 = jnp.float32
VMEM_GRANT = 63 << 20
PLANE = 4
LANE = 128


def dot_nn(a, b):
    return lax.dot_general(a, b, (((1,), (0,)), ((), ())), preferred_element_type=F32)


def dot_nt(a, b):
    return lax.dot_general(a, b, (((1,), (1,)), ((), ())), preferred_element_type=F32)


def dot_tn(a, b):
    return lax.dot_general(a, b, (((0,), (0,)), ((), ())), preferred_element_type=F32)


def aligned(index, size):
    return pl.ds(pl.multiple_of(index * size, size), size)


class Place:
    def __init__(self, n):
        self.n = n
        self.s = lax.axis_index("seq")
        self.t = lax.axis_index("tp")
        self.z = self.s // PLANE
        self.p = lax.rem(self.s, PLANE)
        self.y = self.p // 2
        self.c = lax.rem(self.p, 2)
        base = self.z * PLANE
        self.core_p = self.y * 2 + 1 - self.c
        self.side_p = (1 - self.y) * 2 + self.c
        self.cross_p = (1 - self.y) * 2 + 1 - self.c
        self.core = (base + self.core_p, self.t)
        self.side = (base + self.side_p, self.t)
        self.cross = (base + self.cross_p, self.t)
        self.twin = (self.s, 1 - self.t)

    def other(self, k):
        return lax.rem(self.s + k, self.n)

    def enter(self):
        barrier = pltpu.get_barrier_semaphore()

        def greet(k, unused):
            pl.semaphore_signal(barrier, inc=1, device_id=(self.other(k), self.t), device_id_type=MESH)
            return unused

        lax.fori_loop(1, self.n, greet, 0)
        pl.semaphore_signal(barrier, inc=1, device_id=self.twin, device_id_type=MESH)
        pl.semaphore_wait(barrier, self.n)


def remote(src, dst, send, recv, device):
    return pltpu.make_async_remote_copy(
        src_ref=src, dst_ref=dst, send_sem=send, recv_sem=recv, device_id=device, device_id_type=MESH
    )


class Spread:
    def __init__(self, place, src, dst, send, recv, local, bulk):
        self.place, self.src, self.dst, self.send, self.recv, self.local = place, src, dst, send, recv, local
        self.bulk = bulk

    def copy(self, k):
        place = self.place
        d = place.other(k)
        return remote(self.src(d), self.dst(), self.send, self.recv, (d, place.t))

    def own(self):
        return pltpu.make_async_copy(self.src(self.place.s), self.dst(), self.local)

    def start(self):
        self.own().start()

        def one(k, unused):
            self.copy(k).start()
            return unused

        lax.fori_loop(1, self.place.n, one, 0)

    def start_to(self, d, unused):
        k = lax.rem(d - self.place.s + self.place.n, self.place.n)

        @pl.when(k == 0)
        def _():
            self.own().start()

        @pl.when(k != 0)
        def _():
            self.copy(k).start()

        return unused

    def wait(self):
        self.own().wait()
        remote(self.bulk, self.bulk, self.send, self.recv, self.place.core).wait()


def attention_masks(seg_all, seg_row, seg_col, n, tok):
    def one(i, unused):
        piece = seg_all[i].astype(F32)
        seg_row[:, aligned(i, tok)] = piece
        seg_col[aligned(i, tok), :] = jnp.transpose(jnp.broadcast_to(piece, (tok, tok)))
        return unused

    lax.fori_loop(0, n, one, 0)


def readable(seg_col, seg_row, key_block, query_block, block):
    key_seg = seg_col[aligned(key_block, block), :]
    key_seg = jnp.concatenate([key_seg] * (block // LANE), axis=1)
    query_seg = seg_row[:, aligned(query_block, block)]
    key_pos = key_block * block + lax.broadcasted_iota(jnp.int32, (block, block), 0)
    query_pos = query_block * block + lax.broadcasted_iota(jnp.int32, (block, block), 1)
    return (key_seg == query_seg) & (key_pos <= query_pos)


def split_rows(whole, split, n):
    blk = whole.shape[1] * 2 // n
    for zy in range(n // 2):
        z, y = divmod(zy, 2)
        split[y, :, z * blk : (z + 1) * blk] = whole[:, zy * blk : (zy + 1) * blk]


class Plane:
    def __init__(self, place, split, left, send, recv, local, tokens):
        self.place, self.tokens, self.left = place, tokens, left
        to = left.at[aligned(place.p, tokens), :]
        self.own = pltpu.make_async_copy(split.at[place.y], to, local)
        self.to_core = remote(split.at[place.y], to, send.at[0], recv.at[0], place.core)
        self.to_side = remote(split.at[1 - place.y], to, send.at[1], recv.at[1], place.side)
        passed = left.at[aligned(place.side_p, tokens), :]
        self.on = remote(passed, passed, send.at[2], recv.at[2], place.core)

    def start(self):
        self.to_side.start()
        self.own.start()
        self.to_core.start()

    def forward(self):
        self.to_side.wait()
        self.on.start()

    def gone(self):
        self.own.wait()
        self.to_core.wait_send()

    def finish(self):
        self.to_core.wait_recv()
        self.on.wait()


def vm(shape, dtype):
    return jax.ShapeDtypeStruct(shape, dtype)


class Gather:
    def __init__(self, place, whole, stride, first, land, send, recv, local, tokens):
        cols = land.shape[1]
        to = land.at[aligned(place.p, tokens), :]

        def half(c):
            return whole.at[:, pl.ds(pl.multiple_of(c * stride + first, LANE), cols)]

        c = place.c
        self.own = pltpu.make_async_copy(half(c), to, local)
        self.away = [
            remote(half(c), to, send.at[0], recv.at[0], place.side),
            remote(half(1 - c), to, send.at[1], recv.at[1], place.cross),
            remote(half(1 - c), to, send.at[2], recv.at[2], place.core),
        ]

    def start(self):
        self.own.start()
        for copy in self.away:
            copy.start()

    def wait(self):
        self.own.wait()
        for copy in self.away:
            copy.wait()


class Line:
    def __init__(self, place, nz, blk, gather, land, left, lv, mv, move, got, total, out, turned, sems, work):
        self.place, self.nz, self.blk, self.gather = place, nz, blk, gather
        self.land, self.left, self.move, self.got, self.total, self.out = land, left, move, got, total, out
        self.turned = turned
        self.cols = land.shape[1]
        self.lv, self.mv = lv, mv
        self.acc, self.stage, self.load_sem = work
        self.send, self.recv, self.end_s, self.end_r, self.end_l = sems
        self.at_end = (place.z == 0) | (place.z == nz - 1)

    def load(self, left_too=False, gathered=False):
        if not gathered:
            self.gather.wait()
        copies = []
        if self.land is not self.mv:
            copies.append(pltpu.make_async_copy(self.land, self.mv, self.load_sem.at[0]))
        if left_too and self.left is not self.lv:
            copies.append(pltpu.make_async_copy(self.left, self.lv, self.load_sem.at[1]))
        for copy in copies:
            copy.start()
        for copy in copies:
            copy.wait()

    def product(self, b):
        tile = 2 * LANE

        def one(i, unused):
            at = pl.ds(pl.multiple_of(jnp.minimum(i * tile, self.cols - tile), LANE), tile)
            self.acc[:, at] = dot_tn(self.lv[:, aligned(b, self.blk)], self.mv[:, at])
            return unused

        lax.fori_loop(0, -(-self.cols // tile), one, 0)

    def take(self, slot):
        self.arrival(slot).wait_recv()
        copy = pltpu.make_async_copy(self.got.at[slot], self.stage.at[:, : self.cols], self.load_sem.at[2])
        copy.start()
        copy.wait()
        return self.stage[:, : self.cols].astype(F32)

    def arrival(self, slot):
        return remote(self.move.at[0], self.got.at[slot], self.send.at[0], self.recv.at[slot], self.place.core)

    def route(self, j):
        z, nz = self.place.z, self.nz
        b = jnp.where(z < nz // 2, nz - 1 - j, j)
        b = jnp.where((j == nz - 2) & (z == 1), 0, b)
        b = jnp.where((j == nz - 2) & (z == nz - 2), nz - 1, b)
        b = jnp.where(j == nz - 1, z, b)
        up = b > z
        to = jnp.where(up, z + 1, z - 1)
        slot_in = jnp.where(up, b - z, nz - z + b)
        slot_out = jnp.where(up, b - to, nz - to + b)
        keep = jnp.where(up, b - 1, b)
        last = jnp.where(up, z == 0, z == nz - 1)
        device = (to * PLANE + self.place.p, self.place.t)

        def out():
            return remote(self.move.at[keep], self.got.at[slot_out], self.send.at[keep], self.recv.at[slot_out], device)

        return b, slot_in, keep, last, out

    def step(self, j):
        b, slot_in, keep, last, out = self.route(j)
        self.product(b)
        sends = j < self.nz - 1

        @pl.when(jnp.logical_not(sends))
        def _():
            self.total[...] = self.acc[:, : self.cols]

        @pl.when(sends & last)
        def _():
            self.move[keep] = self.acc[:, : self.cols].astype(BF)

        @pl.when(sends & jnp.logical_not(last))
        def _():
            self.move[keep] = (self.acc[:, : self.cols] + self.take(slot_in)).astype(BF)

        @pl.when(sends)
        def _():
            out().start()

    def steps(self, low, high):
        def one(j, unused):
            self.step(j)
            return unused

        lax.fori_loop(low, high, one, 0)

    def some(self, *order):
        def one(i, unused):
            j = order[0]
            for k, then in enumerate(order):
                j = jnp.where(i == k, then, j)
            self.step(j)
            return unused

        lax.fori_loop(0, len(order), one, 0)

    def begin(self):
        self.steps(0, self.nz)

    def from_end(self):
        self.steps(jnp.where(self.at_end, 0, self.nz - 1), self.nz)

    def between(self, low, high):
        pl.when(jnp.logical_not(self.at_end))(lambda: self.steps(low, high))

    def sent(self):
        def one(j, unused):
            self.route(j)[4]().wait_send()
            return unused

        lax.fori_loop(0, self.nz - 1, one, 0)

    def end(self, c):
        half = self.blk // 2
        mine = self.place.c
        if self.turned is None:
            return self.out.at[:, aligned(mine, self.cols)], self.total.at[aligned(c, half), :]
        turned, stride, first = self.turned
        to = self.out.at[pl.ds(pl.multiple_of(mine * stride + first, LANE), self.cols), :]
        return to, turned.at[first : first + self.cols, aligned(c, half)]

    def away(self):
        to, theirs = self.end(1 - self.place.c)
        return remote(theirs, to, self.end_s, self.end_r, self.place.core)

    def here(self):
        to, mine = self.end(self.place.c)
        return pltpu.make_async_copy(mine, to, self.end_l)

    def finish(self):
        z, nz = self.place.z, self.nz

        @pl.when(z > 0)
        def _():
            self.total[...] += self.take(0)

        @pl.when(z < nz - 1)
        def _():
            self.total[...] += self.take(nz)

        if self.turned is not None:
            turned, _, first = self.turned
            turned[first : first + self.cols, :] = jnp.transpose(self.total[...])
        self.away().start()
        self.here().start()

    def left_here(self):
        self.away().wait_send()
        self.here().wait()

    def arrived(self):
        self.away().wait_recv()


class Weights:
    def __init__(self, weights, buffers, sems, tail_sems, phase, first, cols, ff):
        self.weights, self.buffers, self.sems, self.tail_sems, self.phase = weights, buffers, sems, tail_sems, phase
        self.first, self.each = first, len(weights)
        self.size = buffers.shape[1]
        self.cols = cols
        self.regular = 2 * (cols // self.size)
        self.rest = cols % self.size
        self.rest_two = ff - cols - cols // self.size * self.size

    def slot(self, i, w):
        return self.first + lax.rem(i + self.phase, 2) * self.each + w

    def copies(self, i):
        at = pl.ds(pl.multiple_of(lax.rem(i, 2) * self.cols + i // 2 * self.size, LANE), self.size)
        return [
            pltpu.make_async_copy(ref.at[at, :], self.buffers.at[self.slot(i, w)], self.sems.at[lax.rem(i, 2), w])
            for w, ref in enumerate(self.weights)
        ]

    def tail(self):
        first = self.cols // self.size * self.size
        copies = []
        for w, ref in enumerate(self.weights):
            to = self.buffers.at[self.slot(self.regular, w)]
            copies += [
                pltpu.make_async_copy(ref.at[pl.ds(first, self.rest), :], to.at[pl.ds(0, self.rest), :], self.tail_sems.at[0, w]),
                pltpu.make_async_copy(
                    ref.at[pl.ds(self.cols + first, self.rest_two), :],
                    to.at[pl.ds(self.rest, self.rest_two), :],
                    self.tail_sems.at[1, w],
                ),
            ]
        return copies

    def begin(self, blocks=1):
        self.begun = blocks
        for i in range(blocks):
            for copy in self.copies(i):
                copy.start()

    def run(self, work, after=()):
        first = self.cols // self.size * self.size
        filled = self.rest + self.rest_two

        def one(i, unused):
            is_tail = i == self.regular

            @pl.when((i + 1 < self.regular) & (i + 1 >= self.begun))
            def _():
                for copy in self.copies(i + 1):
                    copy.start()

            @pl.when(i + 1 == self.regular)
            def _():
                for copy in self.tail():
                    copy.start()

            @pl.when(jnp.logical_not(is_tail))
            def _():
                for copy in self.copies(i):
                    copy.wait()

            @pl.when(is_tail)
            def _():
                for copy in self.tail():
                    copy.wait()
                for w in range(self.each):
                    slot = self.slot(self.regular, w)
                    self.buffers[slot, filled:, :] = jnp.zeros((self.size - filled, self.buffers.shape[2]), BF)

            at = lax.rem(i, 2) * self.cols + i // 2 * self.size
            columns = [
                pl.ds(pl.multiple_of(jnp.where(is_tail, tail_at, at + k * LANE), LANE), LANE)
                for k, tail_at in enumerate((first, self.cols + first))
            ]
            work([self.slot(i, w) for w in range(self.each)], columns)
            for at_block, things in after:
                pl.when(i == at_block)(lambda things=things: [thing() for thing in things] and None)
            return unused

        lax.fori_loop(0, self.regular + 1, one, 0)


class Units:
    def __init__(self, place, nz, heads, tok):
        self.place, self.nz, self.heads, self.tok = place, nz, heads, tok
        z, s = place.z, place.s
        self.at_end = (z == 0) | (z == nz - 1)
        self.second = jnp.where(z < nz // 2, s - PLANE, s + PLANE)
        self.near = (jnp.where(z == 0, s + PLANE, s - PLANE), place.t)

    def host(self, u):
        z = u // PLANE
        inner = jnp.clip(z, 1, self.nz - 2)
        return inner * PLANE + lax.rem(u, PLANE), jnp.where(inner == z, 0, 1)

    def unit(self, slot):
        return jnp.where(slot == 0, self.place.s, self.second)

    def home(self, ref, u):
        return ref.at[aligned(u // self.heads, self.tok), aligned(lax.rem(u, self.heads), HEAD_DIM)]


class ToUnits:
    def __init__(self, units, src, land, send, recv, local):
        self.units, self.src, self.land, self.send, self.recv, self.local = units, src, land, send, recv, local
        self.n, self.s, self.t, self.tok = units.place.n, units.place.s, units.place.t, units.tok

    def away(self, u):
        host, slot = self.units.host(u)
        to = self.land.at[slot, aligned(self.s, self.tok), :]
        return remote(self.units.home(self.src, u), to, self.send, self.recv.at[slot], (host, self.t))

    def here(self, u):
        slot = self.units.host(u)[1]
        to = self.land.at[slot, aligned(self.s, self.tok), :]
        return pltpu.make_async_copy(self.units.home(self.src, u), to, self.local.at[slot])

    def start(self, u, unused):
        host = self.units.host(u)[0]
        pl.when(host == self.s)(lambda: self.here(u).start())
        pl.when(host != self.s)(lambda: self.away(u).start())
        return unused

    def bulk(self, copies, recv):
        some = self.land.at[0, pl.ds(0, copies * self.tok), :]
        return remote(some, some, self.send, recv, self.units.place.core)

    def wait(self, slot):
        self.here(self.units.unit(slot)).wait()
        self.bulk(self.n - 1, self.recv.at[slot]).wait_recv()

    def sent(self):
        pl.when(self.units.at_end)(lambda: self.bulk(self.n, self.recv.at[0]).wait_send())
        pl.when(jnp.logical_not(self.units.at_end))(lambda: self.bulk(self.n - 2, self.recv.at[0]).wait_send())


class FromUnits:
    def __init__(self, units, src, whole, send, recv, local):
        self.units, self.src, self.whole, self.send, self.recv, self.local = units, src, whole, send, recv, local
        self.n, self.s, self.t, self.tok = units.place.n, units.place.s, units.place.t, units.tok

    def away(self, slot, d):
        u = self.units.unit(slot)
        src = self.src.at[slot, aligned(d, self.tok), :]
        return remote(src, self.units.home(self.whole, u), self.send.at[slot], self.recv, (d, self.t))

    def here(self, slot):
        src = self.src.at[slot, aligned(self.s, self.tok), :]
        return pltpu.make_async_copy(src, self.units.home(self.whole, self.units.unit(slot)), self.local.at[slot])

    def start(self, slot, low, high):
        def one(d, unused):
            pl.when(d == self.s)(lambda: self.here(slot).start())
            pl.when(d != self.s)(lambda: self.away(slot, d).start())
            return unused

        lax.fori_loop(low, high, one, 0)

    def bulk(self, copies, slot):
        some = self.src.at[0, pl.ds(0, copies * self.tok), :]
        return remote(some, some, self.send.at[slot], self.recv, self.units.place.core)

    def wait(self):
        pl.when(self.units.at_end)(lambda: self.bulk(self.n, 0).wait_recv())

        @pl.when(jnp.logical_not(self.units.at_end))
        def _():
            for slot in range(2):
                self.here(slot).wait()
            self.bulk(self.n - 2, 0).wait_recv()

    def sent(self, slot):
        self.bulk(self.n - 1, slot).wait_send()


def layer_kernel(
    geo, sizes, names,
    x_in, cot_in, key_in, value_in, seg_in, wg_in, wu_in, wd_in, wo_in, wq_in, gain_one, gain_two, *refs,
):
    n, rows, tok, width, half, heads, length = geo
    ff, cols, cuts = sizes
    r = types.SimpleNamespace(**dict(zip(names, refs, strict=True)))
    tokens = rows * tok
    blk = 2 * width // n
    nz = n // PLANE
    place = Place(n)
    s, t, z = place.s, place.t, place.z
    row_s, head_s = s // heads, lax.rem(s, heads)
    mine = aligned(t, half)
    chunk = tokens // 4
    fine = 32
    wbuf = r.wbuf
    size = wbuf.shape[1]
    mid, x_all, cot_all, two_norm, two_own, two_in, one_in = (
        r.mid, r.x_all, r.cot_all, r.two_norm, r.two_own, r.two_in, r.one_in
    )
    mixed, err, one, attended, dq = r.mixed, r.err, r.one, r.attended, r.dq
    d_att = attended
    hidden, d_gate, d_up, sums = r.hidden, r.d_gate, r.d_up, r.sums
    uq, uk, uv, uo, lse, k_t = (ref.at[0] for ref in (r.uqs, r.uks, r.uvs, r.uos, r.lses, r.k_ts))
    delta = r.delta
    seg_all, seg_row, seg_col = r.seg_all, r.seg_row, r.seg_col
    udq, udk, udv = r.udq, r.udk, r.udv
    tp_s, tp_r, a_s, a_r, loc = r.tp_s, r.tp_r, r.a_s, r.a_r, r.loc
    units = Units(place, nz, heads, tok)
    at_end = units.at_end
    place.enter()

    to_x = remote(x_in, x_all.at[:, mine], tp_s.at[0], tp_r.at[0], place.twin)
    to_x.start()
    own_x = pltpu.make_async_copy(x_in, x_all.at[:, mine], loc.at[0])
    own_x.start()

    def piece(ref):
        return lambda d: ref.at[aligned(d // heads, tok), aligned(lax.rem(d, heads), HEAD_DIM)]

    keys = Spread(place, piece(key_in), lambda: uk.at[aligned(s, tok), :], a_s.at[0], a_r.at[0], loc.at[2], uk.at[: length - tok, :])
    vals = Spread(place, piece(value_in), lambda: uv.at[aligned(s, tok), :], a_s.at[1], a_r.at[1], loc.at[3], uv.at[: length - tok, :])
    segs = Spread(place, lambda d: seg_in.at[d // heads], lambda: seg_all.at[s], a_s.at[2], a_r.at[2], loc.at[4], seg_all.at[: n - 1])
    qrys = Spread(place, piece(dq), lambda: uq.at[aligned(s, tok), :], a_s.at[3], a_r.at[3], loc.at[5], uq.at[: length - tok, :])
    segs.start()
    keys.start()
    vals.start()
    to_cot = remote(cot_in, cot_all.at[:, mine], tp_s.at[1], tp_r.at[1], place.twin)
    to_cot.start()
    own_cot = pltpu.make_async_copy(cot_in, cot_all.at[:, mine], loc.at[6])
    own_cot.start()

    def square_copies(k, ref, sems):
        copies = []
        for zy in range(n // 2):
            to = wbuf.at[4 * k + zy // 2, :, (zy % 2) * half : (zy % 2 + 1) * half]
            copies.append(pltpu.make_async_copy(ref.at[zy * blk : (zy + 1) * blk, :], to, sems.at[zy]))
        return copies

    def square_block(k, zy):
        return wbuf[4 * k + zy // 2, :, (zy % 2) * half : (zy % 2 + 1) * half]

    def split_block(ref, at, zy):
        zz, yy = divmod(zy, 2)
        return ref[yy, at, zz * blk : (zz + 1) * blk]

    def store_split(ref, at, now):
        for zy in range(n // 2):
            zz, yy = divmod(zy, 2)
            ref[yy, at, zz * blk : (zz + 1) * blk] = now[:, zy * blk : (zy + 1) * blk]

    load_wq = square_copies(1, wq_in, r.o_sem.at[0])
    load_wo = square_copies(0, wo_in, r.o_sem.at[1])
    for copy in load_wq + load_wo:
        copy.start()
    own_x.wait()
    to_x.wait()

    def first_norm(i, unused):
        at = aligned(i, fine)
        x = x_all[at, :].astype(F32)
        root = lax.rsqrt(jnp.mean(x * x, axis=-1, keepdims=True) + EPSILON)
        store_split(one, at, (x * root * gain_one[...]).astype(BF))
        return unused

    lax.fori_loop(0, tokens // fine, first_norm, 0)
    for copy in load_wq:
        copy.wait()
    every = slice(0, tokens)
    total = jnp.zeros((tokens, half), F32)
    for zy in range(n // 2):
        total += dot_nn(split_block(one, every, zy), square_block(1, zy))
    dq[...] = (total * HEAD_DIM ** (-0.5)).astype(BF)
    qrys.start()
    lv_one, lv_two = r.lv_one, r.lv_two
    left_cot, left_two, left_err, left_one = (
        Plane(place, split, land, r.le_s.at[i], r.le_r.at[i], r.l_loc.at[i], tokens)
        for i, (split, land) in enumerate(((err, lv_one), (mixed, lv_two), (err, r.l_err), (one, r.l_one)))
    )
    left_one.start()

    segs.wait()
    attention_masks(seg_all, seg_row, seg_col, n, tok)
    keys.wait()
    vals.wait()

    def turn_into(ref, to):
        def turn(i, unused):
            at = aligned(i, tok)
            to[:, at] = jnp.transpose(ref[at, :].astype(F32)).astype(BF)
            return unused

        lax.fori_loop(0, n, turn, 0)

    turn_into(uv, k_t)
    qrys.wait()
    block = 512
    owners = block // tok
    back = Spread(
        place,
        lambda d: uo.at[aligned(d, tok), :],
        lambda: attended.at[aligned(row_s, tok), aligned(head_s, HEAD_DIM)],
        a_s.at[4], a_r.at[4], loc.at[8], uo.at[: length - tok, :],
    )

    def query_step(qi, unused):
        query_block = uq[aligned(qi, block), :]

        def key_step(j, carry):
            top, total, acc = carry
            kj = qi - j
            scores = dot_nt(uk[aligned(kj, block), :], query_block)
            scores = jnp.where(readable(seg_col, seg_row, kj, qi, block), scores, NEGATIVE_FILL)
            new_top = jnp.maximum(top, jnp.max(scores, axis=0, keepdims=True))
            weights = jnp.exp(scores - new_top)
            decay = jnp.exp(top - new_top)
            total = total * decay + jnp.sum(weights, axis=0, keepdims=True)
            acc = acc * decay + dot_nn(k_t[:, aligned(kj, block)], weights.astype(BF))
            return new_top, total, acc

        start = (
            jnp.full((1, block), NEGATIVE_FILL, F32),
            jnp.zeros((1, block), F32),
            jnp.zeros((HEAD_DIM, block), F32),
        )
        top, total, acc = lax.fori_loop(0, qi + 1, key_step, start)
        lse[:, aligned(qi, block)] = top + jnp.log(total)
        uo[aligned(qi, block), :] = jnp.transpose(acc / total).astype(BF)
        return lax.fori_loop(qi * owners, (qi + 1) * owners, back.start_to, unused)

    lax.fori_loop(0, length // block, query_step, 0)

    work = (r.acc, r.stage, r.work_sem)
    mv, turned = r.mv, r.turned
    s_first, s_second, t_first, t_second = r.s_first, r.s_second, r.t_first, r.t_second
    sources = (hidden, d_gate, d_up)
    lefts_of = ((lv_one, lv_one), (lv_two, lv_two), (lv_two, lv_two))
    kept = ((s_first, t_first, r.out_down), (s_second, t_second, r.out_gate), (s_first, t_first, r.out_up))
    gots = (r.g0, r.g1, r.g2, r.g3, r.g4, r.g5, r.g6)
    lands = (None, None, None, r.m3, r.m4, r.m5, r.m6)
    plans = []
    for i, (kind, first, wide) in enumerate(cuts):
        at = pl.ds(first, wide)
        left, lv = lefts_of[kind]
        move, total_ref, out_ref = kept[kind]
        here = mv.at[:, at]
        plans.append((
            (sources[kind], cols, first), here if lands[i] is None else lands[i], left, lv, here, move.at[:, :, at], gots[i], total_ref.at[:, at],
            out_ref, (turned, cols, first),
        ))
    for source, left, lv, *rest in (
        (attended, r.l_err, lv_one, r.mv_out, r.s_out, r.g_out, r.t_out, r.out_out),
        (dq, r.l_one, lv_two, r.mv_query, r.s_query, r.g_query, r.t_query, r.out_query),
    ):
        plans.append(((source, half // 2, 0), rest[0], left, lv, *rest, None))
    lines = []
    for i, (source, land, *rest) in enumerate(plans):
        gather = Gather(place, *source, land, r.me_s.at[i], r.me_r.at[i], r.g_loc.at[i], tokens)
        sems = (r.c_s.at[i], r.c_r.at[i], r.e_s.at[i], r.e_r.at[i], r.e_l.at[i])
        lines.append(Line(place, nz, blk, gather, land, *rest, sems, work))
    down_a, down_b, down_c, gate_a, gate_b, up_a, up_b, out, query = lines
    ship = [
        remote(a.at[0], a.at[1], r.sh_s.at[i], r.sh_r.at[i], units.near)
        for i, a in enumerate((r.uqs, r.uks, r.uvs, r.uos, r.lses))
    ]

    @pl.when(at_end)
    def _():
        for copy in ship:
            copy.start()

    own_cot.wait()
    to_cot.wait()

    def split_cot(i, unused):
        at = aligned(i, fine)
        store_split(err, at, cot_all[at, :])
        return unused

    lax.fori_loop(0, tokens // fine, split_cot, 0)
    left_cot.start()
    left_one.forward()
    for copy in load_wo:
        copy.wait()
    back.wait()

    chunks = 4
    wide = width // chunks

    def to_twin(i):
        at = slice(i * wide, (i + 1) * wide)
        return remote(two_own.at[:, at], one_in.at[:, at], tp_s.at[9 + i], tp_r.at[9 + i], place.twin)

    for i in range(chunks):
        for zy in range(2 * i, 2 * i + 2):
            two_own[:, zy * blk : (zy + 1) * blk] = dot_nt(attended[...], square_block(0, zy)).astype(BF)
        to_twin(i).start()
    out.gather.start()
    zeroth_pass = Weights((wd_in,), wbuf, r.w_sem.at[3], r.tail_sem.at[3], 0, 4, cols, ff)
    first_pass = Weights((wg_in, wu_in), wbuf, r.w_sem.at[0], r.tail_sem.at[0], 0, 0, cols, ff)
    second_pass = Weights((wg_in, wu_in), wbuf, r.w_sem.at[1], r.tail_sem.at[1], 0, 4, cols, ff)
    third_pass = Weights((wd_in,), wbuf, r.w_sem.at[2], r.tail_sem.at[2], 0, 4, cols, ff)
    zeroth_pass.begin(2)
    first_pass.begin(2)

    def to_hidden(slots, at):
        now = dot_nt(cot_all[...], wbuf[slots[0]]).astype(BF)
        for k in range(2):
            d_gate[:, at[k]] = now[:, k * LANE : (k + 1) * LANE]

    zeroth_pass.run(to_hidden)
    left_cot.forward()
    square = jnp.zeros((tokens, 1), F32)
    for i in range(chunks):
        to_twin(i).wait()
        at = slice(i * wide, (i + 1) * wide)
        now = x_all[:, at].astype(F32) + (two_own[:, at].astype(F32) + one_in[:, at].astype(F32))
        mid[:, at] = now
        square += jnp.sum(now * now, axis=-1, keepdims=True)
    root_two = lax.rsqrt(square * (1.0 / width) + EPSILON)
    for i in range(chunks):
        at = slice(i * wide, (i + 1) * wide)
        two_norm[:, at] = (mid[:, at] * root_two * gain_two[:, at]).astype(BF)

    def units_block(slots, at):
        x = two_norm[...]
        gate_now, up_now = (dot_nt(x, wbuf[slot]) for slot in slots)
        d_hid = jnp.concatenate([d_gate[:, at[0]], d_gate[:, at[1]]], axis=1).astype(F32)
        sigma = jax.nn.sigmoid(gate_now)
        act = gate_now * sigma
        for ref, now in (
            (hidden, act * up_now),
            (d_gate, d_hid * up_now * sigma * (1.0 + gate_now * (1.0 - sigma))),
            (d_up, d_hid * act),
        ):
            now = now.astype(BF)
            for k in range(2):
                ref[:, at[k]] = now[:, k * LANE : (k + 1) * LANE]

    done_a, done_b = (2 * ((first + wide) // size) for _, first, wide in cuts[:2])

    def split_two(i, unused):
        at = aligned(i, fine)
        store_split(mixed, at, two_norm[at, :])
        return unused

    def begin_down():
        down_a.gather.start()
        lax.fori_loop(0, tokens // fine, split_two, 0)

    def go_on_down():
        down_b.gather.start()
        left_cot.gone()
        left_cot.finish()
        down_a.load()
        down_a.from_end()

    first_pass.run(
        units_block,
        ((done_a - 1, [begin_down]), (done_b - 1, [go_on_down]), (first_pass.regular - 1, [second_pass.begin])),
    )
    down_c.gather.start()
    left_two.start()
    down_b.load()
    down_b.from_end()
    down_a.between(0, 2)

    def block_of(ref, at):
        return jnp.concatenate([ref[:, at[0]], ref[:, at[1]]], axis=1)

    def add_up(pairs):
        for db in range(width // size):
            at = slice(db * size, (db + 1) * size)
            sums[db * tokens : (db + 1) * tokens, :] += sum(dot_nn(a, wbuf[slot, :, at]) for a, slot in pairs)

    def back_units(slots, at):
        add_up([(block_of(d_gate, at), slots[0]), (block_of(d_up, at), slots[1])])

    sums[...] = jnp.zeros_like(sums)
    second_pass.run(back_units)
    for db in range(width // size):
        two_own[:, db * size : (db + 1) * size] = sums[db * tokens : (db + 1) * tokens, :].astype(BF)

    def two_copy(i):
        at = aligned(i, chunk)
        return remote(two_own.at[at, :], two_in.at[at, :], tp_s.at[2 + i], tp_r.at[2 + i], place.twin)

    for i in range(4):
        two_copy(i).start()
    load_wo = square_copies(0, wo_in, r.o_sem.at[2])
    for copy in load_wo:
        copy.start()
    gate_a.gather.start()
    down_a.between(2, 3)
    down_b.between(0, 2)
    down_c.load()
    down_c.from_end()

    third_pass.begin()
    sums[...] = jnp.zeros_like(sums)

    def out_units(slots, at):
        add_up([(block_of(hidden, at), slots[0])])

    third_pass.run(out_units)
    left_two.forward()
    left_two.gone()
    for db in range(width // size):
        per = half // size
        mixed[db // per, :, (db % per) * size : (db % per + 1) * size] = sums[db * tokens : (db + 1) * tokens, :].astype(BF)
    ffn_copy = remote(mixed.at[1 - t], r.ffn_in, tp_s.at[6], tp_r.at[6], place.twin)
    ffn_copy.start()
    per = half // size
    for i in range(per):
        at = t * per + i
        sums[aligned(at, tokens), :] += mid[:, aligned(at, size)]
    hold = pltpu.make_async_copy(sums.at[aligned(t, per * tokens), :], r.mix, loc.at[11])
    hold.start()
    load_wq = square_copies(1, wq_in, r.o_sem.at[3])
    for copy in load_wq:
        copy.start()
    down_b.between(2, 3)
    down_c.between(0, 2)
    hold.wait()

    to_units = ToUnits(units, d_att, r.udo, r.u_s.at[0], r.u_r, r.u_l)
    out.gather.wait()
    for copy in load_wo:
        copy.wait()

    def second_norm(i, gain_sum):
        two_copy(i).wait()

        def some(j, gain_sum):
            at = aligned(i * (chunk // fine) + j, fine)
            m = mid[at, :]
            d2 = two_own[at, :].astype(F32) + two_in[at, :].astype(F32)
            root = lax.rsqrt(jnp.mean(m * m, axis=-1, keepdims=True) + EPSILON)
            gained = d2 * gain_two[...]
            scaled = m * root
            gain_sum = gain_sum + jnp.sum(d2 * scaled, axis=0, keepdims=True)
            slope = jnp.mean(gained * scaled, axis=-1, keepdims=True)
            dm = cot_all[at, :].astype(F32) + root * (gained - scaled * slope)
            mid[at, :] = dm
            store_split(err, at, dm.astype(BF))
            return gain_sum

        gain_sum = lax.fori_loop(0, chunk // fine, some, gain_sum)
        at = aligned(i, chunk)
        total = jnp.zeros((chunk, half), F32)
        for zy in range(n // 2):
            total += dot_nn(split_block(err, at, zy), square_block(0, zy))
        d_att[at, :] = total.astype(BF)
        return gain_sum

    gain_sum = jnp.zeros((1, width), F32)
    per_row = tok // chunk
    for row in range(rows):
        gain_sum = lax.fori_loop(row * per_row, (row + 1) * per_row, second_norm, gain_sum)
        lax.fori_loop(row * heads, (row + 1) * heads, to_units.start, 0)
    gain_part, gain_in = r.gain_part, r.gain_in
    for i in range(n):
        gain_part[0, i] = gain_sum[:, i * (width // n) : (i + 1) * (width // n)]
    spread_gain = [
        Spread(place, lambda d, g=g: gain_part.at[g, d], lambda g=g: gain_in.at[g, s], a_s.at[5 + g], a_r.at[5 + g], loc.at[9 + g],
               gain_in.at[g, : n - 1])
        for g in range(2)
    ]
    spread_gain[0].start()
    gate_b.gather.start()
    down_c.between(2, 3)
    left_two.finish()
    gate_a.load()
    gate_a.from_end()

    back_dq, back_dk, back_dv = (
        FromUnits(units, src, whole, r.f_s.at[i], r.f_r.at[i], r.f_l.at[i])
        for i, (src, whole) in enumerate(((udq, dq), (udk, r.d_keys), (udv, r.d_values)))
    )

    def one_unit(slot, unused):
        unit_q, unit_k, unit_v, unit_o, unit_lse, unit_kt = (
            ref.at[slot] for ref in (r.uqs, r.uks, r.uvs, r.uos, r.lses, r.k_ts)
        )
        unit_do = r.udo.at[slot]
        sums[...] = jnp.zeros_like(sums)
        to_units.wait(slot)

        def turn_delta(i, unused):
            at = aligned(i, tok)
            both = unit_do[at, :].astype(F32) * unit_o[at, :].astype(F32)
            delta[:, at] = jnp.sum(jnp.transpose(both), axis=0, keepdims=True)
            return unused

        lax.fori_loop(0, n, turn_delta, 0)

        def query_step(i, unused_too):
            qi = length // block - 1 - i
            qat = aligned(qi, block)
            qb, dob = unit_q[qat, :], unit_do[qat, :]

            def key_step(kj, dq_t):
                kat = aligned(kj, block)
                scores = dot_nt(unit_k[kat, :], qb) - unit_lse[:, qat]
                probs = jnp.exp(jnp.where(readable(seg_col, seg_row, kj, qi, block), scores, NEGATIVE_FILL))
                d_probs = dot_nt(unit_v[kat, :], dob)
                d_scores = (probs * (d_probs - delta[:, qat])).astype(BF)
                sums[kat, :HEAD_DIM] += dot_nn(d_scores, qb)
                sums[kat, HEAD_DIM:] += dot_nn(probs.astype(BF), dob)
                return dq_t + dot_nn(unit_kt[:, kat], d_scores)

            dq_t = lax.fori_loop(0, qi + 1, key_step, jnp.zeros((HEAD_DIM, block), F32))
            udq[slot, qat, :] = jnp.transpose(dq_t).astype(BF)
            back_dq.start(slot, qi * owners, (qi + 1) * owners)
            udk[slot, qat, :] = sums[qat, :HEAD_DIM].astype(BF)
            udv[slot, qat, :] = sums[qat, HEAD_DIM:].astype(BF)

            @pl.when((slot == 0) & (i == 0))
            def _():
                gate_a.step(1)

            @pl.when((slot == 1) & (i == 0))
            def _():
                gate_a.step(2)
                gate_b.load()
                gate_b.some(nz - 1, 0)

            @pl.when((slot == 1) & (i == 1))
            def _():
                gate_b.step(1)

            return unused_too

        lax.fori_loop(0, length // block, query_step, 0)

        @pl.when(slot == 0)
        def _():
            back_dk.start(0, 0, n)
            back_dv.start(0, 0, n)

        return unused

    def one_copy(i):
        at = aligned(i, chunk)
        return remote(two_own.at[at, :], one_in.at[at, :], tp_s.at[13 + i], tp_r.at[13 + i], place.twin)

    def through_query():
        for copy in load_wq:
            copy.wait()
        back_dq.wait()
        query.gather.start()

        def back_query(i, unused):
            at = aligned(i, chunk)
            for zy in range(n // 2):
                now = dot_nt(dq[at, :], square_block(1, zy)) * HEAD_DIM ** (-0.5)
                two_own[at, zy * blk : (zy + 1) * blk] = now.astype(BF)
            one_copy(i).start()
            return unused

        lax.fori_loop(0, 4, back_query, 0)

    def last_norm(i, gain_sum):
        one_copy(i).wait()

        def some(j, gain_sum):
            at = aligned(i * (chunk // fine) + j, fine)
            x = x_all[at, :].astype(F32)
            d1 = two_own[at, :].astype(F32) + one_in[at, :].astype(F32)
            root = lax.rsqrt(jnp.mean(x * x, axis=-1, keepdims=True) + EPSILON)
            gained = d1 * gain_one[...]
            scaled = x * root
            gain_sum = gain_sum + jnp.sum(d1 * scaled, axis=0, keepdims=True)
            slope = jnp.mean(gained * scaled, axis=-1, keepdims=True)
            mid[at, :] = mid[at, :] + root * (gained - scaled * slope)
            return gain_sum

        return lax.fori_loop(0, chunk // fine, some, gain_sum)

    give = pltpu.make_async_copy(mid.at[:, mine], r.input_grad, loc.at[19])

    def through_first_norm():
        gain_sum = lax.fori_loop(0, 4, last_norm, jnp.zeros((1, width), F32))
        for i in range(n):
            gain_part[1, i] = gain_sum[:, i * (width // n) : (i + 1) * (width // n)]
        spread_gain[1].start()
        give.start()

    def finish_all(*some):
        for line in some:
            line.finish()

    def left_all(*some):
        for line in some:
            line.left_here()

    def sent_all(*some):
        for line in some:
            line.sent()

    def err_here():
        left_err.forward()
        left_err.gone()
        left_err.finish()

    def one_here():
        left_one.gone()
        left_one.finish()

    up_a.gather.start()
    up_b.gather.start()
    left_err.start()

    with jax.named_scope("between"):
        @pl.when(jnp.logical_not(at_end))
        def _():
            for copy in ship:
                copy.wait_recv()
            for slot in range(2):
                turn_into(r.uks.at[slot], r.k_ts.at[slot])
            gate_a.step(0)
            lax.fori_loop(0, 2, one_unit, 0)
            finish_all(down_a, down_b)
            sent_all(down_a, down_b, down_c)
            up_a.load()
            up_a.some(nz - 1, 0)
            gate_b.step(2)
            finish_all(down_c)
            up_a.step(1)
            up_b.load()
            back_dk.start(1, 0, n)
            up_a.step(2)
            up_b.some(nz - 1, 0)
            back_dv.start(1, 0, n)
            through_query()
            up_b.step(1)
            err_here()
            left_all(down_a, down_b)
            finish_all(gate_a)
            left_all(down_c)
            finish_all(gate_b)
            out.load(True, gathered=True)
            up_b.step(2)
            out.some(nz - 1, 0)
            one_here()
            through_first_norm()
            out.step(1)
            query.load(True)
            left_all(gate_a)
            finish_all(up_a)
            out.step(2)
            query.some(nz - 1, 0, 1)
            left_all(gate_b)
            finish_all(up_b)
            query.step(2)
            finish_all(out, query)

    with jax.named_scope("ends"):
        @pl.when(at_end)
        def _():
            gate_b.load()
            gate_b.begin()
            finish_all(down_a, down_b, down_c)
            sent_all(down_a, down_b, down_c)
            up_a.load()
            up_a.begin()
            up_b.load()
            up_b.begin()
            left_all(down_a, down_b, down_c)
            err_here()
            out.load(True, gathered=True)
            out.begin()
            through_query()
            one_here()
            query.load(True)
            query.begin()
            through_first_norm()
            finish_all(gate_a, gate_b)
            left_all(gate_a, gate_b)
            finish_all(up_a, up_b, out, query)

    ffn_copy.wait()
    to_units.sent()
    fetch = pltpu.make_async_copy(r.mix, sums.at[: per * tokens, :], loc.at[11])
    fetch.start()
    fetch.wait()
    for i in range(per):
        at = slice(i * size, (i + 1) * size)
        attended[:, at] = (sums[i * tokens : (i + 1) * tokens, :] + r.ffn_in[:, at].astype(F32)).astype(BF)
    give_mixed = pltpu.make_async_copy(attended, r.out_mixed, loc.at[20])
    give_mixed.start()
    back_dk.wait()
    back_dv.wait()
    for g in range(2):
        spread_gain[g].wait()
        r.gains[g] = jnp.sum(gain_in[g], axis=0)

    @pl.when(at_end)
    def _():
        for copy in ship:
            copy.wait_send()

    @pl.when(jnp.logical_not(at_end))
    def _():
        for slot in range(2):
            for sent in (back_dq, back_dk, back_dv):
                sent.sent(slot)

    give.wait()
    give_mixed.wait()
    for line in lines[3:]:
        line.sent()
    for line in lines[5:]:
        line.left_here()
    for line in lines:
        line.arrived()


def results_kernel(rows, factors, *refs):
    count = len(rows)
    ins, outs, held, sems = refs[:count], refs[count : 2 * count], refs[2 * count : -1], refs[-1]
    come = [pltpu.make_async_copy(ins[i].at[: rows[i]], held[2 * i], sems.at[0, i]) for i in range(count)]
    go = [pltpu.make_async_copy(held[2 * i + 1], outs[i], sems.at[1, i]) for i in range(count)]
    for copy in come:
        copy.start()
    for i, factor in enumerate(factors):
        come[i].wait()
        if factor is not None:
            held[2 * i + 1][...] = held[2 * i][...].astype(F32) * factor
        go[i].start()
    for copy in go:
        copy.wait()


def results(*some):
    anywhere = pl.BlockSpec(memory_space=pl.ANY)
    arrays, rows, factors = zip(*some)
    shapes = [vm((k, *a.shape[1:]), a.dtype if f is None else F32) for a, k, f in some]
    held = []
    for (a, k, f), shape in zip(some, shapes):
        held += [pltpu.VMEM((k, *a.shape[1:]) if f is not None else (8, LANE), a.dtype), pltpu.VMEM(shape.shape, shape.dtype)]

    def kernel(*refs):
        count = len(rows)
        refs = list(refs)
        for i, factor in enumerate(factors):
            if factor is None:
                refs[2 * count + 2 * i] = refs[2 * count + 2 * i + 1]
        results_kernel(rows, factors, *refs)

    return pl.pallas_call(
        kernel,
        out_shape=shapes,
        in_specs=[anywhere] * len(arrays),
        out_specs=[anywhere] * len(arrays),
        scratch_shapes=[*held, pltpu.SemaphoreType.DMA((2, len(arrays)))],
        compiler_params=pltpu.CompilerParams(vmem_limit_bytes=VMEM_GRANT),
        name="results",
    )(*arrays)


def fast_device(
    n, inputs, segments, keys, values, attn_gain, query_weight, out_weight, ffn_gain, gate_weight, up_weight, down_weight,
    cotangent,
):
    rows, tok, half = inputs.shape
    tokens, width, ff = rows * tok, query_weight.shape[0], gate_weight.shape[1]
    heads, length = half // HEAD_DIM, n * tok
    geo = (n, rows, tok, width, half, heads, length)
    blk, nz, size = 2 * width // n, n // PLANE, 2 * LANE
    cols = -(-ff // size) * LANE
    firsts = (0, size, 3 * size, cols)
    thirds = [(firsts[i], firsts[i + 1] - firsts[i]) for i in range(3)]
    halves = [(0, firsts[2]), (firsts[2], cols - firsts[2])]
    cuts = tuple((kind, *cut) for kind, parts in enumerate((thirds, halves, halves)) for cut in parts)
    sizes = (ff, cols, cuts)
    square = half // 2
    n_lines = len(cuts) + 2
    dma = pltpu.SemaphoreType.DMA
    anywhere, here = pl.BlockSpec(memory_space=pl.ANY), pl.BlockSpec(memory_space=pltpu.VMEM)

    def pieces(letter, shapes):
        return {letter + str(i): shape for i, shape in shapes}

    tall, flat_left = vm((2 * cols, blk // 2), F32), vm((PLANE * tokens, width // 2), BF)
    sum_square = vm((nz + 1, blk, square), BF)
    outs = dict(
        out_mixed=vm((tokens, half), BF),
        input_grad=vm((tokens, half), F32),
        d_keys=vm((tokens, half), BF),
        d_values=vm((tokens, half), BF),
        gains=vm((2, 1, width // n), F32),
        out_down=tall,
        out_gate=tall,
        out_up=tall,
        out_out=vm((blk // 2, half), F32),
        out_query=vm((blk // 2, half), F32),
        mix=vm((half // size * tokens, size), F32),
        l_err=flat_left,
        l_one=flat_left,
        g_out=sum_square,
        g_query=sum_square,
        **pieces("m", [(i, vm((PLANE * tokens, w), BF)) for i, (kind, _, w) in enumerate(cuts) if kind > 0]),
        **pieces("g", [(i, vm((nz + 1, blk, w), BF)) for i, (_, _, w) in enumerate(cuts)]),
    )
    row = pltpu.VMEM((1, length), F32)
    act, own = pltpu.VMEM((tokens, width), BF), pltpu.VMEM((tokens, half), BF)
    split = pltpu.VMEM((2, tokens, width // 2), BF)
    hid = pltpu.VMEM((tokens, 2 * cols), BF)
    gain = pltpu.VMEM((2, n, 1, width // n), F32)
    left = pltpu.VMEM((PLANE * tokens, width // 2), BF)
    two = pltpu.VMEM((2, length, HEAD_DIM), BF)
    move, move_square = (pltpu.VMEM((nz - 1, blk, c), BF) for c in (cols, square))
    total, total_square = (pltpu.VMEM((blk, c), F32) for c in (cols, square))
    taken = pltpu.VMEM((PLANE * tokens, square), BF)
    scratch = dict(
        mid=pltpu.VMEM((tokens, width), F32),
        x_all=act, cot_all=act, two_norm=act, two_own=act, two_in=act, one_in=act, mixed=split, err=split, one=split,
        wbuf=pltpu.VMEM((8, size, width), BF),
        attended=own, dq=own, ffn_in=own, hidden=hid, d_gate=hid, d_up=hid,
        sums=pltpu.VMEM((length, size), F32),
        uqs=two, uks=two, uvs=two, uos=two, udo=two, udq=two, udk=two, udv=two,
        delta=row, seg_row=row, lses=pltpu.VMEM((2, 1, length), F32),
        seg_all=pltpu.VMEM((n, 1, tok), segments.dtype),
        seg_col=pltpu.VMEM((length, LANE), F32),
        k_ts=pltpu.VMEM((2, HEAD_DIM, length), BF),
        gain_part=gain, gain_in=gain,
        s_first=move, s_second=move, s_out=move_square, s_query=move_square,
        t_first=total, t_second=total, t_out=total_square, t_query=total_square,
        turned=pltpu.VMEM((cols, blk), F32),
        mv=pltpu.VMEM((PLANE * tokens, cols), BF), mv_out=taken, mv_query=taken,
        lv_one=left, lv_two=left,
        acc=total,
        stage=pltpu.VMEM((blk, cols), BF),
        tp_s=dma((17,)), tp_r=dma((17,)), a_s=dma((7,)), a_r=dma((7,)),
        me_s=dma((n_lines, 3)), me_r=dma((n_lines, 3)), le_s=dma((4, 3)), le_r=dma((4, 3)),
        c_s=dma((n_lines, nz - 1)), c_r=dma((n_lines, nz + 1)),
        e_s=dma((n_lines,)), e_r=dma((n_lines,)), e_l=dma((n_lines,)),
        sh_s=dma((5,)), sh_r=dma((5,)), u_s=dma((1,)), u_r=dma((2,)), u_l=dma((2,)),
        f_s=dma((3, 2)), f_r=dma((3,)), f_l=dma((3, 2)),
        loc=dma((21,)), g_loc=dma((n_lines,)), l_loc=dma((4,)), work_sem=dma((3,)),
        w_sem=dma((4, 2, 2)), tail_sem=dma((4, 2, 2)), o_sem=dma((4, n // 2)),
    )
    names = (*outs, *scratch)

    def flat(a):
        return a.reshape(tokens, half)

    segs = segments.reshape(rows, 1, tok)
    got = pl.pallas_call(
        functools.partial(layer_kernel, geo, sizes, names),
        out_shape=list(outs.values()),
        in_specs=[anywhere] * 10 + [here] * 2,
        out_specs=[here if i == 4 else anywhere for i in range(len(outs))],
        scratch_shapes=list(scratch.values()),
        compiler_params=pltpu.CompilerParams(
            collective_id=0, has_side_effects=True, vmem_limit_bytes=VMEM_GRANT
        ),
        name="layer",
    )(
        flat(inputs), flat(cotangent), flat(keys), flat(values), segs, gate_weight.T, up_weight.T, down_weight.T,
        out_weight, query_weight, attn_gain.reshape(1, width), ffn_gain.reshape(1, width),
    )
    got = types.SimpleNamespace(**dict(zip(outs, got)))

    def shaped(a):
        return a.reshape(rows, tok, half)

    d_keys, d_values, g_query, g_down, g_gate, g_up, input_grad, mixed, g_out = results(
        (got.d_keys, tokens, 1.0),
        (got.d_values, tokens, 1.0),
        (got.out_query, blk // 2, HEAD_DIM ** (-0.5)),
        (got.out_down, ff, None),
        (got.out_gate, ff, None),
        (got.out_up, ff, None),
        (got.input_grad, tokens, None),
        (got.out_mixed, tokens, None),
        (got.out_out, blk // 2, None),
    )
    return (
        shaped(mixed),
        shaped(input_grad),
        shaped(d_keys),
        shaped(d_values),
        got.gains[1, 0],
        g_query,
        g_out,
        got.gains[0, 0],
        g_gate.T,
        g_up.T,
        g_down.T,
    )


def inverse_root(stream):
    return lax.rsqrt(jnp.mean(stream * stream, axis=-1, keepdims=True) + EPSILON)


def key_mask(doc_start, query_pos, begin, row_count):
    key_pos = begin + jnp.arange(row_count, dtype=jnp.int32)
    earlier = key_pos[None, None, :] <= query_pos[None, :, None]
    same_doc = key_pos[None, None, :] >= doc_start[:, :, None]
    return (earlier & same_doc)[:, None]


def per_device(
    inputs,
    segments,
    keys,
    values,
    attn_gain,
    query_weight,
    out_weight,
    ffn_gain,
    gate_weight,
    up_weight,
    down_weight,
    cotangent,
):
    batch_rows, local_tokens, half_width = inputs.shape
    local_heads = half_width // HEAD_DIM
    seq_devices = lax.axis_size("seq")
    row_length = local_tokens * seq_devices
    seq_index = lax.axis_index("seq")
    tp_index = lax.axis_index("tp")
    query_scale = HEAD_DIM ** (-0.5)
    bfloat = jnp.bfloat16
    single = jnp.float32
    whole = lax.all_gather(inputs, "tp", axis=2, tiled=True).astype(single)
    root_one = inverse_root(whole)
    scaled_one = whole * root_one
    normed_one = (scaled_one * attn_gain).astype(bfloat)
    query = (
        jnp.einsum("rtd,de->rte", normed_one, query_weight, preferred_element_type=single)
        * query_scale
    ).astype(bfloat)
    query_heads = query.reshape(batch_rows, local_tokens, local_heads, HEAD_DIM)
    bins = jnp.arange(CUTS + 1, dtype=jnp.int32)
    onehot = (segments[:, :, None] == bins[None, None, :]).astype(single)
    totals = lax.psum(jnp.sum(onehot, axis=1), "seq")
    ends = jnp.cumsum(totals, axis=-1)
    before = ends - totals
    doc_start = jnp.sum(onehot * before[:, None, :], axis=-1).astype(jnp.int32)
    query_pos = seq_index * local_tokens + jnp.arange(local_tokens, dtype=jnp.int32)
    first_needed = jnp.min(doc_start)
    last_needed = seq_index * local_tokens + local_tokens - 1
    start_state = (
        jnp.full((batch_rows, local_heads, local_tokens), NEGATIVE_FILL, single),
        jnp.zeros((batch_rows, local_heads, local_tokens), single),
        jnp.zeros((batch_rows, local_heads, local_tokens, HEAD_DIM), single),
    )
    key_piece = lax.all_gather(keys, "seq", axis=1, tiled=True)
    value_piece = lax.all_gather(values, "seq", axis=1, tiled=True)
    piece_rows = key_piece.shape[1]
    fold_key_block = math.gcd(piece_rows, 512)

    def fold_step(block_index, state):
        running_max, running_sum, running_out = state
        begin = block_index * fold_key_block

        def fold_work(unused):
            key_heads = lax.dynamic_slice_in_dim(
                key_piece, block_index * fold_key_block, fold_key_block, 1
            ).reshape(batch_rows, fold_key_block, local_heads, HEAD_DIM)
            value_heads = lax.dynamic_slice_in_dim(
                value_piece, block_index * fold_key_block, fold_key_block, 1
            ).reshape(batch_rows, fold_key_block, local_heads, HEAD_DIM)
            scores = jnp.einsum(
                "rqhe,rkhe->rhqk", query_heads, key_heads, preferred_element_type=single
            )
            allowed = key_mask(doc_start, query_pos, begin, fold_key_block)
            scores = jnp.where(allowed, scores, NEGATIVE_FILL)
            new_max = jnp.maximum(running_max, jnp.max(scores, axis=-1))
            weights = jnp.where(allowed, jnp.exp(scores - new_max[..., None]), 0.0)
            decay = jnp.exp(running_max - new_max)
            new_sum = running_sum * decay + jnp.sum(weights, axis=-1)
            new_out = running_out * decay[..., None] + jnp.einsum(
                "rhqk,rkhe->rhqe",
                weights.astype(bfloat),
                value_heads,
                preferred_element_type=single,
            )
            return (new_max, new_sum, new_out)

        def keep_state(unused):
            return (running_max, running_sum, running_out)

        needed = (begin <= last_needed) & (begin + fold_key_block - 1 >= first_needed)
        return lax.cond(needed, fold_work, keep_state, 0)

    running_max, running_sum, running_out = lax.fori_loop(
        0, piece_rows // fold_key_block, fold_step, start_state
    )
    log_total = running_max + jnp.log(running_sum)
    attended = running_out / running_sum[..., None]
    attended_low = (
        attended.transpose(0, 2, 1, 3).reshape(batch_rows, local_tokens, half_width).astype(bfloat)
    )
    branch = jnp.einsum("rth,dh->rtd", attended_low, out_weight, preferred_element_type=single)
    middle = whole + lax.psum(branch.astype(jnp.bfloat16), "tp").astype(jnp.float32)
    middle_share = lax.dynamic_slice_in_dim(middle, tp_index * half_width, half_width, 2)
    root_two = inverse_root(middle)
    scaled_two = middle * root_two
    normed_two = (scaled_two * ffn_gain).astype(bfloat)
    gate = jnp.einsum("rtd,df->rtf", normed_two, gate_weight, preferred_element_type=single)
    up_proj = jnp.einsum("rtd,df->rtf", normed_two, up_weight, preferred_element_type=single)
    sigma = jax.nn.sigmoid(gate)
    activated = gate * sigma
    hidden = (activated * up_proj).astype(bfloat)
    ffn_part = jnp.einsum("rtf,df->rtd", hidden, down_weight, preferred_element_type=single)
    output = (
        middle_share
        + lax.psum_scatter(
            ffn_part.astype(jnp.bfloat16), "tp", scatter_dimension=2, tiled=True
        ).astype(jnp.float32)
    ).astype(bfloat)
    grad_out = lax.all_gather(cotangent, "tp", axis=2, tiled=True)
    d_hidden = jnp.einsum("rtd,df->rtf", grad_out, down_weight, preferred_element_type=single)
    d_gate = (d_hidden * up_proj * sigma * (1.0 + gate * (1.0 - sigma))).astype(bfloat)
    d_up = (d_hidden * activated).astype(bfloat)
    d_two_part = jnp.einsum(
        "rtf,df->rtd", d_gate, gate_weight, preferred_element_type=single
    ) + jnp.einsum("rtf,df->rtd", d_up, up_weight, preferred_element_type=single)
    d_two = lax.psum(d_two_part.astype(jnp.bfloat16), "tp").astype(jnp.float32)
    gained_two = d_two * ffn_gain
    d_middle = (
        grad_out.astype(single)
        + root_two * gained_two
        - middle * root_two**3 * jnp.mean(gained_two * middle, axis=-1, keepdims=True)
    )
    normed_rows = normed_two
    gate_term = jnp.einsum("rtd,rtf->df", normed_rows, d_gate, preferred_element_type=single)
    up_term = jnp.einsum("rtd,rtf->df", normed_rows, d_up, preferred_element_type=single)
    down_term = jnp.einsum("rtd,rtf->df", grad_out, hidden, preferred_element_type=single)
    gain_term = jnp.sum(d_two * scaled_two, axis=(0, 1))
    gate_grad, up_grad, down_grad, ffn_gain_grad = lax.psum_scatter(
        (gate_term, up_term, down_term, gain_term), "seq", scatter_dimension=0, tiled=True
    )
    error = d_middle.astype(bfloat)
    d_attended = jnp.einsum("rtd,dh->rth", error, out_weight, preferred_element_type=single).astype(
        bfloat
    )
    d_heads = d_attended.reshape(batch_rows, local_tokens, local_heads, HEAD_DIM)
    carried = jnp.einsum("rqhe,rhqe->rhq", d_heads.astype(single), attended)
    key_all, value_all = (
        lax.all_gather(keys, "seq", axis=1, tiled=True),
        lax.all_gather(values, "seq", axis=1, tiled=True),
    )
    key_block = math.gcd(row_length, 512)

    def block_terms(begin):
        key_heads = lax.dynamic_slice_in_dim(key_all, begin, key_block, 1).reshape(
            batch_rows, key_block, local_heads, HEAD_DIM
        )
        value_heads = lax.dynamic_slice_in_dim(value_all, begin, key_block, 1).reshape(
            batch_rows, key_block, local_heads, HEAD_DIM
        )
        scores = jnp.einsum(
            "rqhe,rkhe->rhqk", query_heads, key_heads, preferred_element_type=single
        )
        allowed = key_mask(doc_start, query_pos, begin, key_block)
        probs = jnp.where(
            allowed, jnp.exp(jnp.where(allowed, scores, NEGATIVE_FILL) - log_total[..., None]), 0.0
        )
        d_probs = jnp.einsum("rqhe,rkhe->rhqk", d_heads, value_heads, preferred_element_type=single)
        d_scores = (probs * (d_probs - carried[..., None])).astype(bfloat)
        query_part = jnp.einsum(
            "rhqk,rkhe->rhqe", d_scores, key_heads, preferred_element_type=single
        )
        return (probs, d_scores, query_part)

    query_zero = jnp.zeros((batch_rows, local_heads, local_tokens, HEAD_DIM), single)

    def back_step(block_index, state):
        d_query, key_terms, value_terms = state
        begin = block_index * key_block

        def back_work(unused):
            probs, d_scores, query_part = block_terms(begin)
            value_part = jnp.einsum(
                "rhqk,rqhe->rkhe", probs.astype(bfloat), d_heads, preferred_element_type=single
            )
            key_part = jnp.einsum(
                "rhqk,rqhe->rkhe", d_scores, query_heads, preferred_element_type=single
            )
            return (
                query_part,
                key_part.reshape(batch_rows, key_block, half_width),
                value_part.reshape(batch_rows, key_block, half_width),
            )

        def skip_block(unused):
            empty_rows = jnp.zeros((batch_rows, key_block, half_width), single)
            return (jnp.zeros_like(d_query), empty_rows, empty_rows)

        needed = (begin <= last_needed) & (begin + key_block - 1 >= first_needed)
        query_part, key_part, value_part = lax.cond(needed, back_work, skip_block, 0)
        return (
            d_query + query_part,
            lax.dynamic_update_slice_in_dim(key_terms, key_part, begin, 1),
            lax.dynamic_update_slice_in_dim(value_terms, value_part, begin, 1),
        )

    back_start = (
        query_zero,
        jnp.zeros((batch_rows, row_length, half_width), single),
        jnp.zeros((batch_rows, row_length, half_width), single),
    )
    d_query, key_terms, value_terms = lax.fori_loop(
        0, row_length // key_block, back_step, back_start
    )
    key_grad, value_grad = (
        lax.psum_scatter(key_terms, "seq", scatter_dimension=1, tiled=True),
        lax.psum_scatter(value_terms, "seq", scatter_dimension=1, tiled=True),
    )
    d_query_rows = (
        d_query.transpose(0, 2, 1, 3).reshape(batch_rows, local_tokens, half_width).astype(bfloat)
    )
    d_one_part = (
        jnp.einsum("rte,de->rtd", d_query_rows, query_weight, preferred_element_type=single)
        * query_scale
    )
    d_one = lax.psum(d_one_part.astype(jnp.bfloat16), "tp").astype(jnp.float32)
    gained_one = d_one * attn_gain
    d_whole = (
        d_middle
        + root_one * gained_one
        - whole * root_one**3 * jnp.mean(gained_one * whole, axis=-1, keepdims=True)
    )
    input_grad = lax.dynamic_slice_in_dim(d_whole, tp_index * half_width, half_width, 2)
    normed_rows = normed_one
    query_term = (
        jnp.einsum("rtd,rte->de", normed_rows, d_query_rows, preferred_element_type=single)
        * query_scale
    )
    out_term = jnp.einsum("rtd,rth->dh", error, attended_low, preferred_element_type=single)
    gain_term = jnp.sum(d_one * scaled_one, axis=(0, 1))
    query_grad, out_grad, attn_gain_grad = lax.psum_scatter(
        (query_term, out_term, gain_term), "seq", scatter_dimension=0, tiled=True
    )
    return (
        output,
        input_grad,
        key_grad,
        value_grad,
        attn_gain_grad,
        query_grad,
        out_grad,
        ffn_gain_grad,
        gate_grad,
        up_grad,
        down_grad,
    )


def solution(mesh):
    in_specs = (
        P(None, "seq", "tp"),
        P(None, "seq"),
        P(None, "seq", "tp"),
        P(None, "seq", "tp"),
        P(),
        P(None, "tp"),
        P(None, "tp"),
        P(),
        P(None, "tp"),
        P(None, "tp"),
        P(None, "tp"),
        P(None, "seq", "tp"),
    )
    out_specs = (
        P(None, "seq", "tp"),
        P(None, "seq", "tp"),
        P(None, "seq", "tp"),
        P(None, "seq", "tp"),
        P("seq"),
        P("seq", "tp"),
        P("seq", "tp"),
        P("seq"),
        P("seq", "tp"),
        P("seq", "tp"),
        P("seq", "tp"),
    )
    n = mesh.shape["seq"]

    def step(inputs, *others):
        rows, tok, half = inputs.shape
        units = rows * (half // HEAD_DIM)
        if units == n == PLANE * PLANE and tok == LANE and mesh.shape["tp"] == 2 and -(-others[7].shape[1] // (2 * LANE)) % 2:
            return fast_device(n, inputs, *others)
        return per_device(inputs, *others)

    return jax.shard_map(
        step, mesh=mesh, in_specs=in_specs, out_specs=out_specs, check_vma=False
    )
```

```python
import functools
import math
import types

import jax
import jax.numpy as jnp
from jax import lax
from jax.experimental import pallas as pl
from jax.experimental.pallas import tpu as pltpu
from jax.sharding import PartitionSpec as P

HEAD_DIM = 128
CUTS = 12


EPSILON = 1e-06
NEGATIVE_FILL = -1e30

MESH = pl.DeviceIdType.MESH
BF = jnp.bfloat16
F32 = jnp.float32
VMEM_GRANT = 63 << 20
PLANE = 4
LANE = 128


def dot_nn(a, b):
    return lax.dot_general(a, b, (((1,), (0,)), ((), ())), preferred_element_type=F32)


def dot_nt(a, b):
    return lax.dot_general(a, b, (((1,), (1,)), ((), ())), preferred_element_type=F32)


def dot_tn(a, b):
    return lax.dot_general(a, b, (((0,), (0,)), ((), ())), preferred_element_type=F32)


def aligned(index, size):
    return pl.ds(pl.multiple_of(index * size, size), size)


class Place:
    def __init__(self, n):
        self.n = n
        self.s = lax.axis_index("seq")
        self.t = lax.axis_index("tp")
        self.z = self.s // PLANE
        self.p = lax.rem(self.s, PLANE)
        self.y = self.p // 2
        self.c = lax.rem(self.p, 2)
        base = self.z * PLANE
        self.core_p = self.y * 2 + 1 - self.c
        self.side_p = (1 - self.y) * 2 + self.c
        self.cross_p = (1 - self.y) * 2 + 1 - self.c
        self.core = (base + self.core_p, self.t)
        self.side = (base + self.side_p, self.t)
        self.cross = (base + self.cross_p, self.t)
        self.twin = (self.s, 1 - self.t)

    def other(self, k):
        return lax.rem(self.s + k, self.n)

    def enter(self):
        barrier = pltpu.get_barrier_semaphore()

        def greet(k, unused):
            pl.semaphore_signal(barrier, inc=1, device_id=(self.other(k), self.t), device_id_type=MESH)
            return unused

        lax.fori_loop(1, self.n, greet, 0)
        pl.semaphore_signal(barrier, inc=1, device_id=self.twin, device_id_type=MESH)
        pl.semaphore_wait(barrier, self.n)


def remote(src, dst, send, recv, device):
    return pltpu.make_async_remote_copy(
        src_ref=src, dst_ref=dst, send_sem=send, recv_sem=recv, device_id=device, device_id_type=MESH
    )


class Spread:
    def __init__(self, place, src, dst, send, recv, local, bulk):
        self.place, self.src, self.dst, self.send, self.recv, self.local = place, src, dst, send, recv, local
        self.bulk = bulk

    def copy(self, k):
        place = self.place
        d = place.other(k)
        return remote(self.src(d), self.dst(), self.send, self.recv, (d, place.t))

    def own(self):
        return pltpu.make_async_copy(self.src(self.place.s), self.dst(), self.local)

    def start(self):
        self.own().start()

        def one(k, unused):
            self.copy(k).start()
            return unused

        lax.fori_loop(1, self.place.n, one, 0)

    def start_to(self, d, unused):
        k = lax.rem(d - self.place.s + self.place.n, self.place.n)

        @pl.when(k == 0)
        def _():
            self.own().start()

        @pl.when(k != 0)
        def _():
            self.copy(k).start()

        return unused

    def wait(self):
        self.own().wait()
        remote(self.bulk, self.bulk, self.send, self.recv, self.place.core).wait()


def attention_masks(seg_all, seg_row, seg_col, n, tok):
    def one(i, unused):
        piece = seg_all[i].astype(F32)
        seg_row[:, aligned(i, tok)] = piece
        seg_col[aligned(i, tok), :] = jnp.transpose(jnp.broadcast_to(piece, (tok, tok)))
        return unused

    lax.fori_loop(0, n, one, 0)


def readable(seg_col, seg_row, key_block, query_block, block):
    key_seg = seg_col[aligned(key_block, block), :]
    key_seg = jnp.concatenate([key_seg] * (block // LANE), axis=1)
    query_seg = seg_row[:, aligned(query_block, block)]
    key_pos = key_block * block + lax.broadcasted_iota(jnp.int32, (block, block), 0)
    query_pos = query_block * block + lax.broadcasted_iota(jnp.int32, (block, block), 1)
    return (key_seg == query_seg) & (key_pos <= query_pos)


def split_rows(whole, split, n):
    blk = whole.shape[1] * 2 // n
    for zy in range(n // 2):
        z, y = divmod(zy, 2)
        split[y, :, z * blk : (z + 1) * blk] = whole[:, zy * blk : (zy + 1) * blk]


class Plane:
    def __init__(self, place, split, left, send, recv, local, tokens):
        self.place, self.tokens, self.left = place, tokens, left
        to = left.at[aligned(place.p, tokens), :]
        self.own = pltpu.make_async_copy(split.at[place.y], to, local)
        self.to_core = remote(split.at[place.y], to, send.at[0], recv.at[0], place.core)
        self.to_side = remote(split.at[1 - place.y], to, send.at[1], recv.at[1], place.side)
        passed = left.at[aligned(place.side_p, tokens), :]
        self.on = remote(passed, passed, send.at[2], recv.at[2], place.core)

    def start(self):
        self.to_side.start()
        self.own.start()
        self.to_core.start()

    def forward(self):
        self.to_side.wait()
        self.on.start()

    def gone(self):
        self.own.wait()
        self.to_core.wait_send()

    def finish(self):
        self.to_core.wait_recv()
        self.on.wait()


def vm(shape, dtype):
    return jax.ShapeDtypeStruct(shape, dtype)


class Gather:
    def __init__(self, place, whole, stride, first, land, send, recv, local, tokens):
        cols = land.shape[1]
        to = land.at[aligned(place.p, tokens), :]

        def half(c):
            return whole.at[:, pl.ds(pl.multiple_of(c * stride + first, LANE), cols)]

        c = place.c
        self.own = pltpu.make_async_copy(half(c), to, local)
        self.away = [
            remote(half(c), to, send, recv, place.side),
            remote(half(1 - c), to, send, recv, place.cross),
            remote(half(1 - c), to, send, recv, place.core),
        ]
        bulk = land.at[: (PLANE - 1) * tokens, :]
        self.all = remote(bulk, bulk, send, recv, place.core)

    def start(self):
        self.own.start()
        for copy in self.away:
            copy.start()

    def wait(self):
        self.own.wait()
        self.all.wait()


class Line:
    def __init__(self, place, nz, blk, gather, land, left, lv, mv, move, got, total, out, turned, sems, work):
        self.place, self.nz, self.blk, self.gather = place, nz, blk, gather
        self.land, self.left, self.move, self.got, self.total, self.out = land, left, move, got, total, out
        self.turned = turned
        self.cols = land.shape[1]
        self.lv, self.mv = lv, mv
        self.acc, self.stage, self.load_sem = work
        self.send, self.recv, self.end_s, self.end_r, self.end_l = sems
        self.at_end = (place.z == 0) | (place.z == nz - 1)

    def load(self, left_too=False, gathered=False):
        if not gathered:
            self.gather.wait()
        copies = []
        if self.land is not self.mv:
            copies.append(pltpu.make_async_copy(self.land, self.mv, self.load_sem.at[0]))
        if left_too and self.left is not self.lv:
            copies.append(pltpu.make_async_copy(self.left, self.lv, self.load_sem.at[1]))
        for copy in copies:
            copy.start()
        for copy in copies:
            copy.wait()

    def product(self, b):
        tile = 2 * LANE

        def one(i, unused):
            at = pl.ds(pl.multiple_of(jnp.minimum(i * tile, self.cols - tile), LANE), tile)
            self.acc[:, at] = dot_tn(self.lv[:, aligned(b, self.blk)], self.mv[:, at])
            return unused

        lax.fori_loop(0, -(-self.cols // tile), one, 0)

    def take(self, slot):
        self.arrival(slot).wait_recv()
        copy = pltpu.make_async_copy(self.got.at[slot], self.stage.at[:, : self.cols], self.load_sem.at[2])
        copy.start()
        copy.wait()
        return self.stage[:, : self.cols].astype(F32)

    def arrival(self, slot):
        return remote(self.move.at[0], self.got.at[slot], self.send.at[0], self.recv.at[slot], self.place.core)

    def route(self, j):
        z, nz = self.place.z, self.nz
        b = jnp.where(z < nz // 2, nz - 1 - j, j)
        b = jnp.where((j == nz - 2) & (z == 1), 0, b)
        b = jnp.where((j == nz - 2) & (z == nz - 2), nz - 1, b)
        b = jnp.where(j == nz - 1, z, b)
        up = b > z
        to = jnp.where(up, z + 1, z - 1)
        slot_in = jnp.where(up, b - z, nz - z + b)
        slot_out = jnp.where(up, b - to, nz - to + b)
        keep = jnp.where(up, b - 1, b)
        last = jnp.where(up, z == 0, z == nz - 1)
        device = (to * PLANE + self.place.p, self.place.t)

        def out():
            return remote(self.move.at[keep], self.got.at[slot_out], self.send.at[keep], self.recv.at[slot_out], device)

        return b, slot_in, keep, last, out

    def step(self, j):
        b, slot_in, keep, last, out = self.route(j)
        self.product(b)
        sends = j < self.nz - 1

        @pl.when(jnp.logical_not(sends))
        def _():
            self.total[...] = self.acc[:, : self.cols]

        @pl.when(sends & last)
        def _():
            self.move[keep] = self.acc[:, : self.cols].astype(BF)

        @pl.when(sends & jnp.logical_not(last))
        def _():
            self.move[keep] = (self.acc[:, : self.cols] + self.take(slot_in)).astype(BF)

        @pl.when(sends)
        def _():
            out().start()

    def steps(self, low, high):
        def one(j, unused):
            self.step(j)
            return unused

        lax.fori_loop(low, high, one, 0)

    def some(self, *order):
        def one(i, unused):
            j = order[0]
            for k, then in enumerate(order):
                j = jnp.where(i == k, then, j)
            self.step(j)
            return unused

        lax.fori_loop(0, len(order), one, 0)

    def begin(self):
        self.steps(0, self.nz)

    def from_end(self):
        self.steps(jnp.where(self.at_end, 0, self.nz - 1), self.nz)

    def between(self, low, high):
        pl.when(jnp.logical_not(self.at_end))(lambda: self.steps(low, high))

    def sent(self):
        def one(j, unused):
            self.route(j)[4]().wait_send()
            return unused

        lax.fori_loop(0, self.nz - 1, one, 0)

    def end(self, c):
        half = self.blk // 2
        mine = self.place.c
        if self.turned is None:
            return self.out.at[:, aligned(mine, self.cols)], self.total.at[aligned(c, half), :]
        turned, stride, first = self.turned
        to = self.out.at[pl.ds(pl.multiple_of(mine * stride + first, LANE), self.cols), :]
        return to, turned.at[first : first + self.cols, aligned(c, half)]

    def away(self):
        to, theirs = self.end(1 - self.place.c)
        return remote(theirs, to, self.end_s, self.end_r, self.place.core)

    def here(self):
        to, mine = self.end(self.place.c)
        return pltpu.make_async_copy(mine, to, self.end_l)

    def finish(self):
        z, nz = self.place.z, self.nz

        @pl.when(z > 0)
        def _():
            self.total[...] += self.take(0)

        @pl.when(z < nz - 1)
        def _():
            self.total[...] += self.take(nz)

        if self.turned is not None:
            turned, _, first = self.turned
            turned[first : first + self.cols, :] = jnp.transpose(self.total[...])
        self.away().start()
        self.here().start()

    def left_here(self):
        self.away().wait_send()
        self.here().wait()

    def arrived(self):
        self.away().wait_recv()


class Weights:
    def __init__(self, weights, buffers, sems, tail_sems, phase, first, cols, ff):
        self.weights, self.buffers, self.sems, self.tail_sems, self.phase = weights, buffers, sems, tail_sems, phase
        self.first, self.each = first, len(weights)
        self.size = buffers.shape[1]
        self.cols = cols
        self.regular = 2 * (cols // self.size)
        self.rest = cols % self.size
        self.rest_two = ff - cols - cols // self.size * self.size

    def slot(self, i, w):
        return self.first + lax.rem(i + self.phase, 2) * self.each + w

    def copies(self, i):
        at = pl.ds(pl.multiple_of(lax.rem(i, 2) * self.cols + i // 2 * self.size, LANE), self.size)
        return [
            pltpu.make_async_copy(ref.at[at, :], self.buffers.at[self.slot(i, w)], self.sems.at[lax.rem(i, 2), w])
            for w, ref in enumerate(self.weights)
        ]

    def tail(self):
        first = self.cols // self.size * self.size
        copies = []
        for w, ref in enumerate(self.weights):
            to = self.buffers.at[self.slot(self.regular, w)]
            copies += [
                pltpu.make_async_copy(ref.at[pl.ds(first, self.rest), :], to.at[pl.ds(0, self.rest), :], self.tail_sems.at[0, w]),
                pltpu.make_async_copy(
                    ref.at[pl.ds(self.cols + first, self.rest_two), :],
                    to.at[pl.ds(self.rest, self.rest_two), :],
                    self.tail_sems.at[1, w],
                ),
            ]
        return copies

    def begin(self, blocks=1):
        self.begun = blocks
        for i in range(blocks):
            for copy in self.copies(i):
                copy.start()

    def run(self, work, after=()):
        first = self.cols // self.size * self.size
        filled = self.rest + self.rest_two

        def one(i, unused):
            is_tail = i == self.regular

            @pl.when((i + 1 < self.regular) & (i + 1 >= self.begun))
            def _():
                for copy in self.copies(i + 1):
                    copy.start()

            @pl.when(i + 1 == self.regular)
            def _():
                for copy in self.tail():
                    copy.start()

            @pl.when(jnp.logical_not(is_tail))
            def _():
                for copy in self.copies(i):
                    copy.wait()

            @pl.when(is_tail)
            def _():
                for copy in self.tail():
                    copy.wait()
                for w in range(self.each):
                    slot = self.slot(self.regular, w)
                    self.buffers[slot, filled:, :] = jnp.zeros((self.size - filled, self.buffers.shape[2]), BF)

            at = lax.rem(i, 2) * self.cols + i // 2 * self.size
            columns = [
                pl.ds(pl.multiple_of(jnp.where(is_tail, tail_at, at + k * LANE), LANE), LANE)
                for k, tail_at in enumerate((first, self.cols + first))
            ]
            work([self.slot(i, w) for w in range(self.each)], columns)
            for at_block, things in after:
                pl.when(i == at_block)(lambda things=things: [thing() for thing in things] and None)
            return unused

        lax.fori_loop(0, self.regular + 1, one, 0)


class Units:
    def __init__(self, place, nz, heads, tok):
        self.place, self.nz, self.heads, self.tok = place, nz, heads, tok
        z, s = place.z, place.s
        self.at_end = (z == 0) | (z == nz - 1)
        self.second = jnp.where(z < nz // 2, s - PLANE, s + PLANE)
        self.near = (jnp.where(z == 0, s + PLANE, s - PLANE), place.t)

    def host(self, u):
        z = u // PLANE
        inner = jnp.clip(z, 1, self.nz - 2)
        return inner * PLANE + lax.rem(u, PLANE), jnp.where(inner == z, 0, 1)

    def unit(self, slot):
        return jnp.where(slot == 0, self.place.s, self.second)

    def home(self, ref, u):
        return ref.at[aligned(u // self.heads, self.tok), aligned(lax.rem(u, self.heads), HEAD_DIM)]


class ToUnits:
    def __init__(self, units, src, land, send, recv, local):
        self.units, self.src, self.land, self.send, self.recv, self.local = units, src, land, send, recv, local
        self.n, self.s, self.t, self.tok = units.place.n, units.place.s, units.place.t, units.tok

    def away(self, u):
        host, slot = self.units.host(u)
        to = self.land.at[slot, aligned(self.s, self.tok), :]
        return remote(self.units.home(self.src, u), to, self.send, self.recv.at[slot], (host, self.t))

    def here(self, u):
        slot = self.units.host(u)[1]
        to = self.land.at[slot, aligned(self.s, self.tok), :]
        return pltpu.make_async_copy(self.units.home(self.src, u), to, self.local.at[slot])

    def start(self, u, unused):
        host = self.units.host(u)[0]
        pl.when(host == self.s)(lambda: self.here(u).start())
        pl.when(host != self.s)(lambda: self.away(u).start())
        return unused

    def bulk(self, copies, recv):
        some = self.land.at[0, pl.ds(0, copies * self.tok), :]
        return remote(some, some, self.send, recv, self.units.place.core)

    def wait(self, slot):
        self.here(self.units.unit(slot)).wait()
        self.bulk(self.n - 1, self.recv.at[slot]).wait_recv()

    def sent(self):
        pl.when(self.units.at_end)(lambda: self.bulk(self.n, self.recv.at[0]).wait_send())
        pl.when(jnp.logical_not(self.units.at_end))(lambda: self.bulk(self.n - 2, self.recv.at[0]).wait_send())


class FromUnits:
    def __init__(self, units, src, whole, send, recv, local):
        self.units, self.src, self.whole, self.send, self.recv, self.local = units, src, whole, send, recv, local
        self.n, self.s, self.t, self.tok = units.place.n, units.place.s, units.place.t, units.tok

    def away(self, slot, d):
        u = self.units.unit(slot)
        src = self.src.at[slot, aligned(d, self.tok), :]
        return remote(src, self.units.home(self.whole, u), self.send.at[slot], self.recv, (d, self.t))

    def here(self, slot):
        src = self.src.at[slot, aligned(self.s, self.tok), :]
        return pltpu.make_async_copy(src, self.units.home(self.whole, self.units.unit(slot)), self.local.at[slot])

    def start(self, slot, low, high):
        def one(d, unused):
            pl.when(d == self.s)(lambda: self.here(slot).start())
            pl.when(d != self.s)(lambda: self.away(slot, d).start())
            return unused

        lax.fori_loop(low, high, one, 0)

    def bulk(self, copies, slot):
        some = self.src.at[0, pl.ds(0, copies * self.tok), :]
        return remote(some, some, self.send.at[slot], self.recv, self.units.place.core)

    def wait(self):
        pl.when(self.units.at_end)(lambda: self.bulk(self.n, 0).wait_recv())

        @pl.when(jnp.logical_not(self.units.at_end))
        def _():
            for slot in range(2):
                self.here(slot).wait()
            self.bulk(self.n - 2, 0).wait_recv()

    def sent(self, slot):
        self.bulk(self.n - 1, slot).wait_send()


def layer_kernel(
    geo, sizes, names,
    x_in, cot_in, key_in, value_in, seg_in, wg_in, wu_in, wd_in, wo_in, wq_in, gain_one, gain_two, *refs,
):
    n, rows, tok, width, half, heads, length = geo
    ff, cols, cuts = sizes
    r = types.SimpleNamespace(**dict(zip(names, refs, strict=True)))
    tokens = rows * tok
    blk = 2 * width // n
    nz = n // PLANE
    place = Place(n)
    s, t, z = place.s, place.t, place.z
    row_s, head_s = s // heads, lax.rem(s, heads)
    mine = aligned(t, half)
    chunk = tokens // 4
    fine = 32
    wbuf = r.wbuf
    size = wbuf.shape[1]
    mid, x_all, cot_all, two_norm, two_own, two_in, one_in = (
        r.mid, r.x_all, r.cot_all, r.two_norm, r.two_own, r.two_in, r.one_in
    )
    mixed, err, one, attended, dq = r.mixed, r.err, r.one, r.attended, r.dq
    d_att = attended
    hidden, d_gate, d_up, sums = r.hidden, r.d_gate, r.d_up, r.sums
    uq, uk, uv, uo, lse, k_t = (ref.at[0] for ref in (r.uqs, r.uks, r.uvs, r.uos, r.lses, r.k_ts))
    delta = r.delta
    seg_all, seg_row, seg_col = r.seg_all, r.seg_row, r.seg_col
    udq, udk, udv = r.udq, r.udk, r.udv
    tp_s, tp_r, a_s, a_r, loc = r.tp_s, r.tp_r, r.a_s, r.a_r, r.loc
    units = Units(place, nz, heads, tok)
    at_end = units.at_end
    place.enter()

    to_x = remote(x_in, x_all.at[:, mine], tp_s.at[0], tp_r.at[0], place.twin)
    to_x.start()
    own_x = pltpu.make_async_copy(x_in, x_all.at[:, mine], loc.at[0])
    own_x.start()

    def piece(ref):
        return lambda d: ref.at[aligned(d // heads, tok), aligned(lax.rem(d, heads), HEAD_DIM)]

    keys = Spread(place, piece(key_in), lambda: uk.at[aligned(s, tok), :], a_s.at[0], a_r.at[0], loc.at[2], uk.at[: length - tok, :])
    vals = Spread(place, piece(value_in), lambda: uv.at[aligned(s, tok), :], a_s.at[1], a_r.at[1], loc.at[3], uv.at[: length - tok, :])
    segs = Spread(place, lambda d: seg_in.at[d // heads], lambda: seg_all.at[s], a_s.at[2], a_r.at[2], loc.at[4], seg_all.at[: n - 1])
    qrys = Spread(place, piece(dq), lambda: uq.at[aligned(s, tok), :], a_s.at[3], a_r.at[3], loc.at[5], uq.at[: length - tok, :])
    segs.start()
    keys.start()
    vals.start()
    to_cot = remote(cot_in, cot_all.at[:, mine], tp_s.at[1], tp_r.at[1], place.twin)
    to_cot.start()
    own_cot = pltpu.make_async_copy(cot_in, cot_all.at[:, mine], loc.at[6])
    own_cot.start()

    def square_copies(k, ref, sems):
        copies = []
        for zy in range(n // 2):
            to = wbuf.at[4 * k + zy // 2, :, (zy % 2) * half : (zy % 2 + 1) * half]
            copies.append(pltpu.make_async_copy(ref.at[zy * blk : (zy + 1) * blk, :], to, sems.at[zy]))
        return copies

    def square_block(k, zy):
        return wbuf[4 * k + zy // 2, :, (zy % 2) * half : (zy % 2 + 1) * half]

    def split_block(ref, at, zy):
        zz, yy = divmod(zy, 2)
        return ref[yy, at, zz * blk : (zz + 1) * blk]

    def store_split(ref, at, now):
        for zy in range(n // 2):
            zz, yy = divmod(zy, 2)
            ref[yy, at, zz * blk : (zz + 1) * blk] = now[:, zy * blk : (zy + 1) * blk]

    load_wq = square_copies(1, wq_in, r.o_sem.at[0])
    load_wo = square_copies(0, wo_in, r.o_sem.at[1])
    for copy in load_wq + load_wo:
        copy.start()
    own_x.wait()
    to_x.wait()

    def first_norm(i, unused):
        at = aligned(i, fine)
        x = x_all[at, :].astype(F32)
        root = lax.rsqrt(jnp.mean(x * x, axis=-1, keepdims=True) + EPSILON)
        store_split(one, at, (x * root * gain_one[...]).astype(BF))
        return unused

    lax.fori_loop(0, tokens // fine, first_norm, 0)
    for copy in load_wq:
        copy.wait()
    every = slice(0, tokens)
    total = jnp.zeros((tokens, half), F32)
    for zy in range(n // 2):
        total += dot_nn(split_block(one, every, zy), square_block(1, zy))
    dq[...] = (total * HEAD_DIM ** (-0.5)).astype(BF)
    qrys.start()
    lv_one, lv_two = r.lv_one, r.lv_two
    left_cot, left_two, left_err, left_one = (
        Plane(place, split, land, r.le_s.at[i], r.le_r.at[i], r.l_loc.at[i], tokens)
        for i, (split, land) in enumerate(((err, lv_one), (mixed, lv_two), (err, r.l_err), (one, r.l_one)))
    )
    left_one.start()

    segs.wait()
    attention_masks(seg_all, seg_row, seg_col, n, tok)
    keys.wait()
    vals.wait()

    def turn_into(ref, to):
        def turn(i, unused):
            at = aligned(i, tok)
            to[:, at] = jnp.transpose(ref[at, :].astype(F32)).astype(BF)
            return unused

        lax.fori_loop(0, n, turn, 0)

    turn_into(uv, k_t)
    qrys.wait()
    block = 512
    owners = block // tok
    back = Spread(
        place,
        lambda d: uo.at[aligned(d, tok), :],
        lambda: attended.at[aligned(row_s, tok), aligned(head_s, HEAD_DIM)],
        a_s.at[4], a_r.at[4], loc.at[8], uo.at[: length - tok, :],
    )

    def query_step(qi, unused):
        query_block = uq[aligned(qi, block), :]

        def key_step(j, carry):
            top, total, acc = carry
            kj = qi - j
            scores = dot_nt(uk[aligned(kj, block), :], query_block)
            scores = jnp.where(readable(seg_col, seg_row, kj, qi, block), scores, NEGATIVE_FILL)
            new_top = jnp.maximum(top, jnp.max(scores, axis=0, keepdims=True))
            weights = jnp.exp(scores - new_top)
            decay = jnp.exp(top - new_top)
            total = total * decay + jnp.sum(weights, axis=0, keepdims=True)
            acc = acc * decay + dot_nn(k_t[:, aligned(kj, block)], weights.astype(BF))
            return new_top, total, acc

        start = (
            jnp.full((1, block), NEGATIVE_FILL, F32),
            jnp.zeros((1, block), F32),
            jnp.zeros((HEAD_DIM, block), F32),
        )
        top, total, acc = lax.fori_loop(0, qi + 1, key_step, start)
        lse[:, aligned(qi, block)] = top + jnp.log(total)
        uo[aligned(qi, block), :] = jnp.transpose(acc / total).astype(BF)
        return lax.fori_loop(qi * owners, (qi + 1) * owners, back.start_to, unused)

    lax.fori_loop(0, length // block, query_step, 0)

    work = (r.acc, r.stage, r.work_sem)
    mv, turned = r.mv, r.turned
    s_first, s_second, t_first, t_second = r.s_first, r.s_second, r.t_first, r.t_second
    sources = (hidden, d_gate, d_up)
    lefts_of = ((lv_one, lv_one), (lv_two, lv_two), (lv_two, lv_two))
    kept = ((s_first, t_first, r.out_down), (s_second, t_second, r.out_gate), (s_first, t_first, r.out_up))
    gots = (r.g0, r.g1, r.g2, r.g3, r.g4, r.g5, r.g6)
    lands = (None, None, None, r.m3, r.m4, r.m5, r.m6)
    plans = []
    for i, (kind, first, wide) in enumerate(cuts):
        at = pl.ds(first, wide)
        left, lv = lefts_of[kind]
        move, total_ref, out_ref = kept[kind]
        here = mv.at[:, at]
        plans.append((
            (sources[kind], cols, first), here if lands[i] is None else lands[i], left, lv, here, move.at[:, :, at], gots[i], total_ref.at[:, at],
            out_ref, (turned, cols, first),
        ))
    for source, left, lv, *rest in (
        (attended, r.l_err, lv_one, r.mv_out, r.s_out, r.g_out, r.t_out, r.out_out),
        (dq, r.l_one, lv_two, r.mv_query, r.s_query, r.g_query, r.t_query, r.out_query),
    ):
        plans.append(((source, half // 2, 0), rest[0], left, lv, *rest, None))
    lines = []
    for i, (source, land, *rest) in enumerate(plans):
        gather = Gather(place, *source, land, r.me_s.at[i], r.me_r.at[i], r.g_loc.at[i], tokens)
        sems = (r.c_s.at[i], r.c_r.at[i], r.e_s.at[i], r.e_r.at[i], r.e_l.at[i])
        lines.append(Line(place, nz, blk, gather, land, *rest, sems, work))
    down_a, down_b, down_c, gate_a, gate_b, up_a, up_b, out, query = lines
    ship = [
        remote(a.at[0], a.at[1], r.sh_s.at[i], r.sh_r.at[i], units.near)
        for i, a in enumerate((r.uqs, r.uks, r.uvs, r.uos, r.lses))
    ]

    @pl.when(at_end)
    def _():
        for copy in ship:
            copy.start()

    own_cot.wait()
    to_cot.wait()

    def split_cot(i, unused):
        at = aligned(i, fine)
        store_split(err, at, cot_all[at, :])
        return unused

    lax.fori_loop(0, tokens // fine, split_cot, 0)
    left_cot.start()
    left_one.forward()
    for copy in load_wo:
        copy.wait()
    back.wait()

    chunks = 4
    wide = width // chunks

    def to_twin(i):
        at = slice(i * wide, (i + 1) * wide)
        return remote(two_own.at[:, at], one_in.at[:, at], tp_s.at[9 + i], tp_r.at[9 + i], place.twin)

    for i in range(chunks):
        for zy in range(2 * i, 2 * i + 2):
            two_own[:, zy * blk : (zy + 1) * blk] = dot_nt(attended[...], square_block(0, zy)).astype(BF)
        to_twin(i).start()
    out.gather.start()
    zeroth_pass = Weights((wd_in,), wbuf, r.w_sem.at[3], r.tail_sem.at[3], 0, 4, cols, ff)
    first_pass = Weights((wg_in, wu_in), wbuf, r.w_sem.at[0], r.tail_sem.at[0], 0, 0, cols, ff)
    second_pass = Weights((wg_in, wu_in), wbuf, r.w_sem.at[1], r.tail_sem.at[1], 0, 4, cols, ff)
    third_pass = Weights((wd_in,), wbuf, r.w_sem.at[2], r.tail_sem.at[2], 0, 4, cols, ff)
    zeroth_pass.begin(2)
    first_pass.begin(2)

    def to_hidden(slots, at):
        now = dot_nt(cot_all[...], wbuf[slots[0]]).astype(BF)
        for k in range(2):
            d_gate[:, at[k]] = now[:, k * LANE : (k + 1) * LANE]

    zeroth_pass.run(to_hidden)
    left_cot.forward()
    square = jnp.zeros((tokens, 1), F32)
    for i in range(chunks):
        to_twin(i).wait()
        at = slice(i * wide, (i + 1) * wide)
        now = x_all[:, at].astype(F32) + (two_own[:, at].astype(F32) + one_in[:, at].astype(F32))
        mid[:, at] = now
        square += jnp.sum(now * now, axis=-1, keepdims=True)
    root_two = lax.rsqrt(square * (1.0 / width) + EPSILON)
    for i in range(chunks):
        at = slice(i * wide, (i + 1) * wide)
        two_norm[:, at] = (mid[:, at] * root_two * gain_two[:, at]).astype(BF)

    def units_block(slots, at):
        x = two_norm[...]
        gate_now, up_now = (dot_nt(x, wbuf[slot]) for slot in slots)
        d_hid = jnp.concatenate([d_gate[:, at[0]], d_gate[:, at[1]]], axis=1).astype(F32)
        sigma = jax.nn.sigmoid(gate_now)
        act = gate_now * sigma
        for ref, now in (
            (hidden, act * up_now),
            (d_gate, d_hid * up_now * sigma * (1.0 + gate_now * (1.0 - sigma))),
            (d_up, d_hid * act),
        ):
            now = now.astype(BF)
            for k in range(2):
                ref[:, at[k]] = now[:, k * LANE : (k + 1) * LANE]

    done_a, done_b = (2 * ((first + wide) // size) for _, first, wide in cuts[:2])

    def split_two(i, unused):
        at = aligned(i, fine)
        store_split(mixed, at, two_norm[at, :])
        return unused

    def begin_down():
        down_a.gather.start()
        lax.fori_loop(0, tokens // fine, split_two, 0)

    def go_on_down():
        down_b.gather.start()
        left_cot.gone()
        left_cot.finish()
        down_a.load()
        down_a.from_end()

    first_pass.run(
        units_block,
        ((done_a - 1, [begin_down]), (done_b - 1, [go_on_down]), (first_pass.regular - 1, [second_pass.begin])),
    )
    down_c.gather.start()
    left_two.start()
    down_b.load()
    down_b.from_end()
    down_a.between(0, 2)

    def block_of(ref, at):
        return jnp.concatenate([ref[:, at[0]], ref[:, at[1]]], axis=1)

    def add_up(pairs):
        for db in range(width // size):
            at = slice(db * size, (db + 1) * size)
            sums[db * tokens : (db + 1) * tokens, :] += sum(dot_nn(a, wbuf[slot, :, at]) for a, slot in pairs)

    def back_units(slots, at):
        add_up([(block_of(d_gate, at), slots[0]), (block_of(d_up, at), slots[1])])

    sums[...] = jnp.zeros_like(sums)
    second_pass.run(back_units)
    for db in range(width // size):
        two_own[:, db * size : (db + 1) * size] = sums[db * tokens : (db + 1) * tokens, :].astype(BF)

    def two_copy(i):
        at = aligned(i, chunk)
        return remote(two_own.at[at, :], two_in.at[at, :], tp_s.at[2 + i], tp_r.at[2 + i], place.twin)

    for i in range(4):
        two_copy(i).start()
    load_wo = square_copies(0, wo_in, r.o_sem.at[2])
    for copy in load_wo:
        copy.start()
    gate_a.gather.start()
    down_a.between(2, 3)
    down_b.between(0, 2)
    down_c.load()
    down_c.from_end()

    third_pass.begin()
    sums[...] = jnp.zeros_like(sums)

    def out_units(slots, at):
        add_up([(block_of(hidden, at), slots[0])])

    third_pass.run(out_units)
    left_two.forward()
    left_two.gone()
    for db in range(width // size):
        per = half // size
        mixed[db // per, :, (db % per) * size : (db % per + 1) * size] = sums[db * tokens : (db + 1) * tokens, :].astype(BF)
    ffn_copy = remote(mixed.at[1 - t], r.ffn_in, tp_s.at[6], tp_r.at[6], place.twin)
    ffn_copy.start()
    per = half // size
    for i in range(per):
        at = t * per + i
        sums[aligned(at, tokens), :] += mid[:, aligned(at, size)]
    hold = pltpu.make_async_copy(sums.at[aligned(t, per * tokens), :], r.mix, loc.at[11])
    hold.start()
    load_wq = square_copies(1, wq_in, r.o_sem.at[3])
    for copy in load_wq:
        copy.start()
    down_b.between(2, 3)
    down_c.between(0, 2)
    hold.wait()

    to_units = ToUnits(units, d_att, r.udo, r.u_s.at[0], r.u_r, r.u_l)
    out.gather.wait()
    for copy in load_wo:
        copy.wait()

    def second_norm(i, gain_sum):
        two_copy(i).wait()

        def some(j, gain_sum):
            at = aligned(i * (chunk // fine) + j, fine)
            m = mid[at, :]
            d2 = two_own[at, :].astype(F32) + two_in[at, :].astype(F32)
            root = lax.rsqrt(jnp.mean(m * m, axis=-1, keepdims=True) + EPSILON)
            gained = d2 * gain_two[...]
            scaled = m * root
            gain_sum = gain_sum + jnp.sum(d2 * scaled, axis=0, keepdims=True)
            slope = jnp.mean(gained * scaled, axis=-1, keepdims=True)
            dm = cot_all[at, :].astype(F32) + root * (gained - scaled * slope)
            mid[at, :] = dm
            store_split(err, at, dm.astype(BF))
            return gain_sum

        gain_sum = lax.fori_loop(0, chunk // fine, some, gain_sum)
        at = aligned(i, chunk)
        total = jnp.zeros((chunk, half), F32)
        for zy in range(n // 2):
            total += dot_nn(split_block(err, at, zy), square_block(0, zy))
        d_att[at, :] = total.astype(BF)
        return gain_sum

    gain_sum = jnp.zeros((1, width), F32)
    per_row = tok // chunk
    for row in range(rows):
        gain_sum = lax.fori_loop(row * per_row, (row + 1) * per_row, second_norm, gain_sum)
        lax.fori_loop(row * heads, (row + 1) * heads, to_units.start, 0)
    gain_part, gain_in = r.gain_part, r.gain_in
    for i in range(n):
        gain_part[0, i] = gain_sum[:, i * (width // n) : (i + 1) * (width // n)]
    spread_gain = [
        Spread(place, lambda d, g=g: gain_part.at[g, d], lambda g=g: gain_in.at[g, s], a_s.at[5 + g], a_r.at[5 + g], loc.at[9 + g],
               gain_in.at[g, : n - 1])
        for g in range(2)
    ]
    spread_gain[0].start()
    gate_b.gather.start()
    down_c.between(2, 3)
    left_two.finish()
    gate_a.load()
    gate_a.from_end()

    back_dq, back_dk, back_dv = (
        FromUnits(units, src, whole, r.f_s.at[i], r.f_r.at[i], r.f_l.at[i])
        for i, (src, whole) in enumerate(((udq, dq), (udk, r.d_keys), (udv, r.d_values)))
    )

    def one_unit(slot, unused):
        unit_q, unit_k, unit_v, unit_o, unit_lse, unit_kt = (
            ref.at[slot] for ref in (r.uqs, r.uks, r.uvs, r.uos, r.lses, r.k_ts)
        )
        unit_do = r.udo.at[slot]
        sums[...] = jnp.zeros_like(sums)
        to_units.wait(slot)

        def turn_delta(i, unused):
            at = aligned(i, tok)
            both = unit_do[at, :].astype(F32) * unit_o[at, :].astype(F32)
            delta[:, at] = jnp.sum(jnp.transpose(both), axis=0, keepdims=True)
            return unused

        lax.fori_loop(0, n, turn_delta, 0)

        def query_step(i, unused_too):
            qi = length // block - 1 - i
            qat = aligned(qi, block)
            qb, dob = unit_q[qat, :], unit_do[qat, :]

            def key_step(kj, dq_t):
                kat = aligned(kj, block)
                scores = dot_nt(unit_k[kat, :], qb) - unit_lse[:, qat]
                probs = jnp.exp(jnp.where(readable(seg_col, seg_row, kj, qi, block), scores, NEGATIVE_FILL))
                d_probs = dot_nt(unit_v[kat, :], dob)
                d_scores = (probs * (d_probs - delta[:, qat])).astype(BF)
                sums[kat, :HEAD_DIM] += dot_nn(d_scores, qb)
                sums[kat, HEAD_DIM:] += dot_nn(probs.astype(BF), dob)
                return dq_t + dot_nn(unit_kt[:, kat], d_scores)

            dq_t = lax.fori_loop(0, qi + 1, key_step, jnp.zeros((HEAD_DIM, block), F32))
            udq[slot, qat, :] = jnp.transpose(dq_t).astype(BF)
            back_dq.start(slot, qi * owners, (qi + 1) * owners)
            udk[slot, qat, :] = sums[qat, :HEAD_DIM].astype(BF)
            udv[slot, qat, :] = sums[qat, HEAD_DIM:].astype(BF)

            @pl.when((slot == 0) & (i == 0))
            def _():
                gate_a.step(1)

            @pl.when((slot == 1) & (i == 0))
            def _():
                gate_a.step(2)
                gate_b.load()
                gate_b.some(nz - 1, 0)

            @pl.when((slot == 1) & (i == 1))
            def _():
                gate_b.step(1)

            return unused_too

        lax.fori_loop(0, length // block, query_step, 0)

        @pl.when(slot == 0)
        def _():
            back_dk.start(0, 0, n)
            back_dv.start(0, 0, n)

        return unused

    def one_copy(i):
        at = aligned(i, chunk)
        return remote(two_own.at[at, :], one_in.at[at, :], tp_s.at[13 + i], tp_r.at[13 + i], place.twin)

    def through_query():
        for copy in load_wq:
            copy.wait()
        back_dq.wait()
        query.gather.start()

        def back_query(i, unused):
            at = aligned(i, chunk)
            for zy in range(n // 2):
                now = dot_nt(dq[at, :], square_block(1, zy)) * HEAD_DIM ** (-0.5)
                two_own[at, zy * blk : (zy + 1) * blk] = now.astype(BF)
            one_copy(i).start()
            return unused

        lax.fori_loop(0, 4, back_query, 0)

    def last_norm(i, gain_sum):
        one_copy(i).wait()

        def some(j, gain_sum):
            at = aligned(i * (chunk // fine) + j, fine)
            x = x_all[at, :].astype(F32)
            d1 = two_own[at, :].astype(F32) + one_in[at, :].astype(F32)
            root = lax.rsqrt(jnp.mean(x * x, axis=-1, keepdims=True) + EPSILON)
            gained = d1 * gain_one[...]
            scaled = x * root
            gain_sum = gain_sum + jnp.sum(d1 * scaled, axis=0, keepdims=True)
            slope = jnp.mean(gained * scaled, axis=-1, keepdims=True)
            mid[at, :] = mid[at, :] + root * (gained - scaled * slope)
            return gain_sum

        return lax.fori_loop(0, chunk // fine, some, gain_sum)

    give = pltpu.make_async_copy(mid.at[:, mine], r.input_grad, loc.at[19])

    def through_first_norm():
        gain_sum = lax.fori_loop(0, 4, last_norm, jnp.zeros((1, width), F32))
        for i in range(n):
            gain_part[1, i] = gain_sum[:, i * (width // n) : (i + 1) * (width // n)]
        spread_gain[1].start()
        give.start()

    def finish_all(*some):
        for line in some:
            line.finish()

    def left_all(*some):
        for line in some:
            line.left_here()

    def sent_all(*some):
        for line in some:
            line.sent()

    def err_here():
        left_err.forward()
        left_err.gone()
        left_err.finish()

    def one_here():
        left_one.gone()
        left_one.finish()

    up_a.gather.start()
    up_b.gather.start()
    left_err.start()

    with jax.named_scope("between"):
        @pl.when(jnp.logical_not(at_end))
        def _():
            for copy in ship:
                copy.wait_recv()
            for slot in range(2):
                turn_into(r.uks.at[slot], r.k_ts.at[slot])
            gate_a.step(0)
            lax.fori_loop(0, 2, one_unit, 0)
            finish_all(down_a, down_b)
            sent_all(down_a, down_b, down_c)
            up_a.load()
            up_a.some(nz - 1, 0)
            gate_b.step(2)
            finish_all(down_c)
            up_a.step(1)
            up_b.load()
            back_dk.start(1, 0, n)
            up_a.step(2)
            up_b.some(nz - 1, 0)
            back_dv.start(1, 0, n)
            through_query()
            up_b.step(1)
            err_here()
            left_all(down_a, down_b)
            finish_all(gate_a)
            left_all(down_c)
            finish_all(gate_b)
            out.load(True, gathered=True)
            up_b.step(2)
            out.some(nz - 1, 0)
            one_here()
            through_first_norm()
            out.step(1)
            query.load(True)
            left_all(gate_a)
            finish_all(up_a)
            out.step(2)
            query.some(nz - 1, 0, 1)
            left_all(gate_b)
            finish_all(up_b)
            query.step(2)
            finish_all(out, query)

    with jax.named_scope("ends"):
        @pl.when(at_end)
        def _():
            gate_b.load()
            gate_b.begin()
            finish_all(down_a, down_b, down_c)
            sent_all(down_a, down_b, down_c)
            up_a.load()
            up_a.begin()
            up_b.load()
            up_b.begin()
            left_all(down_a, down_b, down_c)
            err_here()
            out.load(True, gathered=True)
            out.begin()
            through_query()
            one_here()
            query.load(True)
            query.begin()
            through_first_norm()
            finish_all(gate_a, gate_b)
            left_all(gate_a, gate_b)
            finish_all(up_a, up_b, out, query)

    ffn_copy.wait()
    to_units.sent()
    fetch = pltpu.make_async_copy(r.mix, sums.at[: per * tokens, :], loc.at[11])
    fetch.start()
    fetch.wait()
    for i in range(per):
        at = slice(i * size, (i + 1) * size)
        attended[:, at] = (sums[i * tokens : (i + 1) * tokens, :] + r.ffn_in[:, at].astype(F32)).astype(BF)
    give_mixed = pltpu.make_async_copy(attended, r.out_mixed, loc.at[20])
    give_mixed.start()
    back_dk.wait()
    back_dv.wait()
    for g in range(2):
        spread_gain[g].wait()
        (r.gain_two, r.gain_one)[g][...] = jnp.sum(gain_in[g], axis=0)

    @pl.when(at_end)
    def _():
        for copy in ship:
            copy.wait_send()

    @pl.when(jnp.logical_not(at_end))
    def _():
        for slot in range(2):
            for sent in (back_dq, back_dk, back_dv):
                sent.sent(slot)

    give.wait()
    give_mixed.wait()
    for line in lines[3:]:
        line.sent()
    for line in lines[5:]:
        line.left_here()
    for line in lines:
        line.arrived()


def results_kernel(rows, factors, *refs):
    count = len(rows)
    ins, outs, held, sems = refs[:count], refs[count : 2 * count], refs[2 * count : -1], refs[-1]
    come = [pltpu.make_async_copy(ins[i].at[: rows[i]], held[2 * i], sems.at[0, i]) for i in range(count)]
    go = [pltpu.make_async_copy(held[2 * i + 1], outs[i], sems.at[1, i]) for i in range(count)]
    for copy in come:
        copy.start()
    for i, factor in enumerate(factors):
        come[i].wait()
        if factor is not None:
            held[2 * i + 1][...] = held[2 * i][...].astype(F32) * factor
        go[i].start()
    for copy in go:
        copy.wait()


def results(*some):
    anywhere = pl.BlockSpec(memory_space=pl.ANY)
    arrays, rows, factors = zip(*some)
    shapes = [vm((k, *a.shape[1:]), a.dtype if f is None else F32) for a, k, f in some]
    held = []
    for (a, k, f), shape in zip(some, shapes):
        held += [pltpu.VMEM((k, *a.shape[1:]) if f is not None else (8, LANE), a.dtype), pltpu.VMEM(shape.shape, shape.dtype)]

    def kernel(*refs):
        count = len(rows)
        refs = list(refs)
        for i, factor in enumerate(factors):
            if factor is None:
                refs[2 * count + 2 * i] = refs[2 * count + 2 * i + 1]
        results_kernel(rows, factors, *refs)

    return pl.pallas_call(
        kernel,
        out_shape=shapes,
        in_specs=[anywhere] * len(arrays),
        out_specs=[anywhere] * len(arrays),
        scratch_shapes=[*held, pltpu.SemaphoreType.DMA((2, len(arrays)))],
        compiler_params=pltpu.CompilerParams(vmem_limit_bytes=VMEM_GRANT),
        name="results",
    )(*arrays)


def fast_device(
    n, inputs, segments, keys, values, attn_gain, query_weight, out_weight, ffn_gain, gate_weight, up_weight, down_weight,
    cotangent,
):
    rows, tok, half = inputs.shape
    tokens, width, ff = rows * tok, query_weight.shape[0], gate_weight.shape[1]
    heads, length = half // HEAD_DIM, n * tok
    geo = (n, rows, tok, width, half, heads, length)
    blk, nz, size = 2 * width // n, n // PLANE, 2 * LANE
    cols = -(-ff // size) * LANE
    firsts = (0, size, 3 * size, cols)
    thirds = [(firsts[i], firsts[i + 1] - firsts[i]) for i in range(3)]
    halves = [(0, firsts[2]), (firsts[2], cols - firsts[2])]
    cuts = tuple((kind, *cut) for kind, parts in enumerate((thirds, halves, halves)) for cut in parts)
    sizes = (ff, cols, cuts)
    square = half // 2
    n_lines = len(cuts) + 2
    dma = pltpu.SemaphoreType.DMA
    anywhere, here = pl.BlockSpec(memory_space=pl.ANY), pl.BlockSpec(memory_space=pltpu.VMEM)

    def pieces(letter, shapes):
        return {letter + str(i): shape for i, shape in shapes}

    tall, flat_left = vm((2 * cols, blk // 2), F32), vm((PLANE * tokens, width // 2), BF)
    sum_square = vm((nz + 1, blk, square), BF)
    outs = dict(
        out_mixed=vm((tokens, half), BF),
        input_grad=vm((tokens, half), F32),
        d_keys=vm((tokens, half), BF),
        d_values=vm((tokens, half), BF),
        gain_one=vm((1, width // n), F32),
        gain_two=vm((1, width // n), F32),
        out_down=tall,
        out_gate=tall,
        out_up=tall,
        out_out=vm((blk // 2, half), F32),
        out_query=vm((blk // 2, half), F32),
        mix=vm((half // size * tokens, size), F32),
        l_err=flat_left,
        l_one=flat_left,
        g_out=sum_square,
        g_query=sum_square,
        **pieces("m", [(i, vm((PLANE * tokens, w), BF)) for i, (kind, _, w) in enumerate(cuts) if kind > 0]),
        **pieces("g", [(i, vm((nz + 1, blk, w), BF)) for i, (_, _, w) in enumerate(cuts)]),
    )
    row = pltpu.VMEM((1, length), F32)
    act, own = pltpu.VMEM((tokens, width), BF), pltpu.VMEM((tokens, half), BF)
    split = pltpu.VMEM((2, tokens, width // 2), BF)
    hid = pltpu.VMEM((tokens, 2 * cols), BF)
    gain = pltpu.VMEM((2, n, 1, width // n), F32)
    left = pltpu.VMEM((PLANE * tokens, width // 2), BF)
    two = pltpu.VMEM((2, length, HEAD_DIM), BF)
    move, move_square = (pltpu.VMEM((nz - 1, blk, c), BF) for c in (cols, square))
    total, total_square = (pltpu.VMEM((blk, c), F32) for c in (cols, square))
    taken = pltpu.VMEM((PLANE * tokens, square), BF)
    scratch = dict(
        mid=pltpu.VMEM((tokens, width), F32),
        x_all=act, cot_all=act, two_norm=act, two_own=act, two_in=act, one_in=act, mixed=split, err=split, one=split,
        wbuf=pltpu.VMEM((8, size, width), BF),
        attended=own, dq=own, ffn_in=own, hidden=hid, d_gate=hid, d_up=hid,
        sums=pltpu.VMEM((length, size), F32),
        uqs=two, uks=two, uvs=two, uos=two, udo=two, udq=two, udk=two, udv=two,
        delta=row, seg_row=row, lses=pltpu.VMEM((2, 1, length), F32),
        seg_all=pltpu.VMEM((n, 1, tok), segments.dtype),
        seg_col=pltpu.VMEM((length, LANE), F32),
        k_ts=pltpu.VMEM((2, HEAD_DIM, length), BF),
        gain_part=gain, gain_in=gain,
        s_first=move, s_second=move, s_out=move_square, s_query=move_square,
        t_first=total, t_second=total, t_out=total_square, t_query=total_square,
        turned=pltpu.VMEM((cols, blk), F32),
        mv=pltpu.VMEM((PLANE * tokens, cols), BF), mv_out=taken, mv_query=taken,
        lv_one=left, lv_two=left,
        acc=total,
        stage=pltpu.VMEM((blk, cols), BF),
        tp_s=dma((17,)), tp_r=dma((17,)), a_s=dma((7,)), a_r=dma((7,)),
        me_s=dma((n_lines,)), me_r=dma((n_lines,)), le_s=dma((4, 3)), le_r=dma((4, 3)),
        c_s=dma((n_lines, nz - 1)), c_r=dma((n_lines, nz + 1)),
        e_s=dma((n_lines,)), e_r=dma((n_lines,)), e_l=dma((n_lines,)),
        sh_s=dma((5,)), sh_r=dma((5,)), u_s=dma((1,)), u_r=dma((2,)), u_l=dma((2,)),
        f_s=dma((3, 2)), f_r=dma((3,)), f_l=dma((3, 2)),
        loc=dma((21,)), g_loc=dma((n_lines,)), l_loc=dma((4,)), work_sem=dma((3,)),
        w_sem=dma((4, 2, 2)), tail_sem=dma((4, 2, 2)), o_sem=dma((4, n // 2)),
    )
    names = (*outs, *scratch)

    def flat(a):
        return a.reshape(tokens, half)

    segs = segments.reshape(rows, 1, tok)
    got = pl.pallas_call(
        functools.partial(layer_kernel, geo, sizes, names),
        out_shape=list(outs.values()),
        in_specs=[anywhere] * 10 + [here] * 2,
        out_specs=[here if i in (4, 5) else anywhere for i in range(len(outs))],
        scratch_shapes=list(scratch.values()),
        compiler_params=pltpu.CompilerParams(
            collective_id=0, has_side_effects=True, vmem_limit_bytes=VMEM_GRANT
        ),
        name="layer",
    )(
        flat(inputs), flat(cotangent), flat(keys), flat(values), segs, gate_weight.T, up_weight.T, down_weight.T,
        out_weight, query_weight, attn_gain.reshape(1, width), ffn_gain.reshape(1, width),
    )
    got = types.SimpleNamespace(**dict(zip(outs, got)))

    def shaped(a):
        return a.reshape(rows, tok, half)

    d_keys, d_values, g_query, g_down, g_gate, g_up, input_grad, mixed, g_out, grad_one, grad_two = results(
        (got.d_keys, tokens, 1.0),
        (got.d_values, tokens, 1.0),
        (got.out_query, blk // 2, HEAD_DIM ** (-0.5)),
        (got.out_down, ff, None),
        (got.out_gate, ff, None),
        (got.out_up, ff, None),
        (got.input_grad, tokens, None),
        (got.out_mixed, tokens, None),
        (got.out_out, blk // 2, None),
        (got.gain_one, 1, None),
        (got.gain_two, 1, None),
    )
    return (
        shaped(mixed),
        shaped(input_grad),
        shaped(d_keys),
        shaped(d_values),
        grad_one.reshape(width // n),
        g_query,
        g_out,
        grad_two.reshape(width // n),
        g_gate.T,
        g_up.T,
        g_down.T,
    )


def inverse_root(stream):
    return lax.rsqrt(jnp.mean(stream * stream, axis=-1, keepdims=True) + EPSILON)


def key_mask(doc_start, query_pos, begin, row_count):
    key_pos = begin + jnp.arange(row_count, dtype=jnp.int32)
    earlier = key_pos[None, None, :] <= query_pos[None, :, None]
    same_doc = key_pos[None, None, :] >= doc_start[:, :, None]
    return (earlier & same_doc)[:, None]


def per_device(
    inputs,
    segments,
    keys,
    values,
    attn_gain,
    query_weight,
    out_weight,
    ffn_gain,
    gate_weight,
    up_weight,
    down_weight,
    cotangent,
):
    batch_rows, local_tokens, half_width = inputs.shape
    local_heads = half_width // HEAD_DIM
    seq_devices = lax.axis_size("seq")
    row_length = local_tokens * seq_devices
    seq_index = lax.axis_index("seq")
    tp_index = lax.axis_index("tp")
    query_scale = HEAD_DIM ** (-0.5)
    bfloat = jnp.bfloat16
    single = jnp.float32
    whole = lax.all_gather(inputs, "tp", axis=2, tiled=True).astype(single)
    root_one = inverse_root(whole)
    scaled_one = whole * root_one
    normed_one = (scaled_one * attn_gain).astype(bfloat)
    query = (
        jnp.einsum("rtd,de->rte", normed_one, query_weight, preferred_element_type=single)
        * query_scale
    ).astype(bfloat)
    query_heads = query.reshape(batch_rows, local_tokens, local_heads, HEAD_DIM)
    bins = jnp.arange(CUTS + 1, dtype=jnp.int32)
    onehot = (segments[:, :, None] == bins[None, None, :]).astype(single)
    totals = lax.psum(jnp.sum(onehot, axis=1), "seq")
    ends = jnp.cumsum(totals, axis=-1)
    before = ends - totals
    doc_start = jnp.sum(onehot * before[:, None, :], axis=-1).astype(jnp.int32)
    query_pos = seq_index * local_tokens + jnp.arange(local_tokens, dtype=jnp.int32)
    first_needed = jnp.min(doc_start)
    last_needed = seq_index * local_tokens + local_tokens - 1
    start_state = (
        jnp.full((batch_rows, local_heads, local_tokens), NEGATIVE_FILL, single),
        jnp.zeros((batch_rows, local_heads, local_tokens), single),
        jnp.zeros((batch_rows, local_heads, local_tokens, HEAD_DIM), single),
    )
    key_piece = lax.all_gather(keys, "seq", axis=1, tiled=True)
    value_piece = lax.all_gather(values, "seq", axis=1, tiled=True)
    piece_rows = key_piece.shape[1]
    fold_key_block = math.gcd(piece_rows, 512)

    def fold_step(block_index, state):
        running_max, running_sum, running_out = state
        begin = block_index * fold_key_block

        def fold_work(unused):
            key_heads = lax.dynamic_slice_in_dim(
                key_piece, block_index * fold_key_block, fold_key_block, 1
            ).reshape(batch_rows, fold_key_block, local_heads, HEAD_DIM)
            value_heads = lax.dynamic_slice_in_dim(
                value_piece, block_index * fold_key_block, fold_key_block, 1
            ).reshape(batch_rows, fold_key_block, local_heads, HEAD_DIM)
            scores = jnp.einsum(
                "rqhe,rkhe->rhqk", query_heads, key_heads, preferred_element_type=single
            )
            allowed = key_mask(doc_start, query_pos, begin, fold_key_block)
            scores = jnp.where(allowed, scores, NEGATIVE_FILL)
            new_max = jnp.maximum(running_max, jnp.max(scores, axis=-1))
            weights = jnp.where(allowed, jnp.exp(scores - new_max[..., None]), 0.0)
            decay = jnp.exp(running_max - new_max)
            new_sum = running_sum * decay + jnp.sum(weights, axis=-1)
            new_out = running_out * decay[..., None] + jnp.einsum(
                "rhqk,rkhe->rhqe",
                weights.astype(bfloat),
                value_heads,
                preferred_element_type=single,
            )
            return (new_max, new_sum, new_out)

        def keep_state(unused):
            return (running_max, running_sum, running_out)

        needed = (begin <= last_needed) & (begin + fold_key_block - 1 >= first_needed)
        return lax.cond(needed, fold_work, keep_state, 0)

    running_max, running_sum, running_out = lax.fori_loop(
        0, piece_rows // fold_key_block, fold_step, start_state
    )
    log_total = running_max + jnp.log(running_sum)
    attended = running_out / running_sum[..., None]
    attended_low = (
        attended.transpose(0, 2, 1, 3).reshape(batch_rows, local_tokens, half_width).astype(bfloat)
    )
    branch = jnp.einsum("rth,dh->rtd", attended_low, out_weight, preferred_element_type=single)
    middle = whole + lax.psum(branch.astype(jnp.bfloat16), "tp").astype(jnp.float32)
    middle_share = lax.dynamic_slice_in_dim(middle, tp_index * half_width, half_width, 2)
    root_two = inverse_root(middle)
    scaled_two = middle * root_two
    normed_two = (scaled_two * ffn_gain).astype(bfloat)
    gate = jnp.einsum("rtd,df->rtf", normed_two, gate_weight, preferred_element_type=single)
    up_proj = jnp.einsum("rtd,df->rtf", normed_two, up_weight, preferred_element_type=single)
    sigma = jax.nn.sigmoid(gate)
    activated = gate * sigma
    hidden = (activated * up_proj).astype(bfloat)
    ffn_part = jnp.einsum("rtf,df->rtd", hidden, down_weight, preferred_element_type=single)
    output = (
        middle_share
        + lax.psum_scatter(
            ffn_part.astype(jnp.bfloat16), "tp", scatter_dimension=2, tiled=True
        ).astype(jnp.float32)
    ).astype(bfloat)
    grad_out = lax.all_gather(cotangent, "tp", axis=2, tiled=True)
    d_hidden = jnp.einsum("rtd,df->rtf", grad_out, down_weight, preferred_element_type=single)
    d_gate = (d_hidden * up_proj * sigma * (1.0 + gate * (1.0 - sigma))).astype(bfloat)
    d_up = (d_hidden * activated).astype(bfloat)
    d_two_part = jnp.einsum(
        "rtf,df->rtd", d_gate, gate_weight, preferred_element_type=single
    ) + jnp.einsum("rtf,df->rtd", d_up, up_weight, preferred_element_type=single)
    d_two = lax.psum(d_two_part.astype(jnp.bfloat16), "tp").astype(jnp.float32)
    gained_two = d_two * ffn_gain
    d_middle = (
        grad_out.astype(single)
        + root_two * gained_two
        - middle * root_two**3 * jnp.mean(gained_two * middle, axis=-1, keepdims=True)
    )
    normed_rows = normed_two
    gate_term = jnp.einsum("rtd,rtf->df", normed_rows, d_gate, preferred_element_type=single)
    up_term = jnp.einsum("rtd,rtf->df", normed_rows, d_up, preferred_element_type=single)
    down_term = jnp.einsum("rtd,rtf->df", grad_out, hidden, preferred_element_type=single)
    gain_term = jnp.sum(d_two * scaled_two, axis=(0, 1))
    gate_grad, up_grad, down_grad, ffn_gain_grad = lax.psum_scatter(
        (gate_term, up_term, down_term, gain_term), "seq", scatter_dimension=0, tiled=True
    )
    error = d_middle.astype(bfloat)
    d_attended = jnp.einsum("rtd,dh->rth", error, out_weight, preferred_element_type=single).astype(
        bfloat
    )
    d_heads = d_attended.reshape(batch_rows, local_tokens, local_heads, HEAD_DIM)
    carried = jnp.einsum("rqhe,rhqe->rhq", d_heads.astype(single), attended)
    key_all, value_all = (
        lax.all_gather(keys, "seq", axis=1, tiled=True),
        lax.all_gather(values, "seq", axis=1, tiled=True),
    )
    key_block = math.gcd(row_length, 512)

    def block_terms(begin):
        key_heads = lax.dynamic_slice_in_dim(key_all, begin, key_block, 1).reshape(
            batch_rows, key_block, local_heads, HEAD_DIM
        )
        value_heads = lax.dynamic_slice_in_dim(value_all, begin, key_block, 1).reshape(
            batch_rows, key_block, local_heads, HEAD_DIM
        )
        scores = jnp.einsum(
            "rqhe,rkhe->rhqk", query_heads, key_heads, preferred_element_type=single
        )
        allowed = key_mask(doc_start, query_pos, begin, key_block)
        probs = jnp.where(
            allowed, jnp.exp(jnp.where(allowed, scores, NEGATIVE_FILL) - log_total[..., None]), 0.0
        )
        d_probs = jnp.einsum("rqhe,rkhe->rhqk", d_heads, value_heads, preferred_element_type=single)
        d_scores = (probs * (d_probs - carried[..., None])).astype(bfloat)
        query_part = jnp.einsum(
            "rhqk,rkhe->rhqe", d_scores, key_heads, preferred_element_type=single
        )
        return (probs, d_scores, query_part)

    query_zero = jnp.zeros((batch_rows, local_heads, local_tokens, HEAD_DIM), single)

    def back_step(block_index, state):
        d_query, key_terms, value_terms = state
        begin = block_index * key_block

        def back_work(unused):
            probs, d_scores, query_part = block_terms(begin)
            value_part = jnp.einsum(
                "rhqk,rqhe->rkhe", probs.astype(bfloat), d_heads, preferred_element_type=single
            )
            key_part = jnp.einsum(
                "rhqk,rqhe->rkhe", d_scores, query_heads, preferred_element_type=single
            )
            return (
                query_part,
                key_part.reshape(batch_rows, key_block, half_width),
                value_part.reshape(batch_rows, key_block, half_width),
            )

        def skip_block(unused):
            empty_rows = jnp.zeros((batch_rows, key_block, half_width), single)
            return (jnp.zeros_like(d_query), empty_rows, empty_rows)

        needed = (begin <= last_needed) & (begin + key_block - 1 >= first_needed)
        query_part, key_part, value_part = lax.cond(needed, back_work, skip_block, 0)
        return (
            d_query + query_part,
            lax.dynamic_update_slice_in_dim(key_terms, key_part, begin, 1),
            lax.dynamic_update_slice_in_dim(value_terms, value_part, begin, 1),
        )

    back_start = (
        query_zero,
        jnp.zeros((batch_rows, row_length, half_width), single),
        jnp.zeros((batch_rows, row_length, half_width), single),
    )
    d_query, key_terms, value_terms = lax.fori_loop(
        0, row_length // key_block, back_step, back_start
    )
    key_grad, value_grad = (
        lax.psum_scatter(key_terms, "seq", scatter_dimension=1, tiled=True),
        lax.psum_scatter(value_terms, "seq", scatter_dimension=1, tiled=True),
    )
    d_query_rows = (
        d_query.transpose(0, 2, 1, 3).reshape(batch_rows, local_tokens, half_width).astype(bfloat)
    )
    d_one_part = (
        jnp.einsum("rte,de->rtd", d_query_rows, query_weight, preferred_element_type=single)
        * query_scale
    )
    d_one = lax.psum(d_one_part.astype(jnp.bfloat16), "tp").astype(jnp.float32)
    gained_one = d_one * attn_gain
    d_whole = (
        d_middle
        + root_one * gained_one
        - whole * root_one**3 * jnp.mean(gained_one * whole, axis=-1, keepdims=True)
    )
    input_grad = lax.dynamic_slice_in_dim(d_whole, tp_index * half_width, half_width, 2)
    normed_rows = normed_one
    query_term = (
        jnp.einsum("rtd,rte->de", normed_rows, d_query_rows, preferred_element_type=single)
        * query_scale
    )
    out_term = jnp.einsum("rtd,rth->dh", error, attended_low, preferred_element_type=single)
    gain_term = jnp.sum(d_one * scaled_one, axis=(0, 1))
    query_grad, out_grad, attn_gain_grad = lax.psum_scatter(
        (query_term, out_term, gain_term), "seq", scatter_dimension=0, tiled=True
    )
    return (
        output,
        input_grad,
        key_grad,
        value_grad,
        attn_gain_grad,
        query_grad,
        out_grad,
        ffn_gain_grad,
        gate_grad,
        up_grad,
        down_grad,
    )


def solution(mesh):
    in_specs = (
        P(None, "seq", "tp"),
        P(None, "seq"),
        P(None, "seq", "tp"),
        P(None, "seq", "tp"),
        P(),
        P(None, "tp"),
        P(None, "tp"),
        P(),
        P(None, "tp"),
        P(None, "tp"),
        P(None, "tp"),
        P(None, "seq", "tp"),
    )
    out_specs = (
        P(None, "seq", "tp"),
        P(None, "seq", "tp"),
        P(None, "seq", "tp"),
        P(None, "seq", "tp"),
        P("seq"),
        P("seq", "tp"),
        P("seq", "tp"),
        P("seq"),
        P("seq", "tp"),
        P("seq", "tp"),
        P("seq", "tp"),
    )
    n = mesh.shape["seq"]

    def step(inputs, *others):
        rows, tok, half = inputs.shape
        units = rows * (half // HEAD_DIM)
        if units == n == PLANE * PLANE and tok == LANE and mesh.shape["tp"] == 2 and -(-others[7].shape[1] // (2 * LANE)) % 2:
            return fast_device(n, inputs, *others)
        return per_device(inputs, *others)

    return jax.shard_map(
        step, mesh=mesh, in_specs=in_specs, out_specs=out_specs, check_vma=False
    )
```
